32 devices in a mesh: seq: 16 (over z, y, x), head: 2 (over core).
Axes of the slice: x: 2, y: 2, z: 4, core: 2. Of those that a mesh axis runs over, the one named last changes fastest.
Arguments:
- tokens: bfloat16 [16384, 1024], P('seq'), may hold values from -6 to 6
- cotangent: bfloat16 [16384, 1024], P('seq'), may hold values from -6 to 6
- lengths: int32 [8], replicated, may hold values from 1024 to 8192, as said below
- packing: int32 [8], replicated, may hold values from 0 to 7, each once
- owners: int32 [2, 49], P('head'), may hold values from 0 to 63, as said below
- slot_copy: bfloat16 [128, 1024, 128], P(('seq', 'head')), may hold values from -0.1875 to 0.1875
- slot_master: float32 [128, 1024, 128], P(('seq', 'head')), may hold values from -0.1875 to 0.1875
- slot_first: float32 [128, 1024, 128], P(('seq', 'head'))
- slot_second: float32 [128, 1024, 128], P(('seq', 'head')), as said below
- basis_left: float32 [128, 1024, 1024], P(('seq', 'head')), may hold values from -1 to 1, as said below
- basis_right: float32 [128, 128, 128], P(('seq', 'head')), may hold values from -1 to 1, as said below
- norm_gains: float32 [2, 1024], replicated, may hold values from 0.25 to 1.75
- gains_first: float32 [2, 1024], replicated
- gains_second: float32 [2, 1024], replicated, as said below
- gate_down: float32 [1024, 16], replicated, may hold values from -0.1875 to 0.1875
- down_first: float32 [1024, 16], replicated
- down_second: float32 [1024, 16], replicated, as said below
- gate_up: float32 [17, 512], P(None, 'head')
- upper_first: float32 [17, 512], P(None, 'head')
- upper_second: float32 [17, 512], P(None, 'head'), as said below
- head_gain: float32 [256], replicated, may hold values from 0.25 to 1.75
- head_first: float32 [256], replicated
- head_second: float32 [256], replicated, as said below
- conv_weight: float32 [4, 2048], P(None, 'head'), may hold values from -3 to 3
- conv_first: float32 [4, 2048], P(None, 'head')
- conv_second: float32 [4, 2048], P(None, 'head'), as said below
Outputs:
- result: bfloat16 [16384, 1024], P('seq')
- input_grad: float32 [16384, 1024], P('seq')
- slot_grad: float32 [128, 1024, 128], P(('seq', 'head'))
- master_new: float32 [128, 1024, 128], P(('seq', 'head'))
- first_new: float32 [128, 1024, 128], P(('seq', 'head'))
- second_new: float32 [128, 1024, 128], P(('seq', 'head'))
- copy_new: bfloat16 [128, 1024, 128], P(('seq', 'head'))
- gains_grad: float32 [2, 1024], replicated
- gains_new: float32 [2, 1024], replicated
- gains_first_new: float32 [2, 1024], replicated
- gains_second_new: float32 [2, 1024], replicated
- down_grad: float32 [1024, 16], replicated
- down_new: float32 [1024, 16], replicated
- down_first_new: float32 [1024, 16], replicated
- down_second_new: float32 [1024, 16], replicated
- upper_grad: float32 [17, 512], P(None, 'head')
- upper_new: float32 [17, 512], P(None, 'head')
- upper_first_new: float32 [17, 512], P(None, 'head')
- upper_second_new: float32 [17, 512], P(None, 'head')
- head_grad: float32 [256], replicated
- head_new: float32 [256], replicated
- head_first_new: float32 [256], replicated
- head_second_new: float32 [256], replicated
- conv_grad: float32 [4, 2048], P(None, 'head')
- conv_new: float32 [4, 2048], P(None, 'head')
- conv_first_new: float32 [4, 2048], P(None, 'head')
- conv_second_new: float32 [4, 2048], P(None, 'head')
The draws below stay inside these ranges and needn't reach their ends.
Inputs may be any that keep to these rules, and one draw needn't show every extreme that they name: `owners`: each row lists 49 distinct slots; slots 0 and 63 appear in every row. The lengths sum to 15872; the largest is 8192. `packing`: each sequence appears once. `basis_left`: every [1024, 1024] slice is orthogonal. `basis_right`: every [128, 128] slice is orthogonal. `slot_second`: Positive. `gains_second`: Positive. `down_second`: Positive. `upper_second`: Positive. `head_second`: Positive. `conv_second`: Positive.
All inputs are finite; a program needn't handle non-finite values.
Results may differ from the reference program's by a relative error of at most 0.0095.
The reference program's roundings to bfloat16 on the way count: a program that leaves them out, or rounds other values in their place, can miss the bound.
Values may be sent and summed in bfloat16 or wider, within the bound.
A program may use at most 256 MiB of HBM per device.

```python
import math
import jax
import jax.numpy as jnp
from jax import lax

D = 1024
DK = 128
DV = 256
RANK = 16
CONV = 4
CH = 64
BW = 128
SHORTEST = 1024
HD = 2
KH = 256
VH = 512
FH = 1408
KALL = 512
CHAN = 1024
CALL = 2048
NBLK = 49
SLOTS_DEV = 4
SLOTS = 64
SLOTS_ALL = 128
TOKENS = 16384
NSEQS = 8
LONGEST = 8192
FILLED = 15872
N_SEQ = 16
N_HEAD = 2


def moment_first(key, shape, typical):
    values = jnp.clip(jax.random.normal(key, shape, jnp.float32), -6.0, 6.0)
    return values * (0.7 * typical * math.sqrt(TOKENS))


def moment_second(key, shape, typical):
    logs = jax.random.uniform(key, shape, jnp.float32, math.log(1.0), math.log(4.0))
    return jnp.exp(logs) * (typical * typical * float(TOKENS))


def orthogonal_table(key, count, order_size):

    def one_table(sub_key):
        sign_key, perm_key = jax.random.split(sub_key)
        signs = jnp.where(jax.random.randint(sign_key, (order_size,), 0, 2) == 1, 1.0, -1.0).astype(jnp.float32)
        freqs = jax.random.permutation(perm_key, order_size).astype(jnp.int32)
        row_ids = jnp.arange(order_size, dtype=jnp.int32)
        phase = (2 * row_ids[:, None] + 1) * freqs[None, :] % (4 * order_size)
        angle = math.pi * phase.astype(jnp.float32) / (2.0 * order_size)
        column_norm = jnp.where(freqs == 0, math.sqrt(1.0 / order_size), math.sqrt(2.0 / order_size)).astype(jnp.float32)
        return signs[:, None] * jnp.cos(angle) * column_norm[None, :]
    return jax.vmap(one_table)(jax.random.split(key, count))


def draw_lengths(key, part):
    weight_key, shuffle_key = jax.random.split(jax.random.fold_in(key, 11))
    others = NSEQS - 1
    spare_total = FILLED - LONGEST - SHORTEST * others
    weights = jax.random.randint(weight_key, (others,), 1, 3).astype(jnp.int32)
    extra_len = (spare_total * weights // jnp.sum(weights)).astype(jnp.int32)
    left_over = spare_total - jnp.sum(extra_len)
    extra_len = extra_len + (jnp.arange(others, dtype=jnp.int32) < left_over).astype(jnp.int32)
    listed = jnp.concatenate([jnp.array([LONGEST], jnp.int32), (SHORTEST + extra_len).astype(jnp.int32)])
    shuffle = jax.random.permutation(shuffle_key, NSEQS).astype(jnp.int32)
    return jnp.take(listed, shuffle).astype(jnp.int32)


def draw_owners(key, part):

    def one_row(sub_key):
        first_key, second_key = jax.random.split(sub_key)
        middle = 1 + jax.random.permutation(first_key, SLOTS - 2)[:NBLK - 2]
        listed = jnp.concatenate([jnp.array([0, SLOTS - 1], jnp.int32), middle.astype(jnp.int32)])
        return jax.random.permutation(second_key, listed).astype(jnp.int32)
    return jax.vmap(one_row)(jax.random.split(key, N_HEAD))


def draw_slot_first(key, part):
    return moment_first(key, (SLOTS_ALL, D, BW), 1.0)


def draw_slot_second(key, part):
    return moment_second(key, (SLOTS_ALL, D, BW), 1.0)


def draw_basis_left(key, part):
    return orthogonal_table(key, SLOTS_ALL, D)


def draw_basis_right(key, part):
    return orthogonal_table(key, SLOTS_ALL, BW)


def draw_gains_first(key, part):
    return moment_first(key, (2, D), 1.0)


def draw_gains_second(key, part):
    return moment_second(key, (2, D), 1.0)


def draw_down_first(key, part):
    return moment_first(key, (D, RANK), 1.0)


def draw_down_second(key, part):
    return moment_second(key, (D, RANK), 1.0)


def draw_gate_up(key, part):
    weight_key, bias_key = jax.random.split(key)
    weights = jnp.clip(jax.random.normal(weight_key, (RANK, KALL), jnp.float32), -6.0, 6.0) / math.sqrt(RANK)
    biases = jax.random.uniform(bias_key, (1, KALL), jnp.float32, 0.0, 7.0)
    return jnp.concatenate([weights, biases], axis=0)


def draw_upper_first(key, part):
    return moment_first(key, (RANK + 1, KALL), 0.3)


def draw_upper_second(key, part):
    return moment_second(key, (RANK + 1, KALL), 0.3)


def draw_head_first(key, part):
    return moment_first(key, (DV,), 2.0)


def draw_head_second(key, part):
    return moment_second(key, (DV,), 2.0)


def draw_conv_first(key, part):
    return moment_first(key, (CONV, CALL), 1.0)


def draw_conv_second(key, part):
    return moment_second(key, (CONV, CALL), 1.0)


def block_levels(rng, shape, shards, low, largest):
    level, own = 1.0, jax.random.fold_in(rng, 6)
    for axis_at, parts in shards:
        steps = jnp.exp(jax.random.uniform(jax.random.fold_in(own, axis_at), (parts,), jnp.float32, low / len(shards), largest / len(shards)))
        level = level * jnp.repeat(steps, shape[axis_at] // parts).reshape([-1 if axis == axis_at else 1 for axis in range(len(shape))])
    return level


def gaussian(own_key, extent, deviation, most, cuts=(), kind=jnp.bfloat16):
    level = block_levels(own_key, extent, cuts, -0.22, 0.18) if cuts else 1.0
    result = jax.random.normal(own_key, extent, jnp.float32) * deviation * level
    return jnp.minimum(jnp.maximum(result, -most), most).astype(kind)


def setup_inputs(seed: int = 0) -> dict:
    keys = jax.random.split(jax.random.key(seed), 27)
    tokens = gaussian(keys[0], (TOKENS, D), 1.0, 6.0, ((0, 16),))
    cotangent = gaussian(keys[1], (TOKENS, D), 1.0, 6.0, ((0, 16),))
    lengths = draw_lengths(jax.random.fold_in(keys[26], 71), 0)
    packing = jax.random.permutation(keys[3], NSEQS).astype(jnp.int32)
    owners = draw_owners(jax.random.fold_in(keys[26], 71), 0)
    slot_copy = gaussian(keys[5], (SLOTS_ALL, D, BW), D ** -0.5, 0.1875, ((0, 32),))
    slot_master = gaussian(keys[6], (SLOTS_ALL, D, BW), D ** -0.5, 0.1875, ((0, 32),), jnp.float32)
    slot_first = draw_slot_first(jax.random.fold_in(keys[26], 71), 0)
    slot_second = draw_slot_second(jax.random.fold_in(keys[26], 71), 0)
    basis_left = draw_basis_left(jax.random.fold_in(keys[26], 71), 0)
    basis_right = draw_basis_right(jax.random.fold_in(keys[26], 71), 0)
    norm_gains = jnp.clip(1.0 + 0.15 * jax.random.normal(keys[11], (2, D), jnp.float32), 0.25, 1.75)
    gains_first = draw_gains_first(jax.random.fold_in(keys[26], 71), 0)
    gains_second = draw_gains_second(jax.random.fold_in(keys[26], 71), 0)
    gate_down = gaussian(keys[14], (D, RANK), D ** -0.5, 0.1875, (), jnp.float32)
    down_first = draw_down_first(jax.random.fold_in(keys[26], 71), 0)
    down_second = draw_down_second(jax.random.fold_in(keys[26], 71), 0)
    gate_up = draw_gate_up(jax.random.fold_in(keys[26], 71), 0)
    upper_first = draw_upper_first(jax.random.fold_in(keys[26], 71), 0)
    upper_second = draw_upper_second(jax.random.fold_in(keys[26], 71), 0)
    head_gain = jnp.clip(1.0 + 0.15 * jax.random.normal(keys[20], (DV,), jnp.float32), 0.25, 1.75)
    head_first = draw_head_first(jax.random.fold_in(keys[26], 71), 0)
    head_second = draw_head_second(jax.random.fold_in(keys[26], 71), 0)
    conv_weight = gaussian(keys[23], (CONV, CALL), CONV ** -0.5, 3.0, ((1, 2),), jnp.float32)
    conv_first = draw_conv_first(jax.random.fold_in(keys[26], 71), 0)
    conv_second = draw_conv_second(jax.random.fold_in(keys[26], 71), 0)
    return {"tokens": tokens, "cotangent": cotangent, "lengths": lengths, "packing": packing, "owners": owners, "slot_copy": slot_copy, "slot_master": slot_master, "slot_first": slot_first, "slot_second": slot_second, "basis_left": basis_left, "basis_right": basis_right, "norm_gains": norm_gains, "gains_first": gains_first, "gains_second": gains_second, "gate_down": gate_down, "down_first": down_first, "down_second": down_second, "gate_up": gate_up, "upper_first": upper_first, "upper_second": upper_second, "head_gain": head_gain, "head_first": head_first, "head_second": head_second, "conv_weight": conv_weight, "conv_first": conv_first, "conv_second": conv_second}


@jax.custom_vjp
def low(v):
    return lax.optimization_barrier(v.astype(jnp.bfloat16)).astype(jnp.float32)

@jax.custom_vjp
def low_back(v):
    return v

def low_keep(v):
    return (low(v), None)

def low_pass(kept, grad):
    return (grad,)

def back_keep(v):
    return (v, None)

def back_low(kept, grad):
    return (low(grad),)
low.defvjp(low_keep, low_pass)
low_back.defvjp(back_keep, back_low)
highest_precision = lax.Precision.HIGHEST
norm_epsilon = 1e-06
adam_epsilon = 1e-08
gate_scale = 16.0
moment_decay = 0.5
rate_block = 0.03
rate_gains = 0.45
rate_down = 0.02
rate_upper = 0.6
rate_head = 0.5
rate_conv = 0.1

def rms_apply(values, gain):
    return values * lax.rsqrt(lax.optimization_barrier(jnp.mean(values * values, axis=-1, keepdims=True)) + norm_epsilon) * gain

def segment_of(positions, lengths, packing):
    packed = jnp.take(lengths, packing).astype(jnp.int32)
    starts = (jnp.cumsum(packed) - packed).astype(jnp.int32)
    filled = jnp.sum(packed).astype(jnp.int32)
    counted = lax.optimization_barrier(jnp.sum((starts[None, :] <= positions[:, None]).astype(jnp.int32), axis=1)).astype(jnp.int32)
    return ((counted + (positions >= filled).astype(jnp.int32)).astype(jnp.int32), positions < filled)

def short_conv(mixed_proj, tap_weights, padded_seg, segments):
    padded = jnp.pad(mixed_proj, ((CONV - 1, 0), (0, 0)))
    conv_total = jnp.zeros(mixed_proj.shape, jnp.float32)
    for tap_index in range(CONV):
        same_seg = (padded_seg[tap_index:tap_index + TOKENS] == segments).astype(jnp.float32)[:, None]
        conv_total = conv_total + tap_weights[tap_index] * padded[tap_index:tap_index + TOKENS] * same_seg
    return conv_total

def gla_scan(queries, keys_all, values_all, log_gate, segments):
    tiles = TOKENS // CH
    queries = queries.reshape(tiles, CH, HD, DK)
    keys_all = keys_all.reshape(tiles, CH, HD, DK)
    values_all = values_all.reshape(tiles, CH, HD, DV)
    log_gate = log_gate.reshape(tiles, CH, HD, DK)
    seg_tiles = segments.reshape(tiles, CH)
    previous = jnp.concatenate([jnp.zeros((1,), jnp.int32), seg_tiles[:-1, -1]]).astype(jnp.int32)
    causal = jnp.tril(jnp.ones((CH, CH), jnp.float32))
    score_scale = DK ** (-0.5)

    def tile_step(current_state, pieces):
        piece_query, piece_keys, segment_value_rows, piece_gate, piece_seg, piece_prev = pieces
        cumulative = jnp.cumsum(piece_gate, axis=0)
        final_cumulative_decay = cumulative[-1]
        incoming_carry = (piece_seg == piece_prev).astype(jnp.float32)
        pair_mask = causal * (piece_seg[:, None] == piece_seg[None, :]).astype(jnp.float32)
        tail_mask = (piece_seg == piece_seg[-1]).astype(jnp.float32)
        query_scaled = piece_query * jnp.exp(cumulative) * score_scale
        k_scaled = piece_keys * jnp.exp(-cumulative)
        key_remainder = piece_keys * jnp.exp(final_cumulative_decay[None] - cumulative) * tail_mask[:, None, None]
        scores = jnp.einsum('thk,shk->hts', query_scaled, k_scaled, precision=highest_precision) * pair_mask[None]
        intra_out = jnp.einsum('hts,shv->thv', scores, segment_value_rows, precision=highest_precision)
        cross_piece_output = jnp.einsum('gme,mei->gmi', query_scaled, current_state, precision=highest_precision) * incoming_carry[:, None, None]
        following_state = (jnp.exp(final_cumulative_decay) * incoming_carry[-1])[..., None] * current_state + jnp.einsum('oze,ozj->zej', key_remainder, segment_value_rows, precision=highest_precision)
        return (following_state, cross_piece_output + intra_out)
    initial = jnp.zeros((HD, DK, DV), jnp.float32)
    final_state, outputs = lax.scan(jax.checkpoint(tile_step), initial, (queries, keys_all, values_all, log_gate, seg_tiles, previous))
    return outputs.reshape(TOKENS, HD, DV)

def plain_adam(param, gradient, first, second, rate):
    first_next = moment_decay * first + (1.0 - moment_decay) * gradient
    second_next = moment_decay * second + (1.0 - moment_decay) * gradient * gradient
    return (param - rate * first_next / (jnp.sqrt(second_next) + adam_epsilon), first_next, second_next)

def reference(tokens, cotangent, lengths, packing, owners, slot_copy, slot_master, slot_first, slot_second, basis_left, basis_right, norm_gains, gains_first, gains_second, gate_down, down_first, down_second, gate_up, upper_first, upper_second, head_gain, head_first, head_second, conv_weight, conv_first, conv_second):
    positions = jnp.arange(TOKENS, dtype=jnp.int32)
    segments, valid_mask = segment_of(positions, lengths, packing)
    padded_seg = jnp.concatenate([jnp.zeros((CONV - 1,), jnp.int32), segments])
    count_in = (2 * KH + 2 * VH) // BW
    count_up = 2 * FH // BW
    count_out = VH // BW
    up_end = count_in + count_up
    out_end = up_end + count_out

    def forward(inputs, slot_values, gains, down_map, upper_map, head_scale, conv_taps):
        shaped = slot_values.reshape(N_SEQ, N_HEAD, SLOTS_DEV, D, BW)
        normed = low(rms_apply(inputs, gains[0]))
        lowrank = jnp.dot(normed, low(down_map), precision=highest_precision)
        attn_branch = jnp.zeros((TOKENS, D), jnp.float32)
        group_blocks = []
        for group_index in range(N_HEAD):
            blocks = jnp.take(shaped[:, group_index].reshape(SLOTS, D, BW), owners[group_index], axis=0)
            group_blocks.append(blocks)
            key_cols = upper_map[:, group_index * KH:(group_index + 1) * KH]
            projected = jnp.einsum('td,ndb->tnb', normed, blocks[:count_in], precision=highest_precision).reshape(TOKENS, count_in * BW)
            mixed_proj = low_back(low(projected[:, :CHAN]))
            gate_pre = low_back(projected[:, CHAN:])
            rank_view = low_back(lowrank)
            logits = jnp.dot(rank_view, key_cols[:RANK], precision=highest_precision) + key_cols[RANK]
            log_gate = jax.nn.log_sigmoid(logits) / gate_scale
            conv_cols = conv_taps[:, group_index * CHAN:(group_index + 1) * CHAN]
            active = jax.nn.silu(short_conv(mixed_proj, conv_cols, padded_seg, segments))
            attended = gla_scan(active[:, :KH], active[:, KH:2 * KH], active[:, 2 * KH:], log_gate, segments)
            head_normed = rms_apply(attended, head_scale)
            gated_out = low((head_normed * jax.nn.silu(gate_pre.reshape(TOKENS, HD, DV))).reshape(TOKENS, count_out, BW))
            attn_branch = attn_branch + jnp.einsum('tnb,ndb->td', gated_out, blocks[up_end:out_end], precision=highest_precision)
        hidden_one = inputs + low_back(attn_branch)
        normed_two = low(rms_apply(hidden_one, gains[1]))
        mlp_branch = jnp.zeros((TOKENS, D), jnp.float32)
        for group_index in range(N_HEAD):
            blocks = group_blocks[group_index]
            pair_proj = jnp.einsum('td,ndb->tnb', normed_two, blocks[count_in:up_end], precision=highest_precision).reshape(TOKENS, 2 * FH)
            gate_mlp = low_back(pair_proj[:, :FH])
            up_mlp = low_back(pair_proj[:, FH:])
            hidden = low(jax.nn.silu(gate_mlp) * up_mlp).reshape(TOKENS, FH // BW, BW)
            mlp_branch = mlp_branch + jnp.einsum('tnb,ndb->td', hidden, blocks[out_end:], precision=highest_precision)
        return low(hidden_one + low_back(mlp_branch))
    inputs = tokens.astype(jnp.float32)
    output, pullback = jax.vjp(forward, inputs, slot_copy.astype(jnp.float32), norm_gains, gate_down, gate_up, head_gain, conv_weight)
    upstream = cotangent.astype(jnp.float32) * valid_mask.astype(jnp.float32)[:, None]
    grad_input, slot_grad, gains_grad, down_grad, upper_grad, head_grad, conv_grad = pullback(upstream)
    rotated = jnp.einsum('sij,sik->sjk', basis_left, slot_grad, precision=highest_precision)
    rotated = jnp.einsum('sjk,skl->sjl', rotated, basis_right, precision=highest_precision)
    first_next = moment_decay * slot_first + (1.0 - moment_decay) * rotated
    second_next = moment_decay * slot_second + (1.0 - moment_decay) * rotated * rotated
    direction = first_next / (jnp.sqrt(second_next) + adam_epsilon)
    restored = jnp.einsum('sij,sjk->sik', basis_left, direction, precision=highest_precision)
    restored = jnp.einsum('sik,slk->sil', restored, basis_right, precision=highest_precision)
    master_next = slot_master - rate_block * restored
    gains_next, gains_first_next, gains_second_next = plain_adam(norm_gains, gains_grad, gains_first, gains_second, rate_gains)
    down_next, down_first_next, down_second_next = plain_adam(gate_down, down_grad, down_first, down_second, rate_down)
    upper_next, upper_first_next, upper_second_next = plain_adam(gate_up, upper_grad, upper_first, upper_second, rate_upper)
    head_next, head_first_next, head_second_next = plain_adam(head_gain, head_grad, head_first, head_second, rate_head)
    conv_next, conv_first_next, conv_second_next = plain_adam(conv_weight, conv_grad, conv_first, conv_second, rate_conv)
    return (output.astype(jnp.bfloat16), grad_input, slot_grad, master_next, first_next, second_next, master_next.astype(jnp.bfloat16), gains_grad, gains_next, gains_first_next, gains_second_next, down_grad, down_next, down_first_next, down_second_next, upper_grad, upper_next, upper_first_next, upper_second_next, head_grad, head_next, head_first_next, head_second_next, conv_grad, conv_next, conv_first_next, conv_second_next)
```

```python
import functools

import jax
import jax.numpy as jnp
from jax import lax
from jax.experimental import pallas as pl
from jax.experimental.pallas import tpu as pltpu
from jax.sharding import PartitionSpec as P

MESH = pl.DeviceIdType.MESH

DK = 128
DV = 256
CH = 64


highest_precision = lax.Precision.HIGHEST
norm_epsilon = 1e-06
adam_epsilon = 1e-08
gate_scale = 16.0
moment_decay = 0.5
rate_block = 0.03
rate_gains = 0.45
rate_down = 0.02
rate_upper = 0.6
rate_head = 0.5
rate_conv = 0.1


def axis_sizes(n):
    side=1
    while (side*2)**2*4<=n: side*=2
    return (n//(side*side),side,side)

def coords(me,sizes):
    Z,Y,X=sizes
    return [me//(Y*X),(me//X)%Y,me%X]

def index_of(c,sizes):
    Z,Y,X=sizes
    return (c[0]*Y+c[1])*X+c[2]

def enter(n,me):
    barrier=pltpu.get_barrier_semaphore()
    for j in range(1,n):
        pl.semaphore_signal(barrier,inc=1,device_id={"seq":lax.rem(me+j,n)},device_id_type=MESH)
    pl.semaphore_wait(barrier,n-1)

def remote(src,dst,ss,rs,peer):
    return pltpu.make_async_remote_copy(src_ref=src,dst_ref=dst,send_sem=ss,recv_sem=rs,device_id={"seq":peer},device_id_type=MESH)

def gather_kernel(n,sizes,plan,owners_ref,slot_ref,out_ref,recv,piece,a_send,a_recv,g_send,g_recv,l_sem):
    me=lax.axis_index("seq"); c=coords(me,sizes)
    sd=slot_ref.shape[0]; rows=piece.shape[0]; bw=slot_ref.shape[2]; nb=owners_ref.shape[1]
    enter(n,me)
    def a2a(j):
        p=lax.rem(me+j,n)
        return remote(slot_ref.at[:,pl.ds(p*rows,rows),:],recv.at[pl.ds(me*sd,sd)],a_send.at[j],a_recv.at[j],p)
    for j in range(1,n): a2a(j).start()
    mine=pltpu.make_async_copy(slot_ref.at[:,pl.ds(me*rows,rows),:],recv.at[pl.ds(me*sd,sd)],l_sem.at[0])
    mine.start(); mine.wait()
    for j in range(1,n): a2a(j).wait()
    for b in range(nb):
        piece[:,b*bw:(b+1)*bw]=recv[owners_ref[0,b]]
    own=pltpu.make_async_copy(piece,out_ref.at[c[0],c[1],c[2]],l_sem.at[1])
    own.start()
    def ag(i,k,j):
        lo,hi,order=plan[i]
        ax=order[k]
        idx=tuple(slice(None) if a in order[:k] else c[a] for a in range(3))+(slice(None),pl.ds(lo*bw,(hi-lo)*bw))
        d=list(c); d[ax]=lax.rem(c[ax]+j,sizes[ax])
        src=piece.at[:,pl.ds(lo*bw,(hi-lo)*bw)] if k==0 else out_ref.at[idx]
        s=(i*3+k)*max(sizes)+j
        return remote(src,out_ref.at[idx],g_send.at[s],g_recv.at[s],index_of(d,sizes))
    own.wait()
    streams={}
    for i,p in enumerate(plan): streams.setdefault(p[2],[]).append(i)
    longest=max([len(v) for v in streams.values()],default=0)
    for s in range(longest+2 if plan else 0):
        for k in (2,1,0):
            for order,ids in streams.items():
                if not 0<=s-k<len(ids): continue
                i=ids[s-k]
                if k:
                    for j in range(1,sizes[order[k-1]]): ag(i,k-1,j).wait_recv()
                for j in range(1,sizes[order[k]]): ag(i,k,j).start()
    for i in range(len(plan)):
        for j in range(1,sizes[plan[i][2][2]]): ag(i,2,j).wait_recv()
    for k in range(3):
        for i in range(len(plan)):
            for j in range(1,sizes[plan[i][2][k]]): ag(i,k,j).wait_send()

def gather_weights(slot_copy,owners,plan):
    n=lax.axis_size("seq"); sizes=axis_sizes(n)
    sd,d,bw=slot_copy.shape; nb=owners.shape[1]; rows=d//n
    out=pl.pallas_call(functools.partial(gather_kernel,n,sizes,plan),
        out_shape=jax.ShapeDtypeStruct(sizes+(rows,nb*bw),slot_copy.dtype),
        in_specs=[pl.BlockSpec(memory_space=pltpu.SMEM),pl.BlockSpec(memory_space=pl.ANY)],
        out_specs=pl.BlockSpec(memory_space=pl.ANY),
        scratch_shapes=[pltpu.VMEM((n*sd,rows,bw),slot_copy.dtype),pltpu.VMEM((rows,nb*bw),slot_copy.dtype),
            pltpu.SemaphoreType.DMA((n,)),pltpu.SemaphoreType.DMA((n,)),
            pltpu.SemaphoreType.DMA((len(plan)*3*max(sizes),)),pltpu.SemaphoreType.DMA((len(plan)*3*max(sizes),)),
            pltpu.SemaphoreType.DMA((2,))],
        compiler_params=pltpu.CompilerParams(collective_id=1,has_side_effects=True,vmem_limit_bytes=48<<20),
    )(owners,slot_copy)
    return out.reshape(d,nb*bw)

def scatter_kernel(n,sizes,plan,nin,inv_ref,*refs):
    g_refs=refs[:nin]; out_ref=refs[nin];
    np_=len(plan)
    sc=refs[nin+1:]
    own=sc[0:np_]; b0=sc[np_:2*np_]; b1=sc[2*np_:3*np_]; b2=sc[3*np_:4*np_]
    fin,send,r_send,r_recv,a_send,a_recv,l_sem=sc[4*np_:]
    me=lax.axis_index("seq"); c=coords(me,sizes)
    sd,_,rows,bw=out_ref.shape
    nb=fin.shape[0]-1
    bufs=(b0,b1,b2)
    def part(view,done,left,coord):
        pass
    enter(n,me)
    loads=[]
    for i,(a,lo,hi,base,order) in enumerate(plan):
        ax=order[0]
        idx=tuple(c[ax] if q==ax else slice(None) for q in range(3))+(slice(None),pl.ds(lo*bw,(hi-lo)*bw))
        cp=pltpu.make_async_copy(g_refs[a].at[idx],own[i],l_sem.at[i]); cp.start(); loads.append(cp)
    def rs(i,k,j):
        a,lo,hi,base,order=plan[i]
        ax=order[k]
        d=list(c); d[ax]=lax.rem(c[ax]+j,sizes[ax])
        left=sorted(set(range(3))-set(order[:k]))
        idx=tuple(d[ax] if q==ax else slice(None) for q in left)
        if k==0: src=g_refs[a].at[idx+(slice(None),pl.ds(lo*bw,(hi-lo)*bw))]
        elif k==1: src=own[i].at[idx]
        else: src=b1[i].at[(0,)+idx]
        dst=bufs[k][i].at[j]
        s=(i*3+k)*max(sizes)+j
        return remote(src,dst,r_send.at[s],r_recv.at[s],index_of(d,sizes))
    fin[nb]=jnp.zeros(fin.shape[1:],fin.dtype)
    def combine(i,k):
        a,lo,hi,base,order=plan[i]
        if k==0: loads[i].wait()
        for j in range(1,sizes[order[k]]): rs(i,k,j).wait_recv()
        if k==0:
            s0,s1=own[i].shape[0],own[i].shape[1]
            def add0(t,_):
                u,v=t//s1,t%s1
                tot=own[i][u,v].astype(jnp.float32)
                for j in range(1,sizes[order[0]]): tot=tot+b0[i][j,u,v].astype(jnp.float32)
                own[i][u,v]=tot.astype(own[i].dtype)
                return 0
            lax.fori_loop(0,s0*s1,add0,0)
        elif k==1:
            pos=sorted(set(range(3))-set(order[:1])).index(order[1])
            def add1(t,_):
                at=(c[order[1]],t) if pos==0 else (t,c[order[1]])
                tot=own[i][at].astype(jnp.float32)
                for j in range(1,sizes[order[1]]): tot=tot+b1[i][j,t].astype(jnp.float32)
                b1[i][0,t]=tot.astype(own[i].dtype)
                return 0
            lax.fori_loop(0,sizes[order[2]],add1,0)
        else:
            tot=b1[i][0,c[order[2]]].astype(jnp.float32)
            for j in range(1,sizes[order[2]]): tot=tot+b2[i][j].astype(jnp.float32)
            for b in range(lo,hi): fin[base+b-lo]=tot[:,(b-lo)*bw:(b-lo+1)*bw].astype(fin.dtype)
    streams={}
    for i,p in enumerate(plan): streams.setdefault(p[4],[]).append(i)
    longest=max([len(v) for v in streams.values()],default=0)
    for s in range(longest+3 if plan else 0):
        for k in range(4):
            for order,ids in streams.items():
                if not 0<=s-k<len(ids): continue
                i=ids[s-k]
                if k: combine(i,k-1)
                if k<3:
                    for j in range(1,sizes[order[k]]): rs(i,k,j).start()
    for s in range(send.shape[0]): send[s]=fin[inv_ref[0,s]]
    def a2a(j):
        p=lax.rem(me+j,n)
        return remote(send.at[pl.ds(p*sd,sd)],out_ref.at[:,me],a_send.at[j],a_recv.at[j],p)
    for j in range(1,n): a2a(j).start()
    mine=pltpu.make_async_copy(send.at[pl.ds(me*sd,sd)],out_ref.at[:,me],l_sem.at[np_])
    mine.start(); mine.wait()
    for j in range(1,n): a2a(j).wait()
    for k in range(3):
        for i in range(np_):
            for j in range(1,sizes[plan[i][4][k]]): rs(i,k,j).wait_send()

def scatter_grads(grads,inverse,plan,slots_dev,nb):
    n=lax.axis_size("seq"); sizes=axis_sizes(n)
    d=grads[0].shape[0]; bw=128; rows=d//n
    views=[g.reshape(sizes+(rows,g.shape[1])) for g in grads]
    dt=grads[0].dtype
    own=[];b0=[];b1=[];b2=[]
    for a,lo,hi,base,order in plan:
        w=(hi-lo)*bw
        rem=[sizes[q] for q in range(3) if q!=order[0]]
        own.append(pltpu.VMEM(tuple(rem)+(rows,w),dt))
        b0.append(pltpu.VMEM((sizes[order[0]],)+tuple(rem)+(rows,w),dt))
        b1.append(pltpu.VMEM((sizes[order[1]],sizes[order[2]],rows,w),dt))
        b2.append(pltpu.VMEM((sizes[order[2]],rows,w),dt))
    m=len(plan)*3*max(sizes)
    out=pl.pallas_call(functools.partial(scatter_kernel,n,sizes,plan,len(views)),
        out_shape=jax.ShapeDtypeStruct((slots_dev,n,rows,bw),dt),
        in_specs=[pl.BlockSpec(memory_space=pltpu.SMEM)]+[pl.BlockSpec(memory_space=pl.ANY)]*len(views),
        out_specs=pl.BlockSpec(memory_space=pl.ANY),
        scratch_shapes=own+b0+b1+b2+[pltpu.VMEM((nb+1,rows,bw),dt),pltpu.VMEM((slots_dev*n,rows,bw),dt),
            pltpu.SemaphoreType.DMA((m,)),pltpu.SemaphoreType.DMA((m,)),pltpu.SemaphoreType.DMA((n,)),pltpu.SemaphoreType.DMA((n,)),
            pltpu.SemaphoreType.DMA((len(plan)+1,))],
        compiler_params=pltpu.CompilerParams(collective_id=2,has_side_effects=True,vmem_limit_bytes=60<<20),
    )(inverse,*views)
    return out.reshape(slots_dev,d,bw)


def build_plan(widths, parts, pieces, orders):
    total = sum(widths)
    bounds = [sum(widths[:i]) for i in range(len(widths) + 1)]
    cuts = [round(total * f) for f in (0.0,) + parts]
    plan, at = [], 0
    for i in range(pieces):
        for order, lo, hi in zip(orders, cuts[:-1], cuts[1:], strict=True):
            size = hi - lo
            left = size * (i + 1) // pieces - size * i // pieces
            while left:
                which = max(q for q in range(len(widths)) if bounds[q] <= at)
                step = min(left, bounds[which + 1] - at)
                start = at - bounds[which]
                plan.append((which, start, start + step, at, order))
                at += step
                left -= step
    return plan


def sum_kernel(n, sizes, shared, x_ref, out_ref, mate, acc, bufs, send, recv):
    me, core = lax.axis_index("seq"), lax.axis_index("head")
    c = coords(me, sizes)
    barrier = pltpu.get_barrier_semaphore()
    peers = []
    for ax in range(3):
        for j in range(1, sizes[ax]):
            d = list(c)
            d[ax] = lax.rem(c[ax] + j, sizes[ax])
            peers.append((ax, j, index_of(d, sizes)))
    for _, _, p in peers:
        pl.semaphore_signal(barrier, inc=1, device_id={"seq": p}, device_id_type=MESH)
    pl.semaphore_signal(barrier, inc=1, device_id={"head": 1 - core}, device_id_type=MESH)
    pl.semaphore_wait(barrier, len(peers) + 1)
    swap = pltpu.make_async_remote_copy(
        src_ref=x_ref.at[pl.ds(0, shared)],
        dst_ref=mate,
        send_sem=send.at[0],
        recv_sem=recv.at[0],
        device_id={"head": 1 - core},
        device_id_type=MESH,
    )
    swap.start()
    swap.wait()
    acc[0, 0:shared] = x_ref[0:shared] + mate[...]
    acc[0, shared:] = x_ref[shared:]
    copies = []
    for step, ax in enumerate((2, 1, 0)):
        bufs[ax, c[ax]] = acc[step]
        going = []
        for q, j, p in peers:
            if q == ax:
                going.append(
                    remote(
                        acc.at[step],
                        bufs.at[ax, c[ax]],
                        send.at[1 + ax * max(sizes) + j],
                        recv.at[1 + ax * max(sizes) + j],
                        p,
                    )
                )
        for copy in going:
            copy.start()
        for copy in going:
            copy.wait_recv()
        total = bufs[ax, 0]
        for j in range(1, sizes[ax]):
            total = total + bufs[ax, j]
        if step < 2:
            acc[step + 1] = total
        else:
            out_ref[...] = total
        copies += going
    for copy in copies:
        copy.wait_send()


def sum_small(x, shared):
    n = lax.axis_size("seq")
    sizes = axis_sizes(n)
    most = max(sizes)
    return pl.pallas_call(
        functools.partial(sum_kernel, n, sizes, shared),
        out_shape=jax.ShapeDtypeStruct(x.shape, x.dtype),
        scratch_shapes=[
            pltpu.VMEM((shared,) + x.shape[1:], x.dtype),
            pltpu.VMEM((3,) + x.shape, x.dtype),
            pltpu.VMEM((3, most) + x.shape, x.dtype),
            pltpu.SemaphoreType.DMA((1 + 3 * most,)),
            pltpu.SemaphoreType.DMA((1 + 3 * most,)),
        ],
        compiler_params=pltpu.CompilerParams(
            collective_id=3, has_side_effects=True, vmem_limit_bytes=32 << 20
        ),
    )(x)


def passed_along(array, axis, by):
    devices = lax.axis_size(axis)
    pairs = [(i, i + by) for i in range(devices) if 0 <= i + by < devices]
    return lax.ppermute(array, axis, pairs)


def carried_in(value, axis, join, neutral, backward):
    count, mine = (lax.axis_size(axis), lax.axis_index(axis))
    pieces = jax.tree.map(lambda part: lax.all_gather(part, axis), value)
    if backward:
        pieces = jax.tree.map(lambda part: part[::-1], pieces)
        mine = count - 1 - mine
    running = jax.tree.map(
        lambda part, zero: jnp.full_like(part, 0) + jnp.asarray(zero, part.dtype), value, neutral
    )

    def step(position, running):
        longer = join(running, jax.tree.map(lambda part: part[position], pieces))
        return jax.tree.map(lambda new, old: jnp.where(position < mine, new, old), longer, running)

    return lax.fori_loop(0, count - 1, step, running)


def rms_stats(values):
    return lax.rsqrt(jnp.mean(values * values, axis=-1, keepdims=True) + norm_epsilon)


def rms_back(values, inverse, gain, upstream):
    scaled = gain * upstream
    return inverse * scaled - values * inverse * inverse * inverse * jnp.mean(
        scaled * values, axis=-1, keepdims=True
    )


def swish_slope(values):
    sigmoid = jax.nn.sigmoid(values)
    return sigmoid * (1.0 + values * (1.0 - sigmoid))


def segment_of(positions, lengths, packing):
    packed = jnp.take(lengths, packing)
    starts = jnp.cumsum(packed) - packed
    filled = jnp.sum(packed)
    counted = jnp.sum((starts[None, :] <= positions[:, None]).astype(jnp.int32), axis=1)
    return (counted + (positions >= filled).astype(jnp.int32), positions < filled)


def compose(earlier, later_part):
    return (earlier[0] * later_part[0], later_part[0][..., None] * earlier[1] + later_part[1])


def advance(current_state, piece_pair):
    return (piece_pair[0][..., None] * current_state + piece_pair[1], current_state)


def retreat(adjoint, piece_pair):
    return (piece_pair[1] + piece_pair[0][..., None] * adjoint, adjoint)


def plain_adam(param, gradient, first, second, rate):
    first_next = moment_decay * first + (1.0 - moment_decay) * gradient
    second_next = moment_decay * second + (1.0 - moment_decay) * gradient * gradient
    return (
        param - rate * first_next / (jnp.sqrt(second_next) + adam_epsilon),
        first_next,
        second_next,
    )


def body(
    tokens,
    cotangent,
    lengths,
    packing,
    owners,
    slot_copy,
    slot_master,
    slot_first,
    slot_second,
    basis_left,
    basis_right,
    norm_gains,
    gains_first,
    gains_second,
    gate_down,
    down_first,
    down_second,
    gate_up,
    upper_first,
    upper_second,
    head_gain,
    head_first,
    head_second,
    conv_weight,
    conv_first,
    conv_second,
):
    tok_rows = tokens.shape[0]
    model_width = tokens.shape[1]
    block_width = slot_copy.shape[2]
    rank_width = gate_down.shape[1]
    tap_count = conv_weight.shape[0]
    key_width = gate_up.shape[1]
    channels = conv_weight.shape[1]
    value_width = channels - 2 * key_width
    heads_here = key_width // DK
    tile_len = CH
    tiles = tok_rows // tile_len
    block_total = owners.shape[1]
    count_in = (channels + value_width) // block_width
    count_out = value_width // block_width
    count_down = (block_total - count_in - count_out) // 3
    count_up = 2 * count_down
    up_end = count_in + count_up
    out_end = up_end + count_out
    score_scale = DK ** (-0.5)
    seq_index = lax.axis_index("seq")
    base_pos = seq_index * tok_rows
    ext_pos = base_pos - (tap_count - 1) + jnp.arange(tok_rows + tap_count - 1, dtype=jnp.int32)
    ext_seg, ext_valid = segment_of(ext_pos, lengths, packing)
    own_seg = ext_seg[tap_count - 1 :]
    own_valid = ext_valid[tap_count - 1 :].astype(jnp.float32)
    tile_prev = segment_of(
        base_pos - 1 + tile_len * jnp.arange(tiles, dtype=jnp.int32), lengths, packing
    )[0]
    weights = gather_weights(
        slot_copy,
        owners,
        [
            (at, at + hi - lo, order)
            for _, lo, hi, at, order in build_plan(
                (block_total,), (0.43, 0.86, 1.0), 4, ((0, 1, 2), (0, 2, 1), (2, 1, 0))
            )
        ],
    )
    in_weights = weights[:, : count_in * block_width]
    up_weights = weights[:, count_in * block_width : up_end * block_width]
    out_weights = weights[:, up_end * block_width : out_end * block_width]
    down_weights = weights[:, out_end * block_width :]
    inputs = tokens.astype(jnp.float32)
    inverse_one = rms_stats(inputs)
    normed = (inputs * inverse_one * norm_gains[0]).astype(jnp.bfloat16)
    projected = jnp.dot(normed, in_weights, preferred_element_type=jnp.float32)
    mixed_proj = projected[:, :channels].astype(jnp.bfloat16)
    gate_pre = projected[:, channels:]
    down_low = gate_down.astype(jnp.bfloat16)
    lowrank = jnp.dot(normed, down_low, preferred_element_type=jnp.float32)
    logits = (
        jnp.dot(lowrank, gate_up[:rank_width], precision=highest_precision) + gate_up[rank_width]
    )
    log_gate = jax.nn.log_sigmoid(logits) / gate_scale
    rim_rows = passed_along(mixed_proj[tok_rows - (tap_count - 1) :], "seq", 1)
    extended = jnp.concatenate([rim_rows, mixed_proj], axis=0).astype(jnp.float32)
    same_seg = []
    conv_pre = jnp.zeros((tok_rows, channels), jnp.float32)
    for tap_index in range(tap_count):
        tap_mask = (ext_seg[tap_index : tap_index + tok_rows] == own_seg).astype(jnp.float32)[
            :, None
        ]
        same_seg.append(tap_mask)
        conv_pre = (
            conv_pre
            + conv_weight[tap_index] * extended[tap_index : tap_index + tok_rows] * tap_mask
        )
    active = jax.nn.silu(conv_pre)
    queries = active[:, :key_width].reshape(tiles, tile_len, heads_here, DK)
    keys_all = active[:, key_width : 2 * key_width].reshape(tiles, tile_len, heads_here, DK)
    values_all = active[:, 2 * key_width :].reshape(tiles, tile_len, heads_here, DV)
    log_gates = log_gate.reshape(tiles, tile_len, heads_here, DK)
    seg_tiles = own_seg.reshape(tiles, tile_len)
    incoming_carry = (seg_tiles == tile_prev[:, None]).astype(jnp.float32)
    causal = jnp.tril(jnp.ones((tile_len, tile_len), jnp.float32))
    pair_mask = causal[None] * (seg_tiles[:, :, None] == seg_tiles[:, None, :]).astype(jnp.float32)
    tail_mask = (seg_tiles == seg_tiles[:, -1:]).astype(jnp.float32)
    cumulative = jnp.cumsum(log_gates, axis=1)
    final_cumulative_decay = cumulative[:, -1]
    query_scaled = queries * jnp.exp(cumulative) * score_scale
    k_scaled = keys_all * jnp.exp(-cumulative)
    key_remainder = (
        keys_all
        * jnp.exp(final_cumulative_decay[:, None] - cumulative)
        * tail_mask[:, :, None, None]
    )
    scores = (
        jnp.einsum("cthk,cshk->chts", query_scaled, k_scaled, precision=highest_precision)
        * pair_mask[:, None]
    )
    intra_out = jnp.einsum("chts,cshv->cthv", scores, values_all, precision=highest_precision)
    contrib = jnp.einsum("cshk,cshv->chkv", key_remainder, values_all, precision=highest_precision)
    tile_decay = jnp.exp(final_cumulative_decay) * incoming_carry[:, -1][:, None, None]
    zero_state = jnp.zeros((heads_here, DK, DV), jnp.float32)
    unit_decay = jnp.ones((heads_here, DK), jnp.float32)
    local_end, local_start = lax.scan(advance, zero_state, (tile_decay, contrib))
    running = jnp.cumprod(tile_decay, axis=0)
    before = jnp.concatenate([unit_decay[None], running[:-1]], axis=0)
    device_decay = running[-1]
    incoming = carried_in(
        (device_decay, local_end), "seq", compose, (unit_decay, zero_state), False
    )[1]
    start_state = before[..., None] * incoming[None] + local_start
    cross_piece_output = (
        jnp.einsum("cthk,chkv->cthv", query_scaled, start_state, precision=highest_precision)
        * incoming_carry[:, :, None, None]
    )
    attended = (cross_piece_output + intra_out).reshape(tok_rows, heads_here, DV)
    inverse_head = rms_stats(attended)
    head_normed = attended * inverse_head * head_gain
    gate_view = gate_pre.reshape(tok_rows, heads_here, DV)
    swished = jax.nn.silu(gate_view)
    gated_out = (head_normed * swished).reshape(tok_rows, value_width).astype(jnp.bfloat16)
    attn_part = jnp.einsum(
        "tn,dn->td", gated_out, out_weights, preferred_element_type=jnp.float32
    )
    attn_branch = lax.psum(attn_part, "head")
    hidden_one = inputs + attn_branch
    inverse_two = rms_stats(hidden_one)
    normed_two = (hidden_one * inverse_two * norm_gains[1]).astype(jnp.bfloat16)
    pair_proj = jnp.dot(normed_two, up_weights, preferred_element_type=jnp.float32)
    half_width = pair_proj.shape[1] // 2
    gate_mlp = pair_proj[:, :half_width]
    up_mlp = pair_proj[:, half_width:]
    hidden = (jax.nn.silu(gate_mlp) * up_mlp).astype(jnp.bfloat16)
    mlp_part = jnp.einsum("tn,dn->td", hidden, down_weights, preferred_element_type=jnp.float32)
    mlp_branch = lax.psum(mlp_part.astype(jnp.bfloat16), "head").astype(jnp.float32)
    result = (hidden_one + mlp_branch).astype(jnp.bfloat16)
    upstream = cotangent.astype(jnp.float32) * own_valid[:, None]
    upstream_low = upstream.astype(jnp.bfloat16)
    grad_hidden = jnp.dot(upstream_low, down_weights, preferred_element_type=jnp.float32)
    grad_gate_mlp = grad_hidden * up_mlp * swish_slope(gate_mlp)
    grad_up_mlp = grad_hidden * jax.nn.silu(gate_mlp)
    grad_pair = jnp.concatenate([grad_gate_mlp, grad_up_mlp], axis=1).astype(jnp.bfloat16)
    grad_normed_two = lax.psum(
        jnp.einsum("tn,dn->td", grad_pair, up_weights, preferred_element_type=jnp.float32), "head"
    )
    grad_gains_two = jnp.sum(grad_normed_two * hidden_one * inverse_two, axis=0)
    grad_one = upstream + rms_back(hidden_one, inverse_two, norm_gains[1], grad_normed_two)
    grad_attn = grad_one.astype(jnp.bfloat16)
    grad_gated = jnp.dot(grad_attn, out_weights, preferred_element_type=jnp.float32).reshape(
        tok_rows, heads_here, DV
    )
    grad_gate_pre = (grad_gated * head_normed * swish_slope(gate_view)).reshape(
        tok_rows, value_width
    )
    grad_head_normed = grad_gated * swished
    grad_head_gain = jnp.sum(grad_head_normed * attended * inverse_head, axis=(0, 1))
    grad_attended = rms_back(attended, inverse_head, head_gain, grad_head_normed)
    grad_out = grad_attended.reshape(tiles, tile_len, heads_here, DV)
    weighted = jnp.einsum(
        "cthk,cthv->chkv",
        query_scaled * incoming_carry[:, :, None, None],
        grad_out,
        precision=highest_precision,
    )
    local_adjoint, local_end_adj = lax.scan(
        retreat, zero_state, (tile_decay, weighted), reverse=True
    )
    reverse_run = jnp.cumprod(tile_decay[::-1], axis=0)[::-1]
    after_decay = jnp.concatenate([reverse_run[1:], unit_decay[None]], axis=0)
    outgoing = carried_in(
        (device_decay, local_adjoint), "seq", compose, (unit_decay, zero_state), True
    )[1]
    end_adjoint = after_decay[..., None] * outgoing[None] + local_end_adj
    end_state = tile_decay[..., None] * start_state + contrib
    grad_scores = (
        jnp.einsum("cthv,cshv->chts", grad_out, values_all, precision=highest_precision)
        * pair_mask[:, None]
    )
    grad_q_scaled = jnp.einsum(
        "chts,cshk->cthk", grad_scores, k_scaled, precision=highest_precision
    ) + incoming_carry[:, :, None, None] * jnp.einsum(
        "cthv,chkv->cthk", grad_out, start_state, precision=highest_precision
    )
    grad_queries = grad_q_scaled * jnp.exp(cumulative) * score_scale
    grad_k_scaled = jnp.einsum(
        "chts,cthk->cshk", grad_scores, query_scaled, precision=highest_precision
    )
    grad_k_tail = jnp.einsum(
        "cshv,chkv->cshk", values_all, end_adjoint, precision=highest_precision
    )
    grad_keys = (
        grad_k_scaled * jnp.exp(-cumulative)
        + grad_k_tail
        * jnp.exp(final_cumulative_decay[:, None] - cumulative)
        * tail_mask[:, :, None, None]
    )
    grad_values = jnp.einsum(
        "chts,cthv->cshv", scores, grad_out, precision=highest_precision
    ) + jnp.einsum("cshk,chkv->cshv", key_remainder, end_adjoint, precision=highest_precision)
    boundary = jnp.sum(end_adjoint * end_state, axis=-1)
    grad_cumul = queries * grad_queries - keys_all * grad_keys
    grad_cumul = jnp.concatenate(
        [grad_cumul[:, :-1], grad_cumul[:, -1:] + boundary[:, None]], axis=1
    )
    grad_log_gates = jnp.cumsum(grad_cumul[:, ::-1], axis=1)[:, ::-1]
    grad_active = jnp.concatenate(
        [
            grad_queries.reshape(tok_rows, key_width),
            grad_keys.reshape(tok_rows, key_width),
            grad_values.reshape(tok_rows, value_width),
        ],
        axis=1,
    )
    grad_conv = grad_active * swish_slope(conv_pre)
    grad_extended = jnp.zeros((tok_rows + tap_count - 1, channels), jnp.float32)
    tap_grads = []
    for tap_index in range(tap_count):
        grad_extended = grad_extended + jnp.pad(
            conv_weight[tap_index] * same_seg[tap_index] * grad_conv,
            ((tap_index, tap_count - 1 - tap_index), (0, 0)),
        )
        tap_grads.append(
            jnp.sum(
                same_seg[tap_index] * extended[tap_index : tap_index + tok_rows] * grad_conv, axis=0
            )
        )
    grad_conv_weight = jnp.stack(tap_grads)
    returned = passed_along(grad_extended[: tap_count - 1], "seq", -1)
    grad_mixed = grad_extended[tap_count - 1 :] + jnp.concatenate(
        [jnp.zeros((tok_rows - (tap_count - 1), channels), jnp.float32), returned], axis=0
    )
    grad_logits = grad_log_gates.reshape(tok_rows, key_width) / gate_scale * jax.nn.sigmoid(-logits)
    grad_upper = jnp.concatenate(
        [
            jnp.einsum("tr,tk->rk", lowrank, grad_logits, precision=highest_precision),
            jnp.sum(grad_logits, axis=0, keepdims=True),
        ],
        axis=0,
    )
    grad_lowrank = jnp.einsum(
        "tk,rk->tr", grad_logits, gate_up[:rank_width], precision=highest_precision
    ).astype(jnp.bfloat16)
    grad_down_part = jnp.einsum(
        "tr,td->rd", grad_lowrank, normed, preferred_element_type=jnp.float32
    )
    grad_projected = jnp.concatenate(
        [grad_mixed.astype(jnp.bfloat16), grad_gate_pre.astype(jnp.bfloat16)], axis=1
    )
    grad_normed_part = jnp.einsum(
        "tn,dn->td", grad_projected, in_weights, preferred_element_type=jnp.float32
    ) + jnp.einsum("tr,dr->td", grad_lowrank, down_low, preferred_element_type=jnp.float32)
    grad_normed = lax.psum(grad_normed_part.astype(jnp.bfloat16), "head").astype(jnp.float32)
    grad_gains_one = jnp.sum(grad_normed * inputs * inverse_one, axis=0)
    grad_input = grad_one + rms_back(inputs, inverse_one, norm_gains[0], grad_normed)
    slots_dev = slot_copy.shape[0]
    slot_total = slots_dev * lax.axis_size("seq")
    grads = [
        jnp.einsum("td,tn->dn", left, right, preferred_element_type=jnp.float32).astype(
            jnp.bfloat16
        )
        for left, right in (
            (normed, grad_projected),
            (normed_two, grad_pair),
            (grad_attn, gated_out),
            (upstream_low, hidden),
        )
    ]
    named = jnp.arange(slot_total, dtype=jnp.int32)[:, None] == owners
    inverse = jnp.where(
        jnp.any(named, axis=1),
        jnp.sum(named * jnp.arange(block_total, dtype=jnp.int32), axis=1),
        block_total,
    ).astype(jnp.int32)[None]
    owned_grads = scatter_grads(
        grads,
        inverse,
        build_plan(
            (count_in, count_up, count_out, count_down),
            (0.43, 0.86, 1.0),
            8,
            ((2, 1, 0), (1, 2, 0), (0, 1, 2)),
        ),
        slots_dev,
        block_total,
    ).astype(jnp.float32)
    rotated = jnp.einsum("sij,sik->sjk", basis_left, owned_grads, precision=highest_precision)
    rotated = jnp.einsum("sjk,skl->sjl", rotated, basis_right, precision=highest_precision)
    first_next = moment_decay * slot_first + (1.0 - moment_decay) * rotated
    second_next = moment_decay * slot_second + (1.0 - moment_decay) * rotated * rotated
    direction = first_next / (jnp.sqrt(second_next) + adam_epsilon)
    restored = jnp.einsum("sij,sjk->sik", basis_left, direction, precision=highest_precision)
    restored = jnp.einsum("sik,slk->sil", restored, basis_right, precision=highest_precision)
    master_next = slot_master - rate_block * restored
    shared_rows, own_rows = rank_width + 8, 16
    shared = jnp.concatenate(
        [
            grad_down_part,
            jnp.pad(grad_head_gain, (0, model_width - grad_head_gain.shape[0]))[None],
            jnp.zeros((7, model_width), jnp.float32),
        ]
    )
    flat_upper = grad_upper.reshape(-1)
    upper_rows = -(-flat_upper.shape[0] // model_width)
    alone = jnp.concatenate(
        [
            jnp.stack([grad_gains_one, grad_gains_two]),
            grad_conv_weight,
            jnp.pad(flat_upper, (0, upper_rows * model_width - flat_upper.shape[0])).reshape(
                upper_rows, model_width
            ),
        ]
    )
    alone = jnp.pad(alone, ((0, own_rows - alone.shape[0]), (0, 0)))
    summed = sum_small(jnp.concatenate([shared, alone]), shared_rows)
    down_grad = summed[:rank_width].T
    head_grad = summed[rank_width, : grad_head_gain.shape[0]]
    gains_grad = summed[shared_rows : shared_rows + 2]
    conv_grad = summed[shared_rows + 2 : shared_rows + 2 + tap_count]
    upper_grad = (
        summed[shared_rows + 2 + tap_count : shared_rows + 2 + tap_count + upper_rows]
        .reshape(-1)[: flat_upper.shape[0]]
        .reshape(grad_upper.shape)
    )
    gains_next, gains_first_next, gains_second_next = plain_adam(
        norm_gains, gains_grad, gains_first, gains_second, rate_gains
    )
    down_next, down_first_next, down_second_next = plain_adam(
        gate_down, down_grad, down_first, down_second, rate_down
    )
    upper_next, upper_first_next, upper_second_next = plain_adam(
        gate_up, upper_grad, upper_first, upper_second, rate_upper
    )
    head_next, head_first_next, head_second_next = plain_adam(
        head_gain, head_grad, head_first, head_second, rate_head
    )
    conv_next, conv_first_next, conv_second_next = plain_adam(
        conv_weight, conv_grad, conv_first, conv_second, rate_conv
    )
    return (
        result,
        grad_input,
        owned_grads,
        master_next,
        first_next,
        second_next,
        master_next.astype(jnp.bfloat16),
        gains_grad,
        gains_next,
        gains_first_next,
        gains_second_next,
        down_grad,
        down_next,
        down_first_next,
        down_second_next,
        upper_grad,
        upper_next,
        upper_first_next,
        upper_second_next,
        head_grad,
        head_next,
        head_first_next,
        head_second_next,
        conv_grad,
        conv_next,
        conv_first_next,
        conv_second_next,
    )


def solution(mesh):
    placed = (
        P("seq", None),
        P("seq", None),
        P(),
        P(),
        P("head", None),
        P(("seq", "head"), None, None),
        P(("seq", "head"), None, None),
        P(("seq", "head"), None, None),
        P(("seq", "head"), None, None),
        P(("seq", "head"), None, None),
        P(("seq", "head"), None, None),
        P(),
        P(),
        P(),
        P(),
        P(),
        P(),
        P(None, "head"),
        P(None, "head"),
        P(None, "head"),
        P(),
        P(),
        P(),
        P(None, "head"),
        P(None, "head"),
        P(None, "head"),
    )
    return jax.shard_map(
        body,
        mesh=mesh,
        in_specs=placed,
        out_specs=(
            P("seq", None),
            P("seq", None),
            P(("seq", "head"), None, None),
            P(("seq", "head"), None, None),
            P(("seq", "head"), None, None),
            P(("seq", "head"), None, None),
            P(("seq", "head"), None, None),
            P(),
            P(),
            P(),
            P(),
            P(),
            P(),
            P(),
            P(),
            P(None, "head"),
            P(None, "head"),
            P(None, "head"),
            P(None, "head"),
            P(),
            P(),
            P(),
            P(),
            P(None, "head"),
            P(None, "head"),
            P(None, "head"),
            P(None, "head"),
        ),
        check_vma=False,
    )
```

```python
import functools

import jax
import jax.numpy as jnp
from jax import lax
from jax.experimental import pallas as pl
from jax.experimental.pallas import tpu as pltpu
from jax.sharding import PartitionSpec as P

MESH = pl.DeviceIdType.MESH

DK = 128
DV = 256


highest_precision = lax.Precision.HIGHEST
norm_epsilon = 1e-06
adam_epsilon = 1e-08
gate_scale = 16.0
moment_decay = 0.5
rate_block = 0.03
rate_gains = 0.45
rate_down = 0.02
rate_upper = 0.6
rate_head = 0.5
rate_conv = 0.1


def axis_sizes(n):
    side=1
    while (side*2)**2*4<=n: side*=2
    return (n//(side*side),side,side)

def coords(me,sizes):
    Z,Y,X=sizes
    return [me//(Y*X),(me//X)%Y,me%X]

def index_of(c,sizes):
    Z,Y,X=sizes
    return (c[0]*Y+c[1])*X+c[2]

def enter(n,me):
    barrier=pltpu.get_barrier_semaphore()
    for j in range(1,n):
        pl.semaphore_signal(barrier,inc=1,device_id={"seq":lax.rem(me+j,n)},device_id_type=MESH)
    pl.semaphore_wait(barrier,n-1)

def remote(src,dst,ss,rs,peer):
    return pltpu.make_async_remote_copy(src_ref=src,dst_ref=dst,send_sem=ss,recv_sem=rs,device_id={"seq":peer},device_id_type=MESH)

def gather_kernel(n,sizes,plan,owners_ref,slot_ref,out_ref,recv,piece,a_send,a_recv,g_send,g_recv,l_sem):
    me=lax.axis_index("seq"); c=coords(me,sizes)
    sd=slot_ref.shape[0]; rows=piece.shape[0]; bw=slot_ref.shape[2]; nb=owners_ref.shape[1]
    enter(n,me)
    def a2a(j):
        p=lax.rem(me+j,n)
        return remote(slot_ref.at[:,pl.ds(p*rows,rows),:],recv.at[pl.ds(me*sd,sd)],a_send.at[j],a_recv.at[j],p)
    for j in range(1,n): a2a(j).start()
    mine=pltpu.make_async_copy(slot_ref.at[:,pl.ds(me*rows,rows),:],recv.at[pl.ds(me*sd,sd)],l_sem.at[0])
    mine.start(); mine.wait()
    for j in range(1,n): a2a(j).wait()
    for b in range(nb):
        piece[:,b*bw:(b+1)*bw]=recv[owners_ref[0,b]]
    own=pltpu.make_async_copy(piece,out_ref.at[c[0],c[1],c[2]],l_sem.at[1])
    own.start()
    def ag(i,k,j):
        lo,hi,order=plan[i]
        ax=order[k]
        idx=tuple(slice(None) if a in order[:k] else c[a] for a in range(3))+(slice(None),pl.ds(lo*bw,(hi-lo)*bw))
        d=list(c); d[ax]=lax.rem(c[ax]+j,sizes[ax])
        src=piece.at[:,pl.ds(lo*bw,(hi-lo)*bw)] if k==0 else out_ref.at[idx]
        s=(i*3+k)*max(sizes)+j
        return remote(src,out_ref.at[idx],g_send.at[s],g_recv.at[s],index_of(d,sizes))
    own.wait()
    streams={}
    for i,p in enumerate(plan): streams.setdefault(p[2],[]).append(i)
    longest=max([len(v) for v in streams.values()],default=0)
    for s in range(longest+2 if plan else 0):
        for k in (2,1,0):
            for order,ids in streams.items():
                if not 0<=s-k<len(ids): continue
                i=ids[s-k]
                if k:
                    for j in range(1,sizes[order[k-1]]): ag(i,k-1,j).wait_recv()
                for j in range(1,sizes[order[k]]): ag(i,k,j).start()
    for i in range(len(plan)):
        for j in range(1,sizes[plan[i][2][2]]): ag(i,2,j).wait_recv()
    for k in range(3):
        for i in range(len(plan)):
            for j in range(1,sizes[plan[i][2][k]]): ag(i,k,j).wait_send()

def gather_weights(slot_copy,owners,plan):
    n=lax.axis_size("seq"); sizes=axis_sizes(n)
    sd,d,bw=slot_copy.shape; nb=owners.shape[1]; rows=d//n
    out=pl.pallas_call(functools.partial(gather_kernel,n,sizes,plan),
        out_shape=jax.ShapeDtypeStruct(sizes+(rows,nb*bw),slot_copy.dtype),
        in_specs=[pl.BlockSpec(memory_space=pltpu.SMEM),pl.BlockSpec(memory_space=pl.ANY)],
        out_specs=pl.BlockSpec(memory_space=pl.ANY),
        scratch_shapes=[pltpu.VMEM((n*sd,rows,bw),slot_copy.dtype),pltpu.VMEM((rows,nb*bw),slot_copy.dtype),
            pltpu.SemaphoreType.DMA((n,)),pltpu.SemaphoreType.DMA((n,)),
            pltpu.SemaphoreType.DMA((len(plan)*3*max(sizes),)),pltpu.SemaphoreType.DMA((len(plan)*3*max(sizes),)),
            pltpu.SemaphoreType.DMA((2,))],
        compiler_params=pltpu.CompilerParams(collective_id=1,has_side_effects=True,vmem_limit_bytes=48<<20),
    )(owners,slot_copy)
    return out.reshape(d,nb*bw)

def scatter_kernel(n,sizes,plan,nin,inv_ref,*refs):
    g_refs=refs[:nin]; out_ref=refs[nin];
    np_=len(plan)
    sc=refs[nin+1:]
    own=sc[0:np_]; b0=sc[np_:2*np_]; b1=sc[2*np_:3*np_]; b2=sc[3*np_:4*np_]
    fin,send,r_send,r_recv,a_send,a_recv,l_sem=sc[4*np_:]
    me=lax.axis_index("seq"); c=coords(me,sizes)
    sd,_,rows,bw=out_ref.shape
    nb=fin.shape[0]-1
    bufs=(b0,b1,b2)
    def part(view,done,left,coord):
        pass
    enter(n,me)
    loads=[]
    for i,(a,lo,hi,base,order) in enumerate(plan):
        ax=order[0]
        idx=tuple(c[ax] if q==ax else slice(None) for q in range(3))+(slice(None),pl.ds(lo*bw,(hi-lo)*bw))
        cp=pltpu.make_async_copy(g_refs[a].at[idx],own[i],l_sem.at[i]); cp.start(); loads.append(cp)
    def rs(i,k,j):
        a,lo,hi,base,order=plan[i]
        ax=order[k]
        d=list(c); d[ax]=lax.rem(c[ax]+j,sizes[ax])
        left=sorted(set(range(3))-set(order[:k]))
        idx=tuple(d[ax] if q==ax else slice(None) for q in left)
        if k==0: src=g_refs[a].at[idx+(slice(None),pl.ds(lo*bw,(hi-lo)*bw))]
        elif k==1: src=own[i].at[idx]
        else: src=b1[i].at[(0,)+idx]
        dst=bufs[k][i].at[j]
        s=(i*3+k)*max(sizes)+j
        return remote(src,dst,r_send.at[s],r_recv.at[s],index_of(d,sizes))
    fin[nb]=jnp.zeros(fin.shape[1:],fin.dtype)
    def combine(i,k):
        a,lo,hi,base,order=plan[i]
        if k==0: loads[i].wait()
        for j in range(1,sizes[order[k]]): rs(i,k,j).wait_recv()
        if k==0:
            s0,s1=own[i].shape[0],own[i].shape[1]
            def add0(t,_):
                u,v=t//s1,t%s1
                tot=own[i][u,v].astype(jnp.float32)
                for j in range(1,sizes[order[0]]): tot=tot+b0[i][j,u,v].astype(jnp.float32)
                own[i][u,v]=tot.astype(own[i].dtype)
                return 0
            lax.fori_loop(0,s0*s1,add0,0)
        elif k==1:
            pos=sorted(set(range(3))-set(order[:1])).index(order[1])
            def add1(t,_):
                at=(c[order[1]],t) if pos==0 else (t,c[order[1]])
                tot=own[i][at].astype(jnp.float32)
                for j in range(1,sizes[order[1]]): tot=tot+b1[i][j,t].astype(jnp.float32)
                b1[i][0,t]=tot.astype(own[i].dtype)
                return 0
            lax.fori_loop(0,sizes[order[2]],add1,0)
        else:
            tot=b1[i][0,c[order[2]]].astype(jnp.float32)
            for j in range(1,sizes[order[2]]): tot=tot+b2[i][j].astype(jnp.float32)
            for b in range(lo,hi): fin[base+b-lo]=tot[:,(b-lo)*bw:(b-lo+1)*bw].astype(fin.dtype)
    streams={}
    for i,p in enumerate(plan): streams.setdefault(p[4],[]).append(i)
    longest=max([len(v) for v in streams.values()],default=0)
    for s in range(longest+3 if plan else 0):
        for k in range(4):
            for order,ids in streams.items():
                if not 0<=s-k<len(ids): continue
                i=ids[s-k]
                if k: combine(i,k-1)
                if k<3:
                    for j in range(1,sizes[order[k]]): rs(i,k,j).start()
    for s in range(send.shape[0]): send[s]=fin[inv_ref[0,s]]
    def a2a(j):
        p=lax.rem(me+j,n)
        return remote(send.at[pl.ds(p*sd,sd)],out_ref.at[:,me],a_send.at[j],a_recv.at[j],p)
    for j in range(1,n): a2a(j).start()
    mine=pltpu.make_async_copy(send.at[pl.ds(me*sd,sd)],out_ref.at[:,me],l_sem.at[np_])
    mine.start(); mine.wait()
    for j in range(1,n): a2a(j).wait()
    for k in range(3):
        for i in range(np_):
            for j in range(1,sizes[plan[i][4][k]]): rs(i,k,j).wait_send()

def scatter_grads(grads,inverse,plan,slots_dev,nb):
    n=lax.axis_size("seq"); sizes=axis_sizes(n)
    d=grads[0].shape[0]; bw=128; rows=d//n
    views=[g.reshape(sizes+(rows,g.shape[1])) for g in grads]
    dt=grads[0].dtype
    own=[];b0=[];b1=[];b2=[]
    for a,lo,hi,base,order in plan:
        w=(hi-lo)*bw
        rem=[sizes[q] for q in range(3) if q!=order[0]]
        own.append(pltpu.VMEM(tuple(rem)+(rows,w),dt))
        b0.append(pltpu.VMEM((sizes[order[0]],)+tuple(rem)+(rows,w),dt))
        b1.append(pltpu.VMEM((sizes[order[1]],sizes[order[2]],rows,w),dt))
        b2.append(pltpu.VMEM((sizes[order[2]],rows,w),dt))
    m=len(plan)*3*max(sizes)
    out=pl.pallas_call(functools.partial(scatter_kernel,n,sizes,plan,len(views)),
        out_shape=jax.ShapeDtypeStruct((slots_dev,n,rows,bw),dt),
        in_specs=[pl.BlockSpec(memory_space=pltpu.SMEM)]+[pl.BlockSpec(memory_space=pl.ANY)]*len(views),
        out_specs=pl.BlockSpec(memory_space=pl.ANY),
        scratch_shapes=own+b0+b1+b2+[pltpu.VMEM((nb+1,rows,bw),dt),pltpu.VMEM((slots_dev*n,rows,bw),dt),
            pltpu.SemaphoreType.DMA((m,)),pltpu.SemaphoreType.DMA((m,)),pltpu.SemaphoreType.DMA((n,)),pltpu.SemaphoreType.DMA((n,)),
            pltpu.SemaphoreType.DMA((len(plan)+1,))],
        compiler_params=pltpu.CompilerParams(collective_id=2,has_side_effects=True,vmem_limit_bytes=60<<20),
    )(inverse,*views)
    return out.reshape(slots_dev,d,bw)


def build_plan(widths, parts, pieces, orders):
    total = sum(widths)
    bounds = [sum(widths[:i]) for i in range(len(widths) + 1)]
    cuts = [round(total * f) for f in (0.0,) + parts]
    plan, at = [], 0
    for i in range(pieces):
        for order, lo, hi in zip(orders, cuts[:-1], cuts[1:], strict=True):
            size = hi - lo
            left = size * (i + 1) // pieces - size * i // pieces
            while left:
                which = max(q for q in range(len(widths)) if bounds[q] <= at)
                step = min(left, bounds[which + 1] - at)
                start = at - bounds[which]
                plan.append((which, start, start + step, at, order))
                at += step
                left -= step
    return plan


def sum_kernel(n, sizes, shared, x_ref, out_ref, mate, acc, bufs, send, recv):
    me, core = lax.axis_index("seq"), lax.axis_index("head")
    c = coords(me, sizes)
    barrier = pltpu.get_barrier_semaphore()
    peers = []
    for ax in range(3):
        for j in range(1, sizes[ax]):
            d = list(c)
            d[ax] = lax.rem(c[ax] + j, sizes[ax])
            peers.append((ax, j, index_of(d, sizes)))
    for _, _, p in peers:
        pl.semaphore_signal(barrier, inc=1, device_id={"seq": p}, device_id_type=MESH)
    pl.semaphore_signal(barrier, inc=1, device_id={"head": 1 - core}, device_id_type=MESH)
    pl.semaphore_wait(barrier, len(peers) + 1)
    swap = pltpu.make_async_remote_copy(
        src_ref=x_ref.at[pl.ds(0, shared)],
        dst_ref=mate,
        send_sem=send.at[0],
        recv_sem=recv.at[0],
        device_id={"head": 1 - core},
        device_id_type=MESH,
    )
    swap.start()
    swap.wait()
    acc[0, 0:shared] = x_ref[0:shared] + mate[...]
    acc[0, shared:] = x_ref[shared:]
    copies = []
    for step, ax in enumerate((2, 1, 0)):
        bufs[ax, c[ax]] = acc[step]
        going = []
        for q, j, p in peers:
            if q == ax:
                going.append(
                    remote(
                        acc.at[step],
                        bufs.at[ax, c[ax]],
                        send.at[1 + ax * max(sizes) + j],
                        recv.at[1 + ax * max(sizes) + j],
                        p,
                    )
                )
        for copy in going:
            copy.start()
        for copy in going:
            copy.wait_recv()
        total = bufs[ax, 0]
        for j in range(1, sizes[ax]):
            total = total + bufs[ax, j]
        if step < 2:
            acc[step + 1] = total
        else:
            out_ref[...] = total
        copies += going
    for copy in copies:
        copy.wait_send()


def sum_small(x, shared):
    n = lax.axis_size("seq")
    sizes = axis_sizes(n)
    most = max(sizes)
    return pl.pallas_call(
        functools.partial(sum_kernel, n, sizes, shared),
        out_shape=jax.ShapeDtypeStruct(x.shape, x.dtype),
        scratch_shapes=[
            pltpu.VMEM((shared,) + x.shape[1:], x.dtype),
            pltpu.VMEM((3,) + x.shape, x.dtype),
            pltpu.VMEM((3, most) + x.shape, x.dtype),
            pltpu.SemaphoreType.DMA((1 + 3 * most,)),
            pltpu.SemaphoreType.DMA((1 + 3 * most,)),
        ],
        compiler_params=pltpu.CompilerParams(
            collective_id=3, has_side_effects=True, vmem_limit_bytes=32 << 20
        ),
    )(x)


def passed_along(array, axis, by):
    devices = lax.axis_size(axis)
    pairs = [(i, i + by) for i in range(devices) if 0 <= i + by < devices]
    return lax.ppermute(array, axis, pairs)


NN = (((1,), (0,)), ((), ()))
NT = (((1,), (1,)), ((), ()))
TN = (((0,), (0,)), ((), ()))
TILE = 128


def halves(values):
    high = values.astype(jnp.bfloat16)
    return high, (values - high.astype(jnp.float32)).astype(jnp.bfloat16)


def product(left, right, dims):
    (lh, ll), (rh, rl) = left, right
    dot = functools.partial(
        lax.dot_general, dimension_numbers=dims, preferred_element_type=jnp.float32
    )
    return dot(lh, rh) + (dot(lh, rl) + dot(ll, rh))


def running_sum(table, values):
    first = values.astype(jnp.bfloat16)
    rest = values - first.astype(jnp.float32)
    second, third = halves(rest)
    dot = functools.partial(
        lax.dot_general, dimension_numbers=NN, preferred_element_type=jnp.float32
    )
    return dot(table, first) + (dot(table, second) + dot(table, third))


def sigmoid(values):
    return 1.0 / (1.0 + jnp.exp(-values))


def chain_tools(n, sizes, forward, mine, bufs, send, recv, result):
    me = lax.axis_index("seq")
    c = coords(me, sizes)
    pieces = mine.shape[0]
    across, along, before, held = bufs
    most = max(sizes)
    state = pl.ds(0, TILE)
    decay = pl.ds(TILE, 1)

    def peers(ax):
        return [j for j in range(1, sizes[ax])]

    def to(ax, j):
        d = list(c)
        d[ax] = lax.rem(c[ax] + j, sizes[ax])
        return index_of(d, sizes)

    def line(buf, source, ax, j, p, base):
        s = base + j * pieces + p
        return remote(source.at[p], buf.at[c[ax], p], send.at[s], recv.at[s], to(ax, j))

    def hop(p):
        s = 2 * most * pieces + p
        step = 1 if forward else -1
        d = [lax.rem(c[0] + step + sizes[0], sizes[0]), c[1], c[2]]
        return remote(held.at[1, p], held.at[0, p], send.at[s], recv.at[s], index_of(d, sizes))

    def compose(first, second):
        return (second[1] * first[0] + second[0], first[1] * second[1])

    def reduce_line(buf, ax, p):
        size = sizes[ax]
        order = range(size) if forward else range(size - 1, -1, -1)
        prefix = (jnp.zeros((TILE, TILE), jnp.float32), jnp.ones((1, TILE), jnp.float32))
        total = None
        for i in order:
            item = (buf[i, p, state], buf[i, p, decay])
            longer = compose(prefix, item)
            take = (i < c[ax]) if forward else (i > c[ax])
            prefix = tuple(jnp.where(take, a, b) for a, b in zip(longer, prefix, strict=True))
            total = item if total is None else compose(total, item)
        return prefix, total

    def start_x():
        for p in range(pieces):
            across[c[2], p] = mine[p]
            for j in peers(2):
                line(across, mine, 2, j, p, 0).start()

    def start_y():
        for p in range(pieces):
            for j in peers(2):
                line(across, mine, 2, j, p, 0).wait_recv()
            prefix, total = reduce_line(across, 2, p)
            before[p, state], before[p, decay] = prefix
            held[2, p, state], held[2, p, decay] = total
            held[2, p, pl.ds(TILE + 1, 7)] = jnp.zeros((7, TILE), jnp.float32)
            along[c[1], p] = held[2, p]
            for j in peers(1):
                line(along, held.at[2], 1, j, p, most * pieces).start()

    first_z = 0 if forward else sizes[0] - 1
    last_z = sizes[0] - 1 - first_z

    def start_z():
        for p in range(pieces):
            for j in peers(1):
                line(along, held.at[2], 1, j, p, most * pieces).wait_recv()
            prefix, total = reduce_line(along, 1, p)
            own = (before[p, state], before[p, decay])
            before[p, state], before[p, decay] = compose(prefix, own)
            held[1, p, state], held[1, p, decay] = total
            held[1, p, pl.ds(TILE + 1, 7)] = jnp.zeros((7, TILE), jnp.float32)

            @pl.when(c[0] == first_z)
            def _():
                held[0, p] = jnp.zeros((TILE + 8, TILE), jnp.float32)
                hop(p).start()

    def pass_z(k):
        at = k if forward else sizes[0] - 1 - k

        @pl.when(c[0] == at)
        def _():
            for p in range(pieces):
                hop(p).wait_recv()
                if at != last_z:
                    got = (held[0, p, state], held[0, p, decay])
                    item = (held[1, p, state], held[1, p, decay])
                    held[1, p, state], held[1, p, decay] = compose(got, item)
                    hop(p).start()

    def finish():
        for p in range(pieces):
            result[p] = before[p, decay] * held[0, p, state] + before[p, state]
            for j in peers(2):
                line(across, mine, 2, j, p, 0).wait_send()
            for j in peers(1):
                line(along, held.at[2], 1, j, p, most * pieces).wait_send()

        @pl.when(c[0] != last_z)
        def _():
            for p in range(pieces):
                hop(p).wait_send()

    stages = [start_x, start_y, start_z]
    stages += [functools.partial(pass_z, k) for k in range(1, sizes[0])]
    return stages, finish


def greet(n, sizes, extra):
    c = coords(lax.axis_index("seq"), sizes)
    barrier = pltpu.get_barrier_semaphore()
    count = 0
    for ax in range(3):
        for j in range(1, sizes[ax]):
            d = list(c)
            d[ax] = lax.rem(c[ax] + j, sizes[ax])
            pl.semaphore_signal(
                barrier, inc=1, device_id={"seq": index_of(d, sizes)}, device_id_type=MESH
            )
            count += 1
    for index in extra:
        pl.semaphore_signal(barrier, inc=1, device_id={"seq": index}, device_id_type=MESH)
        count += 1
    pl.semaphore_wait(barrier, count)


def tile_masks(rows_ref, cols_ref, c):
    row = rows_ref[pl.ds(c, 1), :]
    col = cols_ref[pl.ds(pl.multiple_of(c * TILE, TILE), TILE), 6:7]
    i = lax.broadcasted_iota(jnp.int32, (TILE, TILE), 0)
    j = lax.broadcasted_iota(jnp.int32, (TILE, TILE), 1)
    return (i >= j) & (row == col)


def forward_kernel(
    n,
    sizes,
    proj_ref,
    halo_ref,
    lg_ref,
    gate_ref,
    cols_ref,
    rows_ref,
    taps_ref,
    gain_ref,
    conv_ref,
    cum_ref,
    o_ref,
    u_ref,
    start_ref,
    act,
    state,
    prev,
    mine,
    across,
    along,
    before,
    held,
    result,
    send,
    recv,
):
    tiles, channels = proj_ref.shape[0] // TILE, proj_ref.shape[1]
    keys = lg_ref.shape[1]
    heads = keys // DK
    value = DV * heads
    greet(n, sizes, ())
    scale = DK ** (-0.5)
    i = lax.broadcasted_iota(jnp.int32, (TILE, TILE), 0)
    j = lax.broadcasted_iota(jnp.int32, (TILE, TILE), 1)
    lower = (i >= j).astype(jnp.bfloat16)
    prev[...] = halo_ref[...]
    state[...] = jnp.zeros_like(state)
    mine[...] = jnp.zeros_like(mine)
    for p in range(mine.shape[0]):
        mine[p, TILE : TILE + 1] = jnp.ones((1, TILE), jnp.float32)

    def local(c, _):
        at = pl.ds(pl.multiple_of(c * TILE, TILE), TILE)
        for g in range(0, channels, 256):
            wide = slice(g, g + 256)
            block = jnp.concatenate(
                [prev[:, wide].astype(jnp.float32), proj_ref[at, wide].astype(jnp.float32)]
            )
            total = taps_ref[3:4, wide] * block[16:]
            for s in (1, 2, 3):
                total = total + taps_ref[3 - s : 4 - s, wide] * (
                    block[16 - s : 16 - s + TILE] * cols_ref[at, 1 + s : 2 + s]
                )
            conv_ref[at, wide] = total
            act[at, wide] = total * sigmoid(total)
        prev[...] = proj_ref[pl.ds(pl.multiple_of(c * TILE + TILE - 16, 16), 16), :]
        cum = running_sum(lower, lg_ref[at, :])
        cum_ref[at, :] = cum
        last = cum[TILE - 1 : TILE]
        left = act[at, keys : 2 * keys] * jnp.exp(last - cum) * cols_ref[at, 1:2]
        decay = jnp.exp(last) * cols_ref[at, 0:1][TILE - 1 : TILE]
        for h in range(heads):
            kh = slice(h * DK, (h + 1) * DK)
            v = halves(act[at, 2 * keys + h * DV : 2 * keys + (h + 1) * DV])
            start_ref[c, h] = state[h]
            state[h] = state[h] * decay[:, kh] + product(v, halves(left[:, kh]), TN)
            for e in range(DV // TILE):
                p = h * (DV // TILE) + e
                mine[p, TILE : TILE + 1] = mine[p, TILE : TILE + 1] * decay[:, kh]
        return 0

    lax.fori_loop(0, tiles, local, 0)
    for h in range(heads):
        start_ref[tiles, h] = state[h]
        for e in range(DV // TILE):
            mine[h * (DV // TILE) + e, 0:TILE] = state[h, e * TILE : (e + 1) * TILE]
    stages, finish = chain_tools(
        n, sizes, True, mine, (across, along, before, held), send, recv, result
    )
    stages[0]()

    def inside(c, _):
        for k, stage in enumerate(stages[1:]):
            pl.when(c == k + 1)(stage)
        at = pl.ds(pl.multiple_of(c * TILE, TILE), TILE)
        cum = cum_ref[at, :]
        middle = cum[TILE // 2 - 1 : TILE // 2]
        q = act[at, 0:keys] * jnp.exp(cum - middle) * scale
        k = act[at, keys : 2 * keys] * jnp.exp(middle - cum)
        mask = tile_masks(rows_ref, cols_ref, c)
        for h in range(heads):
            kh = slice(h * DK, (h + 1) * DK)
            vh = slice(h * DV, (h + 1) * DV)
            scores = jnp.where(mask, product(halves(q[:, kh]), halves(k[:, kh]), NT), 0.0)
            v = halves(act[at, 2 * keys + h * DV : 2 * keys + (h + 1) * DV])
            o_ref[at, vh] = product(halves(scores), v, NN)
        return 0

    lax.fori_loop(0, tiles, inside, 0)
    finish()
    for h in range(heads):
        for e in range(DV // TILE):
            state[h, e * TILE : (e + 1) * TILE] = result[h * (DV // TILE) + e]

    def outside(c, _):
        at = pl.ds(pl.multiple_of(c * TILE, TILE), TILE)
        cum = cum_ref[at, :]
        q = act[at, 0:keys] * jnp.exp(cum) * scale * cols_ref[at, 0:1]
        decay = jnp.exp(cum[TILE - 1 : TILE]) * cols_ref[at, 0:1][TILE - 1 : TILE]
        for h in range(heads):
            kh = slice(h * DK, (h + 1) * DK)
            vh = slice(h * DV, (h + 1) * DV)
            start = start_ref[c, h] + state[h]
            start_ref[c, h] = start
            state[h] = state[h] * decay[:, kh]
            o = o_ref[at, vh] + product(halves(q[:, kh]), halves(start), NT)
            o_ref[at, vh] = o
            inverse = lax.rsqrt(jnp.mean(o * o, axis=1, keepdims=True) + norm_epsilon)
            gate = gate_ref[at, vh]
            u_ref[at, vh] = (o * inverse * gain_ref[...] * (gate * sigmoid(gate))).astype(
                u_ref.dtype
            )
        return 0

    lax.fori_loop(0, tiles, outside, 0)
    for h in range(heads):
        start_ref[tiles, h] = start_ref[tiles, h] + state[h]


def chain_scratch(sizes, pieces):
    most = max(sizes)
    shape = (pieces, TILE + 8, TILE)
    return [
        pltpu.VMEM(shape, jnp.float32),
        pltpu.VMEM((sizes[2],) + shape, jnp.float32),
        pltpu.VMEM((sizes[1],) + shape, jnp.float32),
        pltpu.VMEM(shape, jnp.float32),
        pltpu.VMEM((3,) + shape, jnp.float32),
        pltpu.VMEM((pieces, TILE, TILE), jnp.float32),
        pltpu.SemaphoreType.DMA(((2 * most + 1) * pieces,)),
        pltpu.SemaphoreType.DMA(((2 * most + 1) * pieces,)),
    ]


def recurrence(proj, halo, log_gate, gate, cols, rows, taps, gain):
    n = lax.axis_size("seq")
    sizes = axis_sizes(n)
    length, channels = proj.shape
    keys = log_gate.shape[1]
    heads = keys // DK
    value = heads * DV
    tiles = length // TILE
    f32 = jnp.float32
    shape = jax.ShapeDtypeStruct
    return pl.pallas_call(
        functools.partial(forward_kernel, n, sizes),
        out_shape=(
            shape((length, channels), f32),
            shape((length, keys), f32),
            shape((length, value), f32),
            shape((length, value), jnp.bfloat16),
            shape((tiles + 1, heads, DV, DK), f32),
        ),
        scratch_shapes=[
            pltpu.VMEM((length, channels), f32),
            pltpu.VMEM((heads, DV, DK), f32),
            pltpu.VMEM((16, channels), proj.dtype),
        ]
        + chain_scratch(sizes, heads * DV // TILE),
        compiler_params=pltpu.CompilerParams(
            collective_id=4, has_side_effects=True, vmem_limit_bytes=56 << 20
        ),
    )(proj, halo, log_gate, gate, cols, rows, taps, gain)


def backward_kernel(
    n,
    sizes,
    proj_ref,
    halo_ref,
    conv_ref,
    cum_ref,
    logits_ref,
    o_ref,
    gate_ref,
    du_ref,
    start_ref,
    cols_ref,
    rows_ref,
    taps_ref,
    gain_ref,
    dproj_ref,
    dgate_ref,
    dlogits_ref,
    dtaps_ref,
    dgain_ref,
    do,
    dact,
    adjoint,
    ends,
    after,
    back,
    tail,
    mine,
    across,
    along,
    before,
    held,
    result,
    send,
    recv,
    b_sem,
):
    tiles, channels = proj_ref.shape[0] // TILE, proj_ref.shape[1]
    keys = cum_ref.shape[1]
    heads = keys // DK
    me = lax.axis_index("seq")
    greet(n, sizes, (lax.rem(me + 1, n), lax.rem(me + n - 1, n)))
    scale = DK ** (-0.5)
    i = lax.broadcasted_iota(jnp.int32, (TILE, TILE), 0)
    j = lax.broadcasted_iota(jnp.int32, (TILE, TILE), 1)
    upper = (i <= j).astype(jnp.bfloat16)
    adjoint[...] = jnp.zeros_like(adjoint)
    mine[...] = jnp.zeros_like(mine)
    dgain_ref[...] = jnp.zeros_like(dgain_ref)
    dtaps_ref[...] = jnp.zeros_like(dtaps_ref)
    for p in range(mine.shape[0]):
        mine[p, TILE : TILE + 1] = jnp.ones((1, TILE), jnp.float32)

    def local(t, _):
        c = tiles - 1 - t
        at = pl.ds(pl.multiple_of(c * TILE, TILE), TILE)
        cum = cum_ref[at, :]
        pre = conv_ref[at, 0:keys]
        q = pre * sigmoid(pre) * jnp.exp(cum) * scale * cols_ref[at, 0:1]
        decay = jnp.exp(cum[TILE - 1 : TILE]) * cols_ref[at, 0:1][TILE - 1 : TILE]
        for h in range(heads):
            kh = slice(h * DK, (h + 1) * DK)
            vh = slice(h * DV, (h + 1) * DV)
            o = o_ref[at, vh]
            inverse = lax.rsqrt(jnp.mean(o * o, axis=1, keepdims=True) + norm_epsilon)
            gate = gate_ref[at, vh]
            sig = sigmoid(gate)
            du = du_ref[at, vh]
            unit = o * inverse
            dgate_ref[at, vh] = (
                du * (unit * gain_ref[...]) * (sig * (1.0 + gate * (1.0 - sig)))
            ).astype(dgate_ref.dtype)
            don = du * (gate * sig)
            dgain_ref[0:1] += jnp.sum(don * unit, axis=0, keepdims=True)
            scaled = gain_ref[...] * don
            grad = inverse * scaled - unit * (
                inverse * inverse * jnp.mean(scaled * o, axis=1, keepdims=True)
            )
            do[at, vh] = grad
            ends[c, h] = adjoint[h]
            adjoint[h] = adjoint[h] * decay[:, kh] + product(halves(grad), halves(q[:, kh]), TN)
            for e in range(DV // TILE):
                p = h * (DV // TILE) + e
                mine[p, TILE : TILE + 1] = mine[p, TILE : TILE + 1] * decay[:, kh]
        return 0

    lax.fori_loop(0, tiles, local, 0)
    for h in range(heads):
        for e in range(DV // TILE):
            mine[h * (DV // TILE) + e, 0:TILE] = adjoint[h, e * TILE : (e + 1) * TILE]
    stages, finish = chain_tools(
        n, sizes, False, mine, (across, along, before, held), send, recv, result
    )
    stages[0]()

    def inside(c, _):
        for k, stage in enumerate(stages[1:]):
            pl.when(c == k + 1)(stage)
        at = pl.ds(pl.multiple_of(c * TILE, TILE), TILE)
        cum = cum_ref[at, :]
        middle = cum[TILE // 2 - 1 : TILE // 2]
        pre = conv_ref[at, 0 : 2 * keys]
        both = pre * sigmoid(pre)
        grow = jnp.exp(cum - middle) * scale
        fall = jnp.exp(middle - cum)
        enter_decay = jnp.exp(cum) * (scale * cols_ref[at, 0:1])
        mask = tile_masks(rows_ref, cols_ref, c)
        for h in range(heads):
            kh = slice(h * DK, (h + 1) * DK)
            vh = slice(h * DV, (h + 1) * DV)
            q = halves(both[:, kh] * grow[:, kh])
            k = halves(both[:, keys + h * DK : keys + (h + 1) * DK] * fall[:, kh])
            prev_v = conv_ref[at, 2 * keys + h * DV : 2 * keys + (h + 1) * DV]
            v = halves(prev_v * sigmoid(prev_v))
            grad = halves(do[at, vh])
            scores = halves(jnp.where(mask, product(q, k, NT), 0.0))
            dscores = halves(jnp.where(mask, product(grad, v, NT), 0.0))
            dact[at, h * DK : (h + 1) * DK] = (
                product(dscores, k, NN) * grow[:, kh]
                + product(grad, halves(start_ref[c, h]), NN) * enter_decay[:, kh]
            )
            dact[at, keys + h * DK : keys + (h + 1) * DK] = (
                product(dscores, q, TN) * fall[:, kh]
            )
            dact[at, 2 * keys + h * DV : 2 * keys + (h + 1) * DV] = product(scores, grad, TN)
        return 0

    lax.fori_loop(0, tiles, inside, 0)
    finish()
    for h in range(heads):
        for e in range(DV // TILE):
            adjoint[h, e * TILE : (e + 1) * TILE] = result[h * (DV // TILE) + e]
    after[...] = jnp.zeros_like(after)

    def outside(t, _):
        c = tiles - 1 - t
        at = pl.ds(pl.multiple_of(c * TILE, TILE), TILE)
        cum = cum_ref[at, :]
        last = cum[TILE - 1 : TILE]
        remain = jnp.exp(last - cum) * cols_ref[at, 1:2]
        decay = jnp.exp(last) * cols_ref[at, 0:1][TILE - 1 : TILE]
        pre = conv_ref[at, 0 : 2 * keys]
        both = pre * sigmoid(pre)
        dkeys, edges = [], []
        for h in range(heads):
            kh = slice(h * DK, (h + 1) * DK)
            wide = slice(2 * keys + h * DV, 2 * keys + (h + 1) * DV)
            k = both[:, keys + h * DK : keys + (h + 1) * DK]
            end = ends[c, h] + adjoint[h]
            adjoint[h] = adjoint[h] * decay[:, kh]
            parts = halves(end)
            pre_v = conv_ref[at, wide]
            v = halves(pre_v * sigmoid(pre_v))
            dkeys.append(
                dact[at, keys + h * DK : keys + (h + 1) * DK]
                + product(v, parts, NN) * remain[:, kh]
            )
            dact[at, wide] += product(halves(k * remain[:, kh]), parts, NT)
            edges.append(jnp.sum(end * start_ref[c + 1, h], axis=0, keepdims=True))
        dk = jnp.concatenate(dkeys, axis=1)
        dq = dact[at, 0:keys]
        dact[at, keys : 2 * keys] = dk
        drift = both[:, 0:keys] * dq - both[:, keys:] * dk
        dl = running_sum(upper, drift) + jnp.concatenate(edges, axis=1)
        dlogits_ref[at, :] = dl * (1.0 / gate_scale) * sigmoid(-logits_ref[at, :])
        behind = jnp.where(
            c == 0,
            halo_ref[...],
            proj_ref[pl.ds(pl.multiple_of(jnp.maximum(c * TILE - 16, 0), 16), 16), :],
        )
        masks = cols_ref[pl.ds(pl.multiple_of(c * TILE, TILE), TILE + 8), :]
        for g in range(0, channels, 256):
            wide = slice(g, g + 256)
            pre = conv_ref[at, wide]
            sig = sigmoid(pre)
            dconv = dact[at, wide] * (sig * (1.0 + pre * (1.0 - sig)))
            block = jnp.concatenate(
                [
                    behind[:, g : g + 256].astype(jnp.float32),
                    proj_ref[at, wide].astype(jnp.float32),
                ]
            )
            grad = jnp.concatenate([dconv, after[:, wide]])
            total = taps_ref[3:4, wide] * dconv
            dtaps_ref[3:4, wide] += jnp.sum(dconv * block[16:], axis=0, keepdims=True)
            first = jnp.zeros((8, 256), jnp.float32)
            for s in (1, 2, 3):
                masked = grad * masks[:, 1 + s : 2 + s]
                tap = taps_ref[3 - s : 4 - s, wide]
                total = total + tap * masked[s : s + TILE]
                dtaps_ref[3 - s : 4 - s, wide] += jnp.sum(
                    masked[:TILE] * block[16 - s : 16 - s + TILE], axis=0, keepdims=True
                )
                first = first + tap * jnp.concatenate(
                    [jnp.zeros((8, 256), jnp.float32), masked[0:8]]
                )[s : s + 8]
            dproj_ref[at, wide] = total.astype(dproj_ref.dtype)
            after[:, wide] = dconv[0:8]
            back[0, :, wide] = first

            @pl.when(c == tiles - 1)
            def _():
                tail[:, wide] = total[TILE - 16 :]

        return 0

    lax.fori_loop(0, tiles, outside, 0)

    home = remote(
        back.at[0], back.at[1], b_sem.at[0], b_sem.at[1], lax.rem(me + n - 1, n)
    )

    @pl.when(me > 0)
    def _():
        home.start()

    @pl.when(me < n - 1)
    def _():
        home.wait_recv()

    @pl.when(me == n - 1)
    def _():
        back[1] = jnp.zeros(back.shape[1:], jnp.float32)

    dproj_ref[pl.ds(tiles * TILE - 16, 16), :] = (
        tail[...] + jnp.concatenate([jnp.zeros((8, channels), jnp.float32), back[1]])
    ).astype(dproj_ref.dtype)

    @pl.when(me > 0)
    def _():
        home.wait_send()


def recurrence_back(
    proj, halo, conv, cum, logits, o, gate, du, starts, cols, rows, taps, gain
):
    n = lax.axis_size("seq")
    sizes = axis_sizes(n)
    length, channels = proj.shape
    keys = cum.shape[1]
    heads = keys // DK
    value = heads * DV
    tiles = length // TILE
    f32 = jnp.float32
    shape = jax.ShapeDtypeStruct
    return pl.pallas_call(
        functools.partial(backward_kernel, n, sizes),
        out_shape=(
            shape((length, channels), jnp.bfloat16),
            shape((length, value), jnp.bfloat16),
            shape((length, keys), f32),
            shape((8, channels), f32),
            shape((8, DV), f32),
        ),
        scratch_shapes=[
            pltpu.VMEM((length, value), f32),
            pltpu.VMEM((length, channels), f32),
            pltpu.VMEM((heads, DV, DK), f32),
            pltpu.VMEM((tiles, heads, DV, DK), f32),
            pltpu.VMEM((8, channels), f32),
            pltpu.VMEM((2, 8, channels), f32),
            pltpu.VMEM((16, channels), f32),
        ]
        + chain_scratch(sizes, heads * DV // TILE)
        + [pltpu.SemaphoreType.DMA((2,))],
        compiler_params=pltpu.CompilerParams(
            collective_id=5, has_side_effects=True, vmem_limit_bytes=60 << 20
        ),
    )(proj, halo, conv, cum, logits, o, gate, du, starts, cols, rows, taps, gain)


def rms_stats(values):
    return lax.rsqrt(jnp.mean(values * values, axis=-1, keepdims=True) + norm_epsilon)


def rms_back(values, inverse, gain, upstream):
    scaled = gain * upstream
    return inverse * scaled - values * inverse * inverse * inverse * jnp.mean(
        scaled * values, axis=-1, keepdims=True
    )


def swish_slope(values):
    sigmoid = jax.nn.sigmoid(values)
    return sigmoid * (1.0 + values * (1.0 - sigmoid))


def segment_of(positions, lengths, packing):
    packed = jnp.take(lengths, packing)
    starts = jnp.cumsum(packed) - packed
    filled = jnp.sum(packed)
    counted = jnp.sum((starts[None, :] <= positions[:, None]).astype(jnp.int32), axis=1)
    return (counted + (positions >= filled).astype(jnp.int32), positions < filled)


def plain_adam(param, gradient, first, second, rate):
    first_next = moment_decay * first + (1.0 - moment_decay) * gradient
    second_next = moment_decay * second + (1.0 - moment_decay) * gradient * gradient
    return (
        param - rate * first_next / (jnp.sqrt(second_next) + adam_epsilon),
        first_next,
        second_next,
    )


def body(
    tokens,
    cotangent,
    lengths,
    packing,
    owners,
    slot_copy,
    slot_master,
    slot_first,
    slot_second,
    basis_left,
    basis_right,
    norm_gains,
    gains_first,
    gains_second,
    gate_down,
    down_first,
    down_second,
    gate_up,
    upper_first,
    upper_second,
    head_gain,
    head_first,
    head_second,
    conv_weight,
    conv_first,
    conv_second,
):
    tok_rows = tokens.shape[0]
    model_width = tokens.shape[1]
    block_width = slot_copy.shape[2]
    rank_width = gate_down.shape[1]
    tap_count = conv_weight.shape[0]
    key_width = gate_up.shape[1]
    channels = conv_weight.shape[1]
    value_width = channels - 2 * key_width
    block_total = owners.shape[1]
    count_in = (channels + value_width) // block_width
    count_out = value_width // block_width
    count_down = (block_total - count_in - count_out) // 3
    count_up = 2 * count_down
    up_end = count_in + count_up
    out_end = up_end + count_out
    seq_index = lax.axis_index("seq")
    base_pos = seq_index * tok_rows
    ext_seg, ext_valid = segment_of(
        base_pos - 8 + jnp.arange(tok_rows + 8, dtype=jnp.int32), lengths, packing
    )
    own_seg = ext_seg[8:]
    own_valid = ext_valid[8:].astype(jnp.float32)
    tiles = tok_rows // TILE
    seg_tiles = own_seg.reshape(tiles, TILE)
    tile_prev = jnp.repeat(ext_seg[7 : 7 + tok_rows : TILE], TILE)
    tile_last = jnp.repeat(seg_tiles[:, -1], TILE)
    same = [tile_prev, tile_last] + [ext_seg[8 - s : 8 - s + tok_rows] for s in (1, 2, 3)]
    cols = jnp.stack(
        [(other == own_seg).astype(jnp.float32) for other in same]
        + [jnp.zeros_like(own_valid), own_seg.astype(jnp.float32), own_valid],
        axis=1,
    )
    cols = jnp.pad(cols, ((0, 8), (0, 0)))
    rows = seg_tiles.astype(jnp.float32)
    rim_tokens = passed_along(tokens[tok_rows - 16 :], "seq", 1).astype(jnp.float32)
    weights = gather_weights(
        slot_copy,
        owners,
        [
            (at, at + hi - lo, order)
            for _, lo, hi, at, order in build_plan(
                (block_total,), (0.43, 0.86, 1.0), 4, ((0, 1, 2), (0, 2, 1), (2, 1, 0))
            )
        ],
    )
    in_weights = weights[:, : count_in * block_width]
    up_weights = weights[:, count_in * block_width : up_end * block_width]
    out_weights = weights[:, up_end * block_width : out_end * block_width]
    down_weights = weights[:, out_end * block_width :]
    inputs = tokens.astype(jnp.float32)
    inverse_one = rms_stats(inputs)
    normed = (inputs * inverse_one * norm_gains[0]).astype(jnp.bfloat16)
    rim_normed = (rim_tokens * rms_stats(rim_tokens) * norm_gains[0]).astype(jnp.bfloat16)
    projected = jnp.dot(normed, in_weights, preferred_element_type=jnp.float32)
    mixed_proj = projected[:, :channels].astype(jnp.bfloat16)
    gate_pre = projected[:, channels:]
    down_low = gate_down.astype(jnp.bfloat16)
    lowrank = jnp.dot(normed, down_low, preferred_element_type=jnp.float32)
    logits = (
        jnp.dot(lowrank, gate_up[:rank_width], precision=highest_precision) + gate_up[rank_width]
    )
    log_gate = jax.nn.log_sigmoid(logits) / gate_scale
    halo = jnp.dot(
        rim_normed, in_weights[:, :channels], preferred_element_type=jnp.float32
    ).astype(jnp.bfloat16)
    gain_row = head_gain[None]
    conv_pre, cumulative, attended, gated_out, starts = recurrence(
        mixed_proj, halo, log_gate, gate_pre, cols, rows, conv_weight, gain_row
    )
    attn_part = jnp.einsum(
        "tn,dn->td", gated_out, out_weights, preferred_element_type=jnp.float32
    )
    attn_branch = lax.psum(attn_part, "head")
    hidden_one = inputs + attn_branch
    inverse_two = rms_stats(hidden_one)
    normed_two = (hidden_one * inverse_two * norm_gains[1]).astype(jnp.bfloat16)
    pair_proj = jnp.dot(normed_two, up_weights, preferred_element_type=jnp.float32)
    half_width = pair_proj.shape[1] // 2
    gate_mlp = pair_proj[:, :half_width]
    up_mlp = pair_proj[:, half_width:]
    hidden = (jax.nn.silu(gate_mlp) * up_mlp).astype(jnp.bfloat16)
    mlp_part = jnp.einsum("tn,dn->td", hidden, down_weights, preferred_element_type=jnp.float32)
    mlp_branch = lax.psum(mlp_part.astype(jnp.bfloat16), "head").astype(jnp.float32)
    result = (hidden_one + mlp_branch).astype(jnp.bfloat16)
    upstream = cotangent.astype(jnp.float32) * own_valid[:, None]
    upstream_low = upstream.astype(jnp.bfloat16)
    grad_hidden = jnp.dot(upstream_low, down_weights, preferred_element_type=jnp.float32)
    grad_gate_mlp = grad_hidden * up_mlp * swish_slope(gate_mlp)
    grad_up_mlp = grad_hidden * jax.nn.silu(gate_mlp)
    grad_pair = jnp.concatenate([grad_gate_mlp, grad_up_mlp], axis=1).astype(jnp.bfloat16)
    grad_normed_two = lax.psum(
        jnp.einsum("tn,dn->td", grad_pair, up_weights, preferred_element_type=jnp.float32), "head"
    )
    grad_gains_two = jnp.sum(grad_normed_two * hidden_one * inverse_two, axis=0)
    grad_one = upstream + rms_back(hidden_one, inverse_two, norm_gains[1], grad_normed_two)
    grad_attn = grad_one.astype(jnp.bfloat16)
    grad_gated = jnp.dot(grad_attn, out_weights, preferred_element_type=jnp.float32)
    grad_mixed, grad_gate_pre, grad_logits, tap_grads, gain_grads = recurrence_back(
        mixed_proj,
        halo,
        conv_pre,
        cumulative,
        logits,
        attended,
        gate_pre,
        grad_gated,
        starts,
        cols,
        rows,
        conv_weight,
        gain_row,
    )
    grad_conv_weight = tap_grads[:tap_count]
    grad_head_gain = gain_grads[0]
    grad_upper = jnp.concatenate(
        [
            jnp.einsum("tr,tk->rk", lowrank, grad_logits, precision=highest_precision),
            jnp.sum(grad_logits, axis=0, keepdims=True),
        ],
        axis=0,
    )
    grad_lowrank = jnp.einsum(
        "tk,rk->tr", grad_logits, gate_up[:rank_width], precision=highest_precision
    ).astype(jnp.bfloat16)
    grad_down_part = jnp.einsum(
        "tr,td->rd", grad_lowrank, normed, preferred_element_type=jnp.float32
    )
    grad_projected = jnp.concatenate(
        [grad_mixed, grad_gate_pre], axis=1
    )
    grad_normed_part = jnp.einsum(
        "tn,dn->td", grad_projected, in_weights, preferred_element_type=jnp.float32
    ) + jnp.einsum("tr,dr->td", grad_lowrank, down_low, preferred_element_type=jnp.float32)
    grad_normed = lax.psum(grad_normed_part.astype(jnp.bfloat16), "head").astype(jnp.float32)
    grad_gains_one = jnp.sum(grad_normed * inputs * inverse_one, axis=0)
    grad_input = grad_one + rms_back(inputs, inverse_one, norm_gains[0], grad_normed)
    slots_dev = slot_copy.shape[0]
    slot_total = slots_dev * lax.axis_size("seq")
    grads = [
        jnp.einsum("td,tn->dn", left, right, preferred_element_type=jnp.float32).astype(
            jnp.bfloat16
        )
        for left, right in (
            (normed, grad_projected),
            (normed_two, grad_pair),
            (grad_attn, gated_out),
            (upstream_low, hidden),
        )
    ]
    named = jnp.arange(slot_total, dtype=jnp.int32)[:, None] == owners
    inverse = jnp.where(
        jnp.any(named, axis=1),
        jnp.sum(named * jnp.arange(block_total, dtype=jnp.int32), axis=1),
        block_total,
    ).astype(jnp.int32)[None]
    owned_grads = scatter_grads(
        grads,
        inverse,
        build_plan(
            (count_in, count_up, count_out, count_down),
            (0.43, 0.86, 1.0),
            8,
            ((2, 1, 0), (1, 2, 0), (0, 1, 2)),
        ),
        slots_dev,
        block_total,
    ).astype(jnp.float32)
    rotated = jnp.einsum("sij,sik->sjk", basis_left, owned_grads, precision=highest_precision)
    rotated = jnp.einsum("sjk,skl->sjl", rotated, basis_right, precision=highest_precision)
    first_next = moment_decay * slot_first + (1.0 - moment_decay) * rotated
    second_next = moment_decay * slot_second + (1.0 - moment_decay) * rotated * rotated
    direction = first_next / (jnp.sqrt(second_next) + adam_epsilon)
    restored = jnp.einsum("sij,sjk->sik", basis_left, direction, precision=highest_precision)
    restored = jnp.einsum("sik,slk->sil", restored, basis_right, precision=highest_precision)
    master_next = slot_master - rate_block * restored
    shared_rows, own_rows = rank_width + 8, 16
    shared = jnp.concatenate(
        [
            grad_down_part,
            jnp.pad(grad_head_gain, (0, model_width - grad_head_gain.shape[0]))[None],
            jnp.zeros((7, model_width), jnp.float32),
        ]
    )
    flat_upper = grad_upper.reshape(-1)
    upper_rows = -(-flat_upper.shape[0] // model_width)
    alone = jnp.concatenate(
        [
            jnp.stack([grad_gains_one, grad_gains_two]),
            grad_conv_weight,
            jnp.pad(flat_upper, (0, upper_rows * model_width - flat_upper.shape[0])).reshape(
                upper_rows, model_width
            ),
        ]
    )
    alone = jnp.pad(alone, ((0, own_rows - alone.shape[0]), (0, 0)))
    summed = sum_small(jnp.concatenate([shared, alone]), shared_rows)
    down_grad = summed[:rank_width].T
    head_grad = summed[rank_width, : grad_head_gain.shape[0]]
    gains_grad = summed[shared_rows : shared_rows + 2]
    conv_grad = summed[shared_rows + 2 : shared_rows + 2 + tap_count]
    upper_grad = (
        summed[shared_rows + 2 + tap_count : shared_rows + 2 + tap_count + upper_rows]
        .reshape(-1)[: flat_upper.shape[0]]
        .reshape(grad_upper.shape)
    )
    gains_next, gains_first_next, gains_second_next = plain_adam(
        norm_gains, gains_grad, gains_first, gains_second, rate_gains
    )
    down_next, down_first_next, down_second_next = plain_adam(
        gate_down, down_grad, down_first, down_second, rate_down
    )
    upper_next, upper_first_next, upper_second_next = plain_adam(
        gate_up, upper_grad, upper_first, upper_second, rate_upper
    )
    head_next, head_first_next, head_second_next = plain_adam(
        head_gain, head_grad, head_first, head_second, rate_head
    )
    conv_next, conv_first_next, conv_second_next = plain_adam(
        conv_weight, conv_grad, conv_first, conv_second, rate_conv
    )
    return (
        result,
        grad_input,
        owned_grads,
        master_next,
        first_next,
        second_next,
        master_next.astype(jnp.bfloat16),
        gains_grad,
        gains_next,
        gains_first_next,
        gains_second_next,
        down_grad,
        down_next,
        down_first_next,
        down_second_next,
        upper_grad,
        upper_next,
        upper_first_next,
        upper_second_next,
        head_grad,
        head_next,
        head_first_next,
        head_second_next,
        conv_grad,
        conv_next,
        conv_first_next,
        conv_second_next,
    )


def solution(mesh):
    placed = (
        P("seq", None),
        P("seq", None),
        P(),
        P(),
        P("head", None),
        P(("seq", "head"), None, None),
        P(("seq", "head"), None, None),
        P(("seq", "head"), None, None),
        P(("seq", "head"), None, None),
        P(("seq", "head"), None, None),
        P(("seq", "head"), None, None),
        P(),
        P(),
        P(),
        P(),
        P(),
        P(),
        P(None, "head"),
        P(None, "head"),
        P(None, "head"),
        P(),
        P(),
        P(),
        P(None, "head"),
        P(None, "head"),
        P(None, "head"),
    )
    return jax.shard_map(
        body,
        mesh=mesh,
        in_specs=placed,
        out_specs=(
            P("seq", None),
            P("seq", None),
            P(("seq", "head"), None, None),
            P(("seq", "head"), None, None),
            P(("seq", "head"), None, None),
            P(("seq", "head"), None, None),
            P(("seq", "head"), None, None),
            P(),
            P(),
            P(),
            P(),
            P(),
            P(),
            P(),
            P(),
            P(None, "head"),
            P(None, "head"),
            P(None, "head"),
            P(None, "head"),
            P(),
            P(),
            P(),
            P(),
            P(None, "head"),
            P(None, "head"),
            P(None, "head"),
            P(None, "head"),
        ),
        check_vma=False,
    )
```

```python
import functools

import jax
import jax.numpy as jnp
from jax import lax
from jax.experimental import pallas as pl
from jax.experimental.pallas import tpu as pltpu
from jax.sharding import PartitionSpec as P

MESH = pl.DeviceIdType.MESH

DK = 128
DV = 256


highest_precision = lax.Precision.HIGHEST
norm_epsilon = 1e-06
adam_epsilon = 1e-08
gate_scale = 16.0
moment_decay = 0.5
rate_block = 0.03
rate_gains = 0.45
rate_down = 0.02
rate_upper = 0.6
rate_head = 0.5
rate_conv = 0.1


def axis_sizes(n):
    side = 1
    while (side * 2) ** 2 * 4 <= n:
        side *= 2
    return (n // (side * side), side, side)


def coords(me, sizes):
    _, rows, columns = sizes
    return [me // (rows * columns), (me // columns) % rows, me % columns]


def index_of(c, sizes):
    _, rows, columns = sizes
    return (c[0] * rows + c[1]) * columns + c[2]


def neighbour(c, sizes, ax, j):
    d = list(c)
    d[ax] = lax.rem(c[ax] + j, sizes[ax])
    return index_of(d, sizes)


def enter(n, me, mate=False):
    barrier = pltpu.get_barrier_semaphore()
    if mate:
        core = lax.axis_index("head")
        pl.semaphore_signal(barrier, inc=1, device_id={"head": 1 - core}, device_id_type=MESH)
    for j in range(1, n):
        pl.semaphore_signal(
            barrier, inc=1, device_id={"seq": lax.rem(me + j, n)}, device_id_type=MESH
        )
    pl.semaphore_wait(barrier, n - 1 + int(mate))


def remote(src, dst, send_sem, recv_sem, peer):
    return pltpu.make_async_remote_copy(
        src_ref=src,
        dst_ref=dst,
        send_sem=send_sem,
        recv_sem=recv_sem,
        device_id={"seq": peer},
        device_id_type=MESH,
    )


def build_plan(widths, parts, pieces, orders, base=0):
    total = sum(widths)
    bounds = [sum(widths[:i]) for i in range(len(widths) + 1)]
    cuts = [round(total * f) for f in (0.0,) + parts]
    plan, at = [], 0
    for i in range(pieces):
        for order, lo, hi in zip(orders, cuts[:-1], cuts[1:], strict=True):
            size = hi - lo
            left = size * (i + 1) // pieces - size * i // pieces
            while left:
                which = max(q for q in range(len(widths)) if bounds[q] <= at)
                step = min(left, bounds[which + 1] - at)
                start = at - bounds[which]
                plan.append((which, start, start + step, at + base, order, i))
                at += step
                left -= step
    return plan


def groups_of(plan):
    streams = {}
    for i, chunk in enumerate(plan):
        streams.setdefault(chunk[4], {}).setdefault(chunk[5], []).append(i)
    return streams


def gather_steps(sizes, plan, piece, outs, bw, send, recv):
    c = coords(lax.axis_index("seq"), sizes)
    most = max(sizes)

    def copies(i, k):
        which, lo, hi, at, order, _ = plan[i]
        ax = order[k]
        wide = pl.ds(lo * bw, (hi - lo) * bw)
        index = tuple(slice(None) if a in order[:k] else c[a] for a in range(3))
        index += (slice(None), wide)
        target = outs[which].at[index]
        source = target if k else piece.at[:, pl.ds(at * bw, (hi - lo) * bw)]
        return [
            remote(
                source,
                target,
                send.at[(i * 3 + k) * most + j],
                recv.at[(i * 3 + k) * most + j],
                neighbour(c, sizes, ax, j),
            )
            for j in range(1, sizes[ax])
        ]

    streams = groups_of(plan)
    longest = max(max(s) for s in streams.values()) + 1

    def step(s):
        for k in (2, 1, 0):
            for groups in streams.values():
                for i in groups.get(s - k, ()):
                    if k:
                        for copy in copies(i, k - 1):
                            copy.wait_recv()
                    for copy in copies(i, k):
                        copy.start()

    def arrived(piece_range):
        for groups in streams.values():
            for s in piece_range:
                for i in groups.get(s, ()):
                    for copy in copies(i, 2):
                        copy.wait_recv()

    def sent():
        for i in range(len(plan)):
            for k in range(3):
                for copy in copies(i, k):
                    copy.wait_send()

    return [functools.partial(step, s) for s in range(longest + 2)], arrived, sent


def scatter_scratch(sizes, plan, rows, bw, dtype):
    own, first, second, third = [], [], [], []
    for _, lo, hi, _, order, _ in plan:
        wide = (hi - lo) * bw
        rest = tuple(sizes[q] for q in range(3) if q != order[0])
        own.append(pltpu.VMEM(rest + (rows, wide), dtype))
        first.append(pltpu.VMEM((sizes[order[0]] - 1,) + rest + (rows, wide), dtype))
        second.append(pltpu.VMEM((sizes[order[1]], sizes[order[2]], rows, wide), dtype))
        third.append(pltpu.VMEM((sizes[order[2]], rows, wide), dtype))
    count = len(plan) * 3 * max(sizes)
    return (
        own
        + first
        + second
        + third
        + [
            pltpu.SemaphoreType.DMA((count,)),
            pltpu.SemaphoreType.DMA((count,)),
            pltpu.SemaphoreType.DMA((len(plan),)),
        ]
    )


def scatter_steps(sizes, plan, grads, scratch, fin, bw):
    c = coords(lax.axis_index("seq"), sizes)
    most, count = max(sizes), len(plan)
    own, first, second, third = (scratch[i * count : (i + 1) * count] for i in range(4))
    send, recv, load = scratch[4 * count :]

    def loading(i):
        which, lo, hi, _, order, _ = plan[i]
        index = tuple(c[q] if q == order[0] else slice(None) for q in range(3))
        index += (slice(None), pl.ds(lo * bw, (hi - lo) * bw))
        return pltpu.make_async_copy(grads[which].at[index], own[i], load.at[i])

    def copies(i, k):
        which, lo, hi, _, order, _ = plan[i]
        ax = order[k]
        left = sorted(set(range(3)) - set(order[:k]))
        result = []
        for j in range(1, sizes[ax]):
            there = lax.rem(c[ax] + j, sizes[ax])
            index = tuple(there if q == ax else slice(None) for q in left)
            if k == 0:
                index += (slice(None), pl.ds(lo * bw, (hi - lo) * bw))
                source, target = grads[which].at[index], first[i].at[j - 1]
            elif k == 1:
                source, target = own[i].at[index], second[i].at[j]
            else:
                source, target = second[i].at[(0,) + index], third[i].at[j]
            s = (i * 3 + k) * most + j
            result.append(
                remote(source, target, send.at[s], recv.at[s], neighbour(c, sizes, ax, j))
            )
        return result

    def combine(i, k):
        _, lo, hi, at, order, _ = plan[i]
        if k == 0:
            loading(i).wait()
        for copy in copies(i, k):
            copy.wait_recv()
        size = sizes[order[k]]
        if k == 0:
            outer, inner = own[i].shape[:2]

            def add(t, _):
                u, v = t // inner, t % inner
                total = own[i][u, v].astype(jnp.float32)
                for j in range(size - 1):
                    total = total + first[i][j, u, v].astype(jnp.float32)
                own[i][u, v] = total.astype(own[i].dtype)
                return 0

            lax.fori_loop(0, outer * inner, add, 0)
        elif k == 1:
            leading = sorted(set(range(3)) - {order[0]}).index(order[1]) == 0

            def add(t, _):
                total = own[i][(c[order[1]], t) if leading else (t, c[order[1]])]
                total = total.astype(jnp.float32)
                for j in range(1, size):
                    total = total + second[i][j, t].astype(jnp.float32)
                second[i][0, t] = total.astype(own[i].dtype)
                return 0

            lax.fori_loop(0, sizes[order[2]], add, 0)
        else:
            total = second[i][0, c[order[2]]].astype(jnp.float32)
            for j in range(1, size):
                total = total + third[i][j].astype(jnp.float32)
            for b in range(hi - lo):
                fin[at + b] = total[:, b * bw : (b + 1) * bw].astype(fin.dtype)

    streams = groups_of(plan)
    longest = max(max(s) for s in streams.values()) + 1

    def step(s):
        for k in range(4):
            for groups in streams.values():
                for i in groups.get(s - k, ()):
                    if k == 0:
                        loading(i).start()
                    else:
                        combine(i, k - 1)
                    if k < 3:
                        for copy in copies(i, k):
                            copy.start()

    def sent():
        for i in range(count):
            for k in range(3):
                for copy in copies(i, k):
                    copy.wait_send()

    return [functools.partial(step, s) for s in range(longest + 3)], sent


SPREAD = ((2, 1, 0), (1, 2, 0), (0, 1, 2))
COLLECT = ((0, 1, 2), (0, 2, 1), (2, 1, 0))
SHARES = (0.43, 0.86, 1.0)


def scatter_kernel(n, sizes, plan, shared, inv_ref, small_ref, grad_ref, early_ref, *refs):
    out_ref, small_out, fin, send, a_send, a_recv, l_sem = refs[:7]
    small = sum_steps(sizes, shared, small_ref, small_out, *refs[-5:])
    me = lax.axis_index("seq")
    slots, _, rows, bw = out_ref.shape
    count = fin.shape[0] - 1 - early_ref.shape[0]
    enter(n, me, True)
    steps, sent = scatter_steps(sizes, plan, [grad_ref], refs[7:-5], fin, bw)
    small[0]()
    steps[0]()
    fin[fin.shape[0] - 1] = jnp.zeros(fin.shape[1:], fin.dtype)
    fin[count : fin.shape[0] - 1] = early_ref[...]
    for s, step in enumerate(steps[1:]):
        step()
        if s + 1 < len(small):
            small[s + 1]()
    for s in range(send.shape[0]):
        send[s] = fin[inv_ref[0, s]]

    def move(j):
        p = lax.rem(me + j, n)
        return remote(
            send.at[pl.ds(p * slots, slots)], out_ref.at[:, me], a_send.at[j], a_recv.at[j], p
        )

    for j in range(1, n):
        move(j).start()
    mine = pltpu.make_async_copy(
        send.at[pl.ds(me * slots, slots)], out_ref.at[:, me], l_sem.at[0]
    )
    mine.start()
    for step in small[len(steps) :]:
        step()
    mine.wait()
    for j in range(1, n):
        move(j).wait()
    sent()


def scatter_grads(grad, early, inverse, slots, small, shared):
    n = lax.axis_size("seq")
    sizes = axis_sizes(n)
    most = max(sizes)
    depth, columns = grad.shape
    _, rows, bw = early.shape
    blocks = columns // bw
    plan = build_plan((blocks,), SHARES, 2, SPREAD)
    shape = jax.ShapeDtypeStruct
    vmem, anywhere = pl.BlockSpec(memory_space=pltpu.VMEM), pl.BlockSpec(memory_space=pl.ANY)
    out, summed = pl.pallas_call(
        functools.partial(scatter_kernel, n, sizes, plan, shared),
        out_shape=(shape((slots, n, rows, bw), grad.dtype), shape(small.shape, small.dtype)),
        in_specs=[pl.BlockSpec(memory_space=pltpu.SMEM), vmem, anywhere, vmem],
        out_specs=(anywhere, vmem),
        scratch_shapes=[
            pltpu.VMEM((blocks + early.shape[0] + 1, rows, bw), grad.dtype),
            pltpu.VMEM((slots * n, rows, bw), grad.dtype),
            pltpu.SemaphoreType.DMA((n,)),
            pltpu.SemaphoreType.DMA((n,)),
            pltpu.SemaphoreType.DMA((1,)),
        ]
        + scatter_scratch(sizes, plan, rows, bw, grad.dtype)
        + [
            pltpu.VMEM((shared,) + small.shape[1:], small.dtype),
            pltpu.VMEM((3,) + small.shape, small.dtype),
            pltpu.VMEM((3, most) + small.shape, small.dtype),
            pltpu.SemaphoreType.DMA((1 + 3 * most,)),
            pltpu.SemaphoreType.DMA((1 + 3 * most,)),
        ],
        compiler_params=pltpu.CompilerParams(
            collective_id=2, has_side_effects=True, vmem_limit_bytes=48 << 20
        ),
    )(inverse, small, grad.reshape(sizes + (rows, columns)), early)
    return out.reshape(slots, depth, bw), summed


def sum_steps(sizes, shared, x_ref, out_ref, mate, acc, bufs, send, recv):
    me, core = lax.axis_index("seq"), lax.axis_index("head")
    c = coords(me, sizes)
    most = max(sizes)
    swap = pltpu.make_async_remote_copy(
        src_ref=x_ref.at[pl.ds(0, shared)],
        dst_ref=mate,
        send_sem=send.at[0],
        recv_sem=recv.at[0],
        device_id={"head": 1 - core},
        device_id_type=MESH,
    )

    def going(step, ax):
        copies = []
        for j in range(1, sizes[ax]):
            d = list(c)
            d[ax] = lax.rem(c[ax] + j, sizes[ax])
            q = 1 + ax * most + j
            copies.append(
                remote(
                    acc.at[step], bufs.at[ax, c[ax]], send.at[q], recv.at[q], index_of(d, sizes)
                )
            )
        return copies

    def total(ax):
        value = bufs[ax, 0]
        for j in range(1, sizes[ax]):
            value = value + bufs[ax, j]
        return value

    def start(step, ax):
        bufs[ax, c[ax]] = acc[step]
        for copy in going(step, ax):
            copy.start()

    def swapped():
        swap.wait()
        acc[0, 0:shared] = x_ref[0:shared] + mate[...]
        acc[0, shared:] = x_ref[shared:]
        start(0, 2)

    def moved(step, ax):
        for copy in going(step, ax):
            copy.wait()
        if step < 2:
            acc[step + 1] = total(ax)
            start(step + 1, ax - 1)
        else:
            out_ref[...] = total(ax)

    return [
        swap.start,
        swapped,
        functools.partial(moved, 0, 2),
        functools.partial(moved, 1, 1),
        functools.partial(moved, 2, 0),
    ]


NN = (((1,), (0,)), ((), ()))
NT = (((1,), (1,)), ((), ()))
TN = (((0,), (0,)), ((), ()))
TILE = 128


def halves(values):
    high = values.astype(jnp.bfloat16)
    return high, (values - high.astype(jnp.float32)).astype(jnp.bfloat16)


def product(left, right, dims):
    (lh, ll), (rh, rl) = left, right
    dot = functools.partial(
        lax.dot_general, dimension_numbers=dims, preferred_element_type=jnp.float32
    )
    return dot(lh, rh) + (dot(lh, rl) + dot(ll, rh))


def running_sum(table, values):
    first = values.astype(jnp.bfloat16)
    rest = values - first.astype(jnp.float32)
    second, third = halves(rest)
    dot = functools.partial(
        lax.dot_general, dimension_numbers=NN, preferred_element_type=jnp.float32
    )
    return dot(table, first) + (dot(table, second) + dot(table, third))


def sigmoid(values):
    return 1.0 / (1.0 + jnp.exp(-values))


def chain_tools(n, sizes, forward, mine, bufs, send, recv, result):
    me = lax.axis_index("seq")
    c = coords(me, sizes)
    pieces = mine.shape[0]
    across, along, before, held = bufs
    most = max(sizes)
    state = pl.ds(0, TILE)
    decay = pl.ds(TILE, 1)

    def peers(ax):
        return [j for j in range(1, sizes[ax])]

    def to(ax, j):
        d = list(c)
        d[ax] = lax.rem(c[ax] + j, sizes[ax])
        return index_of(d, sizes)

    def line(buf, source, ax, j, p, base):
        s = base + j * pieces + p
        return remote(source.at[p], buf.at[c[ax], p], send.at[s], recv.at[s], to(ax, j))

    def hop(p):
        s = 2 * most * pieces + p
        step = 1 if forward else -1
        d = [lax.rem(c[0] + step + sizes[0], sizes[0]), c[1], c[2]]
        return remote(held.at[1, p], held.at[0, p], send.at[s], recv.at[s], index_of(d, sizes))

    def compose(first, second):
        return (second[1] * first[0] + second[0], first[1] * second[1])

    def reduce_line(buf, ax, p):
        size = sizes[ax]
        order = range(size) if forward else range(size - 1, -1, -1)
        prefix = (jnp.zeros((TILE, TILE), jnp.float32), jnp.ones((1, TILE), jnp.float32))
        total = None
        for i in order:
            item = (buf[i, p, state], buf[i, p, decay])
            longer = compose(prefix, item)
            take = (i < c[ax]) if forward else (i > c[ax])
            prefix = tuple(jnp.where(take, a, b) for a, b in zip(longer, prefix, strict=True))
            total = item if total is None else compose(total, item)
        return prefix, total

    def start_x():
        for p in range(pieces):
            across[c[2], p] = mine[p]
            for j in peers(2):
                line(across, mine, 2, j, p, 0).start()

    def start_y():
        for p in range(pieces):
            for j in peers(2):
                line(across, mine, 2, j, p, 0).wait_recv()
            prefix, total = reduce_line(across, 2, p)
            before[p, state], before[p, decay] = prefix
            held[2, p, state], held[2, p, decay] = total
            held[2, p, pl.ds(TILE + 1, 7)] = jnp.zeros((7, TILE), jnp.float32)
            along[c[1], p] = held[2, p]
            for j in peers(1):
                line(along, held.at[2], 1, j, p, most * pieces).start()

    first_z = 0 if forward else sizes[0] - 1
    last_z = sizes[0] - 1 - first_z

    def start_z():
        for p in range(pieces):
            for j in peers(1):
                line(along, held.at[2], 1, j, p, most * pieces).wait_recv()
            prefix, total = reduce_line(along, 1, p)
            own = (before[p, state], before[p, decay])
            before[p, state], before[p, decay] = compose(prefix, own)
            held[1, p, state], held[1, p, decay] = total
            held[1, p, pl.ds(TILE + 1, 7)] = jnp.zeros((7, TILE), jnp.float32)

            @pl.when(c[0] == first_z)
            def _():
                held[0, p] = jnp.zeros((TILE + 8, TILE), jnp.float32)
                hop(p).start()

    def pass_z(k):
        at = k if forward else sizes[0] - 1 - k

        @pl.when(c[0] == at)
        def _():
            for p in range(pieces):
                hop(p).wait_recv()
                if at != last_z:
                    got = (held[0, p, state], held[0, p, decay])
                    item = (held[1, p, state], held[1, p, decay])
                    held[1, p, state], held[1, p, decay] = compose(got, item)
                    hop(p).start()

    def finish():
        for p in range(pieces):
            result[p] = before[p, decay] * held[0, p, state] + before[p, state]
            for j in peers(2):
                line(across, mine, 2, j, p, 0).wait_send()
            for j in peers(1):
                line(along, held.at[2], 1, j, p, most * pieces).wait_send()

        @pl.when(c[0] != last_z)
        def _():
            for p in range(pieces):
                hop(p).wait_send()

    stages = [start_x, start_y, start_z]
    stages += [functools.partial(pass_z, k) for k in range(1, sizes[0])]
    return stages, finish


def greet(n, sizes, extra):
    c = coords(lax.axis_index("seq"), sizes)
    barrier = pltpu.get_barrier_semaphore()
    count = 0
    for ax in range(3):
        for j in range(1, sizes[ax]):
            d = list(c)
            d[ax] = lax.rem(c[ax] + j, sizes[ax])
            pl.semaphore_signal(
                barrier, inc=1, device_id={"seq": index_of(d, sizes)}, device_id_type=MESH
            )
            count += 1
    for index in extra:
        pl.semaphore_signal(barrier, inc=1, device_id={"seq": index}, device_id_type=MESH)
        count += 1
    pl.semaphore_wait(barrier, count)


def tile_masks(rows_ref, cols_ref, c):
    row = rows_ref[pl.ds(c, 1), :]
    col = cols_ref[pl.ds(pl.multiple_of(c * TILE, TILE), TILE), 6:7]
    i = lax.broadcasted_iota(jnp.int32, (TILE, TILE), 0)
    j = lax.broadcasted_iota(jnp.int32, (TILE, TILE), 1)
    return (i >= j) & (row == col)


def forward_kernel(
    n,
    sizes,
    plan,
    ready,
    owners_ref,
    lengths_ref,
    packing_ref,
    slot_ref,
    tokens_ref,
    norm_ref,
    down_ref,
    upper_ref,
    taps_ref,
    gain_ref,
    w_in_out,
    w_up_out,
    w_out_out,
    w_down_out,
    normed_out,
    lowrank_ref,
    logits_out,
    proj_out,
    halo_ref,
    gate_out,
    conv_out,
    cum_out,
    o_out,
    u_out,
    start_out,
    cols_ref,
    rows_ref,
    normed,
    logits_ref,
    proj_ref,
    gate_ref,
    conv_ref,
    cum_ref,
    o_ref,
    u_ref,
    start_ref,
    slots,
    piece,
    w_in,
    rim,
    segs,
    act,
    state,
    prev,
    a_send,
    a_recv,
    g_send,
    g_recv,
    l_sem,
    mine,
    across,
    along,
    before,
    held,
    result,
    send,
    recv,
):
    me = lax.axis_index("seq")
    c3 = coords(me, sizes)
    length, width = tokens_ref.shape
    tiles, channels = length // TILE, proj_ref.shape[1]
    keys = logits_ref.shape[1]
    rank = down_ref.shape[1]
    heads = keys // DK
    value = DV * heads
    slots_dev, _, bw = slot_ref.shape
    rows = piece.shape[0]
    scale = DK ** (-0.5)
    enter(n, me)

    def move(j):
        p = lax.rem(me + j, n)
        return remote(
            slot_ref.at[:, pl.ds(p * rows, rows), :],
            slots.at[pl.ds(me * slots_dev, slots_dev)],
            a_send.at[j],
            a_recv.at[j],
            p,
        )

    for j in range(1, n):
        move(j).start()
    local_move = pltpu.make_async_copy(
        slot_ref.at[:, pl.ds(me * rows, rows), :],
        slots.at[pl.ds(me * slots_dev, slots_dev)],
        l_sem.at[0],
    )
    local_move.start()
    edge = remote(
        tokens_ref.at[pl.ds(length - 16, 16)],
        rim,
        a_send.at[0],
        a_recv.at[0],
        lax.rem(me + 1, n),
    )

    @pl.when(me < n - 1)
    def _():
        edge.start()

    base = me * length
    where_col = base - 8 + lax.broadcasted_iota(jnp.int32, (length + 8, 1), 0)
    lane = lax.broadcasted_iota(jnp.int32, (tiles, TILE), 1)
    where_row = base + TILE * lax.broadcasted_iota(jnp.int32, (tiles, TILE), 0) + lane
    start = jnp.int32(0)
    seg_col = jnp.zeros((length + 8, 1), jnp.float32)
    seg_row = jnp.zeros((tiles, TILE), jnp.float32)
    for q in range(lengths_ref.shape[0]):
        seg_col += (where_col >= start).astype(jnp.float32)
        seg_row += (where_row >= start).astype(jnp.float32)
        start = start + lengths_ref[packing_ref[q]]
    filled = start
    segs[...] = seg_col + (where_col >= filled).astype(jnp.float32)
    rows_ref[...] = seg_row + (where_row >= filled).astype(jnp.float32)
    lane = lax.broadcasted_iota(jnp.int32, (TILE, TILE), 1)
    for c in range(tiles):
        lo = 8 + c * TILE
        own = segs[lo : lo + TILE]
        flags = [segs[lo - 1 : lo], segs[lo + TILE - 1 : lo + TILE]]
        flags += [segs[lo - s : lo - s + TILE] for s in (1, 2, 3)]
        flags = [(other == own).astype(jnp.float32) for other in flags]
        place = base + c * TILE + lax.broadcasted_iota(jnp.int32, (TILE, 1), 0)
        flags += [None, own, (place < filled).astype(jnp.float32)]
        total = jnp.zeros((TILE, TILE), jnp.float32)
        for k, flag in enumerate(flags):
            if flag is not None:
                total = jnp.where(lane == k, flag, total)
        cols_ref[c * TILE : (c + 1) * TILE, :] = total
    cols_ref[length : length + 8, :] = jnp.zeros((8, TILE), jnp.float32)

    def norm(values):
        values = values.astype(jnp.float32)
        inverse = lax.rsqrt(jnp.mean(values * values, axis=1, keepdims=True) + norm_epsilon)
        return (values * inverse * norm_ref[...]).astype(jnp.bfloat16)

    i = lax.broadcasted_iota(jnp.int32, (TILE, TILE), 0)
    j = lax.broadcasted_iota(jnp.int32, (TILE, TILE), 1)
    lower = (i >= j).astype(jnp.bfloat16)
    down_low = down_ref[...].astype(jnp.bfloat16)
    upper = halves(upper_ref[0:rank, :])

    def gates(c, _):
        at = pl.ds(pl.multiple_of(c * TILE, TILE), TILE)
        x = norm(tokens_ref[at, :])
        normed[at, :] = x
        low = lax.dot_general(x, down_low, NN, preferred_element_type=jnp.float32)
        lowrank_ref[at, :] = low
        logits = product(halves(low), upper, NN) + upper_ref[rank : rank + 1, :]
        logits_ref[at, :] = logits
        gate = jnp.minimum(logits, 0.0) - jnp.log1p(jnp.exp(-jnp.abs(logits)))
        cum_ref[at, :] = running_sum(lower, gate * (1.0 / gate_scale))
        return 0

    lax.fori_loop(0, tiles, gates, 0)
    flushes = []

    def flush(source, target):
        copy = pltpu.make_async_copy(source, target, l_sem.at[6 + len(flushes)])
        copy.start()
        flushes.append(copy)

    flush(normed, normed_out)
    flush(logits_ref, logits_out)
    flush(cum_ref, cum_out)

    @pl.when(me > 0)
    def _():
        edge.wait_recv()

    @pl.when(me == 0)
    def _():
        rim[...] = jnp.zeros_like(rim)

    rim[...] = norm(rim[...])

    local_move.wait()
    for j in range(1, n):
        move(j).wait()
    for b in range(owners_ref.shape[1]):
        piece[:, b * bw : (b + 1) * bw] = slots[owners_ref[0, b]]
    outs = (w_in, w_up_out, w_out_out, w_down_out)
    offset, owns = 0, []
    for q, out in enumerate(outs):
        columns = out.shape[4]
        owns.append(
            pltpu.make_async_copy(
                piece.at[:, pl.ds(offset, columns)],
                out.at[c3[0], c3[1], c3[2]],
                l_sem.at[1 + q],
            )
        )
        offset += columns
    for copy in owns:
        copy.start()
    for copy in owns:
        copy.wait()
    steps, arrived, sent = gather_steps(sizes, plan, piece, outs, bw, g_send, g_recv)
    for step in steps[: ready + 2]:
        step()
    arrived(range(ready))
    rest = list(steps[ready + 2 :])
    flush(w_in, w_in_out)

    def advance():
        if rest:
            rest.pop(0)()

    advance()

    def project(r, _):
        at = pl.ds(pl.multiple_of(r * 256, 256), 256)
        x = normed[at, :]
        for lo in range(0, w_in.shape[4], 512):
            part = lax.dot_general(
                x,
                w_in[:, :, :, :, lo : lo + 512].reshape(width, 512),
                NN,
                preferred_element_type=jnp.float32,
            )
            if lo < channels:
                proj_ref[at, lo : lo + 512] = part.astype(proj_ref.dtype)
            else:
                gate_ref[at, lo - channels : lo - channels + 512] = part
        return 0

    lax.fori_loop(0, length // 256, project, 0)
    for lo in range(0, channels, 512):
        halo_ref[:, lo : lo + 512] = lax.dot_general(
            rim[...],
            w_in[:, :, :, :, lo : lo + 512].reshape(width, 512),
            NN,
            preferred_element_type=jnp.float32,
        ).astype(halo_ref.dtype)
    flush(proj_ref, proj_out)
    flush(gate_ref, gate_out)

    prev[...] = halo_ref[...]
    state[...] = jnp.zeros_like(state)
    mine[...] = jnp.zeros_like(mine)
    for p in range(mine.shape[0]):
        mine[p, TILE : TILE + 1] = jnp.ones((1, TILE), jnp.float32)
    first_step = rest.pop(0) if rest else None

    def local(c, _):
        if first_step is not None:
            pl.when(c == tiles // 2)(first_step)
        at = pl.ds(pl.multiple_of(c * TILE, TILE), TILE)
        for g in range(0, channels, 256):
            wide = slice(g, g + 256)
            block = jnp.concatenate(
                [prev[:, wide].astype(jnp.float32), proj_ref[at, wide].astype(jnp.float32)]
            )
            total = taps_ref[3:4, wide] * block[16:]
            for s in (1, 2, 3):
                total = total + taps_ref[3 - s : 4 - s, wide] * (
                    block[16 - s : 16 - s + TILE] * cols_ref[at, 1 + s : 2 + s]
                )
            conv_ref[at, wide] = total
            act[at, wide] = total * sigmoid(total)
        prev[...] = proj_ref[pl.ds(pl.multiple_of(c * TILE + TILE - 16, 16), 16), :]
        cum = cum_ref[at, :]
        last = cum[TILE - 1 : TILE]
        left = act[at, keys : 2 * keys] * jnp.exp(last - cum) * cols_ref[at, 1:2]
        decay = jnp.exp(last) * cols_ref[at, 0:1][TILE - 1 : TILE]
        for h in range(heads):
            kh = slice(h * DK, (h + 1) * DK)
            v = halves(act[at, 2 * keys + h * DV : 2 * keys + (h + 1) * DV])
            start_ref[c, h] = state[h]
            state[h] = state[h] * decay[:, kh] + product(v, halves(left[:, kh]), TN)
            for e in range(DV // TILE):
                p = h * (DV // TILE) + e
                mine[p, TILE : TILE + 1] = mine[p, TILE : TILE + 1] * decay[:, kh]
        return 0

    lax.fori_loop(0, tiles, local, 0)
    flush(conv_ref, conv_out)
    for h in range(heads):
        start_ref[tiles, h] = state[h]
        for e in range(DV // TILE):
            mine[h * (DV // TILE) + e, 0:TILE] = state[h, e * TILE : (e + 1) * TILE]
    stages, finish = chain_tools(
        n, sizes, True, mine, (across, along, before, held), send, recv, result
    )
    stages[0]()
    second_step = rest.pop(0) if rest else None

    def inside(c, _):
        for k, stage in enumerate(stages[1:]):
            pl.when(c == k + 1)(stage)
        if second_step is not None:
            pl.when(c == tiles // 2)(second_step)
        at = pl.ds(pl.multiple_of(c * TILE, TILE), TILE)
        cum = cum_ref[at, :]
        middle = cum[TILE // 2 - 1 : TILE // 2]
        q = act[at, 0:keys] * jnp.exp(cum - middle) * scale
        k = act[at, keys : 2 * keys] * jnp.exp(middle - cum)
        mask = tile_masks(rows_ref, cols_ref, c)
        for h in range(heads):
            kh = slice(h * DK, (h + 1) * DK)
            vh = slice(h * DV, (h + 1) * DV)
            scores = jnp.where(mask, product(halves(q[:, kh]), halves(k[:, kh]), NT), 0.0)
            v = halves(act[at, 2 * keys + h * DV : 2 * keys + (h + 1) * DV])
            o_ref[at, vh] = product(halves(scores), v, NN)
        return 0

    lax.fori_loop(0, tiles, inside, 0)
    finish()
    for h in range(heads):
        for e in range(DV // TILE):
            state[h, e * TILE : (e + 1) * TILE] = result[h * (DV // TILE) + e]

    def outside(c, _):
        at = pl.ds(pl.multiple_of(c * TILE, TILE), TILE)
        cum = cum_ref[at, :]
        q = act[at, 0:keys] * jnp.exp(cum) * scale * cols_ref[at, 0:1]
        decay = jnp.exp(cum[TILE - 1 : TILE]) * cols_ref[at, 0:1][TILE - 1 : TILE]
        for h in range(heads):
            kh = slice(h * DK, (h + 1) * DK)
            vh = slice(h * DV, (h + 1) * DV)
            begin = start_ref[c, h] + state[h]
            start_ref[c, h] = begin
            state[h] = state[h] * decay[:, kh]
            o = o_ref[at, vh] + product(halves(q[:, kh]), halves(begin), NT)
            o_ref[at, vh] = o
            inverse = lax.rsqrt(jnp.mean(o * o, axis=1, keepdims=True) + norm_epsilon)
            gate = gate_ref[at, vh]
            u_ref[at, vh] = (o * inverse * gain_ref[...] * (gate * sigmoid(gate))).astype(
                u_ref.dtype
            )
        return 0

    lax.fori_loop(0, tiles, outside, 0)
    for h in range(heads):
        start_ref[tiles, h] = start_ref[tiles, h] + state[h]
    flush(o_ref, o_out)
    flush(u_ref, u_out)
    flush(start_ref, start_out)
    while rest:
        advance()
    groups = {chunk[5] for chunk in plan}
    arrived(sorted(g for g in groups if g >= ready))
    sent()
    for copy in flushes:
        copy.wait()

    @pl.when(me < n - 1)
    def _():
        edge.wait_send()


def forward(
    owners, lengths, packing, slot_copy, tokens, norm, down, upper, taps, gain, counts
):
    n = lax.axis_size("seq")
    sizes = axis_sizes(n)
    length, width = tokens.shape
    slots_dev, depth, bw = slot_copy.shape
    rows = depth // n
    keys, channels = upper.shape[1], taps.shape[1]
    heads = keys // DK
    value = heads * DV
    tiles = length // TILE
    blocks = sum(counts)
    ready = 2
    plan = build_plan(counts[:1], SHARES, ready, COLLECT)
    plan += [
        (which + 1, lo, hi, at, order, group + ready)
        for which, lo, hi, at, order, group in build_plan(
            counts[1:], SHARES, 4, COLLECT, counts[0]
        )
    ]
    f32, b16 = jnp.float32, jnp.bfloat16
    shape = jax.ShapeDtypeStruct
    vmem, anywhere = pl.BlockSpec(memory_space=pltpu.VMEM), pl.BlockSpec(memory_space=pl.ANY)
    smem = pl.BlockSpec(memory_space=pltpu.SMEM)
    kept = [
        ((length, width), b16),
        ((length, keys), f32),
        ((length, channels), b16),
        ((length, value), f32),
        ((length, channels), f32),
        ((length, keys), f32),
        ((length, value), f32),
        ((length, value), b16),
        ((tiles + 1, heads, DV, DK), f32),
    ]
    big = [shape(*k) for k in kept]
    outs = [shape(sizes + (rows, count * bw), b16) for count in counts]
    outs += [big[0], shape((length, down.shape[1]), f32), big[1], big[2]]
    outs += [shape((16, channels), b16)] + big[3:]
    outs += [shape((length + 8, TILE), f32), shape((tiles, TILE), f32)]
    specs = [anywhere] * 5 + [vmem, anywhere, anywhere, vmem] + [anywhere] * 6 + [vmem, vmem]
    most = max(sizes)
    copies = len(plan) * 3 * most
    result = pl.pallas_call(
        functools.partial(forward_kernel, n, sizes, plan, ready),
        out_shape=tuple(outs),
        in_specs=[smem] * 3 + [anywhere] + [vmem] * 6,
        out_specs=tuple(specs),
        scratch_shapes=[pltpu.VMEM(*k) for k in kept]
        + [
            pltpu.VMEM((n * slots_dev, rows, bw), b16),
            pltpu.VMEM((rows, blocks * bw), b16),
            pltpu.VMEM(sizes + (rows, counts[0] * bw), b16),
            pltpu.VMEM((16, width), b16),
            pltpu.VMEM((length + 8, 1), f32),
            pltpu.VMEM((length, channels), f32),
            pltpu.VMEM((heads, DV, DK), f32),
            pltpu.VMEM((16, channels), b16),
            pltpu.SemaphoreType.DMA((n,)),
            pltpu.SemaphoreType.DMA((n,)),
            pltpu.SemaphoreType.DMA((copies,)),
            pltpu.SemaphoreType.DMA((copies,)),
            pltpu.SemaphoreType.DMA((18,)),
        ]
        + chain_scratch(sizes, heads * DV // TILE),
        compiler_params=pltpu.CompilerParams(
            collective_id=1, has_side_effects=True, vmem_limit_bytes=60 << 20
        ),
    )(owners, lengths, packing, slot_copy, tokens, norm, down, upper, taps, gain)
    return [w.reshape(depth, w.shape[4]) for w in result[:4]], result[4:]


def chain_scratch(sizes, pieces):
    most = max(sizes)
    shape = (pieces, TILE + 8, TILE)
    return [
        pltpu.VMEM(shape, jnp.float32),
        pltpu.VMEM((sizes[2],) + shape, jnp.float32),
        pltpu.VMEM((sizes[1],) + shape, jnp.float32),
        pltpu.VMEM(shape, jnp.float32),
        pltpu.VMEM((3,) + shape, jnp.float32),
        pltpu.VMEM((pieces, TILE, TILE), jnp.float32),
        pltpu.SemaphoreType.DMA(((2 * most + 1) * pieces,)),
        pltpu.SemaphoreType.DMA(((2 * most + 1) * pieces,)),
    ]


def backward_kernel(
    n,
    sizes,
    plan,
    proj_ref,
    halo_ref,
    conv_ref,
    cum_ref,
    logits_ref,
    o_ref,
    gate_ref,
    du_ref,
    start_ref,
    cols_ref,
    rows_ref,
    taps_ref,
    gain_ref,
    g_up_ref,
    g_out_ref,
    g_down_ref,
    dproj_ref,
    dgate_ref,
    dlogits_ref,
    dtaps_ref,
    dgain_ref,
    early_ref,
    do,
    dact,
    adjoint,
    ends,
    after,
    back,
    tail,
    mine,
    across,
    along,
    before,
    held,
    result,
    send,
    recv,
    b_sem,
    *scatter_refs,
):
    tiles, channels = proj_ref.shape[0] // TILE, proj_ref.shape[1]
    keys = cum_ref.shape[1]
    heads = keys // DK
    me = lax.axis_index("seq")
    greet(n, sizes, (lax.rem(me + 1, n), lax.rem(me + n - 1, n)))
    steps, sent = scatter_steps(
        sizes, plan, [g_up_ref, g_out_ref, g_down_ref], scatter_refs, early_ref, TILE
    )
    steps[0]()
    scale = DK ** (-0.5)
    i = lax.broadcasted_iota(jnp.int32, (TILE, TILE), 0)
    j = lax.broadcasted_iota(jnp.int32, (TILE, TILE), 1)
    upper = (i <= j).astype(jnp.bfloat16)
    adjoint[...] = jnp.zeros_like(adjoint)
    mine[...] = jnp.zeros_like(mine)
    dgain_ref[...] = jnp.zeros_like(dgain_ref)
    dtaps_ref[...] = jnp.zeros_like(dtaps_ref)
    for p in range(mine.shape[0]):
        mine[p, TILE : TILE + 1] = jnp.ones((1, TILE), jnp.float32)

    def local(t, _):
        pl.when(t == tiles // 2)(steps[1])
        c = tiles - 1 - t
        at = pl.ds(pl.multiple_of(c * TILE, TILE), TILE)
        cum = cum_ref[at, :]
        pre = conv_ref[at, 0:keys]
        q = pre * sigmoid(pre) * jnp.exp(cum) * scale * cols_ref[at, 0:1]
        decay = jnp.exp(cum[TILE - 1 : TILE]) * cols_ref[at, 0:1][TILE - 1 : TILE]
        for h in range(heads):
            kh = slice(h * DK, (h + 1) * DK)
            vh = slice(h * DV, (h + 1) * DV)
            o = o_ref[at, vh]
            inverse = lax.rsqrt(jnp.mean(o * o, axis=1, keepdims=True) + norm_epsilon)
            gate = gate_ref[at, vh]
            sig = sigmoid(gate)
            du = du_ref[at, vh]
            unit = o * inverse
            dgate_ref[at, vh] = (
                du * (unit * gain_ref[...]) * (sig * (1.0 + gate * (1.0 - sig)))
            ).astype(dgate_ref.dtype)
            don = du * (gate * sig)
            dgain_ref[0:1] += jnp.sum(don * unit, axis=0, keepdims=True)
            scaled = gain_ref[...] * don
            grad = inverse * scaled - unit * (
                inverse * inverse * jnp.mean(scaled * o, axis=1, keepdims=True)
            )
            do[at, vh] = grad
            ends[c, h] = adjoint[h]
            adjoint[h] = adjoint[h] * decay[:, kh] + product(halves(grad), halves(q[:, kh]), TN)
            for e in range(DV // TILE):
                p = h * (DV // TILE) + e
                mine[p, TILE : TILE + 1] = mine[p, TILE : TILE + 1] * decay[:, kh]
        return 0

    lax.fori_loop(0, tiles, local, 0)
    for h in range(heads):
        for e in range(DV // TILE):
            mine[h * (DV // TILE) + e, 0:TILE] = adjoint[h, e * TILE : (e + 1) * TILE]
    stages, finish = chain_tools(
        n, sizes, False, mine, (across, along, before, held), send, recv, result
    )
    stages[0]()

    def inside(c, _):
        for k, stage in enumerate(stages[1:]):
            pl.when(c == k + 1)(stage)
        pl.when(c == 0)(steps[2])
        pl.when(c == tiles - 2)(steps[3])
        at = pl.ds(pl.multiple_of(c * TILE, TILE), TILE)
        cum = cum_ref[at, :]
        middle = cum[TILE // 2 - 1 : TILE // 2]
        pre = conv_ref[at, 0 : 2 * keys]
        both = pre * sigmoid(pre)
        grow = jnp.exp(cum - middle) * scale
        fall = jnp.exp(middle - cum)
        enter_decay = jnp.exp(cum) * (scale * cols_ref[at, 0:1])
        mask = tile_masks(rows_ref, cols_ref, c)
        for h in range(heads):
            kh = slice(h * DK, (h + 1) * DK)
            vh = slice(h * DV, (h + 1) * DV)
            q = halves(both[:, kh] * grow[:, kh])
            k = halves(both[:, keys + h * DK : keys + (h + 1) * DK] * fall[:, kh])
            prev_v = conv_ref[at, 2 * keys + h * DV : 2 * keys + (h + 1) * DV]
            v = halves(prev_v * sigmoid(prev_v))
            grad = halves(do[at, vh])
            scores = halves(jnp.where(mask, product(q, k, NT), 0.0))
            dscores = halves(jnp.where(mask, product(grad, v, NT), 0.0))
            dact[at, h * DK : (h + 1) * DK] = (
                product(dscores, k, NN) * grow[:, kh]
                + product(grad, halves(start_ref[c, h]), NN) * enter_decay[:, kh]
            )
            dact[at, keys + h * DK : keys + (h + 1) * DK] = (
                product(dscores, q, TN) * fall[:, kh]
            )
            dact[at, 2 * keys + h * DV : 2 * keys + (h + 1) * DV] = product(scores, grad, TN)
        return 0

    lax.fori_loop(0, tiles, inside, 0)
    finish()
    for h in range(heads):
        for e in range(DV // TILE):
            adjoint[h, e * TILE : (e + 1) * TILE] = result[h * (DV // TILE) + e]
    after[...] = jnp.zeros_like(after)

    def outside(t, _):
        pl.when(t == tiles // 4)(steps[4])
        pl.when(t == 3 * tiles // 4)(steps[5])
        c = tiles - 1 - t
        at = pl.ds(pl.multiple_of(c * TILE, TILE), TILE)
        cum = cum_ref[at, :]
        last = cum[TILE - 1 : TILE]
        remain = jnp.exp(last - cum) * cols_ref[at, 1:2]
        decay = jnp.exp(last) * cols_ref[at, 0:1][TILE - 1 : TILE]
        pre = conv_ref[at, 0 : 2 * keys]
        both = pre * sigmoid(pre)
        dkeys, edges = [], []
        for h in range(heads):
            kh = slice(h * DK, (h + 1) * DK)
            wide = slice(2 * keys + h * DV, 2 * keys + (h + 1) * DV)
            k = both[:, keys + h * DK : keys + (h + 1) * DK]
            end = ends[c, h] + adjoint[h]
            adjoint[h] = adjoint[h] * decay[:, kh]
            parts = halves(end)
            pre_v = conv_ref[at, wide]
            v = halves(pre_v * sigmoid(pre_v))
            dkeys.append(
                dact[at, keys + h * DK : keys + (h + 1) * DK]
                + product(v, parts, NN) * remain[:, kh]
            )
            dact[at, wide] += product(halves(k * remain[:, kh]), parts, NT)
            edges.append(jnp.sum(end * start_ref[c + 1, h], axis=0, keepdims=True))
        dk = jnp.concatenate(dkeys, axis=1)
        dq = dact[at, 0:keys]
        dact[at, keys : 2 * keys] = dk
        drift = both[:, 0:keys] * dq - both[:, keys:] * dk
        dl = running_sum(upper, drift) + jnp.concatenate(edges, axis=1)
        dlogits_ref[at, :] = dl * (1.0 / gate_scale) * sigmoid(-logits_ref[at, :])
        behind = jnp.where(
            c == 0,
            halo_ref[...],
            proj_ref[pl.ds(pl.multiple_of(jnp.maximum(c * TILE - 16, 0), 16), 16), :],
        )
        masks = cols_ref[pl.ds(pl.multiple_of(c * TILE, TILE), TILE + 8), :]
        for g in range(0, channels, 256):
            wide = slice(g, g + 256)
            pre = conv_ref[at, wide]
            sig = sigmoid(pre)
            dconv = dact[at, wide] * (sig * (1.0 + pre * (1.0 - sig)))
            block = jnp.concatenate(
                [
                    behind[:, g : g + 256].astype(jnp.float32),
                    proj_ref[at, wide].astype(jnp.float32),
                ]
            )
            grad = jnp.concatenate([dconv, after[:, wide]])
            total = taps_ref[3:4, wide] * dconv
            dtaps_ref[3:4, wide] += jnp.sum(dconv * block[16:], axis=0, keepdims=True)
            first = jnp.zeros((8, 256), jnp.float32)
            for s in (1, 2, 3):
                masked = grad * masks[:, 1 + s : 2 + s]
                tap = taps_ref[3 - s : 4 - s, wide]
                total = total + tap * masked[s : s + TILE]
                dtaps_ref[3 - s : 4 - s, wide] += jnp.sum(
                    masked[:TILE] * block[16 - s : 16 - s + TILE], axis=0, keepdims=True
                )
                first = first + tap * jnp.concatenate(
                    [jnp.zeros((8, 256), jnp.float32), masked[0:8]]
                )[s : s + 8]
            dproj_ref[at, wide] = total.astype(dproj_ref.dtype)
            after[:, wide] = dconv[0:8]
            back[0, :, wide] = first

            @pl.when(c == tiles - 1)
            def _():
                tail[:, wide] = total[TILE - 16 :]

        return 0

    lax.fori_loop(0, tiles, outside, 0)

    home = remote(
        back.at[0], back.at[1], b_sem.at[0], b_sem.at[1], lax.rem(me + n - 1, n)
    )

    @pl.when(me > 0)
    def _():
        home.start()

    for step in steps[6:]:
        step()
    sent()

    @pl.when(me < n - 1)
    def _():
        home.wait_recv()

    @pl.when(me == n - 1)
    def _():
        back[1] = jnp.zeros(back.shape[1:], jnp.float32)

    dproj_ref[pl.ds(tiles * TILE - 16, 16), :] = (
        tail[...] + jnp.concatenate([jnp.zeros((8, channels), jnp.float32), back[1]])
    ).astype(dproj_ref.dtype)

    @pl.when(me > 0)
    def _():
        home.wait_send()


def recurrence_back(
    proj, halo, conv, cum, logits, o, gate, du, starts, cols, rows, taps, gain, grads
):
    n = lax.axis_size("seq")
    sizes = axis_sizes(n)
    length, channels = proj.shape
    keys = cum.shape[1]
    heads = keys // DK
    value = heads * DV
    tiles = length // TILE
    f32 = jnp.float32
    shape = jax.ShapeDtypeStruct
    depth = grads[0].shape[0] // n
    plan = build_plan(tuple(g.shape[1] // TILE for g in grads), SHARES, 4, SPREAD)
    blocks = sum(g.shape[1] for g in grads) // TILE
    views = [g.reshape(sizes + (depth, g.shape[1])) for g in grads]
    vmem, anywhere = pl.BlockSpec(memory_space=pltpu.VMEM), pl.BlockSpec(memory_space=pl.ANY)
    return pl.pallas_call(
        functools.partial(backward_kernel, n, sizes, plan),
        in_specs=[vmem] * 13 + [anywhere] * 3,
        out_shape=(
            shape((length, channels), jnp.bfloat16),
            shape((length, value), jnp.bfloat16),
            shape((length, keys), f32),
            shape((8, channels), f32),
            shape((8, DV), f32),
            shape((blocks, depth, TILE), jnp.bfloat16),
        ),
        scratch_shapes=[
            pltpu.VMEM((length, value), f32),
            pltpu.VMEM((length, channels), f32),
            pltpu.VMEM((heads, DV, DK), f32),
            pltpu.VMEM((tiles, heads, DV, DK), f32),
            pltpu.VMEM((8, channels), f32),
            pltpu.VMEM((2, 8, channels), f32),
            pltpu.VMEM((16, channels), f32),
        ]
        + chain_scratch(sizes, heads * DV // TILE)
        + [pltpu.SemaphoreType.DMA((2,))]
        + scatter_scratch(sizes, plan, depth, TILE, jnp.bfloat16),
        compiler_params=pltpu.CompilerParams(
            collective_id=5, has_side_effects=True, vmem_limit_bytes=60 << 20
        ),
    )(proj, halo, conv, cum, logits, o, gate, du, starts, cols, rows, taps, gain, *views)


def adam_kernel(
    grad_ref,
    left_ref,
    right_ref,
    master_ref,
    first_ref,
    second_ref,
    grad_out,
    master_out,
    first_out,
    second_out,
    copy_out,
    high,
    low,
):
    width = left_ref.shape[1]
    step = min(256, width)
    dot = functools.partial(
        lax.dot_general, dimension_numbers=TN, preferred_element_type=jnp.float32
    )
    grad_out[0] = grad_ref[0].astype(jnp.float32)
    total = None
    for r in range(0, width, step):
        at = slice(r, r + step)
        lh, ll = halves(left_ref[0, at, :])
        high[at, :], low[at, :] = lh, ll
        term = dot(grad_ref[0, at, :], lh) + dot(grad_ref[0, at, :], ll)
        total = term if total is None else total + term
    right = halves(right_ref[0])
    rotated = product(right, halves(total), TN).T
    first = moment_decay * first_ref[0] + (1.0 - moment_decay) * rotated
    second = moment_decay * second_ref[0] + (1.0 - moment_decay) * rotated * rotated
    first_out[0] = first
    second_out[0] = second
    direction = first / (jnp.sqrt(second) + adam_epsilon)
    eh, el = halves(product(halves(direction), right, NT))
    both = jnp.concatenate([eh, el], axis=1)
    columns = eh.shape[1]
    dot = functools.partial(
        lax.dot_general, dimension_numbers=NN, preferred_element_type=jnp.float32
    )
    for r in range(0, width, step):
        at = slice(r, r + step)
        pair = dot(high[at, :], both)
        restored = pair[:, :columns] + (pair[:, columns:] + dot(low[at, :], eh))
        master = master_ref[0, at, :] - rate_block * restored
        master_out[0, at, :] = master
        copy_out[0, at, :] = master.astype(copy_out.dtype)


def block_adam(grads, left, right, master, first, second):
    slots, width, columns = master.shape
    tall = pl.BlockSpec((1, width, columns), lambda i: (i, 0, 0))
    shape = jax.ShapeDtypeStruct
    full = shape(master.shape, jnp.float32)
    return pl.pallas_call(
        adam_kernel,
        grid=(slots,),
        out_shape=(full, full, full, full, shape(master.shape, jnp.bfloat16)),
        in_specs=[
            tall,
            pl.BlockSpec((1, width, width), lambda i: (i, 0, 0)),
            pl.BlockSpec((1, columns, columns), lambda i: (i, 0, 0)),
            tall,
            tall,
            tall,
        ],
        out_specs=[tall] * 5,
        scratch_shapes=[
            pltpu.VMEM((width, width), jnp.bfloat16),
            pltpu.VMEM((width, width), jnp.bfloat16),
        ],
        compiler_params=pltpu.CompilerParams(vmem_limit_bytes=48 << 20),
    )(grads, left, right, master, first, second)


def join_kernel(u_ref, w_ref, tok_ref, gain_ref, h_ref, x_ref, inv_ref, send, recv, s_sem, r_sem):
    core = lax.axis_index("head")
    barrier = pltpu.get_barrier_semaphore()
    pl.semaphore_signal(barrier, inc=1, device_id={"head": 1 - core}, device_id_type=MESH)
    pl.semaphore_wait(barrier, 1)
    count = s_sem.shape[0]
    step = u_ref.shape[0] // count

    def swap(t):
        at = pl.ds(t * step, step)
        return pltpu.make_async_remote_copy(
            src_ref=send.at[at],
            dst_ref=recv.at[at],
            send_sem=s_sem.at[t],
            recv_sem=r_sem.at[t],
            device_id={"head": 1 - core},
            device_id_type=MESH,
        )

    for t in range(count):
        at = slice(t * step, (t + 1) * step)
        send[at, :] = lax.dot_general(
            u_ref[at, :], w_ref[...], NT, preferred_element_type=jnp.float32
        ).astype(send.dtype)
        swap(t).start()
    for t in range(count):
        at = slice(t * step, (t + 1) * step)
        swap(t).wait_recv()
        branch = send[at, :].astype(jnp.float32) + recv[at, :].astype(jnp.float32)
        hidden = tok_ref[at, :].astype(jnp.float32) + branch
        inverse = lax.rsqrt(jnp.mean(hidden * hidden, axis=1, keepdims=True) + norm_epsilon)
        h_ref[at, :] = hidden
        inv_ref[at, :] = inverse
        x_ref[at, :] = (hidden * inverse * gain_ref[...]).astype(x_ref.dtype)
    for t in range(count):
        swap(t).wait_send()


def join_heads(u, w, tokens, gain):
    length, width = tokens.shape
    shape = jax.ShapeDtypeStruct
    count = 4
    return pl.pallas_call(
        join_kernel,
        out_shape=(
            shape((length, width), jnp.float32),
            shape((length, width), jnp.bfloat16),
            shape((length, 1), jnp.float32),
        ),
        scratch_shapes=[
            pltpu.VMEM((length, width), jnp.bfloat16),
            pltpu.VMEM((length, width), jnp.bfloat16),
            pltpu.SemaphoreType.DMA((count,)),
            pltpu.SemaphoreType.DMA((count,)),
        ],
        compiler_params=pltpu.CompilerParams(
            collective_id=6, has_side_effects=True, vmem_limit_bytes=48 << 20
        ),
    )(u, w, tokens, gain)


def mlp_kernel(x_ref, up_ref, down_ref, dy_ref, hid_ref, dpair_ref):
    hidden = down_ref.shape[1]
    dot = functools.partial(
        lax.dot_general, dimension_numbers=NN, preferred_element_type=jnp.float32
    )
    x, dy = x_ref[...], dy_ref[...]
    for lo in range(0, hidden, 512):
        hi = min(lo + 512, hidden)
        gate = dot(x, up_ref[:, lo:hi])
        up = dot(x, up_ref[:, hidden + lo : hidden + hi])
        grad = dot(dy, down_ref[:, lo:hi])
        sig = sigmoid(gate)
        swish = gate * sig
        hid_ref[:, lo:hi] = (swish * up).astype(hid_ref.dtype)
        dpair_ref[:, lo:hi] = (grad * up * (sig + swish * (1.0 - sig))).astype(dpair_ref.dtype)
        dpair_ref[:, hidden + lo : hidden + hi] = (grad * swish).astype(dpair_ref.dtype)


def mlp(x, up, down, dy):
    length, width = x.shape
    hidden = down.shape[1]
    step = 256
    shape = jax.ShapeDtypeStruct

    def rows(columns):
        return pl.BlockSpec((step, columns), lambda i: (i, 0))

    def whole(columns):
        return pl.BlockSpec((width, columns), lambda i: (0, 0), pipeline_mode=pl.Buffered(1))

    return pl.pallas_call(
        mlp_kernel,
        grid=(length // step,),
        out_shape=(shape((length, hidden), x.dtype), shape((length, 2 * hidden), x.dtype)),
        in_specs=[rows(width), whole(2 * hidden), whole(hidden), rows(width)],
        out_specs=(rows(hidden), rows(2 * hidden)),
        compiler_params=pltpu.CompilerParams(vmem_limit_bytes=56 << 20),
    )(x, up, down, dy)


def join_back_kernel(
    g_ref,
    w_ref,
    h_ref,
    inv_ref,
    gain_ref,
    dy_ref,
    dh_ref,
    dattn_ref,
    sum_ref,
    send,
    recv,
    s_sem,
    r_sem,
):
    core = lax.axis_index("head")
    barrier = pltpu.get_barrier_semaphore()
    pl.semaphore_signal(barrier, inc=1, device_id={"head": 1 - core}, device_id_type=MESH)
    pl.semaphore_wait(barrier, 1)
    count = s_sem.shape[0]
    step = g_ref.shape[0] // count

    def swap(t):
        at = pl.ds(t * step, step)
        return pltpu.make_async_remote_copy(
            src_ref=send.at[at],
            dst_ref=recv.at[at],
            send_sem=s_sem.at[t],
            recv_sem=r_sem.at[t],
            device_id={"head": 1 - core},
            device_id_type=MESH,
        )

    total = jnp.zeros((1, h_ref.shape[1]), jnp.float32)

    def close(t, total):
        at = slice(t * step, (t + 1) * step)
        swap(t).wait_recv()
        grad = send[at, :] + recv[at, :]
        hidden, inverse = h_ref[at, :], inv_ref[at, :]
        unit = hidden * inverse
        scaled = gain_ref[...] * grad
        mean = jnp.mean(scaled * hidden, axis=1, keepdims=True)
        dh = dy_ref[at, :].astype(jnp.float32) + (
            inverse * scaled - unit * (inverse * inverse * mean)
        )
        dh_ref[at, :] = dh
        dattn_ref[at, :] = dh.astype(dattn_ref.dtype)
        return total + jnp.sum(grad * unit, axis=0, keepdims=True)

    for t in range(count):
        at = slice(t * step, (t + 1) * step)
        send[at, :] = lax.dot_general(
            g_ref[at, :], w_ref[...], NT, preferred_element_type=jnp.float32
        )
        swap(t).start()
        if t:
            total = close(t - 1, total)
    sum_ref[...] = jnp.broadcast_to(close(count - 1, total), sum_ref.shape)
    for t in range(count):
        swap(t).wait_send()


def join_back(grads, w, hidden, inverse, gain, dy):
    length, width = hidden.shape
    shape = jax.ShapeDtypeStruct
    count = 4
    return pl.pallas_call(
        join_back_kernel,
        out_shape=(
            shape((length, width), jnp.float32),
            shape((length, width), jnp.bfloat16),
            shape((8, width), jnp.float32),
        ),
        scratch_shapes=[
            pltpu.VMEM((length, width), jnp.float32),
            pltpu.VMEM((length, width), jnp.float32),
            pltpu.SemaphoreType.DMA((count,)),
            pltpu.SemaphoreType.DMA((count,)),
        ],
        compiler_params=pltpu.CompilerParams(
            collective_id=7, has_side_effects=True, vmem_limit_bytes=56 << 20
        ),
    )(grads, w, hidden, inverse, gain, dy)


def rms_stats(values):
    return lax.rsqrt(jnp.mean(values * values, axis=-1, keepdims=True) + norm_epsilon)


def rms_back(values, inverse, gain, upstream):
    scaled = gain * upstream
    return inverse * scaled - values * inverse * inverse * inverse * jnp.mean(
        scaled * values, axis=-1, keepdims=True
    )


def swish_slope(values):
    sigmoid = jax.nn.sigmoid(values)
    return sigmoid * (1.0 + values * (1.0 - sigmoid))


def plain_adam(param, gradient, first, second, rate):
    first_next = moment_decay * first + (1.0 - moment_decay) * gradient
    second_next = moment_decay * second + (1.0 - moment_decay) * gradient * gradient
    return (
        param - rate * first_next / (jnp.sqrt(second_next) + adam_epsilon),
        first_next,
        second_next,
    )


def body(
    tokens,
    cotangent,
    lengths,
    packing,
    owners,
    slot_copy,
    slot_master,
    slot_first,
    slot_second,
    basis_left,
    basis_right,
    norm_gains,
    gains_first,
    gains_second,
    gate_down,
    down_first,
    down_second,
    gate_up,
    upper_first,
    upper_second,
    head_gain,
    head_first,
    head_second,
    conv_weight,
    conv_first,
    conv_second,
):
    tok_rows = tokens.shape[0]
    model_width = tokens.shape[1]
    block_width = slot_copy.shape[2]
    rank_width = gate_down.shape[1]
    tap_count = conv_weight.shape[0]
    key_width = gate_up.shape[1]
    channels = conv_weight.shape[1]
    value_width = channels - 2 * key_width
    block_total = owners.shape[1]
    count_in = (channels + value_width) // block_width
    count_out = value_width // block_width
    count_down = (block_total - count_in - count_out) // 3
    count_up = 2 * count_down
    (in_weights, up_weights, out_weights, down_weights), kept = forward(
        owners,
        lengths,
        packing,
        slot_copy,
        tokens,
        norm_gains[0:1],
        gate_down,
        gate_up,
        conv_weight,
        head_gain[None],
        (count_in, count_up, count_out, count_down),
    )
    normed, lowrank, logits, mixed_proj, halo, gate_pre = kept[:6]
    conv_pre, cumulative, attended, gated_out, starts, cols, rows = kept[6:]
    own_valid = cols[:tok_rows, 7]
    gain_row = head_gain[None]
    down_low = gate_down.astype(jnp.bfloat16)
    inputs = tokens.astype(jnp.float32)
    inverse_one = rms_stats(inputs)
    hidden_one, normed_two, inverse_two = join_heads(
        gated_out, out_weights, tokens, norm_gains[1:2]
    )
    upstream_low = (cotangent.astype(jnp.float32) * own_valid[:, None]).astype(jnp.bfloat16)
    hidden, grad_pair = mlp(normed_two, up_weights, down_weights, upstream_low)
    mlp_part = jnp.einsum("tn,dn->td", hidden, down_weights, preferred_element_type=jnp.float32)
    mlp_branch = lax.psum(mlp_part.astype(jnp.bfloat16), "head").astype(jnp.float32)
    result = (hidden_one + mlp_branch).astype(jnp.bfloat16)
    grad_one, grad_attn, gains_two = join_back(
        grad_pair, up_weights, hidden_one, inverse_two, norm_gains[1:2], upstream_low
    )
    grad_gains_two = gains_two[0]
    grad_gated = jnp.dot(grad_attn, out_weights, preferred_element_type=jnp.float32)
    early = [
        jnp.einsum("td,tn->dn", left, right, preferred_element_type=jnp.float32).astype(
            jnp.bfloat16
        )
        for left, right in (
            (normed_two, grad_pair),
            (grad_attn, gated_out),
            (upstream_low, hidden),
        )
    ]
    grad_mixed, grad_gate_pre, grad_logits, tap_grads, gain_grads, early = recurrence_back(
        mixed_proj,
        halo,
        conv_pre,
        cumulative,
        logits,
        attended,
        gate_pre,
        grad_gated,
        starts,
        cols,
        rows,
        conv_weight,
        gain_row,
        early,
    )
    grad_conv_weight = tap_grads[:tap_count]
    grad_head_gain = gain_grads[0]
    grad_upper = jnp.concatenate(
        [
            jnp.einsum("tr,tk->rk", lowrank, grad_logits, precision=highest_precision),
            jnp.sum(grad_logits, axis=0, keepdims=True),
        ],
        axis=0,
    )
    grad_lowrank = jnp.einsum(
        "tk,rk->tr", grad_logits, gate_up[:rank_width], precision=highest_precision
    ).astype(jnp.bfloat16)
    grad_down_part = jnp.einsum(
        "tr,td->rd", grad_lowrank, normed, preferred_element_type=jnp.float32
    )
    grad_projected = jnp.concatenate(
        [grad_mixed, grad_gate_pre], axis=1
    )
    grad_normed_part = jnp.einsum(
        "tn,dn->td", grad_projected, in_weights, preferred_element_type=jnp.float32
    ) + jnp.einsum("tr,dr->td", grad_lowrank, down_low, preferred_element_type=jnp.float32)
    grad_normed = lax.psum(grad_normed_part.astype(jnp.bfloat16), "head").astype(jnp.float32)
    grad_gains_one = jnp.sum(grad_normed_part * inputs * inverse_one, axis=0)
    grad_input = grad_one + rms_back(inputs, inverse_one, norm_gains[0], grad_normed)
    shared_rows, own_rows = rank_width + 8, 16
    shared = jnp.concatenate(
        [
            grad_down_part,
            jnp.pad(grad_head_gain, (0, model_width - grad_head_gain.shape[0]))[None],
            grad_gains_one[None],
            jnp.zeros((6, model_width), jnp.float32),
        ]
    )
    flat_upper = grad_upper.reshape(-1)
    upper_rows = -(-flat_upper.shape[0] // model_width)
    alone = jnp.concatenate(
        [
            grad_gains_two[None],
            grad_conv_weight,
            jnp.pad(flat_upper, (0, upper_rows * model_width - flat_upper.shape[0])).reshape(
                upper_rows, model_width
            ),
        ]
    )
    alone = jnp.pad(alone, ((0, own_rows - alone.shape[0]), (0, 0)))
    slots_dev = slot_copy.shape[0]
    slot_total = slots_dev * lax.axis_size("seq")
    late = jnp.einsum(
        "td,tn->dn", normed, grad_projected, preferred_element_type=jnp.float32
    ).astype(jnp.bfloat16)
    named = jnp.arange(slot_total, dtype=jnp.int32)[:, None] == owners
    inverse = jnp.where(
        jnp.any(named, axis=1),
        jnp.sum(named * jnp.arange(block_total, dtype=jnp.int32), axis=1),
        block_total,
    ).astype(jnp.int32)[None]
    owned_grads, summed = scatter_grads(
        late, early, inverse, slots_dev, jnp.concatenate([shared, alone]), shared_rows
    )
    owned_grads, master_next, first_next, second_next, copy_next = block_adam(
        owned_grads, basis_left, basis_right, slot_master, slot_first, slot_second
    )
    down_grad = summed[:rank_width].T
    head_grad = summed[rank_width, : grad_head_gain.shape[0]]
    gains_grad = jnp.stack([summed[rank_width + 1], summed[shared_rows]])
    conv_grad = summed[shared_rows + 1 : shared_rows + 1 + tap_count]
    upper_grad = (
        summed[shared_rows + 1 + tap_count : shared_rows + 1 + tap_count + upper_rows]
        .reshape(-1)[: flat_upper.shape[0]]
        .reshape(grad_upper.shape)
    )
    gains_next, gains_first_next, gains_second_next = plain_adam(
        norm_gains, gains_grad, gains_first, gains_second, rate_gains
    )
    down_next, down_first_next, down_second_next = plain_adam(
        gate_down, down_grad, down_first, down_second, rate_down
    )
    upper_next, upper_first_next, upper_second_next = plain_adam(
        gate_up, upper_grad, upper_first, upper_second, rate_upper
    )
    head_next, head_first_next, head_second_next = plain_adam(
        head_gain, head_grad, head_first, head_second, rate_head
    )
    conv_next, conv_first_next, conv_second_next = plain_adam(
        conv_weight, conv_grad, conv_first, conv_second, rate_conv
    )
    return (
        result,
        grad_input,
        owned_grads,
        master_next,
        first_next,
        second_next,
        copy_next,
        gains_grad,
        gains_next,
        gains_first_next,
        gains_second_next,
        down_grad,
        down_next,
        down_first_next,
        down_second_next,
        upper_grad,
        upper_next,
        upper_first_next,
        upper_second_next,
        head_grad,
        head_next,
        head_first_next,
        head_second_next,
        conv_grad,
        conv_next,
        conv_first_next,
        conv_second_next,
    )


def solution(mesh):
    placed = (
        P("seq", None),
        P("seq", None),
        P(),
        P(),
        P("head", None),
        P(("seq", "head"), None, None),
        P(("seq", "head"), None, None),
        P(("seq", "head"), None, None),
        P(("seq", "head"), None, None),
        P(("seq", "head"), None, None),
        P(("seq", "head"), None, None),
        P(),
        P(),
        P(),
        P(),
        P(),
        P(),
        P(None, "head"),
        P(None, "head"),
        P(None, "head"),
        P(),
        P(),
        P(),
        P(None, "head"),
        P(None, "head"),
        P(None, "head"),
    )
    return jax.shard_map(
        body,
        mesh=mesh,
        in_specs=placed,
        out_specs=(
            P("seq", None),
            P("seq", None),
            P(("seq", "head"), None, None),
            P(("seq", "head"), None, None),
            P(("seq", "head"), None, None),
            P(("seq", "head"), None, None),
            P(("seq", "head"), None, None),
            P(),
            P(),
            P(),
            P(),
            P(),
            P(),
            P(),
            P(),
            P(None, "head"),
            P(None, "head"),
            P(None, "head"),
            P(None, "head"),
            P(),
            P(),
            P(),
            P(),
            P(None, "head"),
            P(None, "head"),
            P(None, "head"),
            P(None, "head"),
        ),
        check_vma=False,
    )
```

```python
import functools

import jax
import jax.numpy as jnp
from jax import lax
from jax.experimental import pallas as pl
from jax.experimental.pallas import tpu as pltpu
from jax.sharding import PartitionSpec as P

MESH = pl.DeviceIdType.MESH

DK = 128
DV = 256


highest_precision = lax.Precision.HIGHEST
norm_epsilon = 1e-06
adam_epsilon = 1e-08
gate_scale = 16.0
moment_decay = 0.5
rate_block = 0.03
rate_gains = 0.45
rate_down = 0.02
rate_upper = 0.6
rate_head = 0.5
rate_conv = 0.1


def axis_sizes(n):
    side = 1
    while (side * 2) ** 2 * 4 <= n:
        side *= 2
    return (n // (side * side), side, side)


def coords(me, sizes):
    _, rows, columns = sizes
    return [me // (rows * columns), (me // columns) % rows, me % columns]


def index_of(c, sizes):
    _, rows, columns = sizes
    return (c[0] * rows + c[1]) * columns + c[2]


def neighbour(c, sizes, ax, j):
    d = list(c)
    d[ax] = lax.rem(c[ax] + j, sizes[ax])
    return index_of(d, sizes)


def enter(n, me, mate=False):
    barrier = pltpu.get_barrier_semaphore()
    if mate:
        core = lax.axis_index("head")
        pl.semaphore_signal(barrier, inc=1, device_id={"head": 1 - core}, device_id_type=MESH)
    for j in range(1, n):
        pl.semaphore_signal(
            barrier, inc=1, device_id={"seq": lax.rem(me + j, n)}, device_id_type=MESH
        )
    pl.semaphore_wait(barrier, n - 1 + int(mate))


def remote(src, dst, send_sem, recv_sem, peer):
    return pltpu.make_async_remote_copy(
        src_ref=src,
        dst_ref=dst,
        send_sem=send_sem,
        recv_sem=recv_sem,
        device_id={"seq": peer},
        device_id_type=MESH,
    )


def build_plan(widths, parts, pieces, orders, base=0):
    total = sum(widths)
    bounds = [sum(widths[:i]) for i in range(len(widths) + 1)]
    cuts = [round(total * f) for f in (0.0,) + parts]
    plan, at = [], 0
    for i in range(pieces):
        for order, lo, hi in zip(orders, cuts[:-1], cuts[1:], strict=True):
            size = hi - lo
            left = size * (i + 1) // pieces - size * i // pieces
            while left:
                which = max(q for q in range(len(widths)) if bounds[q] <= at)
                step = min(left, bounds[which + 1] - at)
                start = at - bounds[which]
                plan.append((which, start, start + step, at + base, order, i))
                at += step
                left -= step
    return plan


def groups_of(plan):
    streams = {}
    for i, chunk in enumerate(plan):
        streams.setdefault(chunk[4], {}).setdefault(chunk[5], []).append(i)
    return streams


def spread_steps(steps, places):
    chosen = [(place, steps.pop(0)) for place in places[: len(steps)]]

    def run(t):
        for place, step in chosen:
            pl.when(t == place)(step)

    return run


FORWARD_PLACES = (1, (4,), (4,), ())
FORWARD_PIECES = 4
BACKWARD_PLACES = ((4,), (0, 6), (2, 6))
BACKWARD_PIECES = 4
MIDDLE_PIECES = 3
MIDDLE_TAKEN = 0


def gather_steps(sizes, plan, piece, outs, bw, send, recv):
    c = coords(lax.axis_index("seq"), sizes)
    most = max(sizes)

    def copies(i, k):
        which, lo, hi, at, order, _ = plan[i]
        ax = order[k]
        wide = pl.ds(lo * bw, (hi - lo) * bw)
        index = tuple(slice(None) if a in order[:k] else c[a] for a in range(3))
        index += (slice(None), wide)
        target = outs[which].at[index]
        source = target if k else piece.at[:, pl.ds(at * bw, (hi - lo) * bw)]
        return [
            remote(
                source,
                target,
                send.at[(i * 3 + k) * most + j],
                recv.at[(i * 3 + k) * most + j],
                neighbour(c, sizes, ax, j),
            )
            for j in range(1, sizes[ax])
        ]

    streams = groups_of(plan)
    longest = max(max(s) for s in streams.values()) + 1

    def step(s):
        for k in (2, 1, 0):
            for groups in streams.values():
                for i in groups.get(s - k, ()):
                    if k:
                        for copy in copies(i, k - 1):
                            copy.wait_recv()
                    for copy in copies(i, k):
                        copy.start()

    def arrived(piece_range):
        for groups in streams.values():
            for s in piece_range:
                for i in groups.get(s, ()):
                    for copy in copies(i, 2):
                        copy.wait_recv()

    def sent():
        for i in range(len(plan)):
            for k in range(3):
                for copy in copies(i, k):
                    copy.wait_send()

    return [functools.partial(step, s) for s in range(longest + 2)], arrived, sent


def scatter_scratch(sizes, plan, rows, bw, dtype, in_place=False):
    own, first, second, third = [], [], [], []
    for _, lo, hi, _, order, _ in plan:
        wide = (hi - lo) * bw
        rest = tuple(sizes[q] for q in range(3) if q != order[0])
        own.append(pltpu.VMEM(rest + (rows, wide), dtype))
        first.append(pltpu.VMEM((sizes[order[0]] - 1,) + rest + (rows, wide), dtype))
        second.append(pltpu.VMEM((sizes[order[1]], sizes[order[2]], rows, wide), dtype))
        third.append(pltpu.VMEM((sizes[order[2]], rows, wide), dtype))
    count = len(plan) * 3 * max(sizes)
    return (
        ([] if in_place else own)
        + first
        + second
        + third
        + [
            pltpu.SemaphoreType.DMA((count,)),
            pltpu.SemaphoreType.DMA((count,)),
            pltpu.SemaphoreType.DMA((len(plan),)),
        ]
    )


def scatter_steps(sizes, plan, grads, scratch, fin, bw, in_place=False):
    c = coords(lax.axis_index("seq"), sizes)
    most, count = max(sizes), len(plan)
    first, second, third = (scratch[-3 - (3 - i) * count :][:count] for i in range(3))
    send, recv, load = scratch[-3:]

    def part(i):
        which, lo, hi, _, order, _ = plan[i]
        index = tuple(c[q] if q == order[0] else slice(None) for q in range(3))
        index += (slice(None), pl.ds(lo * bw, (hi - lo) * bw))
        return grads[which].at[index]

    own = [part(i) for i in range(count)] if in_place else scratch[:count]

    def loading(i):
        return pltpu.make_async_copy(part(i), own[i], load.at[i])

    def copies(i, k):
        which, lo, hi, _, order, _ = plan[i]
        ax = order[k]
        left = sorted(set(range(3)) - set(order[:k]))
        result = []
        for j in range(1, sizes[ax]):
            there = lax.rem(c[ax] + j, sizes[ax])
            index = tuple(there if q == ax else slice(None) for q in left)
            if k == 0:
                index += (slice(None), pl.ds(lo * bw, (hi - lo) * bw))
                source, target = grads[which].at[index], first[i].at[j - 1]
            elif k == 1:
                source, target = own[i].at[index], second[i].at[j]
            else:
                source, target = second[i].at[(0,) + index], third[i].at[j]
            s = (i * 3 + k) * most + j
            result.append(
                remote(source, target, send.at[s], recv.at[s], neighbour(c, sizes, ax, j))
            )
        return result

    def combine(i, k):
        _, lo, hi, at, order, _ = plan[i]
        if k == 0 and not in_place:
            loading(i).wait()
        for copy in copies(i, k):
            copy.wait_recv()
        size = sizes[order[k]]
        if k == 0:
            outer, inner = own[i].shape[:2]

            def add(t, _):
                u, v = t // inner, t % inner
                total = own[i][u, v].astype(jnp.float32)
                for j in range(size - 1):
                    total = total + first[i][j, u, v].astype(jnp.float32)
                own[i][u, v] = total.astype(own[i].dtype)
                return 0

            lax.fori_loop(0, outer * inner, add, 0)
        elif k == 1:
            leading = sorted(set(range(3)) - {order[0]}).index(order[1]) == 0

            def add(t, _):
                total = own[i][(c[order[1]], t) if leading else (t, c[order[1]])]
                total = total.astype(jnp.float32)
                for j in range(1, size):
                    total = total + second[i][j, t].astype(jnp.float32)
                second[i][0, t] = total.astype(own[i].dtype)
                return 0

            lax.fori_loop(0, sizes[order[2]], add, 0)
        else:
            total = second[i][0, c[order[2]]].astype(jnp.float32)
            for j in range(1, size):
                total = total + third[i][j].astype(jnp.float32)
            for b in range(hi - lo):
                fin[at + b] = total[:, b * bw : (b + 1) * bw].astype(fin.dtype)

    streams = groups_of(plan)
    longest = max(max(s) for s in streams.values()) + 1

    def step(s):
        for k in range(4):
            for groups in streams.values():
                for i in groups.get(s - k, ()):
                    if k:
                        combine(i, k - 1)
                    elif not in_place:
                        loading(i).start()
                    if k < 3:
                        for copy in copies(i, k):
                            copy.start()

    def sent():
        for i in range(count):
            for k in range(3):
                for copy in copies(i, k):
                    copy.wait_send()

    return [functools.partial(step, s) for s in range(longest + 3)], sent


SPREAD = ((2, 1, 0), (1, 2, 0), (0, 1, 2))
COLLECT = ((0, 1, 2), (0, 2, 1), (2, 1, 0))
SHARES = (0.43, 0.86, 1.0)


def sum_steps(sizes, shared, x_ref, out_ref, mate, acc, bufs, send, recv):
    me, core = lax.axis_index("seq"), lax.axis_index("head")
    c = coords(me, sizes)
    most = max(sizes)
    swap = pltpu.make_async_remote_copy(
        src_ref=x_ref.at[pl.ds(0, shared)],
        dst_ref=mate,
        send_sem=send.at[0],
        recv_sem=recv.at[0],
        device_id={"head": 1 - core},
        device_id_type=MESH,
    )

    def going(step, ax):
        copies = []
        for j in range(1, sizes[ax]):
            d = list(c)
            d[ax] = lax.rem(c[ax] + j, sizes[ax])
            q = 1 + ax * most + j
            copies.append(
                remote(
                    acc.at[step], bufs.at[ax, c[ax]], send.at[q], recv.at[q], index_of(d, sizes)
                )
            )
        return copies

    def total(ax):
        value = bufs[ax, 0]
        for j in range(1, sizes[ax]):
            value = value + bufs[ax, j]
        return value

    def start(step, ax):
        bufs[ax, c[ax]] = acc[step]
        for copy in going(step, ax):
            copy.start()

    def swapped():
        swap.wait()
        acc[0, 0:shared] = x_ref[0:shared] + mate[...]
        acc[0, shared:] = x_ref[shared:]
        start(0, 2)

    def moved(step, ax):
        for copy in going(step, ax):
            copy.wait()
        if step < 2:
            acc[step + 1] = total(ax)
            start(step + 1, ax - 1)
        else:
            out_ref[...] = total(ax)

    return [
        swap.start,
        swapped,
        functools.partial(moved, 0, 2),
        functools.partial(moved, 1, 1),
        functools.partial(moved, 2, 0),
    ]


NN = (((1,), (0,)), ((), ()))
NT = (((1,), (1,)), ((), ()))
TN = (((0,), (0,)), ((), ()))
TILE = 128


def halves(values):
    high = values.astype(jnp.bfloat16)
    return high, (values - high.astype(jnp.float32)).astype(jnp.bfloat16)


def product(left, right, dims):
    (lh, ll), (rh, rl) = left, right
    dot = functools.partial(
        lax.dot_general, dimension_numbers=dims, preferred_element_type=jnp.float32
    )
    return dot(lh, rh) + (dot(lh, rl) + dot(ll, rh))


def running_sum(table, values):
    first = values.astype(jnp.bfloat16)
    rest = values - first.astype(jnp.float32)
    second, third = halves(rest)
    dot = functools.partial(
        lax.dot_general, dimension_numbers=NN, preferred_element_type=jnp.float32
    )
    return dot(table, first) + (dot(table, second) + dot(table, third))


def sigmoid(values):
    return 1.0 / (1.0 + jnp.exp(-values))


def chain_tools(n, sizes, forward, mine, bufs, send, recv, result):
    me = lax.axis_index("seq")
    c = coords(me, sizes)
    pieces = mine.shape[0]
    across, along, before, held = bufs
    most = max(sizes)
    state = pl.ds(0, TILE)
    decay = pl.ds(TILE, 1)

    def peers(ax):
        return [j for j in range(1, sizes[ax])]

    def to(ax, j):
        d = list(c)
        d[ax] = lax.rem(c[ax] + j, sizes[ax])
        return index_of(d, sizes)

    def line(buf, source, ax, j, p, base):
        s = base + j * pieces + p
        return remote(source.at[p], buf.at[c[ax], p], send.at[s], recv.at[s], to(ax, j))

    def hop(p):
        s = 2 * most * pieces + p
        step = 1 if forward else -1
        d = [lax.rem(c[0] + step + sizes[0], sizes[0]), c[1], c[2]]
        return remote(held.at[1, p], held.at[0, p], send.at[s], recv.at[s], index_of(d, sizes))

    def compose(first, second):
        return (second[1] * first[0] + second[0], first[1] * second[1])

    def reduce_line(buf, ax, p):
        size = sizes[ax]
        order = range(size) if forward else range(size - 1, -1, -1)
        prefix = (jnp.zeros((TILE, TILE), jnp.float32), jnp.ones((1, TILE), jnp.float32))
        total = None
        for i in order:
            item = (buf[i, p, state], buf[i, p, decay])
            longer = compose(prefix, item)
            take = (i < c[ax]) if forward else (i > c[ax])
            prefix = tuple(jnp.where(take, a, b) for a, b in zip(longer, prefix, strict=True))
            total = item if total is None else compose(total, item)
        return prefix, total

    def start_x():
        for p in range(pieces):
            across[c[2], p] = mine[p]
            for j in peers(2):
                line(across, mine, 2, j, p, 0).start()

    def start_y():
        for p in range(pieces):
            for j in peers(2):
                line(across, mine, 2, j, p, 0).wait_recv()
            prefix, total = reduce_line(across, 2, p)
            before[p, state], before[p, decay] = prefix
            held[2, p, state], held[2, p, decay] = total
            held[2, p, pl.ds(TILE + 1, 7)] = jnp.zeros((7, TILE), jnp.float32)
            along[c[1], p] = held[2, p]
            for j in peers(1):
                line(along, held.at[2], 1, j, p, most * pieces).start()

    first_z = 0 if forward else sizes[0] - 1
    last_z = sizes[0] - 1 - first_z

    def start_z():
        for p in range(pieces):
            for j in peers(1):
                line(along, held.at[2], 1, j, p, most * pieces).wait_recv()
            prefix, total = reduce_line(along, 1, p)
            own = (before[p, state], before[p, decay])
            before[p, state], before[p, decay] = compose(prefix, own)
            held[1, p, state], held[1, p, decay] = total
            held[1, p, pl.ds(TILE + 1, 7)] = jnp.zeros((7, TILE), jnp.float32)

            @pl.when(c[0] == first_z)
            def _():
                held[0, p] = jnp.zeros((TILE + 8, TILE), jnp.float32)
                hop(p).start()

    def pass_z(k):
        at = k if forward else sizes[0] - 1 - k

        @pl.when(c[0] == at)
        def _():
            for p in range(pieces):
                hop(p).wait_recv()
                if at != last_z:
                    got = (held[0, p, state], held[0, p, decay])
                    item = (held[1, p, state], held[1, p, decay])
                    held[1, p, state], held[1, p, decay] = compose(got, item)
                    hop(p).start()

    def finish():
        for p in range(pieces):
            result[p] = before[p, decay] * held[0, p, state] + before[p, state]
            for j in peers(2):
                line(across, mine, 2, j, p, 0).wait_send()
            for j in peers(1):
                line(along, held.at[2], 1, j, p, most * pieces).wait_send()

        @pl.when(c[0] != last_z)
        def _():
            for p in range(pieces):
                hop(p).wait_send()

    stages = [start_x, start_y, start_z]
    stages += [functools.partial(pass_z, k) for k in range(1, sizes[0])]
    return stages, finish


def greet(n, sizes, extra):
    c = coords(lax.axis_index("seq"), sizes)
    barrier = pltpu.get_barrier_semaphore()
    count = 0
    for ax in range(3):
        for j in range(1, sizes[ax]):
            d = list(c)
            d[ax] = lax.rem(c[ax] + j, sizes[ax])
            pl.semaphore_signal(
                barrier, inc=1, device_id={"seq": index_of(d, sizes)}, device_id_type=MESH
            )
            count += 1
    for index in extra:
        pl.semaphore_signal(barrier, inc=1, device_id={"seq": index}, device_id_type=MESH)
        count += 1
    pl.semaphore_wait(barrier, count)


def tile_masks(rows_ref, cols_ref, c):
    row = rows_ref[pl.ds(c, 1), :]
    col = cols_ref[pl.ds(pl.multiple_of(c * TILE, TILE), TILE), 6:7]
    i = lax.broadcasted_iota(jnp.int32, (TILE, TILE), 0)
    j = lax.broadcasted_iota(jnp.int32, (TILE, TILE), 1)
    return (i >= j) & (row == col)


def forward_kernel(
    n,
    sizes,
    plan,
    ready,
    owners_ref,
    lengths_ref,
    packing_ref,
    slot_ref,
    tokens_ref,
    norm_ref,
    down_ref,
    upper_ref,
    taps_ref,
    gain_ref,
    w_in_out,
    w_up_out,
    w_out_out,
    w_down_out,
    normed_out,
    lowrank_ref,
    logits_out,
    proj_out,
    halo_ref,
    gate_out,
    conv_out,
    cum_out,
    o_out,
    u_out,
    start_out,
    cols_ref,
    rows_ref,
    normed,
    logits_ref,
    proj_ref,
    gate_ref,
    conv_ref,
    cum_ref,
    o_ref,
    u_ref,
    start_ref,
    slots,
    piece,
    w_in,
    rim,
    segs,
    act,
    state,
    prev,
    a_send,
    a_recv,
    g_send,
    g_recv,
    l_sem,
    mine,
    across,
    along,
    before,
    held,
    result,
    send,
    recv,
):
    me = lax.axis_index("seq")
    c3 = coords(me, sizes)
    length, width = tokens_ref.shape
    tiles, channels = length // TILE, proj_ref.shape[1]
    keys = logits_ref.shape[1]
    rank = down_ref.shape[0]
    heads = keys // DK
    value = DV * heads
    slots_dev, _, bw = slot_ref.shape
    rows = piece.shape[0]
    scale = DK ** (-0.5)
    enter(n, me)

    def move(j):
        p = lax.rem(me + j, n)
        return remote(
            slot_ref.at[:, pl.ds(p * rows, rows), :],
            slots.at[pl.ds(me * slots_dev, slots_dev)],
            a_send.at[j],
            a_recv.at[j],
            p,
        )

    for j in range(1, n):
        move(j).start()
    local_move = pltpu.make_async_copy(
        slot_ref.at[:, pl.ds(me * rows, rows), :],
        slots.at[pl.ds(me * slots_dev, slots_dev)],
        l_sem.at[0],
    )
    local_move.start()
    edge = remote(
        tokens_ref.at[pl.ds(length - 16, 16)],
        rim,
        a_send.at[0],
        a_recv.at[0],
        lax.rem(me + 1, n),
    )

    @pl.when(me < n - 1)
    def _():
        edge.start()

    base = me * length
    where_col = base - 8 + lax.broadcasted_iota(jnp.int32, (length + 8, 1), 0)
    lane = lax.broadcasted_iota(jnp.int32, (tiles, TILE), 1)
    where_row = base + TILE * lax.broadcasted_iota(jnp.int32, (tiles, TILE), 0) + lane
    start = jnp.int32(0)
    seg_col = jnp.zeros((length + 8, 1), jnp.float32)
    seg_row = jnp.zeros((tiles, TILE), jnp.float32)
    for q in range(lengths_ref.shape[0]):
        seg_col += (where_col >= start).astype(jnp.float32)
        seg_row += (where_row >= start).astype(jnp.float32)
        start = start + lengths_ref[packing_ref[q]]
    filled = start
    segs[...] = seg_col + (where_col >= filled).astype(jnp.float32)
    rows_ref[...] = seg_row + (where_row >= filled).astype(jnp.float32)
    lane = lax.broadcasted_iota(jnp.int32, (TILE, TILE), 1)
    for c in range(tiles):
        lo = 8 + c * TILE
        own = segs[lo : lo + TILE]
        flags = [segs[lo - 1 : lo], segs[lo + TILE - 1 : lo + TILE]]
        flags += [segs[lo - s : lo - s + TILE] for s in (1, 2, 3)]
        flags = [(other == own).astype(jnp.float32) for other in flags]
        place = base + c * TILE + lax.broadcasted_iota(jnp.int32, (TILE, 1), 0)
        flags += [None, own, (place < filled).astype(jnp.float32)]
        total = jnp.zeros((TILE, TILE), jnp.float32)
        for k, flag in enumerate(flags):
            if flag is not None:
                total = jnp.where(lane == k, flag, total)
        cols_ref[c * TILE : (c + 1) * TILE, :] = total
    cols_ref[length : length + 8, :] = jnp.zeros((8, TILE), jnp.float32)

    def norm(values):
        values = values.astype(jnp.float32)
        inverse = lax.rsqrt(jnp.mean(values * values, axis=1, keepdims=True) + norm_epsilon)
        return (values * inverse * norm_ref[...]).astype(jnp.bfloat16)

    i = lax.broadcasted_iota(jnp.int32, (TILE, TILE), 0)
    j = lax.broadcasted_iota(jnp.int32, (TILE, TILE), 1)
    lower = (i >= j).astype(jnp.bfloat16)
    down_low = down_ref[...].astype(jnp.bfloat16)
    upper = halves(upper_ref[0:rank, :])

    def gates(c, _):
        at = pl.ds(pl.multiple_of(c * TILE, TILE), TILE)
        x = norm(tokens_ref[at, :])
        normed[at, :] = x
        low = lax.dot_general(x, down_low, NT, preferred_element_type=jnp.float32)
        lowrank_ref[at, :] = low
        logits = product(halves(low), upper, NN) + upper_ref[rank : rank + 1, :]
        logits_ref[at, :] = logits
        gate = jnp.minimum(logits, 0.0) - jnp.log1p(jnp.exp(-jnp.abs(logits)))
        cum_ref[at, :] = running_sum(lower, gate * (1.0 / gate_scale))
        return 0

    lax.fori_loop(0, tiles, gates, 0)
    flushes = []

    def flush(source, target):
        copy = pltpu.make_async_copy(source, target, l_sem.at[6 + len(flushes)])
        copy.start()
        flushes.append(copy)

    flush(normed, normed_out)
    flush(logits_ref, logits_out)
    flush(cum_ref, cum_out)

    @pl.when(me > 0)
    def _():
        edge.wait_recv()

    @pl.when(me == 0)
    def _():
        rim[...] = jnp.zeros_like(rim)

    rim[...] = norm(rim[...])

    local_move.wait()
    for j in range(1, n):
        move(j).wait()
    for b in range(owners_ref.shape[1]):
        piece[:, b * bw : (b + 1) * bw] = slots[owners_ref[0, b]]
    outs = (w_in, w_up_out, w_out_out, w_down_out)
    offset, owns = 0, []
    for q, out in enumerate(outs):
        columns = out.shape[4]
        owns.append(
            pltpu.make_async_copy(
                piece.at[:, pl.ds(offset, columns)],
                out.at[c3[0], c3[1], c3[2]],
                l_sem.at[1 + q],
            )
        )
        offset += columns
    for copy in owns:
        copy.start()
    for copy in owns:
        copy.wait()
    steps, arrived, sent = gather_steps(sizes, plan, piece, outs, bw, g_send, g_recv)
    for step in steps[: ready + 2]:
        step()
    arrived(range(ready))
    rest = list(steps[ready + 2 :])
    flush(w_in, w_in_out)

    for step in rest[: FORWARD_PLACES[0]]:
        step()
    del rest[: FORWARD_PLACES[0]]

    def project(r, _):
        at = pl.ds(pl.multiple_of(r * 256, 256), 256)
        x = normed[at, :]
        for lo in range(0, w_in.shape[4], 512):
            part = lax.dot_general(
                x,
                w_in[:, :, :, :, lo : lo + 512].reshape(width, 512),
                NN,
                preferred_element_type=jnp.float32,
            )
            if lo < channels:
                proj_ref[at, lo : lo + 512] = part.astype(proj_ref.dtype)
            else:
                gate_ref[at, lo - channels : lo - channels + 512] = part
        return 0

    lax.fori_loop(0, length // 256, project, 0)
    for lo in range(0, channels, 512):
        halo_ref[:, lo : lo + 512] = lax.dot_general(
            rim[...],
            w_in[:, :, :, :, lo : lo + 512].reshape(width, 512),
            NN,
            preferred_element_type=jnp.float32,
        ).astype(halo_ref.dtype)
    flush(proj_ref, proj_out)
    flush(gate_ref, gate_out)

    prev[...] = halo_ref[...]
    state[...] = jnp.zeros_like(state)
    mine[...] = jnp.zeros_like(mine)
    for p in range(mine.shape[0]):
        mine[p, TILE : TILE + 1] = jnp.ones((1, TILE), jnp.float32)
    run = spread_steps(rest, FORWARD_PLACES[1])

    def local(c, _):
        run(c)
        at = pl.ds(pl.multiple_of(c * TILE, TILE), TILE)
        for g in range(0, channels, 256):
            wide = slice(g, g + 256)
            block = jnp.concatenate(
                [prev[:, wide].astype(jnp.float32), proj_ref[at, wide].astype(jnp.float32)]
            )
            total = taps_ref[3:4, wide] * block[16:]
            for s in (1, 2, 3):
                total = total + taps_ref[3 - s : 4 - s, wide] * (
                    block[16 - s : 16 - s + TILE] * cols_ref[at, 1 + s : 2 + s]
                )
            conv_ref[at, wide] = total
            act[at, wide] = total * sigmoid(total)
        prev[...] = proj_ref[pl.ds(pl.multiple_of(c * TILE + TILE - 16, 16), 16), :]
        cum = cum_ref[at, :]
        last = cum[TILE - 1 : TILE]
        left = act[at, keys : 2 * keys] * jnp.exp(last - cum) * cols_ref[at, 1:2]
        decay = jnp.exp(last) * cols_ref[at, 0:1][TILE - 1 : TILE]
        for h in range(heads):
            kh = slice(h * DK, (h + 1) * DK)
            v = halves(act[at, 2 * keys + h * DV : 2 * keys + (h + 1) * DV])
            start_ref[c, h] = state[h]
            state[h] = state[h] * decay[:, kh] + product(v, halves(left[:, kh]), TN)
            for e in range(DV // TILE):
                p = h * (DV // TILE) + e
                mine[p, TILE : TILE + 1] = mine[p, TILE : TILE + 1] * decay[:, kh]
        return 0

    lax.fori_loop(0, tiles, local, 0)
    flush(conv_ref, conv_out)
    for h in range(heads):
        start_ref[tiles, h] = state[h]
        for e in range(DV // TILE):
            mine[h * (DV // TILE) + e, 0:TILE] = state[h, e * TILE : (e + 1) * TILE]
    stages, finish = chain_tools(
        n, sizes, True, mine, (across, along, before, held), send, recv, result
    )
    stages[0]()
    run_inside = spread_steps(rest, FORWARD_PLACES[2])

    def inside(c, _):
        for k, stage in enumerate(stages[1:]):
            pl.when(c == k + 1)(stage)
        run_inside(c)
        at = pl.ds(pl.multiple_of(c * TILE, TILE), TILE)
        cum = cum_ref[at, :]
        middle = cum[TILE // 2 - 1 : TILE // 2]
        q = act[at, 0:keys] * jnp.exp(cum - middle) * scale
        k = act[at, keys : 2 * keys] * jnp.exp(middle - cum)
        mask = tile_masks(rows_ref, cols_ref, c)
        for h in range(heads):
            kh = slice(h * DK, (h + 1) * DK)
            vh = slice(h * DV, (h + 1) * DV)
            scores = jnp.where(mask, product(halves(q[:, kh]), halves(k[:, kh]), NT), 0.0)
            v = halves(act[at, 2 * keys + h * DV : 2 * keys + (h + 1) * DV])
            o_ref[at, vh] = product(halves(scores), v, NN)
        return 0

    lax.fori_loop(0, tiles, inside, 0)
    finish()
    for h in range(heads):
        for e in range(DV // TILE):
            state[h, e * TILE : (e + 1) * TILE] = result[h * (DV // TILE) + e]

    run_outside = spread_steps(rest, FORWARD_PLACES[3])

    def outside(c, _):
        run_outside(c)
        at = pl.ds(pl.multiple_of(c * TILE, TILE), TILE)
        cum = cum_ref[at, :]
        q = act[at, 0:keys] * jnp.exp(cum) * scale * cols_ref[at, 0:1]
        decay = jnp.exp(cum[TILE - 1 : TILE]) * cols_ref[at, 0:1][TILE - 1 : TILE]
        for h in range(heads):
            kh = slice(h * DK, (h + 1) * DK)
            vh = slice(h * DV, (h + 1) * DV)
            begin = start_ref[c, h] + state[h]
            start_ref[c, h] = begin
            state[h] = state[h] * decay[:, kh]
            o = o_ref[at, vh] + product(halves(q[:, kh]), halves(begin), NT)
            o_ref[at, vh] = o
            inverse = lax.rsqrt(jnp.mean(o * o, axis=1, keepdims=True) + norm_epsilon)
            gate = gate_ref[at, vh]
            u_ref[at, vh] = (o * inverse * gain_ref[...] * (gate * sigmoid(gate))).astype(
                u_ref.dtype
            )
        return 0

    lax.fori_loop(0, tiles, outside, 0)
    for h in range(heads):
        start_ref[tiles, h] = start_ref[tiles, h] + state[h]
    flush(o_ref, o_out)
    flush(u_ref, u_out)
    flush(start_ref, start_out)
    for step in rest:
        step()
    groups = {chunk[5] for chunk in plan}
    arrived(sorted(g for g in groups if g >= ready))
    sent()
    for copy in flushes:
        copy.wait()

    @pl.when(me < n - 1)
    def _():
        edge.wait_send()


def forward(
    owners, lengths, packing, slot_copy, tokens, norm, down, upper, taps, gain, counts
):
    n = lax.axis_size("seq")
    sizes = axis_sizes(n)
    length, width = tokens.shape
    slots_dev, depth, bw = slot_copy.shape
    rows = depth // n
    keys, channels = upper.shape[1], taps.shape[1]
    heads = keys // DK
    value = heads * DV
    tiles = length // TILE
    blocks = sum(counts)
    ready = 2
    plan = build_plan(counts[:1], SHARES, ready, COLLECT)
    plan += [
        (which + 1, lo, hi, at, order, group + ready)
        for which, lo, hi, at, order, group in build_plan(
            counts[1:], SHARES, FORWARD_PIECES, COLLECT, counts[0]
        )
    ]
    f32, b16 = jnp.float32, jnp.bfloat16
    shape = jax.ShapeDtypeStruct
    vmem, anywhere = pl.BlockSpec(memory_space=pltpu.VMEM), pl.BlockSpec(memory_space=pl.ANY)
    smem = pl.BlockSpec(memory_space=pltpu.SMEM)
    kept = [
        ((length, width), b16),
        ((length, keys), f32),
        ((length, channels), b16),
        ((length, value), f32),
        ((length, channels), f32),
        ((length, keys), f32),
        ((length, value), f32),
        ((length, value), b16),
        ((tiles + 1, heads, DV, DK), f32),
    ]
    big = [shape(*k) for k in kept]
    outs = [shape(sizes + (rows, count * bw), b16) for count in counts]
    outs += [big[0], shape((length, down.shape[0]), f32), big[1], big[2]]
    outs += [shape((16, channels), b16)] + big[3:]
    outs += [shape((length + 8, TILE), f32), shape((tiles, TILE), f32)]
    specs = [anywhere] * 5 + [vmem, anywhere, anywhere, vmem] + [anywhere] * 6 + [vmem, vmem]
    most = max(sizes)
    copies = len(plan) * 3 * most
    result = pl.pallas_call(
        functools.partial(forward_kernel, n, sizes, plan, ready),
        out_shape=tuple(outs),
        in_specs=[smem] * 3 + [anywhere] + [vmem] * 6,
        out_specs=tuple(specs),
        scratch_shapes=[pltpu.VMEM(*k) for k in kept]
        + [
            pltpu.VMEM((n * slots_dev, rows, bw), b16),
            pltpu.VMEM((rows, blocks * bw), b16),
            pltpu.VMEM(sizes + (rows, counts[0] * bw), b16),
            pltpu.VMEM((16, width), b16),
            pltpu.VMEM((length + 8, 1), f32),
            pltpu.VMEM((length, channels), f32),
            pltpu.VMEM((heads, DV, DK), f32),
            pltpu.VMEM((16, channels), b16),
            pltpu.SemaphoreType.DMA((n,)),
            pltpu.SemaphoreType.DMA((n,)),
            pltpu.SemaphoreType.DMA((copies,)),
            pltpu.SemaphoreType.DMA((copies,)),
            pltpu.SemaphoreType.DMA((18,)),
        ]
        + chain_scratch(sizes, heads * DV // TILE),
        compiler_params=pltpu.CompilerParams(
            collective_id=1, has_side_effects=True, vmem_limit_bytes=60 << 20
        ),
    )(owners, lengths, packing, slot_copy, tokens, norm, down, upper, taps, gain)
    return [w.reshape(depth, w.shape[4]) for w in result[:4]], result[4:]


def chain_scratch(sizes, pieces):
    most = max(sizes)
    shape = (pieces, TILE + 8, TILE)
    return [
        pltpu.VMEM(shape, jnp.float32),
        pltpu.VMEM((sizes[2],) + shape, jnp.float32),
        pltpu.VMEM((sizes[1],) + shape, jnp.float32),
        pltpu.VMEM(shape, jnp.float32),
        pltpu.VMEM((3,) + shape, jnp.float32),
        pltpu.VMEM((pieces, TILE, TILE), jnp.float32),
        pltpu.SemaphoreType.DMA(((2 * most + 1) * pieces,)),
        pltpu.SemaphoreType.DMA(((2 * most + 1) * pieces,)),
    ]


def backward_kernel(
    n,
    sizes,
    plan,
    proj_ref,
    halo_ref,
    conv_ref,
    cum_ref,
    logits_ref,
    o_ref,
    gate_ref,
    du_ref,
    start_ref,
    cols_ref,
    rows_ref,
    taps_ref,
    gain_ref,
    g_up_ref,
    g_out_ref,
    dproj_ref,
    dgate_ref,
    dlogits_ref,
    dtaps_ref,
    dgain_ref,
    early_ref,
    do,
    dact,
    adjoint,
    ends,
    after,
    back,
    tail,
    mine,
    across,
    along,
    before,
    held,
    result,
    send,
    recv,
    b_sem,
    *scatter_refs,
):
    tiles, channels = proj_ref.shape[0] // TILE, proj_ref.shape[1]
    keys = cum_ref.shape[1]
    heads = keys // DK
    me = lax.axis_index("seq")
    greet(n, sizes, (lax.rem(me + 1, n), lax.rem(me + n - 1, n)))
    steps, sent = scatter_steps(
        sizes, plan, [g_up_ref, g_out_ref], scatter_refs, early_ref, TILE
    )
    steps.pop(0)()
    run_local = spread_steps(steps, BACKWARD_PLACES[0])
    run_inside = spread_steps(steps, BACKWARD_PLACES[1])
    run_outside = spread_steps(steps, BACKWARD_PLACES[2])
    scale = DK ** (-0.5)
    i = lax.broadcasted_iota(jnp.int32, (TILE, TILE), 0)
    j = lax.broadcasted_iota(jnp.int32, (TILE, TILE), 1)
    upper = (i <= j).astype(jnp.bfloat16)
    adjoint[...] = jnp.zeros_like(adjoint)
    mine[...] = jnp.zeros_like(mine)
    dgain_ref[...] = jnp.zeros_like(dgain_ref)
    dtaps_ref[...] = jnp.zeros_like(dtaps_ref)
    for p in range(mine.shape[0]):
        mine[p, TILE : TILE + 1] = jnp.ones((1, TILE), jnp.float32)

    def local(t, _):
        run_local(t)
        c = tiles - 1 - t
        at = pl.ds(pl.multiple_of(c * TILE, TILE), TILE)
        cum = cum_ref[at, :]
        pre = conv_ref[at, 0:keys]
        q = pre * sigmoid(pre) * jnp.exp(cum) * scale * cols_ref[at, 0:1]
        decay = jnp.exp(cum[TILE - 1 : TILE]) * cols_ref[at, 0:1][TILE - 1 : TILE]
        for h in range(heads):
            kh = slice(h * DK, (h + 1) * DK)
            vh = slice(h * DV, (h + 1) * DV)
            o = o_ref[at, vh]
            inverse = lax.rsqrt(jnp.mean(o * o, axis=1, keepdims=True) + norm_epsilon)
            gate = gate_ref[at, vh]
            sig = sigmoid(gate)
            du = du_ref[at, vh]
            unit = o * inverse
            dgate_ref[at, vh] = (
                du * (unit * gain_ref[...]) * (sig * (1.0 + gate * (1.0 - sig)))
            ).astype(dgate_ref.dtype)
            don = du * (gate * sig)
            dgain_ref[0:1] += jnp.sum(don * unit, axis=0, keepdims=True)
            scaled = gain_ref[...] * don
            grad = inverse * scaled - unit * (
                inverse * inverse * jnp.mean(scaled * o, axis=1, keepdims=True)
            )
            do[at, vh] = grad
            ends[c, h] = adjoint[h]
            adjoint[h] = adjoint[h] * decay[:, kh] + product(halves(grad), halves(q[:, kh]), TN)
            for e in range(DV // TILE):
                p = h * (DV // TILE) + e
                mine[p, TILE : TILE + 1] = mine[p, TILE : TILE + 1] * decay[:, kh]
        return 0

    lax.fori_loop(0, tiles, local, 0)
    for h in range(heads):
        for e in range(DV // TILE):
            mine[h * (DV // TILE) + e, 0:TILE] = adjoint[h, e * TILE : (e + 1) * TILE]
    stages, finish = chain_tools(
        n, sizes, False, mine, (across, along, before, held), send, recv, result
    )
    stages[0]()

    def inside(c, _):
        for k, stage in enumerate(stages[1:]):
            pl.when(c == k + 1)(stage)
        run_inside(c)
        at = pl.ds(pl.multiple_of(c * TILE, TILE), TILE)
        cum = cum_ref[at, :]
        middle = cum[TILE // 2 - 1 : TILE // 2]
        pre = conv_ref[at, 0 : 2 * keys]
        both = pre * sigmoid(pre)
        grow = jnp.exp(cum - middle) * scale
        fall = jnp.exp(middle - cum)
        enter_decay = jnp.exp(cum) * (scale * cols_ref[at, 0:1])
        mask = tile_masks(rows_ref, cols_ref, c)
        for h in range(heads):
            kh = slice(h * DK, (h + 1) * DK)
            vh = slice(h * DV, (h + 1) * DV)
            q = halves(both[:, kh] * grow[:, kh])
            k = halves(both[:, keys + h * DK : keys + (h + 1) * DK] * fall[:, kh])
            prev_v = conv_ref[at, 2 * keys + h * DV : 2 * keys + (h + 1) * DV]
            v = halves(prev_v * sigmoid(prev_v))
            grad = halves(do[at, vh])
            scores = halves(jnp.where(mask, product(q, k, NT), 0.0))
            dscores = halves(jnp.where(mask, product(grad, v, NT), 0.0))
            dact[at, h * DK : (h + 1) * DK] = (
                product(dscores, k, NN) * grow[:, kh]
                + product(grad, halves(start_ref[c, h]), NN) * enter_decay[:, kh]
            )
            dact[at, keys + h * DK : keys + (h + 1) * DK] = (
                product(dscores, q, TN) * fall[:, kh]
            )
            dact[at, 2 * keys + h * DV : 2 * keys + (h + 1) * DV] = product(scores, grad, TN)
        return 0

    lax.fori_loop(0, tiles, inside, 0)
    finish()
    for h in range(heads):
        for e in range(DV // TILE):
            adjoint[h, e * TILE : (e + 1) * TILE] = result[h * (DV // TILE) + e]
    after[...] = jnp.zeros_like(after)

    def outside(t, _):
        run_outside(t)
        c = tiles - 1 - t
        at = pl.ds(pl.multiple_of(c * TILE, TILE), TILE)
        cum = cum_ref[at, :]
        last = cum[TILE - 1 : TILE]
        remain = jnp.exp(last - cum) * cols_ref[at, 1:2]
        decay = jnp.exp(last) * cols_ref[at, 0:1][TILE - 1 : TILE]
        pre = conv_ref[at, 0 : 2 * keys]
        both = pre * sigmoid(pre)
        dkeys, edges = [], []
        for h in range(heads):
            kh = slice(h * DK, (h + 1) * DK)
            wide = slice(2 * keys + h * DV, 2 * keys + (h + 1) * DV)
            k = both[:, keys + h * DK : keys + (h + 1) * DK]
            end = ends[c, h] + adjoint[h]
            adjoint[h] = adjoint[h] * decay[:, kh]
            parts = halves(end)
            pre_v = conv_ref[at, wide]
            v = halves(pre_v * sigmoid(pre_v))
            dkeys.append(
                dact[at, keys + h * DK : keys + (h + 1) * DK]
                + product(v, parts, NN) * remain[:, kh]
            )
            dact[at, wide] += product(halves(k * remain[:, kh]), parts, NT)
            edges.append(jnp.sum(end * start_ref[c + 1, h], axis=0, keepdims=True))
        dk = jnp.concatenate(dkeys, axis=1)
        dq = dact[at, 0:keys]
        dact[at, keys : 2 * keys] = dk
        drift = both[:, 0:keys] * dq - both[:, keys:] * dk
        dl = running_sum(upper, drift) + jnp.concatenate(edges, axis=1)
        dlogits_ref[at, :] = dl * (1.0 / gate_scale) * sigmoid(-logits_ref[at, :])
        behind = jnp.where(
            c == 0,
            halo_ref[...],
            proj_ref[pl.ds(pl.multiple_of(jnp.maximum(c * TILE - 16, 0), 16), 16), :],
        )
        masks = cols_ref[pl.ds(pl.multiple_of(c * TILE, TILE), TILE + 8), :]
        for g in range(0, channels, 256):
            wide = slice(g, g + 256)
            pre = conv_ref[at, wide]
            sig = sigmoid(pre)
            dconv = dact[at, wide] * (sig * (1.0 + pre * (1.0 - sig)))
            block = jnp.concatenate(
                [
                    behind[:, g : g + 256].astype(jnp.float32),
                    proj_ref[at, wide].astype(jnp.float32),
                ]
            )
            grad = jnp.concatenate([dconv, after[:, wide]])
            total = taps_ref[3:4, wide] * dconv
            dtaps_ref[3:4, wide] += jnp.sum(dconv * block[16:], axis=0, keepdims=True)
            first = jnp.zeros((8, 256), jnp.float32)
            for s in (1, 2, 3):
                masked = grad * masks[:, 1 + s : 2 + s]
                tap = taps_ref[3 - s : 4 - s, wide]
                total = total + tap * masked[s : s + TILE]
                dtaps_ref[3 - s : 4 - s, wide] += jnp.sum(
                    masked[:TILE] * block[16 - s : 16 - s + TILE], axis=0, keepdims=True
                )
                first = first + tap * jnp.concatenate(
                    [jnp.zeros((8, 256), jnp.float32), masked[0:8]]
                )[s : s + 8]
            dproj_ref[at, wide] = total.astype(dproj_ref.dtype)
            after[:, wide] = dconv[0:8]
            back[0, :, wide] = first

            @pl.when(c == tiles - 1)
            def _():
                tail[:, wide] = total[TILE - 16 :]

        return 0

    lax.fori_loop(0, tiles, outside, 0)

    home = remote(
        back.at[0], back.at[1], b_sem.at[0], b_sem.at[1], lax.rem(me + n - 1, n)
    )

    @pl.when(me > 0)
    def _():
        home.start()

    for step in steps:
        step()
    sent()

    @pl.when(me < n - 1)
    def _():
        home.wait_recv()

    @pl.when(me == n - 1)
    def _():
        back[1] = jnp.zeros(back.shape[1:], jnp.float32)

    dproj_ref[pl.ds(tiles * TILE - 16, 16), :] = (
        tail[...] + jnp.concatenate([jnp.zeros((8, channels), jnp.float32), back[1]])
    ).astype(dproj_ref.dtype)

    @pl.when(me > 0)
    def _():
        home.wait_send()


def recurrence_back(
    proj, halo, conv, cum, logits, o, gate, du, starts, cols, rows, taps, gain, grads
):
    n = lax.axis_size("seq")
    sizes = axis_sizes(n)
    length, channels = proj.shape
    keys = cum.shape[1]
    heads = keys // DK
    value = heads * DV
    tiles = length // TILE
    f32 = jnp.float32
    shape = jax.ShapeDtypeStruct
    depth = grads[0].shape[3]
    plan = build_plan(tuple(g.shape[4] // TILE for g in grads), SHARES, BACKWARD_PIECES, SPREAD)
    blocks = sum(g.shape[4] for g in grads) // TILE
    vmem, anywhere = pl.BlockSpec(memory_space=pltpu.VMEM), pl.BlockSpec(memory_space=pl.ANY)
    return pl.pallas_call(
        functools.partial(backward_kernel, n, sizes, plan),
        in_specs=[vmem] * 13 + [anywhere] * 2,
        out_shape=(
            shape((length, channels), jnp.bfloat16),
            shape((length, value), jnp.bfloat16),
            shape((length, keys), f32),
            shape((8, channels), f32),
            shape((8, DV), f32),
            shape((blocks, depth, TILE), jnp.bfloat16),
        ),
        scratch_shapes=[
            pltpu.VMEM((length, value), f32),
            pltpu.VMEM((length, channels), f32),
            pltpu.VMEM((heads, DV, DK), f32),
            pltpu.VMEM((tiles, heads, DV, DK), f32),
            pltpu.VMEM((8, channels), f32),
            pltpu.VMEM((2, 8, channels), f32),
            pltpu.VMEM((16, channels), f32),
        ]
        + chain_scratch(sizes, heads * DV // TILE)
        + [pltpu.SemaphoreType.DMA((2,))]
        + scatter_scratch(sizes, plan, depth, TILE, jnp.bfloat16),
        compiler_params=pltpu.CompilerParams(
            collective_id=5, has_side_effects=True, vmem_limit_bytes=60 << 20
        ),
    )(proj, halo, conv, cum, logits, o, gate, du, starts, cols, rows, taps, gain, *grads)


def tail_kernel(
    n,
    sizes,
    plan,
    shared,
    inv_ref,
    early_ref,
    dproj_ref,
    dgate_ref,
    normed_ref,
    dlogits_ref,
    lowrank_ref,
    upper_ref,
    down_ref,
    gain_ref,
    gains_two_ref,
    dtaps_ref,
    dhead_ref,
    w_ref,
    tokens_ref,
    dh_ref,
    out_ref,
    small_out,
    grad_ref,
    turned,
    grads,
    weights,
    tokens,
    dh,
    total,
    trade,
    fin,
    send,
    small,
    a_send,
    a_recv,
    s_send,
    s_recv,
    l_sem,
    *refs,
):
    me, core = lax.axis_index("seq"), lax.axis_index("head")
    slots, _, rows, bw = out_ref.shape
    length, width = normed_ref.shape
    channels = dproj_ref.shape[1]
    keys, rank, tap_count = dlogits_ref.shape[1], down_ref.shape[0], 4
    count = fin.shape[0] - 1 - early_ref.shape[0]
    tiles = s_send.shape[0]
    step_rows = length // tiles
    f32 = jnp.float32
    dot = functools.partial(lax.dot_general, preferred_element_type=f32)
    enter(n, me, True)
    loads = [
        pltpu.make_async_copy(source, target, l_sem.at[1 + q])
        for q, (source, target) in enumerate(((w_ref, weights), (tokens_ref, tokens), (dh_ref, dh)))
    ]
    for load in loads:
        load.start()
    steps, sent = scatter_steps(sizes, plan, [grads], refs[:-5], fin, bw)
    sums = sum_steps(sizes, shared, small, small_out, *refs[-5:])

    plane = width // sizes[0]
    for z in range(sizes[0]):
        turned[:, z * plane : (z + 1) * plane] = normed_ref[z * plane : (z + 1) * plane, :].T

    def block_grads(lo, hi):
        for source, base in ((dproj_ref, 0), (dgate_ref, channels)):
            first, last = max(lo - base, 0), min(hi - base, source.shape[1])
            if first >= last:
                continue

            def one(z, _):
                at = pl.ds(pl.multiple_of(z * plane, plane), plane)
                part = dot(turned[at, :], source[:, first:last], dimension_numbers=NN)
                grads[z, :, :, :, base + first : base + last] = part.astype(grads.dtype).reshape(
                    sizes[1], sizes[2], rows, last - first
                )
                return 0

            lax.fori_loop(0, sizes[0], one, 0)

    cut = max(hi for _, _, hi, _, _, group in plan if group == 0) * bw
    block_grads(0, cut)
    steps[0]()
    block_grads(cut, grads.shape[4])
    steps[1]()
    fin[fin.shape[0] - 1] = jnp.zeros(fin.shape[1:], fin.dtype)
    fin[count : fin.shape[0] - 1] = early_ref[...]

    def swap(t):
        at = pl.ds(t * step_rows, step_rows)
        return pltpu.make_async_remote_copy(
            src_ref=total.at[at],
            dst_ref=trade.at[at],
            send_sem=s_send.at[t],
            recv_sem=s_recv.at[t],
            device_id={"head": 1 - core},
            device_id_type=MESH,
        )

    for load in loads:
        load.wait()
    upper = halves(upper_ref[0:rank, :])
    down_low = down_ref[...].astype(jnp.bfloat16)
    small[...] = jnp.zeros_like(small)
    upper_grad = jnp.zeros((rank, keys), f32)
    bias_grad = jnp.zeros((1, keys), f32)
    for t in range(tiles):
        at = slice(t * step_rows, (t + 1) * step_rows)
        dlogits = dlogits_ref[at, :]
        parts = halves(dlogits)
        dlow = product(parts, upper, NT).astype(jnp.bfloat16)
        upper_grad += product(halves(lowrank_ref[at, :]), parts, TN)
        bias_grad += jnp.sum(dlogits, axis=0, keepdims=True)
        small[0:rank, :] += dot(dlow, normed_ref[at, :], dimension_numbers=TN)
        part = (
            dot(dproj_ref[at, :], weights[:, :channels], dimension_numbers=NT)
            + dot(dgate_ref[at, :], weights[:, channels:], dimension_numbers=NT)
            + dot(dlow, down_low, dimension_numbers=NN)
        )
        total[at, :] = part.astype(total.dtype)
        swap(t).start()
        tok = tokens[at, :].astype(f32)
        inverse = lax.rsqrt(jnp.mean(tok * tok, axis=1, keepdims=True) + norm_epsilon)
        small[rank + 1 : rank + 2, :] += jnp.sum(part * (tok * inverse), axis=0, keepdims=True)
    small[rank : rank + 1, 0:DV] = dhead_ref[0:1, :]
    small[shared : shared + 1, :] = gains_two_ref[0:1, :]
    small[shared + 1 : shared + 1 + tap_count, :] = dtaps_ref[0:tap_count, :]
    per = width // keys
    base = shared + 1 + tap_count
    for r in range(rank + 1):
        row = bias_grad if r == rank else upper_grad[r : r + 1]
        small[base + r // per : base + r // per + 1, (r % per) * keys : (r % per + 1) * keys] = row
    sums[0]()
    steps[2]()
    sums[1]()

    for t in range(tiles):
        at = slice(t * step_rows, (t + 1) * step_rows)
        swap(t).wait_recv()
        dxn = total[at, :].astype(f32) + trade[at, :].astype(f32)
        tok = tokens[at, :].astype(f32)
        inverse = lax.rsqrt(jnp.mean(tok * tok, axis=1, keepdims=True) + norm_epsilon)
        scaled = gain_ref[...] * dxn
        mean = jnp.mean(scaled * tok, axis=1, keepdims=True)
        dh[at, :] = dh[at, :] + (
            inverse * scaled - tok * (inverse * inverse * inverse * mean)
        )
    store = pltpu.make_async_copy(dh, grad_ref, l_sem.at[4])
    store.start()
    for s, step in enumerate(steps[3:]):
        step()
        if s + 2 < len(sums):
            sums[s + 2]()
    for s in range(send.shape[0]):
        send[s] = fin[inv_ref[0, s]]

    def move(j):
        p = lax.rem(me + j, n)
        return remote(
            send.at[pl.ds(p * slots, slots)], out_ref.at[:, me], a_send.at[j], a_recv.at[j], p
        )

    for j in range(1, n):
        move(j).start()
    mine = pltpu.make_async_copy(
        send.at[pl.ds(me * slots, slots)], out_ref.at[:, me], l_sem.at[0]
    )
    mine.start()
    for step in sums[len(steps) - 1 :]:
        step()
    mine.wait()
    for j in range(1, n):
        move(j).wait()
    sent()
    for t in range(tiles):
        swap(t).wait_send()
    store.wait()


def tail(
    inverse, early, dproj, dgate, normed, dlogits, lowrank, upper, down, gain, gains_two,
    dtaps, dhead, weights, tokens, dh, slots
):
    n = lax.axis_size("seq")
    sizes = axis_sizes(n)
    most = max(sizes)
    length, width = normed.shape
    _, rows, bw = early.shape
    columns = dproj.shape[1] + dgate.shape[1]
    blocks = columns // bw
    rank = down.shape[0]
    shared = rank + 8
    plan = build_plan((blocks,), SHARES, 2, SPREAD)
    shape = jax.ShapeDtypeStruct
    vmem, anywhere = pl.BlockSpec(memory_space=pltpu.VMEM), pl.BlockSpec(memory_space=pl.ANY)
    b16, f32 = jnp.bfloat16, jnp.float32
    small = (shared + 16, width)
    tiles = 4
    out, summed, grad = pl.pallas_call(
        functools.partial(tail_kernel, n, sizes, plan, shared),
        out_shape=(
            shape((slots, n, rows, bw), b16),
            shape(small, f32),
            shape((length, width), f32),
        ),
        in_specs=[pl.BlockSpec(memory_space=pltpu.SMEM)] + [vmem] * 12 + [anywhere] * 3,
        out_specs=(anywhere, vmem, anywhere),
        scratch_shapes=[
            pltpu.VMEM((width, length), b16),
            pltpu.VMEM(sizes + (rows, columns), b16),
            pltpu.VMEM((width, columns), b16),
            pltpu.VMEM((length, width), b16),
            pltpu.VMEM((length, width), f32),
            pltpu.VMEM((length, width), b16),
            pltpu.VMEM((length, width), b16),
            pltpu.VMEM((blocks + early.shape[0] + 1, rows, bw), b16),
            pltpu.VMEM((slots * n, rows, bw), b16),
            pltpu.VMEM(small, f32),
            pltpu.SemaphoreType.DMA((n,)),
            pltpu.SemaphoreType.DMA((n,)),
            pltpu.SemaphoreType.DMA((tiles,)),
            pltpu.SemaphoreType.DMA((tiles,)),
            pltpu.SemaphoreType.DMA((5,)),
        ]
        + scatter_scratch(sizes, plan, rows, bw, b16)
        + [
            pltpu.VMEM((shared, width), f32),
            pltpu.VMEM((3,) + small, f32),
            pltpu.VMEM((3, most) + small, f32),
            pltpu.SemaphoreType.DMA((1 + 3 * most,)),
            pltpu.SemaphoreType.DMA((1 + 3 * most,)),
        ],
        compiler_params=pltpu.CompilerParams(
            collective_id=2, has_side_effects=True, vmem_limit_bytes=60 << 20
        ),
    )(
        inverse, early, dproj, dgate, normed, dlogits, lowrank, upper, down, gain, gains_two,
        dtaps, dhead, weights, tokens, dh
    )
    return out.reshape(slots, width, bw), summed, grad


def adam_kernel(
    rates,
    rank,
    taps,
    grad_ref,
    left_ref,
    right_ref,
    master_ref,
    first_ref,
    second_ref,
    summed_ref,
    *refs,
):
    params = [refs[3 * q : 3 * q + 3] for q in range(5)]
    grad_in, result_in = refs[15:17]
    grad_out, master_out, first_out, second_out, copy_out = refs[17:22]
    news = [refs[22 + 4 * q : 26 + 4 * q] for q in range(5)]
    grad_pass, result_ref, high, low = refs[42:]
    grad_pass[...] = grad_in[...]
    result_ref[...] = result_in[...]

    @pl.when(pl.program_id(0) == 0)
    def _():
        shared = rank + 8
        width = summed_ref.shape[1]
        keys = news[2][0].shape[1]
        per = width // keys
        base = shared + 1 + taps
        gains, down, upper, head, conv = news
        gains[0][0:1, :] = summed_ref[rank + 1 : rank + 2, :]
        gains[0][1:2, :] = summed_ref[shared : shared + 1, :]
        down[0][...] = summed_ref[0:rank, :]
        for r in range(rank + 1):
            upper[0][r : r + 1, :] = summed_ref[
                base + r // per : base + r // per + 1, (r % per) * keys : (r % per + 1) * keys
            ]
        head[0][...] = summed_ref[rank : rank + 1, 0:DV]
        conv[0][...] = summed_ref[shared + 1 : shared + 1 + taps, :]
        for (value, first, second), new, rate in zip(params, news, rates, strict=True):
            new[1][...], new[2][...], new[3][...] = plain_adam(
                value[...], new[0][...], first[...], second[...], rate
            )

    width = left_ref.shape[1]
    step = min(256, width)
    dot = functools.partial(
        lax.dot_general, dimension_numbers=TN, preferred_element_type=jnp.float32
    )
    grad_out[0] = grad_ref[0].astype(jnp.float32)
    total = None
    for r in range(0, width, step):
        at = slice(r, r + step)
        lh, ll = halves(left_ref[0, at, :])
        high[at, :], low[at, :] = lh, ll
        term = dot(grad_ref[0, at, :], lh) + dot(grad_ref[0, at, :], ll)
        total = term if total is None else total + term
    right = halves(right_ref[0])
    rotated = product(right, halves(total), TN).T
    first = moment_decay * first_ref[0] + (1.0 - moment_decay) * rotated
    second = moment_decay * second_ref[0] + (1.0 - moment_decay) * rotated * rotated
    first_out[0] = first
    second_out[0] = second
    direction = first / (jnp.sqrt(second) + adam_epsilon)
    eh, el = halves(product(halves(direction), right, NT))
    both = jnp.concatenate([eh, el], axis=1)
    columns = eh.shape[1]
    dot = functools.partial(
        lax.dot_general, dimension_numbers=NN, preferred_element_type=jnp.float32
    )
    for r in range(0, width, step):
        at = slice(r, r + step)
        pair = dot(high[at, :], both)
        restored = pair[:, :columns] + (pair[:, columns:] + dot(low[at, :], eh))
        master = master_ref[0, at, :] - rate_block * restored
        master_out[0, at, :] = master
        copy_out[0, at, :] = master.astype(copy_out.dtype)


def all_adam(grads, left, right, master, first, second, summed, params, grad, result):
    slots, width, columns = master.shape
    tall = pl.BlockSpec((1, width, columns), lambda i: (i, 0, 0))
    length, model = grad.shape
    wide = pl.BlockSpec((length // slots, model), lambda i: (i, 0))
    shape = jax.ShapeDtypeStruct
    full = shape(master.shape, jnp.float32)

    def whole(array):
        return pl.BlockSpec(array.shape, lambda i: (0, 0))

    flat = [array for triple in params for array in triple]
    rates = (rate_gains, rate_down, rate_upper, rate_head, rate_conv)
    news = [triple[0] for triple in params for _ in range(4)]
    return pl.pallas_call(
        functools.partial(adam_kernel, rates, params[1][0].shape[0], params[4][0].shape[0]),
        grid=(slots,),
        out_shape=tuple(
            [full] * 4
            + [shape(master.shape, jnp.bfloat16)]
            + [shape(new.shape, new.dtype) for new in news]
            + [shape(grad.shape, jnp.float32), shape(grad.shape, jnp.bfloat16)]
        ),
        in_specs=[
            tall,
            pl.BlockSpec((1, width, width), lambda i: (i, 0, 0)),
            pl.BlockSpec((1, columns, columns), lambda i: (i, 0, 0)),
            tall,
            tall,
            tall,
            whole(summed),
        ]
        + [whole(array) for array in flat]
        + [wide] * 2,
        out_specs=[tall] * 5 + [whole(new) for new in news] + [wide] * 2,
        scratch_shapes=[
            pltpu.VMEM((width, width), jnp.bfloat16),
            pltpu.VMEM((width, width), jnp.bfloat16),
        ],
        compiler_params=pltpu.CompilerParams(vmem_limit_bytes=56 << 20),
    )(grads, left, right, master, first, second, summed, *flat, grad, result)


def middle_kernel(
    n,
    sizes,
    plan,
    u_ref,
    w_out_ref,
    cols_ref,
    gain_ref,
    tokens_ref,
    w_up_ref,
    w_down_ref,
    cot_ref,
    early_ref,
    sum_ref,
    result_out,
    dh_out,
    du_out,
    g_up_out,
    g_out_out,
    w_up,
    w_down,
    mixed,
    hidden_sum,
    normed,
    inv,
    dy,
    hid,
    dpair,
    turned,
    send,
    recv,
    g_down,
    g_up,
    g_out,
    du,
    free,
    s_sem,
    r_sem,
    l_sem,
    *scatter_refs,
):
    me, core = lax.axis_index("seq"), lax.axis_index("head")
    length, width = normed.shape
    inner = hid.shape[1]
    rows = g_out.shape[3]
    f32 = jnp.float32
    dot = functools.partial(lax.dot_general, preferred_element_type=f32)
    tiles = s_sem.shape[0] // 3
    block = length // tiles
    ats = [slice(t * block, (t + 1) * block) for t in range(tiles)]
    enter(n, me, True)
    loads = [
        pltpu.make_async_copy(source, target, l_sem.at[q])
        for q, (source, target) in enumerate(
            ((tokens_ref, mixed), (w_up_ref, w_up), (w_down_ref, w_down), (cot_ref, dy))
        )
    ]
    for load in loads:
        load.start()
    flushes = []

    def flush(source, target):
        copy = pltpu.make_async_copy(source, target, l_sem.at[4 + len(flushes)])
        copy.start()
        flushes.append(copy)

    steps, sent = scatter_steps(
        sizes, plan, [g_down, g_up], scatter_refs, early_ref, TILE, in_place=True
    )

    def advance(count=1):
        for step in steps[:count]:
            step()
        del steps[:count]

    def swap(phase, t):
        at = pl.ds(t * block, block)
        return pltpu.make_async_remote_copy(
            src_ref=send.at[at],
            dst_ref=recv.at[at],
            send_sem=s_sem.at[phase * tiles + t],
            recv_sem=r_sem.at[phase * tiles + t],
            device_id={"head": 1 - core},
            device_id_type=MESH,
        )

    def exchange(phase, left, right, close):
        if phase:
            for t in range(tiles):
                swap(phase - 1, t).wait_send()
            pl.semaphore_wait(free, 1)
        for t, at in enumerate(ats):
            send[at, :] = dot(left[at, :], right[...], dimension_numbers=NT).astype(send.dtype)
            swap(phase, t).start()
            if t:
                swap(phase, t - 1).wait_recv()
                close(ats[t - 1])
        swap(phase, tiles - 1).wait_recv()
        close(ats[-1])
        if phase < 2:
            pl.semaphore_signal(
                free, inc=1, device_id={"head": 1 - core}, device_id_type=MESH
            )

    def both(at):
        return send[at, :].astype(f32) + recv[at, :].astype(f32)

    loads[0].wait()

    def close_attn(at):
        total = mixed[at, :].astype(f32) + both(at)
        inverse = lax.rsqrt(jnp.mean(total * total, axis=1, keepdims=True) + norm_epsilon)
        hidden_sum[at, :] = total
        inv[at, :] = inverse
        normed[at, :] = (total * inverse * gain_ref[...]).astype(normed.dtype)

    exchange(0, u_ref, w_out_ref, close_attn)
    for load in loads[1:]:
        load.wait()

    def feed(t, _):
        at = pl.ds(pl.multiple_of(t * block, block), block)
        x = normed[at, :]
        grad_y = (dy[at, :].astype(f32) * cols_ref[at, 7:8]).astype(dy.dtype)
        dy[at, :] = grad_y
        for lo in range(0, inner, 512):
            hi = min(lo + 512, inner)
            gate = dot(x, w_up[:, lo:hi], dimension_numbers=NN)
            up = dot(x, w_up[:, inner + lo : inner + hi], dimension_numbers=NN)
            grad = dot(grad_y, w_down[:, lo:hi], dimension_numbers=NN)
            sig = sigmoid(gate)
            swish = gate * sig
            hid[at, lo:hi] = (swish * up).astype(hid.dtype)
            dpair[at, lo:hi] = (grad * up * (sig + swish * (1.0 - sig))).astype(dpair.dtype)
            dpair[at, inner + lo : inner + hi] = (grad * swish).astype(dpair.dtype)
        return 0

    lax.fori_loop(0, tiles, feed, 0)

    plane = width // sizes[0]

    def turn(source):
        for at in ats:
            turned[:, at] = source[at, :].T

    def block_grads(source, target, lo, hi):
        def one(z, _):
            at = pl.ds(pl.multiple_of(z * plane, plane), plane)
            for first in range(lo, hi, 512):
                last = min(first + 512, hi)
                part = dot(turned[at, :], source[:, first:last], dimension_numbers=NN)
                target[z, :, :, :, first:last] = part.astype(target.dtype).reshape(
                    sizes[1], sizes[2], rows, last - first
                )
            return 0

        lax.fori_loop(0, sizes[0], one, 0)

    turn(dy)
    block_grads(hid, g_down, 0, inner)
    advance()
    turn(normed)
    block_grads(dpair, g_up, 0, inner)
    advance()
    block_grads(dpair, g_up, inner, 2 * inner)
    taken = g_up.shape[4] - g_up_out.shape[4]
    flush(g_up.at[:, :, :, :, pl.ds(taken, g_up_out.shape[4])], g_up_out)

    def close_mlp(at):
        mixed[at, :] = (hidden_sum[at, :] + both(at)).astype(mixed.dtype)

    exchange(1, hid, w_down, close_mlp)
    flush(mixed, result_out)
    advance()

    sum_ref[...] = jnp.zeros_like(sum_ref)

    def close_back(at):
        grad = both(at)
        total, inverse = hidden_sum[at, :], inv[at, :]
        unit = total * inverse
        scaled = gain_ref[...] * grad
        mean = jnp.mean(scaled * total, axis=1, keepdims=True)
        dh = dy[at, :].astype(f32) + (inverse * scaled - unit * (inverse * inverse * mean))
        hidden_sum[at, :] = dh
        normed[at, :] = dh.astype(normed.dtype)
        sum_ref[0:1, :] += jnp.sum(grad * unit, axis=0, keepdims=True)
        du[at, :] = dot(normed[at, :], w_out_ref[...], dimension_numbers=NN)

    exchange(2, dpair, w_up, close_back)
    flush(hidden_sum, dh_out)
    flush(du, du_out)
    advance()
    turn(normed)
    block_grads(u_ref, g_out, 0, u_ref.shape[1])
    flush(g_out, g_out_out)
    advance(len(steps))
    sent()
    for t in range(tiles):
        swap(2, t).wait_send()
    for copy in flushes:
        copy.wait()


def middle(u, w_out, cols, gain, tokens, w_up, w_down, cot, taken):
    n = lax.axis_size("seq")
    sizes = axis_sizes(n)
    length, width = tokens.shape
    value, inner = u.shape[1], w_down.shape[1]
    rows = width // n
    f32, b16 = jnp.float32, jnp.bfloat16
    blocks = inner // TILE
    plan = build_plan((blocks, taken) if taken else (blocks,), SHARES, MIDDLE_PIECES, SPREAD)
    shape = jax.ShapeDtypeStruct
    vmem, anywhere = pl.BlockSpec(memory_space=pltpu.VMEM), pl.BlockSpec(memory_space=pl.ANY)
    tiles = 4
    return pl.pallas_call(
        functools.partial(middle_kernel, n, sizes, plan),
        out_shape=(
            shape((blocks + taken, rows, TILE), b16),
            shape((8, width), f32),
            shape((length, width), b16),
            shape((length, width), f32),
            shape((length, value), f32),
            shape(sizes + (rows, 2 * inner - taken * TILE), b16),
            shape(sizes + (rows, value), b16),
        ),
        in_specs=[vmem] * 4 + [anywhere] * 4,
        out_specs=(vmem, vmem) + (anywhere,) * 5,
        scratch_shapes=[
            pltpu.VMEM((width, 2 * inner), b16),
            pltpu.VMEM((width, inner), b16),
            pltpu.VMEM((length, width), b16),
            pltpu.VMEM((length, width), f32),
            pltpu.VMEM((length, width), b16),
            pltpu.VMEM((length, 1), f32),
            pltpu.VMEM((length, width), b16),
            pltpu.VMEM((length, inner), b16),
            pltpu.VMEM((length, 2 * inner), b16),
            pltpu.VMEM((width, length), b16),
            pltpu.VMEM((length, width), b16),
            pltpu.VMEM((length, width), b16),
            pltpu.VMEM(sizes + (rows, inner), b16),
            pltpu.VMEM(sizes + (rows, 2 * inner), b16),
            pltpu.VMEM(sizes + (rows, value), b16),
            pltpu.VMEM((length, value), f32),
            pltpu.SemaphoreType.REGULAR,
            pltpu.SemaphoreType.DMA((3 * tiles,)),
            pltpu.SemaphoreType.DMA((3 * tiles,)),
            pltpu.SemaphoreType.DMA((9,)),
        ]
        + scatter_scratch(sizes, plan, rows, TILE, b16, in_place=True),
        compiler_params=pltpu.CompilerParams(
            collective_id=6, has_side_effects=True, vmem_limit_bytes=62 << 20
        ),
    )(u, w_out, cols, gain, tokens, w_up, w_down, cot)


def plain_adam(param, gradient, first, second, rate):
    first_next = moment_decay * first + (1.0 - moment_decay) * gradient
    second_next = moment_decay * second + (1.0 - moment_decay) * gradient * gradient
    return (
        param - rate * first_next / (jnp.sqrt(second_next) + adam_epsilon),
        first_next,
        second_next,
    )


def body(
    tokens,
    cotangent,
    lengths,
    packing,
    owners,
    slot_copy,
    slot_master,
    slot_first,
    slot_second,
    basis_left,
    basis_right,
    norm_gains,
    gains_first,
    gains_second,
    gate_down,
    down_first,
    down_second,
    gate_up,
    upper_first,
    upper_second,
    head_gain,
    head_first,
    head_second,
    conv_weight,
    conv_first,
    conv_second,
):
    tok_rows = tokens.shape[0]
    model_width = tokens.shape[1]
    block_width = slot_copy.shape[2]
    tap_count = conv_weight.shape[0]
    key_width = gate_up.shape[1]
    channels = conv_weight.shape[1]
    value_width = channels - 2 * key_width
    block_total = owners.shape[1]
    count_in = (channels + value_width) // block_width
    count_out = value_width // block_width
    count_down = (block_total - count_in - count_out) // 3
    count_up = 2 * count_down
    (in_weights, up_weights, out_weights, down_weights), kept = forward(
        owners,
        lengths,
        packing,
        slot_copy,
        tokens,
        norm_gains[0:1],
        gate_down.T,
        gate_up,
        conv_weight,
        head_gain[None],
        (count_in, count_up, count_out, count_down),
    )
    normed, lowrank, logits, mixed_proj, halo, gate_pre = kept[:6]
    conv_pre, cumulative, attended, gated_out, starts, cols, rows = kept[6:]
    gain_row = head_gain[None]
    early, gains_two, result, grad_one, grad_gated, grad_up, grad_out = middle(
        gated_out,
        out_weights,
        cols,
        norm_gains[1:2],
        tokens,
        up_weights,
        down_weights,
        cotangent,
        MIDDLE_TAKEN,
    )
    grad_mixed, grad_gate_pre, grad_logits, tap_grads, gain_grads, later = recurrence_back(
        mixed_proj,
        halo,
        conv_pre,
        cumulative,
        logits,
        attended,
        gate_pre,
        grad_gated,
        starts,
        cols,
        rows,
        conv_weight,
        gain_row,
        (grad_up, grad_out),
    )
    early = jnp.concatenate(
        [early[count_down:], later, early[:count_down]]
    )
    slots_dev = slot_copy.shape[0]
    slot_total = slots_dev * lax.axis_size("seq")
    named = jnp.arange(slot_total, dtype=jnp.int32)[:, None] == owners
    inverse = jnp.where(
        jnp.any(named, axis=1),
        jnp.sum(named * jnp.arange(block_total, dtype=jnp.int32), axis=1),
        block_total,
    ).astype(jnp.int32)[None]
    owned_grads, summed, grad_input = tail(
        inverse,
        early,
        grad_mixed,
        grad_gate_pre,
        normed,
        grad_logits,
        lowrank,
        gate_up,
        gate_down.T,
        norm_gains[0:1],
        gains_two,
        tap_grads,
        gain_grads,
        in_weights,
        tokens,
        grad_one,
        slots_dev,
    )
    params = (
        (norm_gains, gains_first, gains_second),
        (gate_down.T, down_first.T, down_second.T),
        (gate_up, upper_first, upper_second),
        (head_gain[None], head_first[None], head_second[None]),
        (conv_weight, conv_first, conv_second),
    )
    (
        owned_grads,
        master_next,
        first_next,
        second_next,
        copy_next,
        *small_next,
        grad_input,
        result,
    ) = all_adam(
        owned_grads,
        basis_left,
        basis_right,
        slot_master,
        slot_first,
        slot_second,
        summed,
        params,
        grad_input,
        result,
    )
    for q in range(4, 8):
        small_next[q] = small_next[q].T
    for q in range(12, 16):
        small_next[q] = small_next[q][0]
    return (
        result,
        grad_input,
        owned_grads,
        master_next,
        first_next,
        second_next,
        copy_next,
        *small_next,
    )


def solution(mesh):
    placed = (
        P("seq", None),
        P("seq", None),
        P(),
        P(),
        P("head", None),
        P(("seq", "head"), None, None),
        P(("seq", "head"), None, None),
        P(("seq", "head"), None, None),
        P(("seq", "head"), None, None),
        P(("seq", "head"), None, None),
        P(("seq", "head"), None, None),
        P(),
        P(),
        P(),
        P(),
        P(),
        P(),
        P(None, "head"),
        P(None, "head"),
        P(None, "head"),
        P(),
        P(),
        P(),
        P(None, "head"),
        P(None, "head"),
        P(None, "head"),
    )
    return jax.shard_map(
        body,
        mesh=mesh,
        in_specs=placed,
        out_specs=(
            P("seq", None),
            P("seq", None),
            P(("seq", "head"), None, None),
            P(("seq", "head"), None, None),
            P(("seq", "head"), None, None),
            P(("seq", "head"), None, None),
            P(("seq", "head"), None, None),
            P(),
            P(),
            P(),
            P(),
            P(),
            P(),
            P(),
            P(),
            P(None, "head"),
            P(None, "head"),
            P(None, "head"),
            P(None, "head"),
            P(),
            P(),
            P(),
            P(),
            P(None, "head"),
            P(None, "head"),
            P(None, "head"),
            P(None, "head"),
        ),
        check_vma=False,
    )
```

```python
import functools

import jax
import jax.numpy as jnp
from jax import lax
from jax.experimental import pallas as pl
from jax.experimental.pallas import tpu as pltpu
from jax.sharding import PartitionSpec as P

MESH = pl.DeviceIdType.MESH

DK = 128
DV = 256


highest_precision = lax.Precision.HIGHEST
norm_epsilon = 1e-06
adam_epsilon = 1e-08
gate_scale = 16.0
moment_decay = 0.5
rate_block = 0.03
rate_gains = 0.45
rate_down = 0.02
rate_upper = 0.6
rate_head = 0.5
rate_conv = 0.1


def axis_sizes(n):
    side = 1
    while (side * 2) ** 2 * 4 <= n:
        side *= 2
    return (n // (side * side), side, side)


def coords(me, sizes):
    _, rows, columns = sizes
    return [me // (rows * columns), (me // columns) % rows, me % columns]


def index_of(c, sizes):
    _, rows, columns = sizes
    return (c[0] * rows + c[1]) * columns + c[2]


def neighbour(c, sizes, ax, j):
    d = list(c)
    d[ax] = lax.rem(c[ax] + j, sizes[ax])
    return index_of(d, sizes)


def enter(n, me, mate=False):
    barrier = pltpu.get_barrier_semaphore()
    if mate:
        core = lax.axis_index("head")
        pl.semaphore_signal(barrier, inc=1, device_id={"head": 1 - core}, device_id_type=MESH)
    for j in range(1, n):
        pl.semaphore_signal(
            barrier, inc=1, device_id={"seq": lax.rem(me + j, n)}, device_id_type=MESH
        )
    pl.semaphore_wait(barrier, n - 1 + int(mate))


def remote(src, dst, send_sem, recv_sem, peer):
    return pltpu.make_async_remote_copy(
        src_ref=src,
        dst_ref=dst,
        send_sem=send_sem,
        recv_sem=recv_sem,
        device_id={"seq": peer},
        device_id_type=MESH,
    )


def build_plan(widths, parts, pieces, orders, base=0):
    total = sum(widths)
    bounds = [sum(widths[:i]) for i in range(len(widths) + 1)]
    cuts = [round(total * f) for f in (0.0,) + parts]
    plan, at = [], 0
    for i in range(pieces):
        for order, lo, hi in zip(orders, cuts[:-1], cuts[1:], strict=True):
            size = hi - lo
            left = size * (i + 1) // pieces - size * i // pieces
            while left:
                which = max(q for q in range(len(widths)) if bounds[q] <= at)
                step = min(left, bounds[which + 1] - at)
                start = at - bounds[which]
                plan.append((which, start, start + step, at + base, order, i))
                at += step
                left -= step
    return plan


def groups_of(plan):
    streams = {}
    for i, chunk in enumerate(plan):
        streams.setdefault(chunk[4], {}).setdefault(chunk[5], []).append(i)
    return streams


def spread_steps(steps, places):
    chosen = [(place, steps.pop(0)) for place in places[: len(steps)]]

    def run(t):
        for place, step in chosen:
            pl.when(t == place)(step)

    return run


FORWARD_PLACES = (1, (4,), (4,), ())
FORWARD_PIECES = 4
BACKWARD_PLACES = ((4,), (0, 6), (2, 6))
BACKWARD_PIECES = 4
MIDDLE_PIECES = 3
MIDDLE_TAKEN = 6


def gather_steps(sizes, plan, piece, outs, bw, send, recv):
    c = coords(lax.axis_index("seq"), sizes)
    most = max(sizes)

    def copies(i, k):
        which, lo, hi, at, order, _ = plan[i]
        ax = order[k]
        wide = pl.ds(lo * bw, (hi - lo) * bw)
        index = tuple(slice(None) if a in order[:k] else c[a] for a in range(3))
        index += (slice(None), wide)
        target = outs[which].at[index]
        source = target if k else piece.at[:, pl.ds(at * bw, (hi - lo) * bw)]
        return [
            remote(
                source,
                target,
                send.at[(i * 3 + k) * most + j],
                recv.at[(i * 3 + k) * most + j],
                neighbour(c, sizes, ax, j),
            )
            for j in range(1, sizes[ax])
        ]

    streams = groups_of(plan)
    longest = max(max(s) for s in streams.values()) + 1

    def step(s):
        for k in (2, 1, 0):
            for groups in streams.values():
                for i in groups.get(s - k, ()):
                    if k:
                        for copy in copies(i, k - 1):
                            copy.wait_recv()
                    for copy in copies(i, k):
                        copy.start()

    def arrived(piece_range):
        for groups in streams.values():
            for s in piece_range:
                for i in groups.get(s, ()):
                    for copy in copies(i, 2):
                        copy.wait_recv()

    def sent():
        for i in range(len(plan)):
            for k in range(3):
                for copy in copies(i, k):
                    copy.wait_send()

    return [functools.partial(step, s) for s in range(longest + 2)], arrived, sent


def scatter_scratch(sizes, plan, rows, bw, dtype, in_place=False):
    own, first, second, third = [], [], [], []
    for _, lo, hi, _, order, _ in plan:
        wide = (hi - lo) * bw
        rest = tuple(sizes[q] for q in range(3) if q != order[0])
        own.append(pltpu.VMEM(rest + (rows, wide), dtype))
        first.append(pltpu.VMEM((sizes[order[0]] - 1,) + rest + (rows, wide), dtype))
        second.append(pltpu.VMEM((sizes[order[1]], sizes[order[2]], rows, wide), dtype))
        third.append(pltpu.VMEM((sizes[order[2]], rows, wide), dtype))
    count = len(plan) * 3 * max(sizes)
    return (
        ([] if in_place else own)
        + first
        + second
        + third
        + [
            pltpu.SemaphoreType.DMA((count,)),
            pltpu.SemaphoreType.DMA((count,)),
            pltpu.SemaphoreType.DMA((len(plan),)),
        ]
    )


def scatter_steps(sizes, plan, grads, scratch, fin, bw, in_place=False):
    c = coords(lax.axis_index("seq"), sizes)
    most, count = max(sizes), len(plan)
    first, second, third = (scratch[-3 - (3 - i) * count :][:count] for i in range(3))
    send, recv, load = scratch[-3:]

    def part(i):
        which, lo, hi, _, order, _ = plan[i]
        index = tuple(c[q] if q == order[0] else slice(None) for q in range(3))
        index += (slice(None), pl.ds(lo * bw, (hi - lo) * bw))
        return grads[which].at[index]

    own = [part(i) for i in range(count)] if in_place else scratch[:count]

    def loading(i):
        return pltpu.make_async_copy(part(i), own[i], load.at[i])

    def copies(i, k):
        which, lo, hi, _, order, _ = plan[i]
        ax = order[k]
        left = sorted(set(range(3)) - set(order[:k]))
        result = []
        for j in range(1, sizes[ax]):
            there = lax.rem(c[ax] + j, sizes[ax])
            index = tuple(there if q == ax else slice(None) for q in left)
            if k == 0:
                index += (slice(None), pl.ds(lo * bw, (hi - lo) * bw))
                source, target = grads[which].at[index], first[i].at[j - 1]
            elif k == 1:
                source, target = own[i].at[index], second[i].at[j]
            else:
                source, target = second[i].at[(0,) + index], third[i].at[j]
            s = (i * 3 + k) * most + j
            result.append(
                remote(source, target, send.at[s], recv.at[s], neighbour(c, sizes, ax, j))
            )
        return result

    def combine(i, k):
        _, lo, hi, at, order, _ = plan[i]
        if k == 0 and not in_place:
            loading(i).wait()
        for copy in copies(i, k):
            copy.wait_recv()
        size = sizes[order[k]]
        if k == 0:
            outer, inner = own[i].shape[:2]

            def add(t, _):
                u, v = t // inner, t % inner
                total = own[i][u, v].astype(jnp.float32)
                for j in range(size - 1):
                    total = total + first[i][j, u, v].astype(jnp.float32)
                own[i][u, v] = total.astype(own[i].dtype)
                return 0

            lax.fori_loop(0, outer * inner, add, 0)
        elif k == 1:
            leading = sorted(set(range(3)) - {order[0]}).index(order[1]) == 0

            def add(t, _):
                total = own[i][(c[order[1]], t) if leading else (t, c[order[1]])]
                total = total.astype(jnp.float32)
                for j in range(1, size):
                    total = total + second[i][j, t].astype(jnp.float32)
                second[i][0, t] = total.astype(own[i].dtype)
                return 0

            lax.fori_loop(0, sizes[order[2]], add, 0)
        else:
            total = second[i][0, c[order[2]]].astype(jnp.float32)
            for j in range(1, size):
                total = total + third[i][j].astype(jnp.float32)
            for b in range(hi - lo):
                fin[at + b] = total[:, b * bw : (b + 1) * bw].astype(fin.dtype)

    streams = groups_of(plan)
    longest = max(max(s) for s in streams.values()) + 1

    def step(s):
        for k in range(4):
            for groups in streams.values():
                for i in groups.get(s - k, ()):
                    if k:
                        combine(i, k - 1)
                    elif not in_place:
                        loading(i).start()
                    if k < 3:
                        for copy in copies(i, k):
                            copy.start()

    def sent():
        for i in range(count):
            for k in range(3):
                for copy in copies(i, k):
                    copy.wait_send()

    return [functools.partial(step, s) for s in range(longest + 3)], sent


SPREAD = ((2, 1, 0), (1, 2, 0), (0, 1, 2))
COLLECT = ((0, 1, 2), (0, 2, 1), (2, 1, 0))
SHARES = (0.43, 0.86, 1.0)


def sum_steps(sizes, shared, x_ref, out_ref, mate, acc, bufs, send, recv):
    me, core = lax.axis_index("seq"), lax.axis_index("head")
    c = coords(me, sizes)
    most = max(sizes)
    swap = pltpu.make_async_remote_copy(
        src_ref=x_ref.at[pl.ds(0, shared)],
        dst_ref=mate,
        send_sem=send.at[0],
        recv_sem=recv.at[0],
        device_id={"head": 1 - core},
        device_id_type=MESH,
    )

    def going(step, ax):
        copies = []
        for j in range(1, sizes[ax]):
            d = list(c)
            d[ax] = lax.rem(c[ax] + j, sizes[ax])
            q = 1 + ax * most + j
            copies.append(
                remote(
                    acc.at[step], bufs.at[ax, c[ax]], send.at[q], recv.at[q], index_of(d, sizes)
                )
            )
        return copies

    def total(ax):
        value = bufs[ax, 0]
        for j in range(1, sizes[ax]):
            value = value + bufs[ax, j]
        return value

    def start(step, ax):
        bufs[ax, c[ax]] = acc[step]
        for copy in going(step, ax):
            copy.start()

    def swapped():
        swap.wait()
        acc[0, 0:shared] = x_ref[0:shared] + mate[...]
        acc[0, shared:] = x_ref[shared:]
        start(0, 2)

    def moved(step, ax):
        for copy in going(step, ax):
            copy.wait()
        if step < 2:
            acc[step + 1] = total(ax)
            start(step + 1, ax - 1)
        else:
            out_ref[...] = total(ax)

    return [
        swap.start,
        swapped,
        functools.partial(moved, 0, 2),
        functools.partial(moved, 1, 1),
        functools.partial(moved, 2, 0),
    ]


NN = (((1,), (0,)), ((), ()))
NT = (((1,), (1,)), ((), ()))
TN = (((0,), (0,)), ((), ()))
TILE = 128


def halves(values):
    high = values.astype(jnp.bfloat16)
    return high, (values - high.astype(jnp.float32)).astype(jnp.bfloat16)


def product(left, right, dims):
    (lh, ll), (rh, rl) = left, right
    dot = functools.partial(
        lax.dot_general, dimension_numbers=dims, preferred_element_type=jnp.float32
    )
    return dot(lh, rh) + (dot(lh, rl) + dot(ll, rh))


def running_sum(table, values):
    first = values.astype(jnp.bfloat16)
    rest = values - first.astype(jnp.float32)
    second, third = halves(rest)
    dot = functools.partial(
        lax.dot_general, dimension_numbers=NN, preferred_element_type=jnp.float32
    )
    return dot(table, first) + (dot(table, second) + dot(table, third))


def sigmoid(values):
    return 1.0 / (1.0 + jnp.exp(-values))


def chain_tools(n, sizes, forward, mine, bufs, send, recv, result):
    me = lax.axis_index("seq")
    c = coords(me, sizes)
    pieces = mine.shape[0]
    across, along, before, held = bufs
    most = max(sizes)
    state = pl.ds(0, TILE)
    decay = pl.ds(TILE, 1)

    def peers(ax):
        return [j for j in range(1, sizes[ax])]

    def to(ax, j):
        d = list(c)
        d[ax] = lax.rem(c[ax] + j, sizes[ax])
        return index_of(d, sizes)

    def line(buf, source, ax, j, p, base):
        s = base + j * pieces + p
        return remote(source.at[p], buf.at[c[ax], p], send.at[s], recv.at[s], to(ax, j))

    def hop(p):
        s = 2 * most * pieces + p
        step = 1 if forward else -1
        d = [lax.rem(c[0] + step + sizes[0], sizes[0]), c[1], c[2]]
        return remote(held.at[1, p], held.at[0, p], send.at[s], recv.at[s], index_of(d, sizes))

    def compose(first, second):
        return (second[1] * first[0] + second[0], first[1] * second[1])

    def reduce_line(buf, ax, p):
        size = sizes[ax]
        order = range(size) if forward else range(size - 1, -1, -1)
        prefix = (jnp.zeros((TILE, TILE), jnp.float32), jnp.ones((1, TILE), jnp.float32))
        total = None
        for i in order:
            item = (buf[i, p, state], buf[i, p, decay])
            longer = compose(prefix, item)
            take = (i < c[ax]) if forward else (i > c[ax])
            prefix = tuple(jnp.where(take, a, b) for a, b in zip(longer, prefix, strict=True))
            total = item if total is None else compose(total, item)
        return prefix, total

    def start_x():
        for p in range(pieces):
            across[c[2], p] = mine[p]
            for j in peers(2):
                line(across, mine, 2, j, p, 0).start()

    def start_y():
        for p in range(pieces):
            for j in peers(2):
                line(across, mine, 2, j, p, 0).wait_recv()
            prefix, total = reduce_line(across, 2, p)
            before[p, state], before[p, decay] = prefix
            held[2, p, state], held[2, p, decay] = total
            held[2, p, pl.ds(TILE + 1, 7)] = jnp.zeros((7, TILE), jnp.float32)
            along[c[1], p] = held[2, p]
            for j in peers(1):
                line(along, held.at[2], 1, j, p, most * pieces).start()

    first_z = 0 if forward else sizes[0] - 1
    last_z = sizes[0] - 1 - first_z

    def start_z():
        for p in range(pieces):
            for j in peers(1):
                line(along, held.at[2], 1, j, p, most * pieces).wait_recv()
            prefix, total = reduce_line(along, 1, p)
            own = (before[p, state], before[p, decay])
            before[p, state], before[p, decay] = compose(prefix, own)
            held[1, p, state], held[1, p, decay] = total
            held[1, p, pl.ds(TILE + 1, 7)] = jnp.zeros((7, TILE), jnp.float32)

            @pl.when(c[0] == first_z)
            def _():
                held[0, p] = jnp.zeros((TILE + 8, TILE), jnp.float32)
                hop(p).start()

    def pass_z(k):
        at = k if forward else sizes[0] - 1 - k

        @pl.when(c[0] == at)
        def _():
            for p in range(pieces):
                hop(p).wait_recv()
                if at != last_z:
                    got = (held[0, p, state], held[0, p, decay])
                    item = (held[1, p, state], held[1, p, decay])
                    held[1, p, state], held[1, p, decay] = compose(got, item)
                    hop(p).start()

    def finish():
        for p in range(pieces):
            result[p] = before[p, decay] * held[0, p, state] + before[p, state]
            for j in peers(2):
                line(across, mine, 2, j, p, 0).wait_send()
            for j in peers(1):
                line(along, held.at[2], 1, j, p, most * pieces).wait_send()

        @pl.when(c[0] != last_z)
        def _():
            for p in range(pieces):
                hop(p).wait_send()

    stages = [start_x, start_y, start_z]
    stages += [functools.partial(pass_z, k) for k in range(1, sizes[0])]
    return stages, finish


def greet(n, sizes, extra):
    c = coords(lax.axis_index("seq"), sizes)
    barrier = pltpu.get_barrier_semaphore()
    count = 0
    for ax in range(3):
        for j in range(1, sizes[ax]):
            d = list(c)
            d[ax] = lax.rem(c[ax] + j, sizes[ax])
            pl.semaphore_signal(
                barrier, inc=1, device_id={"seq": index_of(d, sizes)}, device_id_type=MESH
            )
            count += 1
    for index in extra:
        pl.semaphore_signal(barrier, inc=1, device_id={"seq": index}, device_id_type=MESH)
        count += 1
    pl.semaphore_wait(barrier, count)


def tile_masks(rows_ref, cols_ref, c):
    row = rows_ref[pl.ds(c, 1), :]
    col = cols_ref[pl.ds(pl.multiple_of(c * TILE, TILE), TILE), 6:7]
    i = lax.broadcasted_iota(jnp.int32, (TILE, TILE), 0)
    j = lax.broadcasted_iota(jnp.int32, (TILE, TILE), 1)
    return (i >= j) & (row == col)


def forward_kernel(
    n,
    sizes,
    plan,
    ready,
    owners_ref,
    lengths_ref,
    packing_ref,
    slot_ref,
    tokens_ref,
    norm_ref,
    down_ref,
    upper_ref,
    taps_ref,
    gain_ref,
    w_in_out,
    w_up_out,
    w_out_out,
    w_down_out,
    normed_out,
    lowrank_ref,
    logits_out,
    proj_out,
    halo_ref,
    gate_out,
    conv_out,
    cum_out,
    o_out,
    u_out,
    start_out,
    cols_ref,
    rows_ref,
    normed,
    logits_ref,
    proj_ref,
    gate_ref,
    conv_ref,
    cum_ref,
    o_ref,
    u_ref,
    start_ref,
    slots,
    piece,
    w_in,
    rim,
    segs,
    act,
    state,
    prev,
    a_send,
    a_recv,
    g_send,
    g_recv,
    l_sem,
    mine,
    across,
    along,
    before,
    held,
    result,
    send,
    recv,
):
    me = lax.axis_index("seq")
    c3 = coords(me, sizes)
    length, width = tokens_ref.shape
    tiles, channels = length // TILE, proj_ref.shape[1]
    keys = logits_ref.shape[1]
    rank = down_ref.shape[0]
    heads = keys // DK
    value = DV * heads
    slots_dev, _, bw = slot_ref.shape
    rows = piece.shape[0]
    scale = DK ** (-0.5)
    enter(n, me)

    def move(j):
        p = lax.rem(me + j, n)
        return remote(
            slot_ref.at[:, pl.ds(p * rows, rows), :],
            slots.at[pl.ds(me * slots_dev, slots_dev)],
            a_send.at[j],
            a_recv.at[j],
            p,
        )

    for j in range(1, n):
        move(j).start()
    local_move = pltpu.make_async_copy(
        slot_ref.at[:, pl.ds(me * rows, rows), :],
        slots.at[pl.ds(me * slots_dev, slots_dev)],
        l_sem.at[0],
    )
    local_move.start()
    edge = remote(
        tokens_ref.at[pl.ds(length - 16, 16)],
        rim,
        a_send.at[0],
        a_recv.at[0],
        lax.rem(me + 1, n),
    )

    @pl.when(me < n - 1)
    def _():
        edge.start()

    base = me * length
    where_col = base - 8 + lax.broadcasted_iota(jnp.int32, (length + 8, 1), 0)
    lane = lax.broadcasted_iota(jnp.int32, (tiles, TILE), 1)
    where_row = base + TILE * lax.broadcasted_iota(jnp.int32, (tiles, TILE), 0) + lane
    start = jnp.int32(0)
    seg_col = jnp.zeros((length + 8, 1), jnp.float32)
    seg_row = jnp.zeros((tiles, TILE), jnp.float32)
    for q in range(lengths_ref.shape[0]):
        seg_col += (where_col >= start).astype(jnp.float32)
        seg_row += (where_row >= start).astype(jnp.float32)
        start = start + lengths_ref[packing_ref[q]]
    filled = start
    segs[...] = seg_col + (where_col >= filled).astype(jnp.float32)
    rows_ref[...] = seg_row + (where_row >= filled).astype(jnp.float32)
    lane = lax.broadcasted_iota(jnp.int32, (TILE, TILE), 1)
    for c in range(tiles):
        lo = 8 + c * TILE
        own = segs[lo : lo + TILE]
        flags = [segs[lo - 1 : lo], segs[lo + TILE - 1 : lo + TILE]]
        flags += [segs[lo - s : lo - s + TILE] for s in (1, 2, 3)]
        flags = [(other == own).astype(jnp.float32) for other in flags]
        place = base + c * TILE + lax.broadcasted_iota(jnp.int32, (TILE, 1), 0)
        flags += [None, own, (place < filled).astype(jnp.float32)]
        total = jnp.zeros((TILE, TILE), jnp.float32)
        for k, flag in enumerate(flags):
            if flag is not None:
                total = jnp.where(lane == k, flag, total)
        cols_ref[c * TILE : (c + 1) * TILE, :] = total
    cols_ref[length : length + 8, :] = jnp.zeros((8, TILE), jnp.float32)

    def norm(values):
        values = values.astype(jnp.float32)
        inverse = lax.rsqrt(jnp.mean(values * values, axis=1, keepdims=True) + norm_epsilon)
        return (values * inverse * norm_ref[...]).astype(jnp.bfloat16)

    i = lax.broadcasted_iota(jnp.int32, (TILE, TILE), 0)
    j = lax.broadcasted_iota(jnp.int32, (TILE, TILE), 1)
    lower = (i >= j).astype(jnp.bfloat16)
    down_low = down_ref[...].astype(jnp.bfloat16)
    upper = halves(upper_ref[0:rank, :])

    def gates(c, _):
        at = pl.ds(pl.multiple_of(c * TILE, TILE), TILE)
        x = norm(tokens_ref[at, :])
        normed[at, :] = x
        low = lax.dot_general(x, down_low, NT, preferred_element_type=jnp.float32)
        lowrank_ref[at, :] = low
        logits = product(halves(low), upper, NN) + upper_ref[rank : rank + 1, :]
        logits_ref[at, :] = logits
        gate = jnp.minimum(logits, 0.0) - jnp.log1p(jnp.exp(-jnp.abs(logits)))
        cum_ref[at, :] = running_sum(lower, gate * (1.0 / gate_scale))
        return 0

    lax.fori_loop(0, tiles, gates, 0)
    flushes = []

    def flush(source, target):
        copy = pltpu.make_async_copy(source, target, l_sem.at[6 + len(flushes)])
        copy.start()
        flushes.append(copy)

    flush(normed, normed_out)
    flush(logits_ref, logits_out)
    flush(cum_ref, cum_out)

    @pl.when(me > 0)
    def _():
        edge.wait_recv()

    @pl.when(me == 0)
    def _():
        rim[...] = jnp.zeros_like(rim)

    rim[...] = norm(rim[...])

    local_move.wait()
    for j in range(1, n):
        move(j).wait()
    for b in range(owners_ref.shape[1]):
        piece[:, b * bw : (b + 1) * bw] = slots[owners_ref[0, b]]
    outs = (w_in, w_up_out, w_out_out, w_down_out)
    offset, owns = 0, []
    for q, out in enumerate(outs):
        columns = out.shape[4]
        owns.append(
            pltpu.make_async_copy(
                piece.at[:, pl.ds(offset, columns)],
                out.at[c3[0], c3[1], c3[2]],
                l_sem.at[1 + q],
            )
        )
        offset += columns
    for copy in owns:
        copy.start()
    steps, arrived, sent = gather_steps(sizes, plan, piece, outs, bw, g_send, g_recv)
    steps[0]()
    for copy in owns:
        copy.wait()
    for step in steps[1 : ready + 2]:
        step()
    arrived(range(ready))
    rest = list(steps[ready + 2 :])
    flush(w_in, w_in_out)

    for step in rest[: FORWARD_PLACES[0]]:
        step()
    del rest[: FORWARD_PLACES[0]]

    def project(r, _):
        at = pl.ds(pl.multiple_of(r * 256, 256), 256)
        x = normed[at, :]
        for lo in range(0, w_in.shape[4], 512):
            part = lax.dot_general(
                x,
                w_in[:, :, :, :, lo : lo + 512].reshape(width, 512),
                NN,
                preferred_element_type=jnp.float32,
            )
            if lo < channels:
                proj_ref[at, lo : lo + 512] = part.astype(proj_ref.dtype)
            else:
                gate_ref[at, lo - channels : lo - channels + 512] = part
        return 0

    lax.fori_loop(0, length // 256, project, 0)
    for lo in range(0, channels, 512):
        halo_ref[:, lo : lo + 512] = lax.dot_general(
            rim[...],
            w_in[:, :, :, :, lo : lo + 512].reshape(width, 512),
            NN,
            preferred_element_type=jnp.float32,
        ).astype(halo_ref.dtype)
    flush(proj_ref, proj_out)
    flush(gate_ref, gate_out)

    prev[...] = halo_ref[...]
    state[...] = jnp.zeros_like(state)
    mine[...] = jnp.zeros_like(mine)
    for p in range(mine.shape[0]):
        mine[p, TILE : TILE + 1] = jnp.ones((1, TILE), jnp.float32)
    run = spread_steps(rest, FORWARD_PLACES[1])

    def local(c, _):
        run(c)
        at = pl.ds(pl.multiple_of(c * TILE, TILE), TILE)
        for g in range(0, channels, 256):
            wide = slice(g, g + 256)
            block = jnp.concatenate(
                [prev[:, wide].astype(jnp.float32), proj_ref[at, wide].astype(jnp.float32)]
            )
            total = taps_ref[3:4, wide] * block[16:]
            for s in (1, 2, 3):
                total = total + taps_ref[3 - s : 4 - s, wide] * (
                    block[16 - s : 16 - s + TILE] * cols_ref[at, 1 + s : 2 + s]
                )
            conv_ref[at, wide] = total
            act[at, wide] = total * sigmoid(total)
        prev[...] = proj_ref[pl.ds(pl.multiple_of(c * TILE + TILE - 16, 16), 16), :]
        cum = cum_ref[at, :]
        last = cum[TILE - 1 : TILE]
        left = act[at, keys : 2 * keys] * jnp.exp(last - cum) * cols_ref[at, 1:2]
        decay = jnp.exp(last) * cols_ref[at, 0:1][TILE - 1 : TILE]
        for h in range(heads):
            kh = slice(h * DK, (h + 1) * DK)
            v = halves(act[at, 2 * keys + h * DV : 2 * keys + (h + 1) * DV])
            start_ref[c, h] = state[h]
            state[h] = state[h] * decay[:, kh] + product(v, halves(left[:, kh]), TN)
            for e in range(DV // TILE):
                p = h * (DV // TILE) + e
                mine[p, TILE : TILE + 1] = mine[p, TILE : TILE + 1] * decay[:, kh]
        return 0

    lax.fori_loop(0, tiles, local, 0)
    flush(conv_ref, conv_out)
    for h in range(heads):
        start_ref[tiles, h] = state[h]
        for e in range(DV // TILE):
            mine[h * (DV // TILE) + e, 0:TILE] = state[h, e * TILE : (e + 1) * TILE]
    stages, finish = chain_tools(
        n, sizes, True, mine, (across, along, before, held), send, recv, result
    )
    stages[0]()
    run_inside = spread_steps(rest, FORWARD_PLACES[2])

    def inside(c, _):
        for k, stage in enumerate(stages[1:]):
            pl.when(c == k + 1)(stage)
        run_inside(c)
        at = pl.ds(pl.multiple_of(c * TILE, TILE), TILE)
        cum = cum_ref[at, :]
        middle = cum[TILE // 2 - 1 : TILE // 2]
        q = act[at, 0:keys] * jnp.exp(cum - middle) * scale
        k = act[at, keys : 2 * keys] * jnp.exp(middle - cum)
        mask = tile_masks(rows_ref, cols_ref, c)
        for h in range(heads):
            kh = slice(h * DK, (h + 1) * DK)
            vh = slice(h * DV, (h + 1) * DV)
            scores = jnp.where(mask, product(halves(q[:, kh]), halves(k[:, kh]), NT), 0.0)
            v = halves(act[at, 2 * keys + h * DV : 2 * keys + (h + 1) * DV])
            o_ref[at, vh] = product(halves(scores), v, NN)
        return 0

    lax.fori_loop(0, tiles, inside, 0)
    finish()
    for h in range(heads):
        for e in range(DV // TILE):
            state[h, e * TILE : (e + 1) * TILE] = result[h * (DV // TILE) + e]

    run_outside = spread_steps(rest, FORWARD_PLACES[3])

    def outside(c, _):
        run_outside(c)
        at = pl.ds(pl.multiple_of(c * TILE, TILE), TILE)
        cum = cum_ref[at, :]
        q = act[at, 0:keys] * jnp.exp(cum) * scale * cols_ref[at, 0:1]
        decay = jnp.exp(cum[TILE - 1 : TILE]) * cols_ref[at, 0:1][TILE - 1 : TILE]
        for h in range(heads):
            kh = slice(h * DK, (h + 1) * DK)
            vh = slice(h * DV, (h + 1) * DV)
            begin = start_ref[c, h] + state[h]
            start_ref[c, h] = begin
            state[h] = state[h] * decay[:, kh]
            o = o_ref[at, vh] + product(halves(q[:, kh]), halves(begin), NT)
            o_ref[at, vh] = o
            inverse = lax.rsqrt(jnp.mean(o * o, axis=1, keepdims=True) + norm_epsilon)
            gate = gate_ref[at, vh]
            u_ref[at, vh] = (o * inverse * gain_ref[...] * (gate * sigmoid(gate))).astype(
                u_ref.dtype
            )
        return 0

    lax.fori_loop(0, tiles, outside, 0)
    for h in range(heads):
        start_ref[tiles, h] = start_ref[tiles, h] + state[h]
    flush(o_ref, o_out)
    flush(u_ref, u_out)
    flush(start_ref, start_out)
    for step in rest:
        step()
    groups = {chunk[5] for chunk in plan}
    arrived(sorted(g for g in groups if g >= ready))
    sent()
    for copy in flushes:
        copy.wait()

    @pl.when(me < n - 1)
    def _():
        edge.wait_send()


def forward(
    owners, lengths, packing, slot_copy, tokens, norm, down, upper, taps, gain, counts
):
    n = lax.axis_size("seq")
    sizes = axis_sizes(n)
    length, width = tokens.shape
    slots_dev, depth, bw = slot_copy.shape
    rows = depth // n
    keys, channels = upper.shape[1], taps.shape[1]
    heads = keys // DK
    value = heads * DV
    tiles = length // TILE
    blocks = sum(counts)
    ready = 2
    plan = build_plan(counts[:1], SHARES, ready, COLLECT)
    plan += [
        (which + 1, lo, hi, at, order, group + ready)
        for which, lo, hi, at, order, group in build_plan(
            counts[1:], SHARES, FORWARD_PIECES, COLLECT, counts[0]
        )
    ]
    f32, b16 = jnp.float32, jnp.bfloat16
    shape = jax.ShapeDtypeStruct
    vmem, anywhere = pl.BlockSpec(memory_space=pltpu.VMEM), pl.BlockSpec(memory_space=pl.ANY)
    smem = pl.BlockSpec(memory_space=pltpu.SMEM)
    kept = [
        ((length, width), b16),
        ((length, keys), f32),
        ((length, channels), b16),
        ((length, value), f32),
        ((length, channels), f32),
        ((length, keys), f32),
        ((length, value), f32),
        ((length, value), b16),
        ((tiles + 1, heads, DV, DK), f32),
    ]
    big = [shape(*k) for k in kept]
    outs = [shape(sizes + (rows, count * bw), b16) for count in counts]
    outs += [big[0], shape((length, down.shape[0]), f32), big[1], big[2]]
    outs += [shape((16, channels), b16)] + big[3:]
    outs += [shape((length + 8, TILE), f32), shape((tiles, TILE), f32)]
    specs = [anywhere] * 5 + [vmem, anywhere, anywhere, vmem] + [anywhere] * 6 + [vmem, vmem]
    most = max(sizes)
    copies = len(plan) * 3 * most
    result = pl.pallas_call(
        functools.partial(forward_kernel, n, sizes, plan, ready),
        out_shape=tuple(outs),
        in_specs=[smem] * 3 + [anywhere] + [vmem] * 6,
        out_specs=tuple(specs),
        scratch_shapes=[pltpu.VMEM(*k) for k in kept]
        + [
            pltpu.VMEM((n * slots_dev, rows, bw), b16),
            pltpu.VMEM((rows, blocks * bw), b16),
            pltpu.VMEM(sizes + (rows, counts[0] * bw), b16),
            pltpu.VMEM((16, width), b16),
            pltpu.VMEM((length + 8, 1), f32),
            pltpu.VMEM((length, channels), f32),
            pltpu.VMEM((heads, DV, DK), f32),
            pltpu.VMEM((16, channels), b16),
            pltpu.SemaphoreType.DMA((n,)),
            pltpu.SemaphoreType.DMA((n,)),
            pltpu.SemaphoreType.DMA((copies,)),
            pltpu.SemaphoreType.DMA((copies,)),
            pltpu.SemaphoreType.DMA((18,)),
        ]
        + chain_scratch(sizes, heads * DV // TILE),
        compiler_params=pltpu.CompilerParams(
            collective_id=1, has_side_effects=True, vmem_limit_bytes=60 << 20
        ),
    )(owners, lengths, packing, slot_copy, tokens, norm, down, upper, taps, gain)
    return [w.reshape(depth, w.shape[4]) for w in result[:4]], result[4:]


def chain_scratch(sizes, pieces):
    most = max(sizes)
    shape = (pieces, TILE + 8, TILE)
    return [
        pltpu.VMEM(shape, jnp.float32),
        pltpu.VMEM((sizes[2],) + shape, jnp.float32),
        pltpu.VMEM((sizes[1],) + shape, jnp.float32),
        pltpu.VMEM(shape, jnp.float32),
        pltpu.VMEM((3,) + shape, jnp.float32),
        pltpu.VMEM((pieces, TILE, TILE), jnp.float32),
        pltpu.SemaphoreType.DMA(((2 * most + 1) * pieces,)),
        pltpu.SemaphoreType.DMA(((2 * most + 1) * pieces,)),
    ]


def backward_kernel(
    n,
    sizes,
    plan,
    proj_in,
    halo_ref,
    conv_in,
    cum_in,
    logits_in,
    o_in,
    gate_in,
    du_in,
    start_in,
    cols_ref,
    rows_ref,
    taps_ref,
    gain_ref,
    g_up_ref,
    g_out_ref,
    dproj_out,
    dgate_out,
    dlogits_out,
    dtaps_ref,
    dgain_ref,
    early_ref,
    proj_ref,
    conv_ref,
    cum_ref,
    logits_ref,
    o_ref,
    gate_ref,
    du_ref,
    start_ref,
    dproj_ref,
    dgate_ref,
    dlogits_ref,
    t_sem,
    l_sem,
    do,
    dact,
    adjoint,
    ends,
    after,
    back,
    tail,
    mine,
    across,
    along,
    before,
    held,
    result,
    send,
    recv,
    b_sem,
    *scatter_refs,
):
    tiles, channels = proj_ref.shape[0] // TILE, proj_ref.shape[1]
    keys = cum_ref.shape[1]
    heads = keys // DK
    me = lax.axis_index("seq")
    by_tile = (
        (du_in, du_ref),
        (o_in, o_ref),
        (gate_in, gate_ref),
        (cum_in, cum_ref),
        (conv_in.at[:, pl.ds(0, keys)], conv_ref.at[:, pl.ds(0, keys)]),
    )
    rest = pl.ds(keys, channels - keys)
    whole = (
        (conv_in.at[:, rest], conv_ref.at[:, rest]),
        (start_in, start_ref),
        (proj_in, proj_ref),
        (logits_in, logits_ref),
        (dgate_ref, dgate_out),
        (dlogits_ref, dlogits_out),
        (dproj_ref, dproj_out),
    )

    def tile_load(q, c):
        at = pl.ds(pl.multiple_of(c * TILE, TILE), TILE)
        source, target = by_tile[q]
        return pltpu.make_async_copy(source.at[at], target.at[at], t_sem.at[q, c])

    def load(q):
        source, target = whole[q]
        return pltpu.make_async_copy(source, target, l_sem.at[q])

    for c in range(tiles - 1, -1, -1):
        for q in range(len(by_tile)):
            tile_load(q, c).start()
    for q in range(4):
        load(q).start()
    greet(n, sizes, (lax.rem(me + 1, n), lax.rem(me + n - 1, n)))
    steps, sent = scatter_steps(
        sizes, plan, [g_up_ref, g_out_ref], scatter_refs, early_ref, TILE
    )
    steps.pop(0)()
    run_local = spread_steps(steps, BACKWARD_PLACES[0])
    run_inside = spread_steps(steps, BACKWARD_PLACES[1])
    run_outside = spread_steps(steps, BACKWARD_PLACES[2])
    scale = DK ** (-0.5)
    i = lax.broadcasted_iota(jnp.int32, (TILE, TILE), 0)
    j = lax.broadcasted_iota(jnp.int32, (TILE, TILE), 1)
    upper = (i <= j).astype(jnp.bfloat16)
    adjoint[...] = jnp.zeros_like(adjoint)
    mine[...] = jnp.zeros_like(mine)
    dgain_ref[...] = jnp.zeros_like(dgain_ref)
    dtaps_ref[...] = jnp.zeros_like(dtaps_ref)
    for p in range(mine.shape[0]):
        mine[p, TILE : TILE + 1] = jnp.ones((1, TILE), jnp.float32)

    def local(t, _):
        run_local(t)
        c = tiles - 1 - t
        for q in range(len(by_tile)):
            tile_load(q, c).wait()
        at = pl.ds(pl.multiple_of(c * TILE, TILE), TILE)
        cum = cum_ref[at, :]
        pre = conv_ref[at, 0:keys]
        q = pre * sigmoid(pre) * jnp.exp(cum) * scale * cols_ref[at, 0:1]
        decay = jnp.exp(cum[TILE - 1 : TILE]) * cols_ref[at, 0:1][TILE - 1 : TILE]
        for h in range(heads):
            kh = slice(h * DK, (h + 1) * DK)
            vh = slice(h * DV, (h + 1) * DV)
            o = o_ref[at, vh]
            inverse = lax.rsqrt(jnp.mean(o * o, axis=1, keepdims=True) + norm_epsilon)
            gate = gate_ref[at, vh]
            sig = sigmoid(gate)
            du = du_ref[at, vh]
            unit = o * inverse
            dgate_ref[at, vh] = (
                du * (unit * gain_ref[...]) * (sig * (1.0 + gate * (1.0 - sig)))
            ).astype(dgate_ref.dtype)
            don = du * (gate * sig)
            dgain_ref[0:1] += jnp.sum(don * unit, axis=0, keepdims=True)
            scaled = gain_ref[...] * don
            grad = inverse * scaled - unit * (
                inverse * inverse * jnp.mean(scaled * o, axis=1, keepdims=True)
            )
            do[at, vh] = grad
            ends[c, h] = adjoint[h]
            adjoint[h] = adjoint[h] * decay[:, kh] + product(halves(grad), halves(q[:, kh]), TN)
            for e in range(DV // TILE):
                p = h * (DV // TILE) + e
                mine[p, TILE : TILE + 1] = mine[p, TILE : TILE + 1] * decay[:, kh]
        return 0

    lax.fori_loop(0, tiles, local, 0)
    load(4).start()
    for h in range(heads):
        for e in range(DV // TILE):
            mine[h * (DV // TILE) + e, 0:TILE] = adjoint[h, e * TILE : (e + 1) * TILE]
    stages, finish = chain_tools(
        n, sizes, False, mine, (across, along, before, held), send, recv, result
    )
    stages[0]()
    load(0).wait()
    load(1).wait()

    def inside(c, _):
        for k, stage in enumerate(stages[1:]):
            pl.when(c == k + 1)(stage)
        run_inside(c)
        at = pl.ds(pl.multiple_of(c * TILE, TILE), TILE)
        cum = cum_ref[at, :]
        middle = cum[TILE // 2 - 1 : TILE // 2]
        pre = conv_ref[at, 0 : 2 * keys]
        both = pre * sigmoid(pre)
        grow = jnp.exp(cum - middle) * scale
        fall = jnp.exp(middle - cum)
        enter_decay = jnp.exp(cum) * (scale * cols_ref[at, 0:1])
        mask = tile_masks(rows_ref, cols_ref, c)
        for h in range(heads):
            kh = slice(h * DK, (h + 1) * DK)
            vh = slice(h * DV, (h + 1) * DV)
            q = halves(both[:, kh] * grow[:, kh])
            k = halves(both[:, keys + h * DK : keys + (h + 1) * DK] * fall[:, kh])
            prev_v = conv_ref[at, 2 * keys + h * DV : 2 * keys + (h + 1) * DV]
            v = halves(prev_v * sigmoid(prev_v))
            grad = halves(do[at, vh])
            scores = halves(jnp.where(mask, product(q, k, NT), 0.0))
            dscores = halves(jnp.where(mask, product(grad, v, NT), 0.0))
            dact[at, h * DK : (h + 1) * DK] = (
                product(dscores, k, NN) * grow[:, kh]
                + product(grad, halves(start_ref[c, h]), NN) * enter_decay[:, kh]
            )
            dact[at, keys + h * DK : keys + (h + 1) * DK] = (
                product(dscores, q, TN) * fall[:, kh]
            )
            dact[at, 2 * keys + h * DV : 2 * keys + (h + 1) * DV] = product(scores, grad, TN)
        return 0

    lax.fori_loop(0, tiles, inside, 0)
    finish()
    for h in range(heads):
        for e in range(DV // TILE):
            adjoint[h, e * TILE : (e + 1) * TILE] = result[h * (DV // TILE) + e]
    after[...] = jnp.zeros_like(after)
    load(2).wait()
    load(3).wait()

    def outside(t, _):
        run_outside(t)
        c = tiles - 1 - t
        at = pl.ds(pl.multiple_of(c * TILE, TILE), TILE)
        cum = cum_ref[at, :]
        last = cum[TILE - 1 : TILE]
        remain = jnp.exp(last - cum) * cols_ref[at, 1:2]
        decay = jnp.exp(last) * cols_ref[at, 0:1][TILE - 1 : TILE]
        pre = conv_ref[at, 0 : 2 * keys]
        both = pre * sigmoid(pre)
        dkeys, edges = [], []
        for h in range(heads):
            kh = slice(h * DK, (h + 1) * DK)
            wide = slice(2 * keys + h * DV, 2 * keys + (h + 1) * DV)
            k = both[:, keys + h * DK : keys + (h + 1) * DK]
            end = ends[c, h] + adjoint[h]
            adjoint[h] = adjoint[h] * decay[:, kh]
            parts = halves(end)
            pre_v = conv_ref[at, wide]
            v = halves(pre_v * sigmoid(pre_v))
            dkeys.append(
                dact[at, keys + h * DK : keys + (h + 1) * DK]
                + product(v, parts, NN) * remain[:, kh]
            )
            dact[at, wide] += product(halves(k * remain[:, kh]), parts, NT)
            edges.append(jnp.sum(end * start_ref[c + 1, h], axis=0, keepdims=True))
        dk = jnp.concatenate(dkeys, axis=1)
        dq = dact[at, 0:keys]
        dact[at, keys : 2 * keys] = dk
        drift = both[:, 0:keys] * dq - both[:, keys:] * dk
        dl = running_sum(upper, drift) + jnp.concatenate(edges, axis=1)
        dlogits_ref[at, :] = dl * (1.0 / gate_scale) * sigmoid(-logits_ref[at, :])
        behind = jnp.where(
            c == 0,
            halo_ref[...],
            proj_ref[pl.ds(pl.multiple_of(jnp.maximum(c * TILE - 16, 0), 16), 16), :],
        )
        masks = cols_ref[pl.ds(pl.multiple_of(c * TILE, TILE), TILE + 8), :]
        for g in range(0, channels, 256):
            wide = slice(g, g + 256)
            pre = conv_ref[at, wide]
            sig = sigmoid(pre)
            dconv = dact[at, wide] * (sig * (1.0 + pre * (1.0 - sig)))
            block = jnp.concatenate(
                [
                    behind[:, g : g + 256].astype(jnp.float32),
                    proj_ref[at, wide].astype(jnp.float32),
                ]
            )
            grad = jnp.concatenate([dconv, after[:, wide]])
            total = taps_ref[3:4, wide] * dconv
            dtaps_ref[3:4, wide] += jnp.sum(dconv * block[16:], axis=0, keepdims=True)
            first = jnp.zeros((8, 256), jnp.float32)
            for s in (1, 2, 3):
                masked = grad * masks[:, 1 + s : 2 + s]
                tap = taps_ref[3 - s : 4 - s, wide]
                total = total + tap * masked[s : s + TILE]
                dtaps_ref[3 - s : 4 - s, wide] += jnp.sum(
                    masked[:TILE] * block[16 - s : 16 - s + TILE], axis=0, keepdims=True
                )
                first = first + tap * jnp.concatenate(
                    [jnp.zeros((8, 256), jnp.float32), masked[0:8]]
                )[s : s + 8]
            dproj_ref[at, wide] = total.astype(dproj_ref.dtype)
            after[:, wide] = dconv[0:8]
            back[0, :, wide] = first

            @pl.when(c == tiles - 1)
            def _():
                tail[:, wide] = total[TILE - 16 :]

        return 0

    lax.fori_loop(0, tiles, outside, 0)
    load(5).start()

    home = remote(
        back.at[0], back.at[1], b_sem.at[0], b_sem.at[1], lax.rem(me + n - 1, n)
    )

    @pl.when(me > 0)
    def _():
        home.start()

    for step in steps[:1]:
        step()

    @pl.when(me < n - 1)
    def _():
        home.wait_recv()

    @pl.when(me == n - 1)
    def _():
        back[1] = jnp.zeros(back.shape[1:], jnp.float32)

    dproj_ref[pl.ds(tiles * TILE - 16, 16), :] = (
        tail[...] + jnp.concatenate([jnp.zeros((8, channels), jnp.float32), back[1]])
    ).astype(dproj_ref.dtype)
    load(6).start()
    for step in steps[1:]:
        step()
    sent()

    @pl.when(me > 0)
    def _():
        home.wait_send()

    for q in (4, 5, 6):
        load(q).wait()


def recurrence_back(
    proj, halo, conv, cum, logits, o, gate, du, starts, cols, rows, taps, gain, grads
):
    n = lax.axis_size("seq")
    sizes = axis_sizes(n)
    length, channels = proj.shape
    keys = cum.shape[1]
    heads = keys // DK
    value = heads * DV
    tiles = length // TILE
    f32 = jnp.float32
    shape = jax.ShapeDtypeStruct
    depth = grads[0].shape[3]
    plan = build_plan(tuple(g.shape[4] // TILE for g in grads), SHARES, BACKWARD_PIECES, SPREAD)
    blocks = sum(g.shape[4] for g in grads) // TILE
    vmem, anywhere = pl.BlockSpec(memory_space=pltpu.VMEM), pl.BlockSpec(memory_space=pl.ANY)
    return pl.pallas_call(
        functools.partial(backward_kernel, n, sizes, plan),
        in_specs=[anywhere, vmem] + [anywhere] * 7 + [vmem] * 4 + [anywhere] * 2,
        out_specs=(anywhere,) * 3 + (vmem,) * 3,
        out_shape=(
            shape((length, channels), jnp.bfloat16),
            shape((length, value), jnp.bfloat16),
            shape((length, keys), f32),
            shape((8, channels), f32),
            shape((8, DV), f32),
            shape((blocks, depth, TILE), jnp.bfloat16),
        ),
        scratch_shapes=[
            pltpu.VMEM((length, channels), jnp.bfloat16),
            pltpu.VMEM((length, channels), f32),
            pltpu.VMEM((length, keys), f32),
            pltpu.VMEM((length, keys), f32),
            pltpu.VMEM((length, value), f32),
            pltpu.VMEM((length, value), f32),
            pltpu.VMEM((length, value), f32),
            pltpu.VMEM(starts.shape, f32),
            pltpu.VMEM((length, channels), jnp.bfloat16),
            pltpu.VMEM((length, value), jnp.bfloat16),
            pltpu.VMEM((length, keys), f32),
            pltpu.SemaphoreType.DMA((5, tiles)),
            pltpu.SemaphoreType.DMA((7,)),
            pltpu.VMEM((length, value), f32),
            pltpu.VMEM((length, channels), f32),
            pltpu.VMEM((heads, DV, DK), f32),
            pltpu.VMEM((tiles, heads, DV, DK), f32),
            pltpu.VMEM((8, channels), f32),
            pltpu.VMEM((2, 8, channels), f32),
            pltpu.VMEM((16, channels), f32),
        ]
        + chain_scratch(sizes, heads * DV // TILE)
        + [pltpu.SemaphoreType.DMA((2,))]
        + scatter_scratch(sizes, plan, depth, TILE, jnp.bfloat16),
        compiler_params=pltpu.CompilerParams(
            collective_id=5, has_side_effects=True, vmem_limit_bytes=60 << 20
        ),
    )(proj, halo, conv, cum, logits, o, gate, du, starts, cols, rows, taps, gain, *grads)


def tail_kernel(
    n,
    sizes,
    plan,
    shared,
    taken,
    inv_ref,
    early_ref,
    later_ref,
    dproj_ref,
    dgate_ref,
    normed_ref,
    dlogits_ref,
    lowrank_ref,
    upper_ref,
    down_ref,
    gain_ref,
    gains_two_ref,
    dtaps_ref,
    dhead_ref,
    w_ref,
    tokens_ref,
    dh_ref,
    left_ref,
    out_ref,
    small_out,
    grad_ref,
    left_out,
    grads,
    weights,
    tokens,
    dh,
    total,
    trade,
    fin,
    send,
    small,
    wide,
    narrow,
    b_sem,
    a_send,
    a_recv,
    s_send,
    s_recv,
    l_sem,
    *refs,
):
    me, core = lax.axis_index("seq"), lax.axis_index("head")
    slots, _, rows, bw = out_ref.shape
    length, width = normed_ref.shape
    channels = dproj_ref.shape[1]
    keys, rank, tap_count = dlogits_ref.shape[1], down_ref.shape[0], 4
    downs = early_ref.shape[0] - taken
    count = fin.shape[0] - 1 - early_ref.shape[0] - later_ref.shape[0]
    tiles = s_send.shape[0]
    step_rows = length // tiles
    f32 = jnp.float32
    dot = functools.partial(lax.dot_general, preferred_element_type=f32)
    enter(n, me, True)
    loads = [
        pltpu.make_async_copy(source, target, l_sem.at[1 + q])
        for q, (source, target) in enumerate(((w_ref, weights), (tokens_ref, tokens), (dh_ref, dh)))
    ]
    for load in loads:
        load.start()
    block = wide.shape[1]
    per_slot = left_ref.shape[1] // block
    total_blocks = left_ref.shape[0] * per_slot

    def basis_load(k):
        at = (k // per_slot, pl.ds(k % per_slot * block, block))
        return pltpu.make_async_copy(left_ref.at[at], wide.at[k % 2], b_sem.at[k % 2])

    def basis_store(k):
        at = (k // per_slot, pl.ds(k % per_slot * block, block))
        return pltpu.make_async_copy(narrow.at[k % 2], left_out.at[at], b_sem.at[2 + k % 2])

    pending = list(range(total_blocks))

    def narrow_basis(count):
        for k in pending[:count]:
            basis_load(k).wait()
            if k >= 2:
                basis_store(k - 2).wait()
            narrow[k % 2] = wide[k % 2].astype(narrow.dtype)
            basis_store(k).start()
            if k + 2 < total_blocks:
                basis_load(k + 2).start()
        del pending[:count]

    for k in range(min(2, total_blocks)):
        basis_load(k).start()
    steps, sent = scatter_steps(sizes, plan, [grads], refs[:-5], fin, bw, in_place=True)
    sums = sum_steps(sizes, shared, small, small_out, *refs[-5:])

    def block_grads(lo, hi):
        for source, base in ((dproj_ref, 0), (dgate_ref, channels)):
            first, last = max(lo - base, 0), min(hi - base, source.shape[1])
            if first >= last:
                continue

            part = dot(normed_ref[...], source[:, first:last], dimension_numbers=TN)
            grads[:, :, :, :, base + first : base + last] = part.astype(grads.dtype).reshape(
                sizes + (rows, last - first)
            )

    cut = max(hi for _, _, hi, _, _, group in plan if group == 0) * bw
    block_grads(0, cut)
    steps[0]()
    block_grads(cut, grads.shape[4])
    steps[1]()
    fin[fin.shape[0] - 1] = jnp.zeros(fin.shape[1:], fin.dtype)
    if taken:
        fin[count : count + taken] = early_ref[downs:]
    fin[count + taken : fin.shape[0] - 1 - downs] = later_ref[...]
    fin[fin.shape[0] - 1 - downs : fin.shape[0] - 1] = early_ref[0:downs]

    def swap(t):
        at = pl.ds(t * step_rows, step_rows)
        return pltpu.make_async_remote_copy(
            src_ref=total.at[at],
            dst_ref=trade.at[at],
            send_sem=s_send.at[t],
            recv_sem=s_recv.at[t],
            device_id={"head": 1 - core},
            device_id_type=MESH,
        )

    for load in loads:
        load.wait()
    upper = halves(upper_ref[0:rank, :])
    down_low = down_ref[...].astype(jnp.bfloat16)
    small[...] = jnp.zeros_like(small)
    upper_grad = jnp.zeros((rank, keys), f32)
    bias_grad = jnp.zeros((1, keys), f32)
    for t in range(tiles):
        at = slice(t * step_rows, (t + 1) * step_rows)
        dlogits = dlogits_ref[at, :]
        parts = halves(dlogits)
        dlow = product(parts, upper, NT).astype(jnp.bfloat16)
        upper_grad += product(halves(lowrank_ref[at, :]), parts, TN)
        bias_grad += jnp.sum(dlogits, axis=0, keepdims=True)
        small[0:rank, :] += dot(dlow, normed_ref[at, :], dimension_numbers=TN)
        part = (
            dot(dproj_ref[at, :], weights[:, :channels], dimension_numbers=NT)
            + dot(dgate_ref[at, :], weights[:, channels:], dimension_numbers=NT)
            + dot(dlow, down_low, dimension_numbers=NN)
        )
        total[at, :] = part.astype(total.dtype)
        swap(t).start()
        tok = tokens[at, :].astype(f32)
        inverse = lax.rsqrt(jnp.mean(tok * tok, axis=1, keepdims=True) + norm_epsilon)
        small[rank + 1 : rank + 2, :] += jnp.sum(part * (tok * inverse), axis=0, keepdims=True)
    small[rank : rank + 1, 0:DV] = dhead_ref[0:1, :]
    small[shared : shared + 1, :] = gains_two_ref[0:1, :]
    small[shared + 1 : shared + 1 + tap_count, :] = dtaps_ref[0:tap_count, :]
    per = width // keys
    base = shared + 1 + tap_count
    for r in range(rank + 1):
        row = bias_grad if r == rank else upper_grad[r : r + 1]
        small[base + r // per : base + r // per + 1, (r % per) * keys : (r % per + 1) * keys] = row
    sums[0]()
    narrow_basis(2)
    steps[2]()
    sums[1]()

    for t in range(tiles):
        at = slice(t * step_rows, (t + 1) * step_rows)
        swap(t).wait_recv()
        dxn = total[at, :].astype(f32) + trade[at, :].astype(f32)
        tok = tokens[at, :].astype(f32)
        inverse = lax.rsqrt(jnp.mean(tok * tok, axis=1, keepdims=True) + norm_epsilon)
        scaled = gain_ref[...] * dxn
        mean = jnp.mean(scaled * tok, axis=1, keepdims=True)
        dh[at, :] = dh[at, :] + (
            inverse * scaled - tok * (inverse * inverse * inverse * mean)
        )
    store = pltpu.make_async_copy(dh, grad_ref, l_sem.at[4])
    store.start()
    for s, step in enumerate(steps[3:]):
        narrow_basis(3)
        step()
        if s + 2 < len(sums):
            sums[s + 2]()
    for s in range(send.shape[0]):
        send[s] = fin[inv_ref[0, s]]

    def move(j):
        p = lax.rem(me + j, n)
        return remote(
            send.at[pl.ds(p * slots, slots)], out_ref.at[:, me], a_send.at[j], a_recv.at[j], p
        )

    for j in range(1, n):
        move(j).start()
    mine = pltpu.make_async_copy(
        send.at[pl.ds(me * slots, slots)], out_ref.at[:, me], l_sem.at[0]
    )
    mine.start()
    for step in sums[len(steps) - 1 :]:
        step()
    narrow_basis(len(pending))
    mine.wait()
    for j in range(1, n):
        move(j).wait()
    sent()
    for k in range(max(0, total_blocks - 2), total_blocks):
        basis_store(k).wait()
    for t in range(tiles):
        swap(t).wait_send()
    store.wait()


def tail(
    inverse, early, later, dproj, dgate, normed, dlogits, lowrank, upper, down, gain, gains_two,
    dtaps, dhead, weights, tokens, dh, left, slots, taken
):
    n = lax.axis_size("seq")
    sizes = axis_sizes(n)
    most = max(sizes)
    length, width = normed.shape
    _, rows, bw = early.shape
    columns = dproj.shape[1] + dgate.shape[1]
    blocks = columns // bw
    rank = down.shape[0]
    shared = rank + 8
    plan = build_plan((blocks,), SHARES, 2, SPREAD)
    shape = jax.ShapeDtypeStruct
    vmem, anywhere = pl.BlockSpec(memory_space=pltpu.VMEM), pl.BlockSpec(memory_space=pl.ANY)
    b16, f32 = jnp.bfloat16, jnp.float32
    small = (shared + 16, width)
    tiles = 4
    out, summed, grad, left = pl.pallas_call(
        functools.partial(tail_kernel, n, sizes, plan, shared, taken),
        out_shape=(
            shape((slots, n, rows, bw), b16),
            shape(small, f32),
            shape((length, width), f32),
            shape(left.shape, b16),
        ),
        in_specs=[pl.BlockSpec(memory_space=pltpu.SMEM)] + [vmem] * 13 + [anywhere] * 4,
        out_specs=(anywhere, vmem, anywhere, anywhere),
        scratch_shapes=[
            pltpu.VMEM(sizes + (rows, columns), b16),
            pltpu.VMEM((width, columns), b16),
            pltpu.VMEM((length, width), b16),
            pltpu.VMEM((length, width), f32),
            pltpu.VMEM((length, width), b16),
            pltpu.VMEM((length, width), b16),
            pltpu.VMEM((blocks + early.shape[0] + later.shape[0] + 1, rows, bw), b16),
            pltpu.VMEM((slots * n, rows, bw), b16),
            pltpu.VMEM(small, f32),
            pltpu.VMEM((2, width // 4, width), f32),
            pltpu.VMEM((2, width // 4, width), b16),
            pltpu.SemaphoreType.DMA((4,)),
            pltpu.SemaphoreType.DMA((n,)),
            pltpu.SemaphoreType.DMA((n,)),
            pltpu.SemaphoreType.DMA((tiles,)),
            pltpu.SemaphoreType.DMA((tiles,)),
            pltpu.SemaphoreType.DMA((5,)),
        ]
        + scatter_scratch(sizes, plan, rows, bw, b16, in_place=True)
        + [
            pltpu.VMEM((shared, width), f32),
            pltpu.VMEM((3,) + small, f32),
            pltpu.VMEM((3, most) + small, f32),
            pltpu.SemaphoreType.DMA((1 + 3 * most,)),
            pltpu.SemaphoreType.DMA((1 + 3 * most,)),
        ],
        compiler_params=pltpu.CompilerParams(
            collective_id=2, has_side_effects=True, vmem_limit_bytes=60 << 20
        ),
    )(
        inverse, early, later, dproj, dgate, normed, dlogits, lowrank, upper, down, gain, gains_two,
        dtaps, dhead, weights, tokens, dh, left
    )
    return out.reshape(slots, width, bw), summed, grad, left


def adam_kernel(
    rates,
    rank,
    taps,
    grad_ref,
    left_ref,
    right_ref,
    master_ref,
    first_ref,
    second_ref,
    summed_ref,
    *refs,
):
    params = [refs[3 * q : 3 * q + 3] for q in range(5)]
    grad_in, result_in = refs[15:17]
    grad_out, master_out, first_out, second_out, copy_out = refs[17:22]
    news = [refs[22 + 4 * q : 26 + 4 * q] for q in range(5)]
    grad_pass, result_ref = refs[42:]
    grad_pass[...] = grad_in[...]
    result_ref[...] = result_in[...]

    @pl.when(pl.program_id(0) == 0)
    def _():
        shared = rank + 8
        width = summed_ref.shape[1]
        keys = news[2][0].shape[1]
        per = width // keys
        base = shared + 1 + taps
        gains, down, upper, head, conv = news
        gains[0][0:1, :] = summed_ref[rank + 1 : rank + 2, :]
        gains[0][1:2, :] = summed_ref[shared : shared + 1, :]
        down[0][...] = summed_ref[0:rank, :]
        for r in range(rank + 1):
            upper[0][r : r + 1, :] = summed_ref[
                base + r // per : base + r // per + 1, (r % per) * keys : (r % per + 1) * keys
            ]
        head[0][...] = summed_ref[rank : rank + 1, 0:DV]
        conv[0][...] = summed_ref[shared + 1 : shared + 1 + taps, :]
        for (value, first, second), new, rate in zip(params, news, rates, strict=True):
            new[1][...], new[2][...], new[3][...] = plain_adam(
                value[...], new[0][...], first[...], second[...], rate
            )

    width = left_ref.shape[1]
    step = min(256, width)
    dot = functools.partial(
        lax.dot_general, dimension_numbers=TN, preferred_element_type=jnp.float32
    )
    grad_out[0] = grad_ref[0].astype(jnp.float32)
    left = left_ref[0]
    dot = functools.partial(lax.dot_general, preferred_element_type=jnp.float32)
    right = halves(right_ref[0])
    rotated = dot(left, grad_ref[0], dimension_numbers=TN)
    rotated = product(halves(rotated), right, NN)
    first = moment_decay * first_ref[0] + (1.0 - moment_decay) * rotated
    second = moment_decay * second_ref[0] + (1.0 - moment_decay) * rotated * rotated
    first_out[0] = first
    second_out[0] = second
    direction = first / (jnp.sqrt(second) + adam_epsilon)
    turned = product(halves(direction), right, NT).astype(left.dtype)
    master = master_ref[0] - rate_block * dot(left, turned, dimension_numbers=NN)
    master_out[0] = master
    copy_out[0] = master.astype(copy_out.dtype)


def all_adam(grads, left, right, master, first, second, summed, params, grad, result):
    slots, width, columns = master.shape
    tall = pl.BlockSpec((1, width, columns), lambda i: (i, 0, 0))
    length, model = grad.shape
    wide = pl.BlockSpec((length // slots, model), lambda i: (i, 0))
    shape = jax.ShapeDtypeStruct
    full = shape(master.shape, jnp.float32)

    def whole(array):
        return pl.BlockSpec(array.shape, lambda i: (0, 0))

    flat = [array for triple in params for array in triple]
    rates = (rate_gains, rate_down, rate_upper, rate_head, rate_conv)
    news = [triple[0] for triple in params for _ in range(4)]
    return pl.pallas_call(
        functools.partial(adam_kernel, rates, params[1][0].shape[0], params[4][0].shape[0]),
        grid=(slots,),
        out_shape=tuple(
            [full] * 4
            + [shape(master.shape, jnp.bfloat16)]
            + [shape(new.shape, new.dtype) for new in news]
            + [shape(grad.shape, jnp.float32), shape(grad.shape, jnp.bfloat16)]
        ),
        in_specs=[
            tall,
            pl.BlockSpec((1, width, width), lambda i: (i, 0, 0)),
            pl.BlockSpec((1, columns, columns), lambda i: (i, 0, 0)),
            tall,
            tall,
            tall,
            whole(summed),
        ]
        + [whole(array) for array in flat]
        + [wide] * 2,
        out_specs=[tall] * 5 + [whole(new) for new in news] + [wide] * 2,
        compiler_params=pltpu.CompilerParams(vmem_limit_bytes=56 << 20),
    )(grads, left, right, master, first, second, summed, *flat, grad, result)


def middle_kernel(
    n,
    sizes,
    plan,
    u_ref,
    w_out_ref,
    cols_ref,
    gain_ref,
    tokens_ref,
    w_up_ref,
    w_down_ref,
    cot_ref,
    early_ref,
    sum_ref,
    result_out,
    dh_out,
    du_out,
    g_up_out,
    g_out_out,
    w_up,
    w_down,
    mixed,
    hidden_sum,
    normed,
    inv,
    dy,
    hid,
    dpair,
    send,
    recv,
    g_down,
    g_up,
    g_out,
    du,
    free,
    s_sem,
    r_sem,
    l_sem,
    *scatter_refs,
):
    me, core = lax.axis_index("seq"), lax.axis_index("head")
    length, width = normed.shape
    inner = hid.shape[1]
    rows = g_out.shape[3]
    f32 = jnp.float32
    dot = functools.partial(lax.dot_general, preferred_element_type=f32)
    tiles = s_sem.shape[0] // 3
    block = length // tiles
    ats = [slice(t * block, (t + 1) * block) for t in range(tiles)]
    enter(n, me, True)
    loads = [
        pltpu.make_async_copy(source, target, l_sem.at[q])
        for q, (source, target) in enumerate(
            ((tokens_ref, mixed), (w_up_ref, w_up), (w_down_ref, w_down), (cot_ref, dy))
        )
    ]
    for load in loads:
        load.start()
    flushes = []

    def flush(source, target):
        copy = pltpu.make_async_copy(source, target, l_sem.at[4 + len(flushes)])
        copy.start()
        flushes.append(copy)

    steps, sent = scatter_steps(
        sizes, plan, [g_down, g_up], scatter_refs, early_ref, TILE, in_place=True
    )

    def advance(count=1):
        for step in steps[:count]:
            step()
        del steps[:count]

    def swap(phase, t):
        at = pl.ds(t * block, block)
        return pltpu.make_async_remote_copy(
            src_ref=send.at[at],
            dst_ref=recv.at[at],
            send_sem=s_sem.at[phase * tiles + t],
            recv_sem=r_sem.at[phase * tiles + t],
            device_id={"head": 1 - core},
            device_id_type=MESH,
        )

    def exchange(phase, left, right, close):
        if phase:
            for t in range(tiles):
                swap(phase - 1, t).wait_send()
            pl.semaphore_wait(free, 1)
        for t, at in enumerate(ats):
            send[at, :] = dot(left[at, :], right[...], dimension_numbers=NT).astype(send.dtype)
            swap(phase, t).start()
            if t:
                swap(phase, t - 1).wait_recv()
                close(ats[t - 1])
        swap(phase, tiles - 1).wait_recv()
        close(ats[-1])
        if phase < 2:
            pl.semaphore_signal(
                free, inc=1, device_id={"head": 1 - core}, device_id_type=MESH
            )

    def both(at):
        return send[at, :].astype(f32) + recv[at, :].astype(f32)

    loads[0].wait()

    def close_attn(at):
        total = mixed[at, :].astype(f32) + both(at)
        inverse = lax.rsqrt(jnp.mean(total * total, axis=1, keepdims=True) + norm_epsilon)
        hidden_sum[at, :] = total
        inv[at, :] = inverse
        normed[at, :] = (total * inverse * gain_ref[...]).astype(normed.dtype)

    exchange(0, u_ref, w_out_ref, close_attn)
    for load in loads[1:]:
        load.wait()

    def feed(t, _):
        at = pl.ds(pl.multiple_of(t * block, block), block)
        x = normed[at, :]
        grad_y = (dy[at, :].astype(f32) * cols_ref[at, 7:8]).astype(dy.dtype)
        dy[at, :] = grad_y
        for lo in range(0, inner, 512):
            hi = min(lo + 512, inner)
            gate = dot(x, w_up[:, lo:hi], dimension_numbers=NN)
            up = dot(x, w_up[:, inner + lo : inner + hi], dimension_numbers=NN)
            grad = dot(grad_y, w_down[:, lo:hi], dimension_numbers=NN)
            sig = sigmoid(gate)
            swish = gate * sig
            hid[at, lo:hi] = (swish * up).astype(hid.dtype)
            dpair[at, lo:hi] = (grad * up * (sig + swish * (1.0 - sig))).astype(dpair.dtype)
            dpair[at, inner + lo : inner + hi] = (grad * swish).astype(dpair.dtype)
        return 0

    lax.fori_loop(0, tiles, feed, 0)

    def block_grads(left, source, target, lo, hi):
        for first in range(lo, hi, 512):
            last = min(first + 512, hi)
            part = dot(left[...], source[:, first:last], dimension_numbers=TN)
            target[:, :, :, :, first:last] = part.astype(target.dtype).reshape(
                sizes + (rows, last - first)
            )

    block_grads(dy, hid, g_down, 0, inner)
    advance()
    block_grads(normed, dpair, g_up, 0, inner)
    advance()
    block_grads(normed, dpair, g_up, inner, 2 * inner)
    taken = g_up.shape[4] - g_up_out.shape[4]
    flush(g_up.at[:, :, :, :, pl.ds(taken, g_up_out.shape[4])], g_up_out)

    def close_mlp(at):
        mixed[at, :] = (hidden_sum[at, :] + both(at)).astype(mixed.dtype)

    exchange(1, hid, w_down, close_mlp)
    flush(mixed, result_out)
    advance()

    sum_ref[...] = jnp.zeros_like(sum_ref)

    def close_back(at):
        grad = both(at)
        total, inverse = hidden_sum[at, :], inv[at, :]
        unit = total * inverse
        scaled = gain_ref[...] * grad
        mean = jnp.mean(scaled * total, axis=1, keepdims=True)
        dh = dy[at, :].astype(f32) + (inverse * scaled - unit * (inverse * inverse * mean))
        hidden_sum[at, :] = dh
        normed[at, :] = dh.astype(normed.dtype)
        sum_ref[0:1, :] += jnp.sum(grad * unit, axis=0, keepdims=True)
        du[at, :] = dot(normed[at, :], w_out_ref[...], dimension_numbers=NN)

    exchange(2, dpair, w_up, close_back)
    flush(hidden_sum, dh_out)
    flush(du, du_out)
    advance()
    block_grads(normed, u_ref, g_out, 0, u_ref.shape[1])
    flush(g_out, g_out_out)
    advance(len(steps))
    sent()
    for t in range(tiles):
        swap(2, t).wait_send()
    for copy in flushes:
        copy.wait()


def middle(u, w_out, cols, gain, tokens, w_up, w_down, cot, taken):
    n = lax.axis_size("seq")
    sizes = axis_sizes(n)
    length, width = tokens.shape
    value, inner = u.shape[1], w_down.shape[1]
    rows = width // n
    f32, b16 = jnp.float32, jnp.bfloat16
    blocks = inner // TILE
    plan = build_plan((blocks, taken) if taken else (blocks,), SHARES, MIDDLE_PIECES, SPREAD)
    shape = jax.ShapeDtypeStruct
    vmem, anywhere = pl.BlockSpec(memory_space=pltpu.VMEM), pl.BlockSpec(memory_space=pl.ANY)
    tiles = 4
    return pl.pallas_call(
        functools.partial(middle_kernel, n, sizes, plan),
        out_shape=(
            shape((blocks + taken, rows, TILE), b16),
            shape((8, width), f32),
            shape((length, width), b16),
            shape((length, width), f32),
            shape((length, value), f32),
            shape(sizes + (rows, 2 * inner - taken * TILE), b16),
            shape(sizes + (rows, value), b16),
        ),
        in_specs=[vmem] * 4 + [anywhere] * 4,
        out_specs=(vmem, vmem) + (anywhere,) * 5,
        scratch_shapes=[
            pltpu.VMEM((width, 2 * inner), b16),
            pltpu.VMEM((width, inner), b16),
            pltpu.VMEM((length, width), b16),
            pltpu.VMEM((length, width), f32),
            pltpu.VMEM((length, width), b16),
            pltpu.VMEM((length, 1), f32),
            pltpu.VMEM((length, width), b16),
            pltpu.VMEM((length, inner), b16),
            pltpu.VMEM((length, 2 * inner), b16),
            pltpu.VMEM((length, width), b16),
            pltpu.VMEM((length, width), b16),
            pltpu.VMEM(sizes + (rows, inner), b16),
            pltpu.VMEM(sizes + (rows, 2 * inner), b16),
            pltpu.VMEM(sizes + (rows, value), b16),
            pltpu.VMEM((length, value), f32),
            pltpu.SemaphoreType.REGULAR,
            pltpu.SemaphoreType.DMA((3 * tiles,)),
            pltpu.SemaphoreType.DMA((3 * tiles,)),
            pltpu.SemaphoreType.DMA((9,)),
        ]
        + scatter_scratch(sizes, plan, rows, TILE, b16, in_place=True),
        compiler_params=pltpu.CompilerParams(
            collective_id=6, has_side_effects=True, vmem_limit_bytes=62 << 20
        ),
    )(u, w_out, cols, gain, tokens, w_up, w_down, cot)


def plain_adam(param, gradient, first, second, rate):
    first_next = moment_decay * first + (1.0 - moment_decay) * gradient
    second_next = moment_decay * second + (1.0 - moment_decay) * gradient * gradient
    return (
        param - rate * first_next / (jnp.sqrt(second_next) + adam_epsilon),
        first_next,
        second_next,
    )


def body(
    tokens,
    cotangent,
    lengths,
    packing,
    owners,
    slot_copy,
    slot_master,
    slot_first,
    slot_second,
    basis_left,
    basis_right,
    norm_gains,
    gains_first,
    gains_second,
    gate_down,
    down_first,
    down_second,
    gate_up,
    upper_first,
    upper_second,
    head_gain,
    head_first,
    head_second,
    conv_weight,
    conv_first,
    conv_second,
):
    tok_rows = tokens.shape[0]
    model_width = tokens.shape[1]
    block_width = slot_copy.shape[2]
    tap_count = conv_weight.shape[0]
    key_width = gate_up.shape[1]
    channels = conv_weight.shape[1]
    value_width = channels - 2 * key_width
    block_total = owners.shape[1]
    count_in = (channels + value_width) // block_width
    count_out = value_width // block_width
    count_down = (block_total - count_in - count_out) // 3
    count_up = 2 * count_down
    (in_weights, up_weights, out_weights, down_weights), kept = forward(
        owners,
        lengths,
        packing,
        slot_copy,
        tokens,
        norm_gains[0:1],
        gate_down.T,
        gate_up,
        conv_weight,
        head_gain[None],
        (count_in, count_up, count_out, count_down),
    )
    normed, lowrank, logits, mixed_proj, halo, gate_pre = kept[:6]
    conv_pre, cumulative, attended, gated_out, starts, cols, rows = kept[6:]
    gain_row = head_gain[None]
    early, gains_two, result, grad_one, grad_gated, grad_up, grad_out = middle(
        gated_out,
        out_weights,
        cols,
        norm_gains[1:2],
        tokens,
        up_weights,
        down_weights,
        cotangent,
        MIDDLE_TAKEN,
    )
    grad_mixed, grad_gate_pre, grad_logits, tap_grads, gain_grads, later = recurrence_back(
        mixed_proj,
        halo,
        conv_pre,
        cumulative,
        logits,
        attended,
        gate_pre,
        grad_gated,
        starts,
        cols,
        rows,
        conv_weight,
        gain_row,
        (grad_up, grad_out),
    )
    slots_dev = slot_copy.shape[0]
    slot_total = slots_dev * lax.axis_size("seq")
    named = jnp.arange(slot_total, dtype=jnp.int32)[:, None] == owners
    inverse = jnp.where(
        jnp.any(named, axis=1),
        jnp.sum(named * jnp.arange(block_total, dtype=jnp.int32), axis=1),
        block_total,
    ).astype(jnp.int32)[None]
    owned_grads, summed, grad_input, left_low = tail(
        inverse,
        early,
        later,
        grad_mixed,
        grad_gate_pre,
        normed,
        grad_logits,
        lowrank,
        gate_up,
        gate_down.T,
        norm_gains[0:1],
        gains_two,
        tap_grads,
        gain_grads,
        in_weights,
        tokens,
        grad_one,
        basis_left,
        slots_dev,
        MIDDLE_TAKEN,
    )
    params = (
        (norm_gains, gains_first, gains_second),
        (gate_down.T, down_first.T, down_second.T),
        (gate_up, upper_first, upper_second),
        (head_gain[None], head_first[None], head_second[None]),
        (conv_weight, conv_first, conv_second),
    )
    (
        owned_grads,
        master_next,
        first_next,
        second_next,
        copy_next,
        *small_next,
        grad_input,
        result,
    ) = all_adam(
        owned_grads,
        left_low,
        basis_right,
        slot_master,
        slot_first,
        slot_second,
        summed,
        params,
        grad_input,
        result,
    )
    for q in range(4, 8):
        small_next[q] = small_next[q].T
    for q in range(12, 16):
        small_next[q] = small_next[q][0]
    return (
        result,
        grad_input,
        owned_grads,
        master_next,
        first_next,
        second_next,
        copy_next,
        *small_next,
    )


def solution(mesh):
    placed = (
        P("seq", None),
        P("seq", None),
        P(),
        P(),
        P("head", None),
        P(("seq", "head"), None, None),
        P(("seq", "head"), None, None),
        P(("seq", "head"), None, None),
        P(("seq", "head"), None, None),
        P(("seq", "head"), None, None),
        P(("seq", "head"), None, None),
        P(),
        P(),
        P(),
        P(),
        P(),
        P(),
        P(None, "head"),
        P(None, "head"),
        P(None, "head"),
        P(),
        P(),
        P(),
        P(None, "head"),
        P(None, "head"),
        P(None, "head"),
    )
    return jax.shard_map(
        body,
        mesh=mesh,
        in_specs=placed,
        out_specs=(
            P("seq", None),
            P("seq", None),
            P(("seq", "head"), None, None),
            P(("seq", "head"), None, None),
            P(("seq", "head"), None, None),
            P(("seq", "head"), None, None),
            P(("seq", "head"), None, None),
            P(),
            P(),
            P(),
            P(),
            P(),
            P(),
            P(),
            P(),
            P(None, "head"),
            P(None, "head"),
            P(None, "head"),
            P(None, "head"),
            P(),
            P(),
            P(),
            P(),
            P(None, "head"),
            P(None, "head"),
            P(None, "head"),
            P(None, "head"),
        ),
        check_vma=False,
    )
```

```python
import functools

import jax
import jax.numpy as jnp
from jax import lax
from jax.experimental import pallas as pl
from jax.experimental.pallas import tpu as pltpu
from jax.sharding import PartitionSpec as P

MESH = pl.DeviceIdType.MESH

DK = 128
DV = 256


highest_precision = lax.Precision.HIGHEST
norm_epsilon = 1e-06
adam_epsilon = 1e-08
gate_scale = 16.0
moment_decay = 0.5
rate_block = 0.03
rate_gains = 0.45
rate_down = 0.02
rate_upper = 0.6
rate_head = 0.5
rate_conv = 0.1


def axis_sizes(n):
    side = 1
    while (side * 2) ** 2 * 4 <= n:
        side *= 2
    return (n // (side * side), side, side)


def coords(me, sizes):
    _, rows, columns = sizes
    return [me // (rows * columns), (me // columns) % rows, me % columns]


def index_of(c, sizes):
    _, rows, columns = sizes
    return (c[0] * rows + c[1]) * columns + c[2]


def neighbour(c, sizes, ax, j):
    d = list(c)
    d[ax] = lax.rem(c[ax] + j, sizes[ax])
    return index_of(d, sizes)


def enter(n, me, mate=False):
    barrier = pltpu.get_barrier_semaphore()
    if mate:
        core = lax.axis_index("head")
        pl.semaphore_signal(barrier, inc=1, device_id={"head": 1 - core}, device_id_type=MESH)
    for j in range(1, n):
        pl.semaphore_signal(
            barrier, inc=1, device_id={"seq": lax.rem(me + j, n)}, device_id_type=MESH
        )
    pl.semaphore_wait(barrier, n - 1 + int(mate))


def remote(src, dst, send_sem, recv_sem, peer):
    return pltpu.make_async_remote_copy(
        src_ref=src,
        dst_ref=dst,
        send_sem=send_sem,
        recv_sem=recv_sem,
        device_id={"seq": peer},
        device_id_type=MESH,
    )


def build_plan(widths, parts, pieces, orders, base=0):
    total = sum(widths)
    bounds = [sum(widths[:i]) for i in range(len(widths) + 1)]
    cuts = [round(total * f) for f in (0.0,) + parts]
    plan, at = [], 0
    for i in range(pieces):
        for order, lo, hi in zip(orders, cuts[:-1], cuts[1:], strict=True):
            size = hi - lo
            left = size * (i + 1) // pieces - size * i // pieces
            while left:
                which = max(q for q in range(len(widths)) if bounds[q] <= at)
                step = min(left, bounds[which + 1] - at)
                start = at - bounds[which]
                plan.append((which, start, start + step, at + base, order, i))
                at += step
                left -= step
    return plan


def groups_of(plan):
    streams = {}
    for i, chunk in enumerate(plan):
        streams.setdefault(chunk[4], {}).setdefault(chunk[5], []).append(i)
    return streams


def spread_steps(steps, places):
    chosen = [(place, steps.pop(0)) for place in places[: len(steps)]]

    def run(t):
        for place, step in chosen:
            pl.when(t == place)(step)

    return run


FORWARD_PLACES = (1, (4,), (4,), ())
FORWARD_PIECES = 4
BACKWARD_PLACES = ((4,), (0, 6), (2, 6))
BACKWARD_PIECES = 4
MIDDLE_PIECES = 3
MIDDLE_TAKEN = 6


def gather_steps(sizes, plan, piece, outs, bw, send, recv):
    c = coords(lax.axis_index("seq"), sizes)
    most = max(sizes)

    def copies(i, k):
        which, lo, hi, at, order, _ = plan[i]
        ax = order[k]
        wide = pl.ds(lo * bw, (hi - lo) * bw)
        index = tuple(slice(None) if a in order[:k] else c[a] for a in range(3))
        index += (slice(None), wide)
        target = outs[which].at[index]
        source = target if k else piece.at[:, pl.ds(at * bw, (hi - lo) * bw)]
        return [
            remote(
                source,
                target,
                send.at[(i * 3 + k) * most + j],
                recv.at[(i * 3 + k) * most + j],
                neighbour(c, sizes, ax, j),
            )
            for j in range(1, sizes[ax])
        ]

    streams = groups_of(plan)
    longest = max(max(s) for s in streams.values()) + 1

    def step(s):
        for k in (2, 1, 0):
            for groups in streams.values():
                for i in groups.get(s - k, ()):
                    if k:
                        for copy in copies(i, k - 1):
                            copy.wait_recv()
                    for copy in copies(i, k):
                        copy.start()

    def arrived(piece_range):
        for groups in streams.values():
            for s in piece_range:
                for i in groups.get(s, ()):
                    for copy in copies(i, 2):
                        copy.wait_recv()

    def sent():
        for i in range(len(plan)):
            for k in range(3):
                for copy in copies(i, k):
                    copy.wait_send()

    return [functools.partial(step, s) for s in range(longest + 2)], arrived, sent


def scatter_scratch(sizes, plan, rows, bw, dtype, in_place=False):
    own, first, second, third = [], [], [], []
    for _, lo, hi, _, order, _ in plan:
        wide = (hi - lo) * bw
        rest = tuple(sizes[q] for q in range(3) if q != order[0])
        own.append(pltpu.VMEM(rest + (rows, wide), dtype))
        first.append(pltpu.VMEM((sizes[order[0]] - 1,) + rest + (rows, wide), dtype))
        second.append(pltpu.VMEM((sizes[order[1]], sizes[order[2]], rows, wide), dtype))
        third.append(pltpu.VMEM((sizes[order[2]], rows, wide), dtype))
    count = len(plan) * 3 * max(sizes)
    return (
        ([] if in_place else own)
        + first
        + second
        + third
        + [
            pltpu.SemaphoreType.DMA((count,)),
            pltpu.SemaphoreType.DMA((count,)),
            pltpu.SemaphoreType.DMA((len(plan),)),
        ]
    )


def scatter_steps(sizes, plan, grads, scratch, fin, bw, in_place=False):
    c = coords(lax.axis_index("seq"), sizes)
    most, count = max(sizes), len(plan)
    first, second, third = (scratch[-3 - (3 - i) * count :][:count] for i in range(3))
    send, recv, load = scratch[-3:]

    def part(i):
        which, lo, hi, _, order, _ = plan[i]
        index = tuple(c[q] if q == order[0] else slice(None) for q in range(3))
        index += (slice(None), pl.ds(lo * bw, (hi - lo) * bw))
        return grads[which].at[index]

    own = [part(i) for i in range(count)] if in_place else scratch[:count]

    def loading(i):
        return pltpu.make_async_copy(part(i), own[i], load.at[i])

    def copies(i, k):
        which, lo, hi, _, order, _ = plan[i]
        ax = order[k]
        left = sorted(set(range(3)) - set(order[:k]))
        result = []
        for j in range(1, sizes[ax]):
            there = lax.rem(c[ax] + j, sizes[ax])
            index = tuple(there if q == ax else slice(None) for q in left)
            if k == 0:
                index += (slice(None), pl.ds(lo * bw, (hi - lo) * bw))
                source, target = grads[which].at[index], first[i].at[j - 1]
            elif k == 1:
                source, target = own[i].at[index], second[i].at[j]
            else:
                source, target = second[i].at[(0,) + index], third[i].at[j]
            s = (i * 3 + k) * most + j
            result.append(
                remote(source, target, send.at[s], recv.at[s], neighbour(c, sizes, ax, j))
            )
        return result

    def combine(i, k):
        _, lo, hi, at, order, _ = plan[i]
        if k == 0 and not in_place:
            loading(i).wait()
        for copy in copies(i, k):
            copy.wait_recv()
        size = sizes[order[k]]
        if k == 0:
            outer, inner = own[i].shape[:2]

            def add(t, _):
                u, v = t // inner, t % inner
                total = own[i][u, v].astype(jnp.float32)
                for j in range(size - 1):
                    total = total + first[i][j, u, v].astype(jnp.float32)
                own[i][u, v] = total.astype(own[i].dtype)
                return 0

            lax.fori_loop(0, outer * inner, add, 0)
        elif k == 1:
            leading = sorted(set(range(3)) - {order[0]}).index(order[1]) == 0

            def add(t, _):
                total = own[i][(c[order[1]], t) if leading else (t, c[order[1]])]
                total = total.astype(jnp.float32)
                for j in range(1, size):
                    total = total + second[i][j, t].astype(jnp.float32)
                second[i][0, t] = total.astype(own[i].dtype)
                return 0

            lax.fori_loop(0, sizes[order[2]], add, 0)
        else:
            total = second[i][0, c[order[2]]].astype(jnp.float32)
            for j in range(1, size):
                total = total + third[i][j].astype(jnp.float32)
            for b in range(hi - lo):
                fin[at + b] = total[:, b * bw : (b + 1) * bw].astype(fin.dtype)

    streams = groups_of(plan)
    longest = max(max(s) for s in streams.values()) + 1

    def step(s):
        for k in range(4):
            for groups in streams.values():
                for i in groups.get(s - k, ()):
                    if k:
                        combine(i, k - 1)
                    elif not in_place:
                        loading(i).start()
                    if k < 3:
                        for copy in copies(i, k):
                            copy.start()

    def sent():
        for i in range(count):
            for k in range(3):
                for copy in copies(i, k):
                    copy.wait_send()

    return [functools.partial(step, s) for s in range(longest + 3)], sent


SPREAD = ((2, 1, 0), (1, 2, 0), (0, 1, 2))
COLLECT = ((0, 1, 2), (0, 2, 1), (2, 1, 0))
SHARES = (0.43, 0.86, 1.0)


def sum_steps(sizes, shared, x_ref, out_ref, mate, acc, bufs, send, recv):
    me, core = lax.axis_index("seq"), lax.axis_index("head")
    c = coords(me, sizes)
    most = max(sizes)
    swap = pltpu.make_async_remote_copy(
        src_ref=x_ref.at[pl.ds(0, shared)],
        dst_ref=mate,
        send_sem=send.at[0],
        recv_sem=recv.at[0],
        device_id={"head": 1 - core},
        device_id_type=MESH,
    )

    def going(step, ax):
        copies = []
        for j in range(1, sizes[ax]):
            d = list(c)
            d[ax] = lax.rem(c[ax] + j, sizes[ax])
            q = 1 + ax * most + j
            copies.append(
                remote(
                    acc.at[step], bufs.at[ax, c[ax]], send.at[q], recv.at[q], index_of(d, sizes)
                )
            )
        return copies

    def total(ax):
        value = bufs[ax, 0]
        for j in range(1, sizes[ax]):
            value = value + bufs[ax, j]
        return value

    def start(step, ax):
        bufs[ax, c[ax]] = acc[step]
        for copy in going(step, ax):
            copy.start()

    def swapped():
        swap.wait()
        acc[0, 0:shared] = x_ref[0:shared] + mate[...]
        acc[0, shared:] = x_ref[shared:]
        start(0, 2)

    def moved(step, ax):
        for copy in going(step, ax):
            copy.wait()
        if step < 2:
            acc[step + 1] = total(ax)
            start(step + 1, ax - 1)
        else:
            out_ref[...] = total(ax)

    return [
        swap.start,
        swapped,
        functools.partial(moved, 0, 2),
        functools.partial(moved, 1, 1),
        functools.partial(moved, 2, 0),
    ]


NN = (((1,), (0,)), ((), ()))
NT = (((1,), (1,)), ((), ()))
TN = (((0,), (0,)), ((), ()))
TILE = 128
LONGEST = 8192


def halves(values):
    high = values.astype(jnp.bfloat16)
    return high, (values - high.astype(jnp.float32)).astype(jnp.bfloat16)


def product(left, right, dims):
    (lh, ll), (rh, rl) = left, right
    dot = functools.partial(
        lax.dot_general, dimension_numbers=dims, preferred_element_type=jnp.float32
    )
    return dot(lh, rh) + (dot(lh, rl) + dot(ll, rh))


def running_sum(table, values):
    first = values.astype(jnp.bfloat16)
    rest = values - first.astype(jnp.float32)
    second, third = halves(rest)
    dot = functools.partial(
        lax.dot_general, dimension_numbers=NN, preferred_element_type=jnp.float32
    )
    return dot(table, first) + (dot(table, second) + dot(table, third))


def sigmoid(values):
    return 1.0 / (1.0 + jnp.exp(-values))


def chain_tools(n, sizes, forward, mine, bufs, send, recv, result):
    me = lax.axis_index("seq")
    c = coords(me, sizes)
    pieces = mine.shape[0]
    across, along, before, held = bufs
    most = max(sizes)
    state = pl.ds(0, TILE)
    decay = pl.ds(TILE, 1)

    def peers(ax):
        return [j for j in range(1, sizes[ax])]

    def to(ax, j):
        d = list(c)
        d[ax] = lax.rem(c[ax] + j, sizes[ax])
        return index_of(d, sizes)

    def line(buf, source, ax, j, p, base):
        s = base + j * pieces + p
        return remote(source.at[p], buf.at[c[ax], p], send.at[s], recv.at[s], to(ax, j))

    place = c[0] if forward else sizes[0] - 1 - c[0]

    def hop(k, p):
        s = (2 * most + k) * pieces + p
        step = 1 if forward else -1
        d = [lax.rem(c[0] + step + sizes[0], sizes[0]), c[1], c[2]]
        return remote(
            held.at[1 + 2 * k, p], held.at[2 * k, p], send.at[s], recv.at[s], index_of(d, sizes)
        )

    def compose(first, second):
        return (second[1] * first[0] + second[0], first[1] * second[1])

    def reduce_line(buf, ax, p):
        size = sizes[ax]
        order = range(size) if forward else range(size - 1, -1, -1)
        prefix = (jnp.zeros((TILE, TILE), jnp.float32), jnp.ones((1, TILE), jnp.float32))
        total = None
        for i in order:
            item = (buf[i, p, state], buf[i, p, decay])
            longer = compose(prefix, item)
            take = (i < c[ax]) if forward else (i > c[ax])
            prefix = tuple(jnp.where(take, a, b) for a, b in zip(longer, prefix, strict=True))
            total = item if total is None else compose(total, item)
        return prefix, total

    def start_x():
        for p in range(pieces):
            across[c[2], p] = mine[p]
            for j in peers(2):
                line(across, mine, 2, j, p, 0).start()

    def start_y():
        for p in range(pieces):
            for j in peers(2):
                line(across, mine, 2, j, p, 0).wait_recv()
            prefix, total = reduce_line(across, 2, p)
            before[p, state], before[p, decay] = prefix
            held[4, p, state], held[4, p, decay] = total
            held[4, p, pl.ds(TILE + 1, 7)] = jnp.zeros((7, TILE), jnp.float32)
            along[c[1], p] = held[4, p]
            for j in peers(1):
                line(along, held.at[4], 1, j, p, most * pieces).start()

    def start_z():
        for p in range(pieces):
            for j in peers(1):
                line(along, held.at[4], 1, j, p, most * pieces).wait_recv()
            prefix, total = reduce_line(along, 1, p)
            own = (before[p, state], before[p, decay])
            before[p, state], before[p, decay] = compose(prefix, own)
            held[1, p, state], held[1, p, decay] = total
            held[1, p, pl.ds(TILE + 1, 7)] = jnp.zeros((7, TILE), jnp.float32)

            @pl.when(place < sizes[0] - 1)
            def _():
                hop(0, p).start()

    def pass_z():
        @pl.when(place > 0)
        def _():
            for p in range(pieces):
                hop(0, p).wait_recv()

                @pl.when(place < sizes[0] - 1)
                def _():
                    got = (held[0, p, state], held[0, p, decay])
                    item = (held[1, p, state], held[1, p, decay])
                    held[3, p, state], held[3, p, decay] = compose(got, item)
                    held[3, p, pl.ds(TILE + 1, 7)] = jnp.zeros((7, TILE), jnp.float32)
                    hop(1, p).start()

    def finish():
        for p in range(pieces):

            @pl.when(place == 0)
            def _():
                result[p] = before[p, state]

            @pl.when(place == 1)
            def _():
                result[p] = before[p, decay] * held[0, p, state] + before[p, state]

            @pl.when(place > 1)
            def _():
                hop(1, p).wait_recv()
                result[p] = before[p, decay] * held[2, p, state] + before[p, state]

            for j in peers(2):
                line(across, mine, 2, j, p, 0).wait_send()
            for j in peers(1):
                line(along, held.at[4], 1, j, p, most * pieces).wait_send()

        @pl.when(place < sizes[0] - 1)
        def _():
            for p in range(pieces):
                hop(0, p).wait_send()

        @pl.when((place > 0) & (place < sizes[0] - 1))
        def _():
            for p in range(pieces):
                hop(1, p).wait_send()

    return [start_x, start_y, start_z, pass_z], finish


def greet(n, sizes, extra):
    c = coords(lax.axis_index("seq"), sizes)
    barrier = pltpu.get_barrier_semaphore()
    count = 0
    for ax in range(3):
        for j in range(1, sizes[ax]):
            d = list(c)
            d[ax] = lax.rem(c[ax] + j, sizes[ax])
            pl.semaphore_signal(
                barrier, inc=1, device_id={"seq": index_of(d, sizes)}, device_id_type=MESH
            )
            count += 1
    for index in extra:
        pl.semaphore_signal(barrier, inc=1, device_id={"seq": index}, device_id_type=MESH)
        count += 1
    pl.semaphore_wait(barrier, count)


def tile_masks(rows_ref, cols_ref, c):
    row = rows_ref[pl.ds(c, 1), :]
    col = cols_ref[pl.ds(pl.multiple_of(c * TILE, TILE), TILE), 6:7]
    i = lax.broadcasted_iota(jnp.int32, (TILE, TILE), 0)
    j = lax.broadcasted_iota(jnp.int32, (TILE, TILE), 1)
    return (i >= j) & (row == col)


def forward_kernel(
    n,
    sizes,
    plan,
    ready,
    owners_ref,
    lengths_ref,
    packing_ref,
    slot_ref,
    tokens_ref,
    norm_ref,
    down_ref,
    upper_ref,
    taps_ref,
    gain_ref,
    w_in_out,
    w_up_out,
    w_out_out,
    w_down_out,
    normed_out,
    lowrank_ref,
    logits_out,
    proj_out,
    halo_ref,
    gate_out,
    conv_out,
    cum_out,
    o_out,
    u_out,
    start_out,
    cols_ref,
    rows_ref,
    normed,
    logits_ref,
    proj_ref,
    gate_ref,
    conv_ref,
    cum_ref,
    o_ref,
    u_ref,
    start_ref,
    slots,
    piece,
    w_in,
    rim,
    segs,
    act,
    state,
    prev,
    a_send,
    a_recv,
    g_send,
    g_recv,
    l_sem,
    mine,
    across,
    along,
    before,
    held,
    result,
    send,
    recv,
):
    me = lax.axis_index("seq")
    c3 = coords(me, sizes)
    length, width = tokens_ref.shape
    tiles, channels = length // TILE, proj_ref.shape[1]
    keys = logits_ref.shape[1]
    rank = down_ref.shape[0]
    heads = keys // DK
    value = DV * heads
    slots_dev, _, bw = slot_ref.shape
    rows = piece.shape[0]
    scale = DK ** (-0.5)
    enter(n, me)

    def move(j):
        p = lax.rem(me + j, n)
        return remote(
            slot_ref.at[:, pl.ds(p * rows, rows), :],
            slots.at[pl.ds(me * slots_dev, slots_dev)],
            a_send.at[j],
            a_recv.at[j],
            p,
        )

    for j in range(1, n):
        move(j).start()
    local_move = pltpu.make_async_copy(
        slot_ref.at[:, pl.ds(me * rows, rows), :],
        slots.at[pl.ds(me * slots_dev, slots_dev)],
        l_sem.at[0],
    )
    local_move.start()
    edge = remote(
        tokens_ref.at[pl.ds(length - 16, 16)],
        rim,
        a_send.at[0],
        a_recv.at[0],
        lax.rem(me + 1, n),
    )

    @pl.when(me < n - 1)
    def _():
        edge.start()

    base = me * length
    where_col = base - 8 + lax.broadcasted_iota(jnp.int32, (length + 8, 1), 0)
    lane = lax.broadcasted_iota(jnp.int32, (tiles, TILE), 1)
    where_row = base + TILE * lax.broadcasted_iota(jnp.int32, (tiles, TILE), 0) + lane
    start = jnp.int32(0)
    seg_col = jnp.zeros((length + 8, 1), jnp.float32)
    seg_row = jnp.zeros((tiles, TILE), jnp.float32)
    for q in range(lengths_ref.shape[0]):
        seg_col += (where_col >= start).astype(jnp.float32)
        seg_row += (where_row >= start).astype(jnp.float32)
        start = start + lengths_ref[packing_ref[q]]
    filled = start
    segs[...] = seg_col + (where_col >= filled).astype(jnp.float32)
    rows_ref[...] = seg_row + (where_row >= filled).astype(jnp.float32)
    lane = lax.broadcasted_iota(jnp.int32, (TILE, TILE), 1)
    for c in range(tiles):
        lo = 8 + c * TILE
        own = segs[lo : lo + TILE]
        flags = [segs[lo - 1 : lo], segs[lo + TILE - 1 : lo + TILE]]
        flags += [segs[lo - s : lo - s + TILE] for s in (1, 2, 3)]
        flags = [(other == own).astype(jnp.float32) for other in flags]
        place = base + c * TILE + lax.broadcasted_iota(jnp.int32, (TILE, 1), 0)
        flags += [None, own, (place < filled).astype(jnp.float32)]
        total = jnp.zeros((TILE, TILE), jnp.float32)
        for k, flag in enumerate(flags):
            if flag is not None:
                total = jnp.where(lane == k, flag, total)
        cols_ref[c * TILE : (c + 1) * TILE, :] = total
    cols_ref[length : length + 8, :] = jnp.zeros((8, TILE), jnp.float32)

    def norm(values):
        values = values.astype(jnp.float32)
        inverse = lax.rsqrt(jnp.mean(values * values, axis=1, keepdims=True) + norm_epsilon)
        return (values * inverse * norm_ref[...]).astype(jnp.bfloat16)

    i = lax.broadcasted_iota(jnp.int32, (TILE, TILE), 0)
    j = lax.broadcasted_iota(jnp.int32, (TILE, TILE), 1)
    lower = (i >= j).astype(jnp.bfloat16)
    down_low = down_ref[...].astype(jnp.bfloat16)
    upper = halves(upper_ref[0:rank, :])

    def gates(c, _):
        at = pl.ds(pl.multiple_of(c * TILE, TILE), TILE)
        x = norm(tokens_ref[at, :])
        normed[at, :] = x
        low = lax.dot_general(x, down_low, NT, preferred_element_type=jnp.float32)
        lowrank_ref[at, :] = low
        logits = product(halves(low), upper, NN) + upper_ref[rank : rank + 1, :]
        logits_ref[at, :] = logits
        gate = jnp.minimum(logits, 0.0) - jnp.log1p(jnp.exp(-jnp.abs(logits)))
        cum_ref[at, :] = running_sum(lower, gate * (1.0 / gate_scale))
        return 0

    lax.fori_loop(0, tiles, gates, 0)
    flushes = []

    def flush(source, target):
        copy = pltpu.make_async_copy(source, target, l_sem.at[6 + len(flushes)])
        copy.start()
        flushes.append(copy)

    flush(normed, normed_out)
    flush(logits_ref, logits_out)
    flush(cum_ref, cum_out)

    @pl.when(me > 0)
    def _():
        edge.wait_recv()

    @pl.when(me == 0)
    def _():
        rim[...] = jnp.zeros_like(rim)

    rim[...] = norm(rim[...])

    local_move.wait()
    for j in range(1, n):
        move(j).wait()
    for b in range(owners_ref.shape[1]):
        piece[:, b * bw : (b + 1) * bw] = slots[owners_ref[0, b]]
    outs = (w_in, w_up_out, w_out_out, w_down_out)
    offset, owns = 0, []
    for q, out in enumerate(outs):
        columns = out.shape[4]
        owns.append(
            pltpu.make_async_copy(
                piece.at[:, pl.ds(offset, columns)],
                out.at[c3[0], c3[1], c3[2]],
                l_sem.at[1 + q],
            )
        )
        offset += columns
    for copy in owns:
        copy.start()
    steps, arrived, sent = gather_steps(sizes, plan, piece, outs, bw, g_send, g_recv)
    steps[0]()
    for copy in owns:
        copy.wait()
    for step in steps[1 : ready + 2]:
        step()
    arrived(range(ready))
    rest = list(steps[ready + 2 :])
    flush(w_in, w_in_out)

    for step in rest[: FORWARD_PLACES[0]]:
        step()
    del rest[: FORWARD_PLACES[0]]

    def project(r, _):
        at = pl.ds(pl.multiple_of(r * 256, 256), 256)
        x = normed[at, :]
        for lo in range(0, w_in.shape[4], 512):
            part = lax.dot_general(
                x,
                w_in[:, :, :, :, lo : lo + 512].reshape(width, 512),
                NN,
                preferred_element_type=jnp.float32,
            )
            if lo < channels:
                proj_ref[at, lo : lo + 512] = part.astype(proj_ref.dtype)
            else:
                gate_ref[at, lo - channels : lo - channels + 512] = part
        return 0

    lax.fori_loop(0, length // 256, project, 0)
    for lo in range(0, channels, 512):
        halo_ref[:, lo : lo + 512] = lax.dot_general(
            rim[...],
            w_in[:, :, :, :, lo : lo + 512].reshape(width, 512),
            NN,
            preferred_element_type=jnp.float32,
        ).astype(halo_ref.dtype)
    flush(proj_ref, proj_out)
    flush(gate_ref, gate_out)

    prev[...] = halo_ref[...]
    state[...] = jnp.zeros_like(state)
    mine[...] = jnp.zeros_like(mine)
    for p in range(mine.shape[0]):
        mine[p, TILE : TILE + 1] = jnp.ones((1, TILE), jnp.float32)
    run = spread_steps(rest, FORWARD_PLACES[1])

    def local(c, _):
        run(c)
        at = pl.ds(pl.multiple_of(c * TILE, TILE), TILE)
        for g in range(0, channels, 256):
            wide = slice(g, g + 256)
            block = jnp.concatenate(
                [prev[:, wide].astype(jnp.float32), proj_ref[at, wide].astype(jnp.float32)]
            )
            total = taps_ref[3:4, wide] * block[16:]
            for s in (1, 2, 3):
                total = total + taps_ref[3 - s : 4 - s, wide] * (
                    block[16 - s : 16 - s + TILE] * cols_ref[at, 1 + s : 2 + s]
                )
            conv_ref[at, wide] = total
            act[at, wide] = total * sigmoid(total)
        prev[...] = proj_ref[pl.ds(pl.multiple_of(c * TILE + TILE - 16, 16), 16), :]
        cum = cum_ref[at, :]
        last = cum[TILE - 1 : TILE]
        left = act[at, keys : 2 * keys] * jnp.exp(last - cum) * cols_ref[at, 1:2]
        decay = jnp.exp(last) * cols_ref[at, 0:1][TILE - 1 : TILE]
        for h in range(heads):
            kh = slice(h * DK, (h + 1) * DK)
            v = halves(act[at, 2 * keys + h * DV : 2 * keys + (h + 1) * DV])
            start_ref[c, h] = state[h]
            state[h] = state[h] * decay[:, kh] + product(v, halves(left[:, kh]), TN)
            for e in range(DV // TILE):
                p = h * (DV // TILE) + e
                mine[p, TILE : TILE + 1] = mine[p, TILE : TILE + 1] * decay[:, kh]
        return 0

    lax.fori_loop(0, tiles, local, 0)
    flush(conv_ref, conv_out)
    for h in range(heads):
        start_ref[tiles, h] = state[h]
        for e in range(DV // TILE):
            mine[h * (DV // TILE) + e, 0:TILE] = state[h, e * TILE : (e + 1) * TILE]
    stages, finish = chain_tools(
        n, sizes, True, mine, (across, along, before, held), send, recv, result
    )
    stages[0]()
    run_inside = spread_steps(rest, FORWARD_PLACES[2])

    def inside(c, _):
        for k, stage in enumerate(stages[1:]):
            pl.when(c == k + 1)(stage)
        run_inside(c)
        at = pl.ds(pl.multiple_of(c * TILE, TILE), TILE)
        cum = cum_ref[at, :]
        middle = cum[TILE // 2 - 1 : TILE // 2]
        q = act[at, 0:keys] * jnp.exp(cum - middle) * scale
        k = act[at, keys : 2 * keys] * jnp.exp(middle - cum)
        mask = tile_masks(rows_ref, cols_ref, c)
        for h in range(heads):
            kh = slice(h * DK, (h + 1) * DK)
            vh = slice(h * DV, (h + 1) * DV)
            scores = jnp.where(mask, product(halves(q[:, kh]), halves(k[:, kh]), NT), 0.0)
            v = halves(act[at, 2 * keys + h * DV : 2 * keys + (h + 1) * DV])
            o_ref[at, vh] = product(halves(scores), v, NN)
        return 0

    lax.fori_loop(0, tiles, inside, 0)
    finish()
    for h in range(heads):
        for e in range(DV // TILE):
            state[h, e * TILE : (e + 1) * TILE] = result[h * (DV // TILE) + e]

    run_outside = spread_steps(rest, FORWARD_PLACES[3])

    def outside(c, _):
        run_outside(c)
        at = pl.ds(pl.multiple_of(c * TILE, TILE), TILE)
        cum = cum_ref[at, :]
        q = act[at, 0:keys] * jnp.exp(cum) * scale * cols_ref[at, 0:1]
        decay = jnp.exp(cum[TILE - 1 : TILE]) * cols_ref[at, 0:1][TILE - 1 : TILE]
        for h in range(heads):
            kh = slice(h * DK, (h + 1) * DK)
            vh = slice(h * DV, (h + 1) * DV)
            begin = start_ref[c, h] + state[h]
            start_ref[c, h] = begin
            state[h] = state[h] * decay[:, kh]
            o = o_ref[at, vh] + product(halves(q[:, kh]), halves(begin), NT)
            o_ref[at, vh] = o
            inverse = lax.rsqrt(jnp.mean(o * o, axis=1, keepdims=True) + norm_epsilon)
            gate = gate_ref[at, vh]
            u_ref[at, vh] = (o * inverse * gain_ref[...] * (gate * sigmoid(gate))).astype(
                u_ref.dtype
            )
        return 0

    lax.fori_loop(0, tiles, outside, 0)
    for h in range(heads):
        start_ref[tiles, h] = start_ref[tiles, h] + state[h]
    flush(o_ref, o_out)
    flush(u_ref, u_out)
    flush(start_ref, start_out)
    for step in rest:
        step()
    groups = {chunk[5] for chunk in plan}
    arrived(sorted(g for g in groups if g >= ready))
    sent()
    for copy in flushes:
        copy.wait()

    @pl.when(me < n - 1)
    def _():
        edge.wait_send()


def forward(
    owners, lengths, packing, slot_copy, tokens, norm, down, upper, taps, gain, counts
):
    n = lax.axis_size("seq")
    sizes = axis_sizes(n)
    length, width = tokens.shape
    slots_dev, depth, bw = slot_copy.shape
    rows = depth // n
    keys, channels = upper.shape[1], taps.shape[1]
    heads = keys // DK
    value = heads * DV
    tiles = length // TILE
    blocks = sum(counts)
    ready = 2
    plan = build_plan(counts[:1], SHARES, ready, COLLECT)
    plan += [
        (which + 1, lo, hi, at, order, group + ready)
        for which, lo, hi, at, order, group in build_plan(
            counts[1:], SHARES, FORWARD_PIECES, COLLECT, counts[0]
        )
    ]
    f32, b16 = jnp.float32, jnp.bfloat16
    shape = jax.ShapeDtypeStruct
    vmem, anywhere = pl.BlockSpec(memory_space=pltpu.VMEM), pl.BlockSpec(memory_space=pl.ANY)
    smem = pl.BlockSpec(memory_space=pltpu.SMEM)
    kept = [
        ((length, width), b16),
        ((length, keys), f32),
        ((length, channels), b16),
        ((length, value), f32),
        ((length, channels), f32),
        ((length, keys), f32),
        ((length, value), f32),
        ((length, value), b16),
        ((tiles + 1, heads, DV, DK), f32),
    ]
    big = [shape(*k) for k in kept]
    outs = [shape(sizes + (rows, count * bw), b16) for count in counts]
    outs += [big[0], shape((length, down.shape[0]), f32), big[1], big[2]]
    outs += [shape((16, channels), b16)] + big[3:]
    outs += [shape((length + 8, TILE), f32), shape((tiles, TILE), f32)]
    specs = [anywhere] * 5 + [vmem, anywhere, anywhere, vmem] + [anywhere] * 6 + [vmem, vmem]
    most = max(sizes)
    copies = len(plan) * 3 * most
    result = pl.pallas_call(
        functools.partial(forward_kernel, n, sizes, plan, ready),
        out_shape=tuple(outs),
        in_specs=[smem] * 3 + [anywhere] + [vmem] * 6,
        out_specs=tuple(specs),
        scratch_shapes=[pltpu.VMEM(*k) for k in kept]
        + [
            pltpu.VMEM((n * slots_dev, rows, bw), b16),
            pltpu.VMEM((rows, blocks * bw), b16),
            pltpu.VMEM(sizes + (rows, counts[0] * bw), b16),
            pltpu.VMEM((16, width), b16),
            pltpu.VMEM((length + 8, 1), f32),
            pltpu.VMEM((length, channels), f32),
            pltpu.VMEM((heads, DV, DK), f32),
            pltpu.VMEM((16, channels), b16),
            pltpu.SemaphoreType.DMA((n,)),
            pltpu.SemaphoreType.DMA((n,)),
            pltpu.SemaphoreType.DMA((copies,)),
            pltpu.SemaphoreType.DMA((copies,)),
            pltpu.SemaphoreType.DMA((18,)),
        ]
        + chain_scratch(sizes, heads * DV // TILE, length),
        compiler_params=pltpu.CompilerParams(
            collective_id=1, has_side_effects=True, vmem_limit_bytes=60 << 20
        ),
    )(owners, lengths, packing, slot_copy, tokens, norm, down, upper, taps, gain)
    return [w.reshape(depth, w.shape[4]) for w in result[:4]], result[4:]


def chain_scratch(sizes, pieces, length):
    assert 2 * sizes[1] * sizes[2] * length >= LONGEST
    most = max(sizes)
    shape = (pieces, TILE + 8, TILE)
    return [
        pltpu.VMEM(shape, jnp.float32),
        pltpu.VMEM((sizes[2],) + shape, jnp.float32),
        pltpu.VMEM((sizes[1],) + shape, jnp.float32),
        pltpu.VMEM(shape, jnp.float32),
        pltpu.VMEM((5,) + shape, jnp.float32),
        pltpu.VMEM((pieces, TILE, TILE), jnp.float32),
        pltpu.SemaphoreType.DMA(((2 * most + 2) * pieces,)),
        pltpu.SemaphoreType.DMA(((2 * most + 2) * pieces,)),
    ]


def backward_kernel(
    n,
    sizes,
    plan,
    proj_in,
    halo_ref,
    conv_in,
    cum_in,
    logits_in,
    o_in,
    gate_in,
    du_in,
    start_in,
    cols_ref,
    rows_ref,
    taps_ref,
    gain_ref,
    g_up_ref,
    g_out_ref,
    dproj_out,
    dgate_out,
    dlogits_out,
    dtaps_ref,
    dgain_ref,
    early_ref,
    proj_ref,
    conv_ref,
    cum_ref,
    logits_ref,
    o_ref,
    gate_ref,
    du_ref,
    start_ref,
    dproj_ref,
    dgate_ref,
    dlogits_ref,
    t_sem,
    l_sem,
    do,
    dact,
    adjoint,
    ends,
    after,
    back,
    tail,
    mine,
    across,
    along,
    before,
    held,
    result,
    send,
    recv,
    b_sem,
    *scatter_refs,
):
    tiles, channels = proj_ref.shape[0] // TILE, proj_ref.shape[1]
    keys = cum_ref.shape[1]
    heads = keys // DK
    me = lax.axis_index("seq")
    by_tile = (
        (du_in, du_ref),
        (o_in, o_ref),
        (gate_in, gate_ref),
        (cum_in, cum_ref),
        (conv_in.at[:, pl.ds(0, keys)], conv_ref.at[:, pl.ds(0, keys)]),
    )
    rest = pl.ds(keys, channels - keys)
    whole = (
        (conv_in.at[:, rest], conv_ref.at[:, rest]),
        (start_in, start_ref),
        (proj_in, proj_ref),
        (logits_in, logits_ref),
        (dgate_ref, dgate_out),
        (dlogits_ref, dlogits_out),
        (dproj_ref, dproj_out),
    )

    def tile_load(q, c):
        at = pl.ds(pl.multiple_of(c * TILE, TILE), TILE)
        source, target = by_tile[q]
        return pltpu.make_async_copy(source.at[at], target.at[at], t_sem.at[q, c])

    def load(q):
        source, target = whole[q]
        return pltpu.make_async_copy(source, target, l_sem.at[q])

    for c in range(tiles - 1, -1, -1):
        for q in range(len(by_tile)):
            tile_load(q, c).start()
    for q in range(4):
        load(q).start()
    greet(n, sizes, (lax.rem(me + 1, n), lax.rem(me + n - 1, n)))
    steps, sent = scatter_steps(
        sizes, plan, [g_up_ref, g_out_ref], scatter_refs, early_ref, TILE
    )
    steps.pop(0)()
    run_local = spread_steps(steps, BACKWARD_PLACES[0])
    run_inside = spread_steps(steps, BACKWARD_PLACES[1])
    run_outside = spread_steps(steps, BACKWARD_PLACES[2])
    scale = DK ** (-0.5)
    i = lax.broadcasted_iota(jnp.int32, (TILE, TILE), 0)
    j = lax.broadcasted_iota(jnp.int32, (TILE, TILE), 1)
    upper = (i <= j).astype(jnp.bfloat16)
    adjoint[...] = jnp.zeros_like(adjoint)
    mine[...] = jnp.zeros_like(mine)
    dgain_ref[...] = jnp.zeros_like(dgain_ref)
    dtaps_ref[...] = jnp.zeros_like(dtaps_ref)
    for p in range(mine.shape[0]):
        mine[p, TILE : TILE + 1] = jnp.ones((1, TILE), jnp.float32)

    def local(t, _):
        run_local(t)
        c = tiles - 1 - t
        for q in range(len(by_tile)):
            tile_load(q, c).wait()
        at = pl.ds(pl.multiple_of(c * TILE, TILE), TILE)
        cum = cum_ref[at, :]
        pre = conv_ref[at, 0:keys]
        q = pre * sigmoid(pre) * jnp.exp(cum) * scale * cols_ref[at, 0:1]
        decay = jnp.exp(cum[TILE - 1 : TILE]) * cols_ref[at, 0:1][TILE - 1 : TILE]
        for h in range(heads):
            kh = slice(h * DK, (h + 1) * DK)
            vh = slice(h * DV, (h + 1) * DV)
            o = o_ref[at, vh]
            inverse = lax.rsqrt(jnp.mean(o * o, axis=1, keepdims=True) + norm_epsilon)
            gate = gate_ref[at, vh]
            sig = sigmoid(gate)
            du = du_ref[at, vh]
            unit = o * inverse
            dgate_ref[at, vh] = (
                du * (unit * gain_ref[...]) * (sig * (1.0 + gate * (1.0 - sig)))
            ).astype(dgate_ref.dtype)
            don = du * (gate * sig)
            dgain_ref[0:1] += jnp.sum(don * unit, axis=0, keepdims=True)
            scaled = gain_ref[...] * don
            grad = inverse * scaled - unit * (
                inverse * inverse * jnp.mean(scaled * o, axis=1, keepdims=True)
            )
            do[at, vh] = grad
            ends[c, h] = adjoint[h]
            adjoint[h] = adjoint[h] * decay[:, kh] + product(halves(grad), halves(q[:, kh]), TN)
            for e in range(DV // TILE):
                p = h * (DV // TILE) + e
                mine[p, TILE : TILE + 1] = mine[p, TILE : TILE + 1] * decay[:, kh]
        return 0

    lax.fori_loop(0, tiles, local, 0)
    load(4).start()
    for h in range(heads):
        for e in range(DV // TILE):
            mine[h * (DV // TILE) + e, 0:TILE] = adjoint[h, e * TILE : (e + 1) * TILE]
    stages, finish = chain_tools(
        n, sizes, False, mine, (across, along, before, held), send, recv, result
    )
    stages[0]()
    load(0).wait()
    load(1).wait()

    def inside(c, _):
        for k, stage in enumerate(stages[1:]):
            pl.when(c == k + 1)(stage)
        run_inside(c)
        at = pl.ds(pl.multiple_of(c * TILE, TILE), TILE)
        cum = cum_ref[at, :]
        middle = cum[TILE // 2 - 1 : TILE // 2]
        pre = conv_ref[at, 0 : 2 * keys]
        both = pre * sigmoid(pre)
        grow = jnp.exp(cum - middle) * scale
        fall = jnp.exp(middle - cum)
        enter_decay = jnp.exp(cum) * (scale * cols_ref[at, 0:1])
        mask = tile_masks(rows_ref, cols_ref, c)
        for h in range(heads):
            kh = slice(h * DK, (h + 1) * DK)
            vh = slice(h * DV, (h + 1) * DV)
            q = halves(both[:, kh] * grow[:, kh])
            k = halves(both[:, keys + h * DK : keys + (h + 1) * DK] * fall[:, kh])
            prev_v = conv_ref[at, 2 * keys + h * DV : 2 * keys + (h + 1) * DV]
            v = halves(prev_v * sigmoid(prev_v))
            grad = halves(do[at, vh])
            scores = halves(jnp.where(mask, product(q, k, NT), 0.0))
            dscores = halves(jnp.where(mask, product(grad, v, NT), 0.0))
            dact[at, h * DK : (h + 1) * DK] = (
                product(dscores, k, NN) * grow[:, kh]
                + product(grad, halves(start_ref[c, h]), NN) * enter_decay[:, kh]
            )
            dact[at, keys + h * DK : keys + (h + 1) * DK] = (
                product(dscores, q, TN) * fall[:, kh]
            )
            dact[at, 2 * keys + h * DV : 2 * keys + (h + 1) * DV] = product(scores, grad, TN)
        return 0

    lax.fori_loop(0, tiles, inside, 0)
    finish()
    for h in range(heads):
        for e in range(DV // TILE):
            adjoint[h, e * TILE : (e + 1) * TILE] = result[h * (DV // TILE) + e]
    after[...] = jnp.zeros_like(after)
    load(2).wait()
    load(3).wait()

    def outside(t, _):
        run_outside(t)
        c = tiles - 1 - t
        at = pl.ds(pl.multiple_of(c * TILE, TILE), TILE)
        cum = cum_ref[at, :]
        last = cum[TILE - 1 : TILE]
        remain = jnp.exp(last - cum) * cols_ref[at, 1:2]
        decay = jnp.exp(last) * cols_ref[at, 0:1][TILE - 1 : TILE]
        pre = conv_ref[at, 0 : 2 * keys]
        both = pre * sigmoid(pre)
        dkeys, edges = [], []
        for h in range(heads):
            kh = slice(h * DK, (h + 1) * DK)
            wide = slice(2 * keys + h * DV, 2 * keys + (h + 1) * DV)
            k = both[:, keys + h * DK : keys + (h + 1) * DK]
            end = ends[c, h] + adjoint[h]
            adjoint[h] = adjoint[h] * decay[:, kh]
            parts = halves(end)
            pre_v = conv_ref[at, wide]
            v = halves(pre_v * sigmoid(pre_v))
            dkeys.append(
                dact[at, keys + h * DK : keys + (h + 1) * DK]
                + product(v, parts, NN) * remain[:, kh]
            )
            dact[at, wide] += product(halves(k * remain[:, kh]), parts, NT)
            edges.append(jnp.sum(end * start_ref[c + 1, h], axis=0, keepdims=True))
        dk = jnp.concatenate(dkeys, axis=1)
        dq = dact[at, 0:keys]
        dact[at, keys : 2 * keys] = dk
        drift = both[:, 0:keys] * dq - both[:, keys:] * dk
        dl = running_sum(upper, drift) + jnp.concatenate(edges, axis=1)
        dlogits_ref[at, :] = dl * (1.0 / gate_scale) * sigmoid(-logits_ref[at, :])
        behind = jnp.where(
            c == 0,
            halo_ref[...],
            proj_ref[pl.ds(pl.multiple_of(jnp.maximum(c * TILE - 16, 0), 16), 16), :],
        )
        masks = cols_ref[pl.ds(pl.multiple_of(c * TILE, TILE), TILE + 8), :]
        for g in range(0, channels, 256):
            wide = slice(g, g + 256)
            pre = conv_ref[at, wide]
            sig = sigmoid(pre)
            dconv = dact[at, wide] * (sig * (1.0 + pre * (1.0 - sig)))
            block = jnp.concatenate(
                [
                    behind[:, g : g + 256].astype(jnp.float32),
                    proj_ref[at, wide].astype(jnp.float32),
                ]
            )
            grad = jnp.concatenate([dconv, after[:, wide]])
            total = taps_ref[3:4, wide] * dconv
            dtaps_ref[3:4, wide] += jnp.sum(dconv * block[16:], axis=0, keepdims=True)
            first = jnp.zeros((8, 256), jnp.float32)
            for s in (1, 2, 3):
                masked = grad * masks[:, 1 + s : 2 + s]
                tap = taps_ref[3 - s : 4 - s, wide]
                total = total + tap * masked[s : s + TILE]
                dtaps_ref[3 - s : 4 - s, wide] += jnp.sum(
                    masked[:TILE] * block[16 - s : 16 - s + TILE], axis=0, keepdims=True
                )
                first = first + tap * jnp.concatenate(
                    [jnp.zeros((8, 256), jnp.float32), masked[0:8]]
                )[s : s + 8]
            dproj_ref[at, wide] = total.astype(dproj_ref.dtype)
            after[:, wide] = dconv[0:8]
            back[0, :, wide] = first

            @pl.when(c == tiles - 1)
            def _():
                tail[:, wide] = total[TILE - 16 :]

        return 0

    lax.fori_loop(0, tiles, outside, 0)
    load(5).start()

    home = remote(
        back.at[0], back.at[1], b_sem.at[0], b_sem.at[1], lax.rem(me + n - 1, n)
    )

    @pl.when(me > 0)
    def _():
        home.start()

    for step in steps[:1]:
        step()

    @pl.when(me < n - 1)
    def _():
        home.wait_recv()

    @pl.when(me == n - 1)
    def _():
        back[1] = jnp.zeros(back.shape[1:], jnp.float32)

    dproj_ref[pl.ds(tiles * TILE - 16, 16), :] = (
        tail[...] + jnp.concatenate([jnp.zeros((8, channels), jnp.float32), back[1]])
    ).astype(dproj_ref.dtype)
    load(6).start()
    for step in steps[1:]:
        step()
    sent()

    @pl.when(me > 0)
    def _():
        home.wait_send()

    for q in (4, 5, 6):
        load(q).wait()


def recurrence_back(
    proj, halo, conv, cum, logits, o, gate, du, starts, cols, rows, taps, gain, grads
):
    n = lax.axis_size("seq")
    sizes = axis_sizes(n)
    length, channels = proj.shape
    keys = cum.shape[1]
    heads = keys // DK
    value = heads * DV
    tiles = length // TILE
    f32 = jnp.float32
    shape = jax.ShapeDtypeStruct
    depth = grads[0].shape[3]
    plan = build_plan(tuple(g.shape[4] // TILE for g in grads), SHARES, BACKWARD_PIECES, SPREAD)
    blocks = sum(g.shape[4] for g in grads) // TILE
    vmem, anywhere = pl.BlockSpec(memory_space=pltpu.VMEM), pl.BlockSpec(memory_space=pl.ANY)
    return pl.pallas_call(
        functools.partial(backward_kernel, n, sizes, plan),
        in_specs=[anywhere, vmem] + [anywhere] * 7 + [vmem] * 4 + [anywhere] * 2,
        out_specs=(anywhere,) * 3 + (vmem,) * 3,
        out_shape=(
            shape((length, channels), jnp.bfloat16),
            shape((length, value), jnp.bfloat16),
            shape((length, keys), f32),
            shape((8, channels), f32),
            shape((8, DV), f32),
            shape((blocks, depth, TILE), jnp.bfloat16),
        ),
        scratch_shapes=[
            pltpu.VMEM((length, channels), jnp.bfloat16),
            pltpu.VMEM((length, channels), f32),
            pltpu.VMEM((length, keys), f32),
            pltpu.VMEM((length, keys), f32),
            pltpu.VMEM((length, value), f32),
            pltpu.VMEM((length, value), f32),
            pltpu.VMEM((length, value), f32),
            pltpu.VMEM(starts.shape, f32),
            pltpu.VMEM((length, channels), jnp.bfloat16),
            pltpu.VMEM((length, value), jnp.bfloat16),
            pltpu.VMEM((length, keys), f32),
            pltpu.SemaphoreType.DMA((5, tiles)),
            pltpu.SemaphoreType.DMA((7,)),
            pltpu.VMEM((length, value), f32),
            pltpu.VMEM((length, channels), f32),
            pltpu.VMEM((heads, DV, DK), f32),
            pltpu.VMEM((tiles, heads, DV, DK), f32),
            pltpu.VMEM((8, channels), f32),
            pltpu.VMEM((2, 8, channels), f32),
            pltpu.VMEM((16, channels), f32),
        ]
        + chain_scratch(sizes, heads * DV // TILE, length)
        + [pltpu.SemaphoreType.DMA((2,))]
        + scatter_scratch(sizes, plan, depth, TILE, jnp.bfloat16),
        compiler_params=pltpu.CompilerParams(
            collective_id=5, has_side_effects=True, vmem_limit_bytes=60 << 20
        ),
    )(proj, halo, conv, cum, logits, o, gate, du, starts, cols, rows, taps, gain, *grads)


def tail_kernel(
    n,
    sizes,
    plan,
    shared,
    taken,
    inv_ref,
    early_ref,
    later_ref,
    dproj_ref,
    dgate_ref,
    normed_ref,
    dlogits_ref,
    lowrank_ref,
    upper_ref,
    down_ref,
    gain_ref,
    gains_two_ref,
    dtaps_ref,
    dhead_ref,
    w_ref,
    tokens_ref,
    dh_ref,
    left_ref,
    out_ref,
    small_out,
    grad_ref,
    left_out,
    grads,
    weights,
    tokens,
    dh,
    total,
    trade,
    fin,
    send,
    small,
    wide,
    narrow,
    b_sem,
    a_send,
    a_recv,
    s_send,
    s_recv,
    l_sem,
    *refs,
):
    me, core = lax.axis_index("seq"), lax.axis_index("head")
    slots, _, rows, bw = out_ref.shape
    length, width = normed_ref.shape
    channels = dproj_ref.shape[1]
    keys, rank, tap_count = dlogits_ref.shape[1], down_ref.shape[0], 4
    downs = early_ref.shape[0] - taken
    count = fin.shape[0] - 1 - early_ref.shape[0] - later_ref.shape[0]
    tiles = s_send.shape[0]
    step_rows = length // tiles
    f32 = jnp.float32
    dot = functools.partial(lax.dot_general, preferred_element_type=f32)
    enter(n, me, True)
    loads = [
        pltpu.make_async_copy(source, target, l_sem.at[1 + q])
        for q, (source, target) in enumerate(((w_ref, weights), (tokens_ref, tokens), (dh_ref, dh)))
    ]
    for load in loads:
        load.start()
    block = wide.shape[1]
    per_slot = left_ref.shape[1] // block
    total_blocks = left_ref.shape[0] * per_slot

    def basis_load(k):
        at = (k // per_slot, pl.ds(k % per_slot * block, block))
        return pltpu.make_async_copy(left_ref.at[at], wide.at[k % 2], b_sem.at[k % 2])

    def basis_store(k):
        at = (k // per_slot, pl.ds(k % per_slot * block, block))
        return pltpu.make_async_copy(narrow.at[k % 2], left_out.at[at], b_sem.at[2 + k % 2])

    pending = list(range(total_blocks))

    def narrow_basis(count):
        for k in pending[:count]:
            basis_load(k).wait()
            if k >= 2:
                basis_store(k - 2).wait()
            narrow[k % 2] = wide[k % 2].astype(narrow.dtype)
            basis_store(k).start()
            if k + 2 < total_blocks:
                basis_load(k + 2).start()
        del pending[:count]

    for k in range(min(2, total_blocks)):
        basis_load(k).start()
    steps, sent = scatter_steps(sizes, plan, [grads], refs[:-5], fin, bw, in_place=True)
    sums = sum_steps(sizes, shared, small, small_out, *refs[-5:])

    def block_grads(lo, hi):
        for source, base in ((dproj_ref, 0), (dgate_ref, channels)):
            first, last = max(lo - base, 0), min(hi - base, source.shape[1])
            if first >= last:
                continue

            part = dot(normed_ref[...], source[:, first:last], dimension_numbers=TN)
            grads[:, :, :, :, base + first : base + last] = part.astype(grads.dtype).reshape(
                sizes + (rows, last - first)
            )

    cut = max(hi for _, _, hi, _, _, group in plan if group == 0) * bw
    block_grads(0, cut)
    steps[0]()
    block_grads(cut, grads.shape[4])
    steps[1]()
    fin[fin.shape[0] - 1] = jnp.zeros(fin.shape[1:], fin.dtype)
    if taken:
        fin[count : count + taken] = early_ref[downs:]
    fin[count + taken : fin.shape[0] - 1 - downs] = later_ref[...]
    fin[fin.shape[0] - 1 - downs : fin.shape[0] - 1] = early_ref[0:downs]

    def swap(t):
        at = pl.ds(t * step_rows, step_rows)
        return pltpu.make_async_remote_copy(
            src_ref=total.at[at],
            dst_ref=trade.at[at],
            send_sem=s_send.at[t],
            recv_sem=s_recv.at[t],
            device_id={"head": 1 - core},
            device_id_type=MESH,
        )

    for load in loads:
        load.wait()
    upper = halves(upper_ref[0:rank, :])
    down_low = down_ref[...].astype(jnp.bfloat16)
    small[...] = jnp.zeros_like(small)
    upper_grad = jnp.zeros((rank, keys), f32)
    bias_grad = jnp.zeros((1, keys), f32)
    for t in range(tiles):
        at = slice(t * step_rows, (t + 1) * step_rows)
        dlogits = dlogits_ref[at, :]
        parts = halves(dlogits)
        dlow = product(parts, upper, NT).astype(jnp.bfloat16)
        upper_grad += product(halves(lowrank_ref[at, :]), parts, TN)
        bias_grad += jnp.sum(dlogits, axis=0, keepdims=True)
        small[0:rank, :] += dot(dlow, normed_ref[at, :], dimension_numbers=TN)
        part = (
            dot(dproj_ref[at, :], weights[:, :channels], dimension_numbers=NT)
            + dot(dgate_ref[at, :], weights[:, channels:], dimension_numbers=NT)
            + dot(dlow, down_low, dimension_numbers=NN)
        )
        total[at, :] = part.astype(total.dtype)
        swap(t).start()
        tok = tokens[at, :].astype(f32)
        inverse = lax.rsqrt(jnp.mean(tok * tok, axis=1, keepdims=True) + norm_epsilon)
        small[rank + 1 : rank + 2, :] += jnp.sum(part * (tok * inverse), axis=0, keepdims=True)
    small[rank : rank + 1, 0:DV] = dhead_ref[0:1, :]
    small[shared : shared + 1, :] = gains_two_ref[0:1, :]
    small[shared + 1 : shared + 1 + tap_count, :] = dtaps_ref[0:tap_count, :]
    per = width // keys
    base = shared + 1 + tap_count
    for r in range(rank + 1):
        row = bias_grad if r == rank else upper_grad[r : r + 1]
        small[base + r // per : base + r // per + 1, (r % per) * keys : (r % per + 1) * keys] = row
    sums[0]()
    narrow_basis(2)
    steps[2]()
    sums[1]()

    for t in range(tiles):
        at = slice(t * step_rows, (t + 1) * step_rows)
        swap(t).wait_recv()
        dxn = total[at, :].astype(f32) + trade[at, :].astype(f32)
        tok = tokens[at, :].astype(f32)
        inverse = lax.rsqrt(jnp.mean(tok * tok, axis=1, keepdims=True) + norm_epsilon)
        scaled = gain_ref[...] * dxn
        mean = jnp.mean(scaled * tok, axis=1, keepdims=True)
        dh[at, :] = dh[at, :] + (
            inverse * scaled - tok * (inverse * inverse * inverse * mean)
        )
    store = pltpu.make_async_copy(dh, grad_ref, l_sem.at[4])
    store.start()
    for s, step in enumerate(steps[3:]):
        narrow_basis(3)
        step()
        if s + 2 < len(sums):
            sums[s + 2]()
    for s in range(send.shape[0]):
        send[s] = fin[inv_ref[0, s]]

    def move(j):
        p = lax.rem(me + j, n)
        return remote(
            send.at[pl.ds(p * slots, slots)], out_ref.at[:, me], a_send.at[j], a_recv.at[j], p
        )

    for j in range(1, n):
        move(j).start()
    mine = pltpu.make_async_copy(
        send.at[pl.ds(me * slots, slots)], out_ref.at[:, me], l_sem.at[0]
    )
    mine.start()
    for step in sums[len(steps) - 1 :]:
        step()
    narrow_basis(len(pending))
    mine.wait()
    for j in range(1, n):
        move(j).wait()
    sent()
    for k in range(max(0, total_blocks - 2), total_blocks):
        basis_store(k).wait()
    for t in range(tiles):
        swap(t).wait_send()
    store.wait()


def tail(
    inverse, early, later, dproj, dgate, normed, dlogits, lowrank, upper, down, gain, gains_two,
    dtaps, dhead, weights, tokens, dh, left, slots, taken
):
    n = lax.axis_size("seq")
    sizes = axis_sizes(n)
    most = max(sizes)
    length, width = normed.shape
    _, rows, bw = early.shape
    columns = dproj.shape[1] + dgate.shape[1]
    blocks = columns // bw
    rank = down.shape[0]
    shared = rank + 8
    plan = build_plan((blocks,), SHARES, 3, SPREAD)
    shape = jax.ShapeDtypeStruct
    vmem, anywhere = pl.BlockSpec(memory_space=pltpu.VMEM), pl.BlockSpec(memory_space=pl.ANY)
    b16, f32 = jnp.bfloat16, jnp.float32
    small = (shared + 16, width)
    tiles = 4
    out, summed, grad, left = pl.pallas_call(
        functools.partial(tail_kernel, n, sizes, plan, shared, taken),
        out_shape=(
            shape((slots, n, rows, bw), b16),
            shape(small, f32),
            shape((length, width), f32),
            shape(left.shape, b16),
        ),
        in_specs=[pl.BlockSpec(memory_space=pltpu.SMEM)] + [vmem] * 13 + [anywhere] * 4,
        out_specs=(anywhere, vmem, anywhere, anywhere),
        scratch_shapes=[
            pltpu.VMEM(sizes + (rows, columns), b16),
            pltpu.VMEM((width, columns), b16),
            pltpu.VMEM((length, width), b16),
            pltpu.VMEM((length, width), f32),
            pltpu.VMEM((length, width), b16),
            pltpu.VMEM((length, width), b16),
            pltpu.VMEM((blocks + early.shape[0] + later.shape[0] + 1, rows, bw), b16),
            pltpu.VMEM((slots * n, rows, bw), b16),
            pltpu.VMEM(small, f32),
            pltpu.VMEM((2, width // 4, width), f32),
            pltpu.VMEM((2, width // 4, width), b16),
            pltpu.SemaphoreType.DMA((4,)),
            pltpu.SemaphoreType.DMA((n,)),
            pltpu.SemaphoreType.DMA((n,)),
            pltpu.SemaphoreType.DMA((tiles,)),
            pltpu.SemaphoreType.DMA((tiles,)),
            pltpu.SemaphoreType.DMA((5,)),
        ]
        + scatter_scratch(sizes, plan, rows, bw, b16, in_place=True)
        + [
            pltpu.VMEM((shared, width), f32),
            pltpu.VMEM((3,) + small, f32),
            pltpu.VMEM((3, most) + small, f32),
            pltpu.SemaphoreType.DMA((1 + 3 * most,)),
            pltpu.SemaphoreType.DMA((1 + 3 * most,)),
        ],
        compiler_params=pltpu.CompilerParams(
            collective_id=2, has_side_effects=True, vmem_limit_bytes=60 << 20
        ),
    )(
        inverse, early, later, dproj, dgate, normed, dlogits, lowrank, upper, down, gain, gains_two,
        dtaps, dhead, weights, tokens, dh, left
    )
    return out.reshape(slots, width, bw), summed, grad, left


def adam_kernel(
    rates,
    rank,
    taps,
    grad_ref,
    left_ref,
    right_ref,
    master_ref,
    first_ref,
    second_ref,
    summed_ref,
    *refs,
):
    params = [refs[3 * q : 3 * q + 3] for q in range(5)]
    grad_in, result_in = refs[15:17]
    grad_out, master_out, first_out, second_out, copy_out = refs[17:22]
    news = [refs[22 + 4 * q : 26 + 4 * q] for q in range(5)]
    grad_pass, result_ref = refs[42:]
    grad_pass[...] = grad_in[...]
    result_ref[...] = result_in[...]

    @pl.when(pl.program_id(0) == 0)
    def _():
        shared = rank + 8
        width = summed_ref.shape[1]
        keys = news[2][0].shape[1]
        per = width // keys
        base = shared + 1 + taps
        gains, down, upper, head, conv = news
        gains[0][0:1, :] = summed_ref[rank + 1 : rank + 2, :]
        gains[0][1:2, :] = summed_ref[shared : shared + 1, :]
        down[0][...] = summed_ref[0:rank, :]
        for r in range(rank + 1):
            upper[0][r : r + 1, :] = summed_ref[
                base + r // per : base + r // per + 1, (r % per) * keys : (r % per + 1) * keys
            ]
        head[0][...] = summed_ref[rank : rank + 1, 0:DV]
        conv[0][...] = summed_ref[shared + 1 : shared + 1 + taps, :]
        for (value, first, second), new, rate in zip(params, news, rates, strict=True):
            new[1][...], new[2][...], new[3][...] = plain_adam(
                value[...], new[0][...], first[...], second[...], rate
            )

    width = left_ref.shape[1]
    step = min(256, width)
    dot = functools.partial(
        lax.dot_general, dimension_numbers=TN, preferred_element_type=jnp.float32
    )
    grad_out[0] = grad_ref[0].astype(jnp.float32)
    left = left_ref[0]
    dot = functools.partial(lax.dot_general, preferred_element_type=jnp.float32)
    right = halves(right_ref[0])
    rotated = dot(left, grad_ref[0], dimension_numbers=TN)
    rotated = product(halves(rotated), right, NN)
    first = moment_decay * first_ref[0] + (1.0 - moment_decay) * rotated
    second = moment_decay * second_ref[0] + (1.0 - moment_decay) * rotated * rotated
    first_out[0] = first
    second_out[0] = second
    direction = first / (jnp.sqrt(second) + adam_epsilon)
    turned = product(halves(direction), right, NT).astype(left.dtype)
    master = master_ref[0] - rate_block * dot(left, turned, dimension_numbers=NN)
    master_out[0] = master
    copy_out[0] = master.astype(copy_out.dtype)


def all_adam(grads, left, right, master, first, second, summed, params, grad, result):
    slots, width, columns = master.shape
    tall = pl.BlockSpec((1, width, columns), lambda i: (i, 0, 0))
    length, model = grad.shape
    wide = pl.BlockSpec((length // slots, model), lambda i: (i, 0))
    shape = jax.ShapeDtypeStruct
    full = shape(master.shape, jnp.float32)

    def whole(array):
        return pl.BlockSpec(array.shape, lambda i: (0, 0))

    flat = [array for triple in params for array in triple]
    rates = (rate_gains, rate_down, rate_upper, rate_head, rate_conv)
    news = [triple[0] for triple in params for _ in range(4)]
    return pl.pallas_call(
        functools.partial(adam_kernel, rates, params[1][0].shape[0], params[4][0].shape[0]),
        grid=(slots,),
        out_shape=tuple(
            [full] * 4
            + [shape(master.shape, jnp.bfloat16)]
            + [shape(new.shape, new.dtype) for new in news]
            + [shape(grad.shape, jnp.float32), shape(grad.shape, jnp.bfloat16)]
        ),
        in_specs=[
            tall,
            pl.BlockSpec((1, width, width), lambda i: (i, 0, 0)),
            pl.BlockSpec((1, columns, columns), lambda i: (i, 0, 0)),
            tall,
            tall,
            tall,
            whole(summed),
        ]
        + [whole(array) for array in flat]
        + [wide] * 2,
        out_specs=[tall] * 5 + [whole(new) for new in news] + [wide] * 2,
        compiler_params=pltpu.CompilerParams(vmem_limit_bytes=56 << 20),
    )(grads, left, right, master, first, second, summed, *flat, grad, result)


def middle_kernel(
    n,
    sizes,
    plan,
    u_ref,
    w_out_ref,
    cols_ref,
    gain_ref,
    tokens_ref,
    w_up_ref,
    w_down_ref,
    cot_ref,
    early_ref,
    sum_ref,
    result_out,
    dh_out,
    du_out,
    g_up_out,
    g_out_out,
    w_up,
    w_down,
    mixed,
    hidden_sum,
    normed,
    inv,
    dy,
    hid,
    dpair,
    send,
    recv,
    g_down,
    g_up,
    g_out,
    du,
    free,
    s_sem,
    r_sem,
    l_sem,
    *scatter_refs,
):
    me, core = lax.axis_index("seq"), lax.axis_index("head")
    length, width = normed.shape
    inner = hid.shape[1]
    rows = g_out.shape[3]
    f32 = jnp.float32
    dot = functools.partial(lax.dot_general, preferred_element_type=f32)
    tiles = s_sem.shape[0] // 3
    block = length // tiles
    ats = [slice(t * block, (t + 1) * block) for t in range(tiles)]
    enter(n, me, True)
    loads = [
        pltpu.make_async_copy(source, target, l_sem.at[q])
        for q, (source, target) in enumerate(
            ((tokens_ref, mixed), (w_up_ref, w_up), (w_down_ref, w_down), (cot_ref, dy))
        )
    ]
    for load in loads:
        load.start()
    flushes = []

    def flush(source, target):
        copy = pltpu.make_async_copy(source, target, l_sem.at[4 + len(flushes)])
        copy.start()
        flushes.append(copy)

    steps, sent = scatter_steps(
        sizes, plan, [g_down, g_up], scatter_refs, early_ref, TILE, in_place=True
    )

    def advance(count=1):
        for step in steps[:count]:
            step()
        del steps[:count]

    def swap(phase, t):
        at = pl.ds(t * block, block)
        return pltpu.make_async_remote_copy(
            src_ref=send.at[at],
            dst_ref=recv.at[at],
            send_sem=s_sem.at[phase * tiles + t],
            recv_sem=r_sem.at[phase * tiles + t],
            device_id={"head": 1 - core},
            device_id_type=MESH,
        )

    def exchange(phase, left, right, close):
        if phase:
            for t in range(tiles):
                swap(phase - 1, t).wait_send()
            pl.semaphore_wait(free, 1)
        for t, at in enumerate(ats):
            send[at, :] = dot(left[at, :], right[...], dimension_numbers=NT).astype(send.dtype)
            swap(phase, t).start()
            if t:
                swap(phase, t - 1).wait_recv()
                close(ats[t - 1])
        swap(phase, tiles - 1).wait_recv()
        close(ats[-1])
        if phase < 2:
            pl.semaphore_signal(
                free, inc=1, device_id={"head": 1 - core}, device_id_type=MESH
            )

    def both(at):
        return send[at, :].astype(f32) + recv[at, :].astype(f32)

    loads[0].wait()

    def close_attn(at):
        total = mixed[at, :].astype(f32) + both(at)
        inverse = lax.rsqrt(jnp.mean(total * total, axis=1, keepdims=True) + norm_epsilon)
        hidden_sum[at, :] = total
        inv[at, :] = inverse
        normed[at, :] = (total * inverse * gain_ref[...]).astype(normed.dtype)

    exchange(0, u_ref, w_out_ref, close_attn)
    for load in loads[1:]:
        load.wait()

    def feed(t, _):
        at = pl.ds(pl.multiple_of(t * block, block), block)
        x = normed[at, :]
        grad_y = (dy[at, :].astype(f32) * cols_ref[at, 7:8]).astype(dy.dtype)
        dy[at, :] = grad_y
        for lo in range(0, inner, 512):
            hi = min(lo + 512, inner)
            gate = dot(x, w_up[:, lo:hi], dimension_numbers=NN)
            up = dot(x, w_up[:, inner + lo : inner + hi], dimension_numbers=NN)
            grad = dot(grad_y, w_down[:, lo:hi], dimension_numbers=NN)
            sig = sigmoid(gate)
            swish = gate * sig
            hid[at, lo:hi] = (swish * up).astype(hid.dtype)
            dpair[at, lo:hi] = (grad * up * (sig + swish * (1.0 - sig))).astype(dpair.dtype)
            dpair[at, inner + lo : inner + hi] = (grad * swish).astype(dpair.dtype)
        return 0

    lax.fori_loop(0, tiles, feed, 0)

    def block_grads(left, source, target, lo, hi):
        for first in range(lo, hi, 512):
            last = min(first + 512, hi)
            part = dot(left[...], source[:, first:last], dimension_numbers=TN)
            target[:, :, :, :, first:last] = part.astype(target.dtype).reshape(
                sizes + (rows, last - first)
            )

    block_grads(dy, hid, g_down, 0, inner)
    advance()
    block_grads(normed, dpair, g_up, 0, inner)
    advance()
    block_grads(normed, dpair, g_up, inner, 2 * inner)
    taken = g_up.shape[4] - g_up_out.shape[4]
    flush(g_up.at[:, :, :, :, pl.ds(taken, g_up_out.shape[4])], g_up_out)

    def close_mlp(at):
        mixed[at, :] = (hidden_sum[at, :] + both(at)).astype(mixed.dtype)

    exchange(1, hid, w_down, close_mlp)
    flush(mixed, result_out)
    advance()

    sum_ref[...] = jnp.zeros_like(sum_ref)

    def close_back(at):
        grad = both(at)
        total, inverse = hidden_sum[at, :], inv[at, :]
        unit = total * inverse
        scaled = gain_ref[...] * grad
        mean = jnp.mean(scaled * total, axis=1, keepdims=True)
        dh = dy[at, :].astype(f32) + (inverse * scaled - unit * (inverse * inverse * mean))
        hidden_sum[at, :] = dh
        normed[at, :] = dh.astype(normed.dtype)
        sum_ref[0:1, :] += jnp.sum(grad * unit, axis=0, keepdims=True)
        du[at, :] = dot(normed[at, :], w_out_ref[...], dimension_numbers=NN)

    exchange(2, dpair, w_up, close_back)
    flush(hidden_sum, dh_out)
    flush(du, du_out)
    advance()
    block_grads(normed, u_ref, g_out, 0, u_ref.shape[1])
    flush(g_out, g_out_out)
    advance(len(steps))
    sent()
    for t in range(tiles):
        swap(2, t).wait_send()
    for copy in flushes:
        copy.wait()


def middle(u, w_out, cols, gain, tokens, w_up, w_down, cot, taken):
    n = lax.axis_size("seq")
    sizes = axis_sizes(n)
    length, width = tokens.shape
    value, inner = u.shape[1], w_down.shape[1]
    rows = width // n
    f32, b16 = jnp.float32, jnp.bfloat16
    blocks = inner // TILE
    plan = build_plan((blocks, taken) if taken else (blocks,), SHARES, MIDDLE_PIECES, SPREAD)
    shape = jax.ShapeDtypeStruct
    vmem, anywhere = pl.BlockSpec(memory_space=pltpu.VMEM), pl.BlockSpec(memory_space=pl.ANY)
    tiles = 4
    return pl.pallas_call(
        functools.partial(middle_kernel, n, sizes, plan),
        out_shape=(
            shape((blocks + taken, rows, TILE), b16),
            shape((8, width), f32),
            shape((length, width), b16),
            shape((length, width), f32),
            shape((length, value), f32),
            shape(sizes + (rows, 2 * inner - taken * TILE), b16),
            shape(sizes + (rows, value), b16),
        ),
        in_specs=[vmem] * 4 + [anywhere] * 4,
        out_specs=(vmem, vmem) + (anywhere,) * 5,
        scratch_shapes=[
            pltpu.VMEM((width, 2 * inner), b16),
            pltpu.VMEM((width, inner), b16),
            pltpu.VMEM((length, width), b16),
            pltpu.VMEM((length, width), f32),
            pltpu.VMEM((length, width), b16),
            pltpu.VMEM((length, 1), f32),
            pltpu.VMEM((length, width), b16),
            pltpu.VMEM((length, inner), b16),
            pltpu.VMEM((length, 2 * inner), b16),
            pltpu.VMEM((length, width), b16),
            pltpu.VMEM((length, width), b16),
            pltpu.VMEM(sizes + (rows, inner), b16),
            pltpu.VMEM(sizes + (rows, 2 * inner), b16),
            pltpu.VMEM(sizes + (rows, value), b16),
            pltpu.VMEM((length, value), f32),
            pltpu.SemaphoreType.REGULAR,
            pltpu.SemaphoreType.DMA((3 * tiles,)),
            pltpu.SemaphoreType.DMA((3 * tiles,)),
            pltpu.SemaphoreType.DMA((9,)),
        ]
        + scatter_scratch(sizes, plan, rows, TILE, b16, in_place=True),
        compiler_params=pltpu.CompilerParams(
            collective_id=6, has_side_effects=True, vmem_limit_bytes=62 << 20
        ),
    )(u, w_out, cols, gain, tokens, w_up, w_down, cot)


def plain_adam(param, gradient, first, second, rate):
    first_next = moment_decay * first + (1.0 - moment_decay) * gradient
    second_next = moment_decay * second + (1.0 - moment_decay) * gradient * gradient
    return (
        param - rate * first_next / (jnp.sqrt(second_next) + adam_epsilon),
        first_next,
        second_next,
    )


def body(
    tokens,
    cotangent,
    lengths,
    packing,
    owners,
    slot_copy,
    slot_master,
    slot_first,
    slot_second,
    basis_left,
    basis_right,
    norm_gains,
    gains_first,
    gains_second,
    gate_down,
    down_first,
    down_second,
    gate_up,
    upper_first,
    upper_second,
    head_gain,
    head_first,
    head_second,
    conv_weight,
    conv_first,
    conv_second,
):
    tok_rows = tokens.shape[0]
    model_width = tokens.shape[1]
    block_width = slot_copy.shape[2]
    tap_count = conv_weight.shape[0]
    key_width = gate_up.shape[1]
    channels = conv_weight.shape[1]
    value_width = channels - 2 * key_width
    block_total = owners.shape[1]
    count_in = (channels + value_width) // block_width
    count_out = value_width // block_width
    count_down = (block_total - count_in - count_out) // 3
    count_up = 2 * count_down
    (in_weights, up_weights, out_weights, down_weights), kept = forward(
        owners,
        lengths,
        packing,
        slot_copy,
        tokens,
        norm_gains[0:1],
        gate_down.T,
        gate_up,
        conv_weight,
        head_gain[None],
        (count_in, count_up, count_out, count_down),
    )
    normed, lowrank, logits, mixed_proj, halo, gate_pre = kept[:6]
    conv_pre, cumulative, attended, gated_out, starts, cols, rows = kept[6:]
    gain_row = head_gain[None]
    early, gains_two, result, grad_one, grad_gated, grad_up, grad_out = middle(
        gated_out,
        out_weights,
        cols,
        norm_gains[1:2],
        tokens,
        up_weights,
        down_weights,
        cotangent,
        MIDDLE_TAKEN,
    )
    grad_mixed, grad_gate_pre, grad_logits, tap_grads, gain_grads, later = recurrence_back(
        mixed_proj,
        halo,
        conv_pre,
        cumulative,
        logits,
        attended,
        gate_pre,
        grad_gated,
        starts,
        cols,
        rows,
        conv_weight,
        gain_row,
        (grad_up, grad_out),
    )
    slots_dev = slot_copy.shape[0]
    slot_total = slots_dev * lax.axis_size("seq")
    named = jnp.arange(slot_total, dtype=jnp.int32)[:, None] == owners
    inverse = jnp.where(
        jnp.any(named, axis=1),
        jnp.sum(named * jnp.arange(block_total, dtype=jnp.int32), axis=1),
        block_total,
    ).astype(jnp.int32)[None]
    owned_grads, summed, grad_input, left_low = tail(
        inverse,
        early,
        later,
        grad_mixed,
        grad_gate_pre,
        normed,
        grad_logits,
        lowrank,
        gate_up,
        gate_down.T,
        norm_gains[0:1],
        gains_two,
        tap_grads,
        gain_grads,
        in_weights,
        tokens,
        grad_one,
        basis_left,
        slots_dev,
        MIDDLE_TAKEN,
    )
    params = (
        (norm_gains, gains_first, gains_second),
        (gate_down.T, down_first.T, down_second.T),
        (gate_up, upper_first, upper_second),
        (head_gain[None], head_first[None], head_second[None]),
        (conv_weight, conv_first, conv_second),
    )
    (
        owned_grads,
        master_next,
        first_next,
        second_next,
        copy_next,
        *small_next,
        grad_input,
        result,
    ) = all_adam(
        owned_grads,
        left_low,
        basis_right,
        slot_master,
        slot_first,
        slot_second,
        summed,
        params,
        grad_input,
        result,
    )
    for q in range(4, 8):
        small_next[q] = small_next[q].T
    for q in range(12, 16):
        small_next[q] = small_next[q][0]
    return (
        result,
        grad_input,
        owned_grads,
        master_next,
        first_next,
        second_next,
        copy_next,
        *small_next,
    )


def solution(mesh):
    placed = (
        P("seq", None),
        P("seq", None),
        P(),
        P(),
        P("head", None),
        P(("seq", "head"), None, None),
        P(("seq", "head"), None, None),
        P(("seq", "head"), None, None),
        P(("seq", "head"), None, None),
        P(("seq", "head"), None, None),
        P(("seq", "head"), None, None),
        P(),
        P(),
        P(),
        P(),
        P(),
        P(),
        P(None, "head"),
        P(None, "head"),
        P(None, "head"),
        P(),
        P(),
        P(),
        P(None, "head"),
        P(None, "head"),
        P(None, "head"),
    )
    return jax.shard_map(
        body,
        mesh=mesh,
        in_specs=placed,
        out_specs=(
            P("seq", None),
            P("seq", None),
            P(("seq", "head"), None, None),
            P(("seq", "head"), None, None),
            P(("seq", "head"), None, None),
            P(("seq", "head"), None, None),
            P(("seq", "head"), None, None),
            P(),
            P(),
            P(),
            P(),
            P(),
            P(),
            P(),
            P(),
            P(None, "head"),
            P(None, "head"),
            P(None, "head"),
            P(None, "head"),
            P(),
            P(),
            P(),
            P(),
            P(None, "head"),
            P(None, "head"),
            P(None, "head"),
            P(None, "head"),
        ),
        check_vma=False,
    )
```

```python
import functools

import jax
import jax.numpy as jnp
from jax import lax
from jax.experimental import pallas as pl
from jax.experimental.pallas import tpu as pltpu
from jax.sharding import PartitionSpec as P

MESH = pl.DeviceIdType.MESH

DK = 128
DV = 256


highest_precision = lax.Precision.HIGHEST
norm_epsilon = 1e-06
adam_epsilon = 1e-08
gate_scale = 16.0
moment_decay = 0.5
rate_block = 0.03
rate_gains = 0.45
rate_down = 0.02
rate_upper = 0.6
rate_head = 0.5
rate_conv = 0.1


def axis_sizes(n):
    side = 1
    while (side * 2) ** 2 * 4 <= n:
        side *= 2
    return (n // (side * side), side, side)


def coords(me, sizes):
    _, rows, columns = sizes
    return [me // (rows * columns), (me // columns) % rows, me % columns]


def index_of(c, sizes):
    _, rows, columns = sizes
    return (c[0] * rows + c[1]) * columns + c[2]


def neighbour(c, sizes, ax, j):
    d = list(c)
    d[ax] = lax.rem(c[ax] + j, sizes[ax])
    return index_of(d, sizes)


def announce(n, me, mate=False):
    barrier = pltpu.get_barrier_semaphore()
    if mate:
        core = lax.axis_index("head")
        pl.semaphore_signal(barrier, inc=1, device_id={"head": 1 - core}, device_id_type=MESH)
    for j in range(1, n):
        pl.semaphore_signal(
            barrier, inc=1, device_id={"seq": lax.rem(me + j, n)}, device_id_type=MESH
        )


def enter(n, me, mate=False):
    announce(n, me, mate)
    pl.semaphore_wait(pltpu.get_barrier_semaphore(), n - 1 + int(mate))


def remote(src, dst, send_sem, recv_sem, peer):
    return pltpu.make_async_remote_copy(
        src_ref=src,
        dst_ref=dst,
        send_sem=send_sem,
        recv_sem=recv_sem,
        device_id={"seq": peer},
        device_id_type=MESH,
    )


def build_plan(widths, parts, pieces, orders, base=0):
    total = sum(widths)
    bounds = [sum(widths[:i]) for i in range(len(widths) + 1)]
    cuts = [round(total * f) for f in (0.0,) + parts]
    plan, at = [], 0
    for i in range(pieces):
        for order, lo, hi in zip(orders, cuts[:-1], cuts[1:], strict=True):
            size = hi - lo
            left = size * (i + 1) // pieces - size * i // pieces
            while left:
                which = max(q for q in range(len(widths)) if bounds[q] <= at)
                step = min(left, bounds[which + 1] - at)
                start = at - bounds[which]
                plan.append((which, start, start + step, at + base, order, i))
                at += step
                left -= step
    return plan


def groups_of(plan):
    streams = {}
    for i, chunk in enumerate(plan):
        streams.setdefault(chunk[4], {}).setdefault(chunk[5], []).append(i)
    return streams


def spread_steps(steps, places):
    chosen = [(place, steps.pop(0)) for place in places[: len(steps)]]

    def run(t):
        for place, step in chosen:
            pl.when(t == place)(step)

    return run


FORWARD_PLACES = (1, (4,), (4,), ())
FORWARD_PIECES = 4
BACKWARD_PLACES = ((4,), (0, 6), (2, 6))
BACKWARD_PIECES = 4
MIDDLE_PIECES = 3
MIDDLE_TAKEN = 6


def gather_steps(sizes, plan, piece, outs, bw, send, recv):
    c = coords(lax.axis_index("seq"), sizes)
    most = max(sizes)

    def copies(i, k):
        which, lo, hi, at, order, _ = plan[i]
        ax = order[k]
        wide = pl.ds(lo * bw, (hi - lo) * bw)
        index = tuple(slice(None) if a in order[:k] else c[a] for a in range(3))
        index += (slice(None), wide)
        target = outs[which].at[index]
        source = target if k else piece.at[:, pl.ds(at * bw, (hi - lo) * bw)]
        return [
            remote(
                source,
                target,
                send.at[(i * 3 + k) * most + j],
                recv.at[(i * 3 + k) * most + j],
                neighbour(c, sizes, ax, j),
            )
            for j in range(1, sizes[ax])
        ]

    streams = groups_of(plan)
    longest = max(max(s) for s in streams.values()) + 1

    def step(s):
        for k in (2, 1, 0):
            for groups in streams.values():
                for i in groups.get(s - k, ()):
                    if k:
                        for copy in copies(i, k - 1):
                            copy.wait_recv()
                    for copy in copies(i, k):
                        copy.start()

    def arrived(piece_range):
        for groups in streams.values():
            for s in piece_range:
                for i in groups.get(s, ()):
                    for copy in copies(i, 2):
                        copy.wait_recv()

    def sent():
        for i in range(len(plan)):
            for k in range(3):
                for copy in copies(i, k):
                    copy.wait_send()

    return [functools.partial(step, s) for s in range(longest + 2)], arrived, sent


def scatter_scratch(sizes, plan, rows, bw, dtype, in_place=False):
    own, first, second, third = [], [], [], []
    for _, lo, hi, _, order, _ in plan:
        wide = (hi - lo) * bw
        rest = tuple(sizes[q] for q in range(3) if q != order[0])
        own.append(pltpu.VMEM(rest + (rows, wide), dtype))
        first.append(pltpu.VMEM((sizes[order[0]] - 1,) + rest + (rows, wide), dtype))
        second.append(pltpu.VMEM((sizes[order[1]], sizes[order[2]], rows, wide), dtype))
        third.append(pltpu.VMEM((sizes[order[2]], rows, wide), dtype))
    count = len(plan) * 3 * max(sizes)
    return (
        ([] if in_place else own)
        + first
        + second
        + third
        + [
            pltpu.SemaphoreType.DMA((count,)),
            pltpu.SemaphoreType.DMA((count,)),
            pltpu.SemaphoreType.DMA((len(plan),)),
        ]
    )


def scatter_steps(sizes, plan, grads, scratch, fin, bw, in_place=False):
    c = coords(lax.axis_index("seq"), sizes)
    most, count = max(sizes), len(plan)
    first, second, third = (scratch[-3 - (3 - i) * count :][:count] for i in range(3))
    send, recv, load = scratch[-3:]

    def part(i):
        which, lo, hi, _, order, _ = plan[i]
        index = tuple(c[q] if q == order[0] else slice(None) for q in range(3))
        index += (slice(None), pl.ds(lo * bw, (hi - lo) * bw))
        return grads[which].at[index]

    own = [part(i) for i in range(count)] if in_place else scratch[:count]

    def loading(i):
        return pltpu.make_async_copy(part(i), own[i], load.at[i])

    def copies(i, k):
        which, lo, hi, _, order, _ = plan[i]
        ax = order[k]
        left = sorted(set(range(3)) - set(order[:k]))
        result = []
        for j in range(1, sizes[ax]):
            there = lax.rem(c[ax] + j, sizes[ax])
            index = tuple(there if q == ax else slice(None) for q in left)
            if k == 0:
                index += (slice(None), pl.ds(lo * bw, (hi - lo) * bw))
                source, target = grads[which].at[index], first[i].at[j - 1]
            elif k == 1:
                source, target = own[i].at[index], second[i].at[j]
            else:
                source, target = second[i].at[(0,) + index], third[i].at[j]
            s = (i * 3 + k) * most + j
            result.append(
                remote(source, target, send.at[s], recv.at[s], neighbour(c, sizes, ax, j))
            )
        return result

    def combine(i, k):
        _, lo, hi, at, order, _ = plan[i]
        if k == 0 and not in_place:
            loading(i).wait()
        for copy in copies(i, k):
            copy.wait_recv()
        size = sizes[order[k]]
        if k == 0:
            outer, inner = own[i].shape[:2]

            def add(t, _):
                u, v = t // inner, t % inner
                total = own[i][u, v].astype(jnp.float32)
                for j in range(size - 1):
                    total = total + first[i][j, u, v].astype(jnp.float32)
                own[i][u, v] = total.astype(own[i].dtype)
                return 0

            lax.fori_loop(0, outer * inner, add, 0)
        elif k == 1:
            leading = sorted(set(range(3)) - {order[0]}).index(order[1]) == 0

            def add(t, _):
                total = own[i][(c[order[1]], t) if leading else (t, c[order[1]])]
                total = total.astype(jnp.float32)
                for j in range(1, size):
                    total = total + second[i][j, t].astype(jnp.float32)
                second[i][0, t] = total.astype(own[i].dtype)
                return 0

            lax.fori_loop(0, sizes[order[2]], add, 0)
        else:
            total = second[i][0, c[order[2]]].astype(jnp.float32)
            for j in range(1, size):
                total = total + third[i][j].astype(jnp.float32)
            for b in range(hi - lo):
                fin[at + b] = total[:, b * bw : (b + 1) * bw].astype(fin.dtype)

    streams = groups_of(plan)
    longest = max(max(s) for s in streams.values()) + 1

    def step(s):
        for k in range(4):
            for groups in streams.values():
                for i in groups.get(s - k, ()):
                    if k:
                        combine(i, k - 1)
                    elif not in_place:
                        loading(i).start()
                    if k < 3:
                        for copy in copies(i, k):
                            copy.start()

    def sent():
        for i in range(count):
            for k in range(3):
                for copy in copies(i, k):
                    copy.wait_send()

    return [functools.partial(step, s) for s in range(longest + 3)], sent


SPREAD = ((2, 1, 0), (1, 2, 0), (0, 1, 2))
COLLECT = ((0, 1, 2), (0, 2, 1), (2, 1, 0))
SHARES = (0.43, 0.86, 1.0)


def sum_steps(sizes, shared, x_ref, out_ref, mate, acc, bufs, send, recv):
    me, core = lax.axis_index("seq"), lax.axis_index("head")
    c = coords(me, sizes)
    most = max(sizes)
    swap = pltpu.make_async_remote_copy(
        src_ref=x_ref.at[pl.ds(0, shared)],
        dst_ref=mate,
        send_sem=send.at[0],
        recv_sem=recv.at[0],
        device_id={"head": 1 - core},
        device_id_type=MESH,
    )

    def going(step, ax):
        copies = []
        for j in range(1, sizes[ax]):
            d = list(c)
            d[ax] = lax.rem(c[ax] + j, sizes[ax])
            q = 1 + ax * most + j
            copies.append(
                remote(
                    acc.at[step], bufs.at[ax, c[ax]], send.at[q], recv.at[q], index_of(d, sizes)
                )
            )
        return copies

    def total(ax):
        value = bufs[ax, 0]
        for j in range(1, sizes[ax]):
            value = value + bufs[ax, j]
        return value

    def start(step, ax):
        bufs[ax, c[ax]] = acc[step]
        for copy in going(step, ax):
            copy.start()

    def swapped():
        swap.wait()
        acc[0, 0:shared] = x_ref[0:shared] + mate[...]
        acc[0, shared:] = x_ref[shared:]
        start(0, 2)

    def moved(step, ax):
        for copy in going(step, ax):
            copy.wait()
        if step < 2:
            acc[step + 1] = total(ax)
            start(step + 1, ax - 1)
        else:
            out_ref[...] = total(ax)

    return [
        swap.start,
        swapped,
        functools.partial(moved, 0, 2),
        functools.partial(moved, 1, 1),
        functools.partial(moved, 2, 0),
    ]


NN = (((1,), (0,)), ((), ()))
NT = (((1,), (1,)), ((), ()))
TN = (((0,), (0,)), ((), ()))
TILE = 128
LONGEST = 8192


def halves(values):
    high = values.astype(jnp.bfloat16)
    return high, (values - high.astype(jnp.float32)).astype(jnp.bfloat16)


def product(left, right, dims):
    (lh, ll), (rh, rl) = left, right
    dot = functools.partial(
        lax.dot_general, dimension_numbers=dims, preferred_element_type=jnp.float32
    )
    return dot(lh, rh) + (dot(lh, rl) + dot(ll, rh))


def running_sum(table, values):
    first = values.astype(jnp.bfloat16)
    rest = values - first.astype(jnp.float32)
    second, third = halves(rest)
    dot = functools.partial(
        lax.dot_general, dimension_numbers=NN, preferred_element_type=jnp.float32
    )
    return dot(table, first) + (dot(table, second) + dot(table, third))


def sigmoid(values):
    return 1.0 / (1.0 + jnp.exp(-values))


def chain_tools(n, sizes, forward, mine, bufs, send, recv, result):
    me = lax.axis_index("seq")
    c = coords(me, sizes)
    pieces = mine.shape[0]
    across, along, before, held = bufs
    most = max(sizes)
    state = pl.ds(0, TILE)
    decay = pl.ds(TILE, 1)

    def peers(ax):
        return [j for j in range(1, sizes[ax])]

    def to(ax, j):
        d = list(c)
        d[ax] = lax.rem(c[ax] + j, sizes[ax])
        return index_of(d, sizes)

    def line(buf, source, ax, j, p, base):
        s = base + j * pieces + p
        return remote(source.at[p], buf.at[c[ax], p], send.at[s], recv.at[s], to(ax, j))

    place = c[0] if forward else sizes[0] - 1 - c[0]

    def hop(k, p):
        s = (2 * most + k) * pieces + p
        step = 1 if forward else -1
        d = [lax.rem(c[0] + step + sizes[0], sizes[0]), c[1], c[2]]
        return remote(
            held.at[1 + 2 * k, p], held.at[2 * k, p], send.at[s], recv.at[s], index_of(d, sizes)
        )

    def compose(first, second):
        return (second[1] * first[0] + second[0], first[1] * second[1])

    def reduce_line(buf, ax, p):
        size = sizes[ax]
        order = range(size) if forward else range(size - 1, -1, -1)
        prefix = (jnp.zeros((TILE, TILE), jnp.float32), jnp.ones((1, TILE), jnp.float32))
        total = None
        for i in order:
            item = (buf[i, p, state], buf[i, p, decay])
            longer = compose(prefix, item)
            take = (i < c[ax]) if forward else (i > c[ax])
            prefix = tuple(jnp.where(take, a, b) for a, b in zip(longer, prefix, strict=True))
            total = item if total is None else compose(total, item)
        return prefix, total

    def start_x():
        for p in range(pieces):
            across[c[2], p] = mine[p]
            for j in peers(2):
                line(across, mine, 2, j, p, 0).start()

    def start_y():
        for p in range(pieces):
            for j in peers(2):
                line(across, mine, 2, j, p, 0).wait_recv()
            prefix, total = reduce_line(across, 2, p)
            before[p, state], before[p, decay] = prefix
            held[4, p, state], held[4, p, decay] = total
            held[4, p, pl.ds(TILE + 1, 7)] = jnp.zeros((7, TILE), jnp.float32)
            along[c[1], p] = held[4, p]
            for j in peers(1):
                line(along, held.at[4], 1, j, p, most * pieces).start()

    def start_z():
        for p in range(pieces):
            for j in peers(1):
                line(along, held.at[4], 1, j, p, most * pieces).wait_recv()
            prefix, total = reduce_line(along, 1, p)
            own = (before[p, state], before[p, decay])
            before[p, state], before[p, decay] = compose(prefix, own)
            held[1, p, state], held[1, p, decay] = total
            held[1, p, pl.ds(TILE + 1, 7)] = jnp.zeros((7, TILE), jnp.float32)

            @pl.when(place < sizes[0] - 1)
            def _():
                hop(0, p).start()

    def pass_z():
        @pl.when(place > 0)
        def _():
            for p in range(pieces):
                hop(0, p).wait_recv()

                @pl.when(place < sizes[0] - 1)
                def _():
                    got = (held[0, p, state], held[0, p, decay])
                    item = (held[1, p, state], held[1, p, decay])
                    held[3, p, state], held[3, p, decay] = compose(got, item)
                    held[3, p, pl.ds(TILE + 1, 7)] = jnp.zeros((7, TILE), jnp.float32)
                    hop(1, p).start()

    def finish():
        for p in range(pieces):

            @pl.when(place == 0)
            def _():
                result[p] = before[p, state]

            @pl.when(place == 1)
            def _():
                result[p] = before[p, decay] * held[0, p, state] + before[p, state]

            @pl.when(place > 1)
            def _():
                hop(1, p).wait_recv()
                result[p] = before[p, decay] * held[2, p, state] + before[p, state]

            for j in peers(2):
                line(across, mine, 2, j, p, 0).wait_send()
            for j in peers(1):
                line(along, held.at[4], 1, j, p, most * pieces).wait_send()

        @pl.when(place < sizes[0] - 1)
        def _():
            for p in range(pieces):
                hop(0, p).wait_send()

        @pl.when((place > 0) & (place < sizes[0] - 1))
        def _():
            for p in range(pieces):
                hop(1, p).wait_send()

    return [start_x, start_y, start_z, pass_z], finish


def greet(n, sizes, extra):
    c = coords(lax.axis_index("seq"), sizes)
    barrier = pltpu.get_barrier_semaphore()
    count = 0
    for ax in range(3):
        for j in range(1, sizes[ax]):
            d = list(c)
            d[ax] = lax.rem(c[ax] + j, sizes[ax])
            pl.semaphore_signal(
                barrier, inc=1, device_id={"seq": index_of(d, sizes)}, device_id_type=MESH
            )
            count += 1
    for index in extra:
        pl.semaphore_signal(barrier, inc=1, device_id={"seq": index}, device_id_type=MESH)
        count += 1
    pl.semaphore_wait(barrier, count)


def tile_masks(rows_ref, cols_ref, c):
    row = rows_ref[pl.ds(c, 1), :]
    col = cols_ref[pl.ds(pl.multiple_of(c * TILE, TILE), TILE), 6:7]
    i = lax.broadcasted_iota(jnp.int32, (TILE, TILE), 0)
    j = lax.broadcasted_iota(jnp.int32, (TILE, TILE), 1)
    return (i >= j) & (row == col)


def forward_kernel(
    n,
    sizes,
    plan,
    ready,
    owners_ref,
    lengths_ref,
    packing_ref,
    slot_ref,
    tokens_ref,
    norm_ref,
    down_ref,
    upper_ref,
    taps_ref,
    gain_ref,
    w_in_out,
    w_up_out,
    w_out_out,
    w_down_out,
    normed_out,
    lowrank_ref,
    logits_out,
    proj_out,
    halo_ref,
    gate_out,
    conv_out,
    cum_out,
    o_out,
    u_out,
    start_out,
    cols_ref,
    rows_ref,
    normed,
    logits_ref,
    proj_ref,
    gate_ref,
    conv_ref,
    cum_ref,
    o_ref,
    u_ref,
    start_ref,
    slots,
    piece,
    w_in,
    rim,
    segs,
    act,
    state,
    prev,
    a_send,
    a_recv,
    g_send,
    g_recv,
    l_sem,
    mine,
    across,
    along,
    before,
    held,
    result,
    send,
    recv,
):
    me = lax.axis_index("seq")
    c3 = coords(me, sizes)
    length, width = tokens_ref.shape
    tiles, channels = length // TILE, proj_ref.shape[1]
    keys = logits_ref.shape[1]
    rank = down_ref.shape[0]
    heads = keys // DK
    value = DV * heads
    slots_dev, _, bw = slot_ref.shape
    rows = piece.shape[0]
    scale = DK ** (-0.5)
    enter(n, me)

    def move(j):
        p = lax.rem(me + j, n)
        return remote(
            slot_ref.at[:, pl.ds(p * rows, rows), :],
            slots.at[pl.ds(me * slots_dev, slots_dev)],
            a_send.at[j],
            a_recv.at[j],
            p,
        )

    for j in range(1, n):
        move(j).start()
    local_move = pltpu.make_async_copy(
        slot_ref.at[:, pl.ds(me * rows, rows), :],
        slots.at[pl.ds(me * slots_dev, slots_dev)],
        l_sem.at[0],
    )
    local_move.start()
    edge = remote(
        tokens_ref.at[pl.ds(length - 16, 16)],
        rim,
        a_send.at[0],
        a_recv.at[0],
        lax.rem(me + 1, n),
    )

    @pl.when(me < n - 1)
    def _():
        edge.start()

    base = me * length
    where_col = base - 8 + lax.broadcasted_iota(jnp.int32, (length + 8, 1), 0)
    lane = lax.broadcasted_iota(jnp.int32, (tiles, TILE), 1)
    where_row = base + TILE * lax.broadcasted_iota(jnp.int32, (tiles, TILE), 0) + lane
    start = jnp.int32(0)
    seg_col = jnp.zeros((length + 8, 1), jnp.float32)
    seg_row = jnp.zeros((tiles, TILE), jnp.float32)
    for q in range(lengths_ref.shape[0]):
        seg_col += (where_col >= start).astype(jnp.float32)
        seg_row += (where_row >= start).astype(jnp.float32)
        start = start + lengths_ref[packing_ref[q]]
    filled = start
    segs[...] = seg_col + (where_col >= filled).astype(jnp.float32)
    rows_ref[...] = seg_row + (where_row >= filled).astype(jnp.float32)
    lane = lax.broadcasted_iota(jnp.int32, (TILE, TILE), 1)
    for c in range(tiles):
        lo = 8 + c * TILE
        own = segs[lo : lo + TILE]
        flags = [segs[lo - 1 : lo], segs[lo + TILE - 1 : lo + TILE]]
        flags += [segs[lo - s : lo - s + TILE] for s in (1, 2, 3)]
        flags = [(other == own).astype(jnp.float32) for other in flags]
        place = base + c * TILE + lax.broadcasted_iota(jnp.int32, (TILE, 1), 0)
        flags += [None, own, (place < filled).astype(jnp.float32)]
        total = jnp.zeros((TILE, TILE), jnp.float32)
        for k, flag in enumerate(flags):
            if flag is not None:
                total = jnp.where(lane == k, flag, total)
        cols_ref[c * TILE : (c + 1) * TILE, :] = total
    cols_ref[length : length + 8, :] = jnp.zeros((8, TILE), jnp.float32)

    def norm(values):
        values = values.astype(jnp.float32)
        inverse = lax.rsqrt(jnp.mean(values * values, axis=1, keepdims=True) + norm_epsilon)
        return (values * inverse * norm_ref[0:1, :]).astype(jnp.bfloat16)

    i = lax.broadcasted_iota(jnp.int32, (TILE, TILE), 0)
    j = lax.broadcasted_iota(jnp.int32, (TILE, TILE), 1)
    lower = (i >= j).astype(jnp.bfloat16)
    down_low = down_ref[...].astype(jnp.bfloat16)
    upper = halves(upper_ref[0:rank, :])

    def gates(c, _):
        at = pl.ds(pl.multiple_of(c * TILE, TILE), TILE)
        x = norm(tokens_ref[at, :])
        normed[at, :] = x
        low = lax.dot_general(x, down_low, NT, preferred_element_type=jnp.float32)
        lowrank_ref[at, :] = low
        logits = product(halves(low), upper, NN) + upper_ref[rank : rank + 1, :]
        logits_ref[at, :] = logits
        gate = jnp.minimum(logits, 0.0) - jnp.log1p(jnp.exp(-jnp.abs(logits)))
        cum_ref[at, :] = running_sum(lower, gate * (1.0 / gate_scale))
        return 0

    lax.fori_loop(0, tiles, gates, 0)
    flushes = []

    def flush(source, target):
        copy = pltpu.make_async_copy(source, target, l_sem.at[6 + len(flushes)])
        copy.start()
        flushes.append(copy)

    flush(normed, normed_out)
    flush(logits_ref, logits_out)
    flush(cum_ref, cum_out)

    @pl.when(me > 0)
    def _():
        edge.wait_recv()

    @pl.when(me == 0)
    def _():
        rim[...] = jnp.zeros_like(rim)

    rim[...] = norm(rim[...])

    local_move.wait()
    for j in range(1, n):
        move(j).wait()
    for b in range(owners_ref.shape[1]):
        piece[:, b * bw : (b + 1) * bw] = slots[owners_ref[0, b]]
    outs = (w_in, w_up_out, w_out_out, w_down_out)
    offset, owns = 0, []
    for q, out in enumerate(outs):
        columns = out.shape[4]
        owns.append(
            pltpu.make_async_copy(
                piece.at[:, pl.ds(offset, columns)],
                out.at[c3[0], c3[1], c3[2]],
                l_sem.at[1 + q],
            )
        )
        offset += columns
    for copy in owns:
        copy.start()
    steps, arrived, sent = gather_steps(sizes, plan, piece, outs, bw, g_send, g_recv)
    steps[0]()
    for copy in owns:
        copy.wait()
    for step in steps[1 : ready + 2]:
        step()
    arrived(range(ready))
    rest = list(steps[ready + 2 :])
    flush(w_in, w_in_out)

    for step in rest[: FORWARD_PLACES[0]]:
        step()
    del rest[: FORWARD_PLACES[0]]

    def project(r, _):
        at = pl.ds(pl.multiple_of(r * 256, 256), 256)
        x = normed[at, :]
        for lo in range(0, w_in.shape[4], 512):
            part = lax.dot_general(
                x,
                w_in[:, :, :, :, lo : lo + 512].reshape(width, 512),
                NN,
                preferred_element_type=jnp.float32,
            )
            if lo < channels:
                proj_ref[at, lo : lo + 512] = part.astype(proj_ref.dtype)
            else:
                gate_ref[at, lo - channels : lo - channels + 512] = part
        return 0

    lax.fori_loop(0, length // 256, project, 0)
    for lo in range(0, channels, 512):
        halo_ref[:, lo : lo + 512] = lax.dot_general(
            rim[...],
            w_in[:, :, :, :, lo : lo + 512].reshape(width, 512),
            NN,
            preferred_element_type=jnp.float32,
        ).astype(halo_ref.dtype)
    flush(proj_ref, proj_out)
    flush(gate_ref, gate_out)

    prev[...] = halo_ref[...]
    state[...] = jnp.zeros_like(state)
    mine[...] = jnp.zeros_like(mine)
    for p in range(mine.shape[0]):
        mine[p, TILE : TILE + 1] = jnp.ones((1, TILE), jnp.float32)
    run = spread_steps(rest, FORWARD_PLACES[1])

    def local(c, _):
        run(c)
        at = pl.ds(pl.multiple_of(c * TILE, TILE), TILE)
        for g in range(0, channels, 256):
            wide = slice(g, g + 256)
            block = jnp.concatenate(
                [prev[:, wide].astype(jnp.float32), proj_ref[at, wide].astype(jnp.float32)]
            )
            total = taps_ref[3:4, wide] * block[16:]
            for s in (1, 2, 3):
                total = total + taps_ref[3 - s : 4 - s, wide] * (
                    block[16 - s : 16 - s + TILE] * cols_ref[at, 1 + s : 2 + s]
                )
            conv_ref[at, wide] = total
            act[at, wide] = total * sigmoid(total)
        prev[...] = proj_ref[pl.ds(pl.multiple_of(c * TILE + TILE - 16, 16), 16), :]
        cum = cum_ref[at, :]
        last = cum[TILE - 1 : TILE]
        left = act[at, keys : 2 * keys] * jnp.exp(last - cum) * cols_ref[at, 1:2]
        decay = jnp.exp(last) * cols_ref[at, 0:1][TILE - 1 : TILE]
        for h in range(heads):
            kh = slice(h * DK, (h + 1) * DK)
            v = halves(act[at, 2 * keys + h * DV : 2 * keys + (h + 1) * DV])
            start_ref[c, h] = state[h]
            state[h] = state[h] * decay[:, kh] + product(v, halves(left[:, kh]), TN)
            for e in range(DV // TILE):
                p = h * (DV // TILE) + e
                mine[p, TILE : TILE + 1] = mine[p, TILE : TILE + 1] * decay[:, kh]
        return 0

    lax.fori_loop(0, tiles, local, 0)
    flush(conv_ref, conv_out)
    for h in range(heads):
        start_ref[tiles, h] = state[h]
        for e in range(DV // TILE):
            mine[h * (DV // TILE) + e, 0:TILE] = state[h, e * TILE : (e + 1) * TILE]
    stages, finish = chain_tools(
        n, sizes, True, mine, (across, along, before, held), send, recv, result
    )
    stages[0]()
    run_inside = spread_steps(rest, FORWARD_PLACES[2])

    def inside(c, _):
        for k, stage in enumerate(stages[1:]):
            pl.when(c == k + 1)(stage)
        run_inside(c)
        at = pl.ds(pl.multiple_of(c * TILE, TILE), TILE)
        cum = cum_ref[at, :]
        middle = cum[TILE // 2 - 1 : TILE // 2]
        q = act[at, 0:keys] * jnp.exp(cum - middle) * scale
        k = act[at, keys : 2 * keys] * jnp.exp(middle - cum)
        mask = tile_masks(rows_ref, cols_ref, c)
        for h in range(heads):
            kh = slice(h * DK, (h + 1) * DK)
            vh = slice(h * DV, (h + 1) * DV)
            scores = jnp.where(mask, product(halves(q[:, kh]), halves(k[:, kh]), NT), 0.0)
            v = halves(act[at, 2 * keys + h * DV : 2 * keys + (h + 1) * DV])
            o_ref[at, vh] = product(halves(scores), v, NN)
        return 0

    lax.fori_loop(0, tiles, inside, 0)
    finish()
    for h in range(heads):
        for e in range(DV // TILE):
            state[h, e * TILE : (e + 1) * TILE] = result[h * (DV // TILE) + e]

    run_outside = spread_steps(rest, FORWARD_PLACES[3])

    def outside(c, _):
        run_outside(c)
        at = pl.ds(pl.multiple_of(c * TILE, TILE), TILE)
        cum = cum_ref[at, :]
        q = act[at, 0:keys] * jnp.exp(cum) * scale * cols_ref[at, 0:1]
        decay = jnp.exp(cum[TILE - 1 : TILE]) * cols_ref[at, 0:1][TILE - 1 : TILE]
        for h in range(heads):
            kh = slice(h * DK, (h + 1) * DK)
            vh = slice(h * DV, (h + 1) * DV)
            begin = start_ref[c, h] + state[h]
            start_ref[c, h] = begin
            state[h] = state[h] * decay[:, kh]
            o = o_ref[at, vh] + product(halves(q[:, kh]), halves(begin), NT)
            o_ref[at, vh] = o
            inverse = lax.rsqrt(jnp.mean(o * o, axis=1, keepdims=True) + norm_epsilon)
            gate = gate_ref[at, vh]
            u_ref[at, vh] = (o * inverse * gain_ref[...] * (gate * sigmoid(gate))).astype(
                u_ref.dtype
            )
        return 0

    lax.fori_loop(0, tiles, outside, 0)
    for h in range(heads):
        start_ref[tiles, h] = start_ref[tiles, h] + state[h]
    flush(o_ref, o_out)
    flush(u_ref, u_out)
    flush(start_ref, start_out)
    for step in rest:
        step()
    groups = {chunk[5] for chunk in plan}
    arrived(sorted(g for g in groups if g >= ready))
    sent()
    for copy in flushes:
        copy.wait()

    @pl.when(me < n - 1)
    def _():
        edge.wait_send()


def forward(
    owners, lengths, packing, slot_copy, tokens, norm, down, upper, taps, gain, counts
):
    n = lax.axis_size("seq")
    sizes = axis_sizes(n)
    length, width = tokens.shape
    slots_dev, depth, bw = slot_copy.shape
    rows = depth // n
    keys, channels = upper.shape[1], taps.shape[1]
    heads = keys // DK
    value = heads * DV
    tiles = length // TILE
    blocks = sum(counts)
    ready = 2
    plan = build_plan(counts[:1], SHARES, ready, COLLECT)
    plan += [
        (which + 1, lo, hi, at, order, group + ready)
        for which, lo, hi, at, order, group in build_plan(
            counts[1:], SHARES, FORWARD_PIECES, COLLECT, counts[0]
        )
    ]
    f32, b16 = jnp.float32, jnp.bfloat16
    shape = jax.ShapeDtypeStruct
    vmem, anywhere = pl.BlockSpec(memory_space=pltpu.VMEM), pl.BlockSpec(memory_space=pl.ANY)
    smem = pl.BlockSpec(memory_space=pltpu.SMEM)
    kept = [
        ((length, width), b16),
        ((length, keys), f32),
        ((length, channels), b16),
        ((length, value), f32),
        ((length, channels), f32),
        ((length, keys), f32),
        ((length, value), f32),
        ((length, value), b16),
        ((tiles + 1, heads, DV, DK), f32),
    ]
    big = [shape(*k) for k in kept]
    outs = [shape(sizes + (rows, count * bw), b16) for count in counts]
    outs += [big[0], shape((length, down.shape[0]), f32), big[1], big[2]]
    outs += [shape((16, channels), b16)] + big[3:]
    outs += [shape((length + 8, TILE), f32), shape((tiles, TILE), f32)]
    specs = [anywhere] * 5 + [vmem, anywhere, anywhere, vmem] + [anywhere] * 6 + [vmem, vmem]
    most = max(sizes)
    copies = len(plan) * 3 * most
    result = pl.pallas_call(
        functools.partial(forward_kernel, n, sizes, plan, ready),
        out_shape=tuple(outs),
        in_specs=[smem] * 3 + [anywhere] + [vmem] * 6,
        out_specs=tuple(specs),
        scratch_shapes=[pltpu.VMEM(*k) for k in kept]
        + [
            pltpu.VMEM((n * slots_dev, rows, bw), b16),
            pltpu.VMEM((rows, blocks * bw), b16),
            pltpu.VMEM(sizes + (rows, counts[0] * bw), b16),
            pltpu.VMEM((16, width), b16),
            pltpu.VMEM((length + 8, 1), f32),
            pltpu.VMEM((length, channels), f32),
            pltpu.VMEM((heads, DV, DK), f32),
            pltpu.VMEM((16, channels), b16),
            pltpu.SemaphoreType.DMA((n,)),
            pltpu.SemaphoreType.DMA((n,)),
            pltpu.SemaphoreType.DMA((copies,)),
            pltpu.SemaphoreType.DMA((copies,)),
            pltpu.SemaphoreType.DMA((18,)),
        ]
        + chain_scratch(sizes, heads * DV // TILE, length),
        compiler_params=pltpu.CompilerParams(
            collective_id=1, has_side_effects=True, vmem_limit_bytes=60 << 20
        ),
    )(owners, lengths, packing, slot_copy, tokens, norm, down, upper, taps, gain)
    return [w.reshape(depth, w.shape[4]) for w in result[:4]], result[4:]


def chain_scratch(sizes, pieces, length):
    assert 2 * sizes[1] * sizes[2] * length >= LONGEST
    most = max(sizes)
    shape = (pieces, TILE + 8, TILE)
    return [
        pltpu.VMEM(shape, jnp.float32),
        pltpu.VMEM((sizes[2],) + shape, jnp.float32),
        pltpu.VMEM((sizes[1],) + shape, jnp.float32),
        pltpu.VMEM(shape, jnp.float32),
        pltpu.VMEM((5,) + shape, jnp.float32),
        pltpu.VMEM((pieces, TILE, TILE), jnp.float32),
        pltpu.SemaphoreType.DMA(((2 * most + 2) * pieces,)),
        pltpu.SemaphoreType.DMA(((2 * most + 2) * pieces,)),
    ]


def backward_kernel(
    n,
    sizes,
    plan,
    proj_in,
    halo_ref,
    conv_in,
    cum_in,
    logits_in,
    o_in,
    gate_in,
    du_in,
    start_in,
    cols_ref,
    rows_ref,
    taps_ref,
    gain_ref,
    g_up_ref,
    g_out_ref,
    dproj_out,
    dgate_out,
    dlogits_out,
    dtaps_ref,
    dgain_ref,
    early_ref,
    proj_ref,
    conv_ref,
    cum_ref,
    logits_ref,
    o_ref,
    gate_ref,
    du_ref,
    start_ref,
    dproj_ref,
    dgate_ref,
    dlogits_ref,
    t_sem,
    l_sem,
    do,
    dact,
    adjoint,
    ends,
    after,
    back,
    tail,
    mine,
    across,
    along,
    before,
    held,
    result,
    send,
    recv,
    b_sem,
    *scatter_refs,
):
    tiles, channels = proj_ref.shape[0] // TILE, proj_ref.shape[1]
    keys = cum_ref.shape[1]
    heads = keys // DK
    me = lax.axis_index("seq")
    by_tile = (
        (du_in, du_ref),
        (o_in, o_ref),
        (gate_in, gate_ref),
        (cum_in, cum_ref),
        (conv_in.at[:, pl.ds(0, keys)], conv_ref.at[:, pl.ds(0, keys)]),
    )
    rest = pl.ds(keys, channels - keys)
    whole = (
        (conv_in.at[:, rest], conv_ref.at[:, rest]),
        (start_in, start_ref),
        (proj_in, proj_ref),
        (logits_in, logits_ref),
        (dgate_ref, dgate_out),
        (dlogits_ref, dlogits_out),
        (dproj_ref, dproj_out),
    )

    def tile_load(q, c):
        at = pl.ds(pl.multiple_of(c * TILE, TILE), TILE)
        source, target = by_tile[q]
        return pltpu.make_async_copy(source.at[at], target.at[at], t_sem.at[q, c])

    def load(q):
        source, target = whole[q]
        return pltpu.make_async_copy(source, target, l_sem.at[q])

    for c in range(tiles - 1, -1, -1):
        for q in range(len(by_tile)):
            tile_load(q, c).start()
    for q in range(4):
        load(q).start()
    greet(n, sizes, (lax.rem(me + 1, n), lax.rem(me + n - 1, n)))
    steps, sent = scatter_steps(
        sizes, plan, [g_up_ref, g_out_ref], scatter_refs, early_ref, TILE
    )
    steps.pop(0)()
    run_local = spread_steps(steps, BACKWARD_PLACES[0])
    run_inside = spread_steps(steps, BACKWARD_PLACES[1])
    run_outside = spread_steps(steps, BACKWARD_PLACES[2])
    scale = DK ** (-0.5)
    i = lax.broadcasted_iota(jnp.int32, (TILE, TILE), 0)
    j = lax.broadcasted_iota(jnp.int32, (TILE, TILE), 1)
    upper = (i <= j).astype(jnp.bfloat16)
    adjoint[...] = jnp.zeros_like(adjoint)
    mine[...] = jnp.zeros_like(mine)
    dgain_ref[...] = jnp.zeros_like(dgain_ref)
    dtaps_ref[...] = jnp.zeros_like(dtaps_ref)
    for p in range(mine.shape[0]):
        mine[p, TILE : TILE + 1] = jnp.ones((1, TILE), jnp.float32)

    def local(t, _):
        run_local(t)
        c = tiles - 1 - t
        for q in range(len(by_tile)):
            tile_load(q, c).wait()
        at = pl.ds(pl.multiple_of(c * TILE, TILE), TILE)
        cum = cum_ref[at, :]
        pre = conv_ref[at, 0:keys]
        q = pre * sigmoid(pre) * jnp.exp(cum) * scale * cols_ref[at, 0:1]
        decay = jnp.exp(cum[TILE - 1 : TILE]) * cols_ref[at, 0:1][TILE - 1 : TILE]
        for h in range(heads):
            kh = slice(h * DK, (h + 1) * DK)
            vh = slice(h * DV, (h + 1) * DV)
            o = o_ref[at, vh]
            inverse = lax.rsqrt(jnp.mean(o * o, axis=1, keepdims=True) + norm_epsilon)
            gate = gate_ref[at, vh]
            sig = sigmoid(gate)
            du = du_ref[at, vh]
            unit = o * inverse
            dgate_ref[at, vh] = (
                du * (unit * gain_ref[...]) * (sig * (1.0 + gate * (1.0 - sig)))
            ).astype(dgate_ref.dtype)
            don = du * (gate * sig)
            dgain_ref[0:1] += jnp.sum(don * unit, axis=0, keepdims=True)
            scaled = gain_ref[...] * don
            grad = inverse * scaled - unit * (
                inverse * inverse * jnp.mean(scaled * o, axis=1, keepdims=True)
            )
            do[at, vh] = grad
            ends[c, h] = adjoint[h]
            adjoint[h] = adjoint[h] * decay[:, kh] + product(halves(grad), halves(q[:, kh]), TN)
            for e in range(DV // TILE):
                p = h * (DV // TILE) + e
                mine[p, TILE : TILE + 1] = mine[p, TILE : TILE + 1] * decay[:, kh]
        return 0

    lax.fori_loop(0, tiles, local, 0)
    load(4).start()
    for h in range(heads):
        for e in range(DV // TILE):
            mine[h * (DV // TILE) + e, 0:TILE] = adjoint[h, e * TILE : (e + 1) * TILE]
    stages, finish = chain_tools(
        n, sizes, False, mine, (across, along, before, held), send, recv, result
    )
    stages[0]()
    load(0).wait()
    load(1).wait()

    def inside(c, _):
        for k, stage in enumerate(stages[1:]):
            pl.when(c == k + 1)(stage)
        run_inside(c)
        at = pl.ds(pl.multiple_of(c * TILE, TILE), TILE)
        cum = cum_ref[at, :]
        middle = cum[TILE // 2 - 1 : TILE // 2]
        pre = conv_ref[at, 0 : 2 * keys]
        both = pre * sigmoid(pre)
        grow = jnp.exp(cum - middle) * scale
        fall = jnp.exp(middle - cum)
        enter_decay = jnp.exp(cum) * (scale * cols_ref[at, 0:1])
        mask = tile_masks(rows_ref, cols_ref, c)
        for h in range(heads):
            kh = slice(h * DK, (h + 1) * DK)
            vh = slice(h * DV, (h + 1) * DV)
            q = halves(both[:, kh] * grow[:, kh])
            k = halves(both[:, keys + h * DK : keys + (h + 1) * DK] * fall[:, kh])
            prev_v = conv_ref[at, 2 * keys + h * DV : 2 * keys + (h + 1) * DV]
            v = halves(prev_v * sigmoid(prev_v))
            grad = halves(do[at, vh])
            scores = halves(jnp.where(mask, product(q, k, NT), 0.0))
            dscores = halves(jnp.where(mask, product(grad, v, NT), 0.0))
            dact[at, h * DK : (h + 1) * DK] = (
                product(dscores, k, NN) * grow[:, kh]
                + product(grad, halves(start_ref[c, h]), NN) * enter_decay[:, kh]
            )
            dact[at, keys + h * DK : keys + (h + 1) * DK] = (
                product(dscores, q, TN) * fall[:, kh]
            )
            dact[at, 2 * keys + h * DV : 2 * keys + (h + 1) * DV] = product(scores, grad, TN)
        return 0

    lax.fori_loop(0, tiles, inside, 0)
    finish()
    for h in range(heads):
        for e in range(DV // TILE):
            adjoint[h, e * TILE : (e + 1) * TILE] = result[h * (DV // TILE) + e]
    after[...] = jnp.zeros_like(after)
    load(2).wait()
    load(3).wait()

    def outside(t, _):
        run_outside(t)
        c = tiles - 1 - t
        at = pl.ds(pl.multiple_of(c * TILE, TILE), TILE)
        cum = cum_ref[at, :]
        last = cum[TILE - 1 : TILE]
        remain = jnp.exp(last - cum) * cols_ref[at, 1:2]
        decay = jnp.exp(last) * cols_ref[at, 0:1][TILE - 1 : TILE]
        pre = conv_ref[at, 0 : 2 * keys]
        both = pre * sigmoid(pre)
        dkeys, edges = [], []
        for h in range(heads):
            kh = slice(h * DK, (h + 1) * DK)
            wide = slice(2 * keys + h * DV, 2 * keys + (h + 1) * DV)
            k = both[:, keys + h * DK : keys + (h + 1) * DK]
            end = ends[c, h] + adjoint[h]
            adjoint[h] = adjoint[h] * decay[:, kh]
            parts = halves(end)
            pre_v = conv_ref[at, wide]
            v = halves(pre_v * sigmoid(pre_v))
            dkeys.append(
                dact[at, keys + h * DK : keys + (h + 1) * DK]
                + product(v, parts, NN) * remain[:, kh]
            )
            dact[at, wide] += product(halves(k * remain[:, kh]), parts, NT)
            edges.append(jnp.sum(end * start_ref[c + 1, h], axis=0, keepdims=True))
        dk = jnp.concatenate(dkeys, axis=1)
        dq = dact[at, 0:keys]
        dact[at, keys : 2 * keys] = dk
        drift = both[:, 0:keys] * dq - both[:, keys:] * dk
        dl = running_sum(upper, drift) + jnp.concatenate(edges, axis=1)
        dlogits_ref[at, :] = dl * (1.0 / gate_scale) * sigmoid(-logits_ref[at, :])
        behind = jnp.where(
            c == 0,
            halo_ref[...],
            proj_ref[pl.ds(pl.multiple_of(jnp.maximum(c * TILE - 16, 0), 16), 16), :],
        )
        masks = cols_ref[pl.ds(pl.multiple_of(c * TILE, TILE), TILE + 8), :]
        for g in range(0, channels, 256):
            wide = slice(g, g + 256)
            pre = conv_ref[at, wide]
            sig = sigmoid(pre)
            dconv = dact[at, wide] * (sig * (1.0 + pre * (1.0 - sig)))
            block = jnp.concatenate(
                [
                    behind[:, g : g + 256].astype(jnp.float32),
                    proj_ref[at, wide].astype(jnp.float32),
                ]
            )
            grad = jnp.concatenate([dconv, after[:, wide]])
            total = taps_ref[3:4, wide] * dconv
            dtaps_ref[3:4, wide] += jnp.sum(dconv * block[16:], axis=0, keepdims=True)
            first = jnp.zeros((8, 256), jnp.float32)
            for s in (1, 2, 3):
                masked = grad * masks[:, 1 + s : 2 + s]
                tap = taps_ref[3 - s : 4 - s, wide]
                total = total + tap * masked[s : s + TILE]
                dtaps_ref[3 - s : 4 - s, wide] += jnp.sum(
                    masked[:TILE] * block[16 - s : 16 - s + TILE], axis=0, keepdims=True
                )
                first = first + tap * jnp.concatenate(
                    [jnp.zeros((8, 256), jnp.float32), masked[0:8]]
                )[s : s + 8]
            dproj_ref[at, wide] = total.astype(dproj_ref.dtype)
            after[:, wide] = dconv[0:8]
            back[0, :, wide] = first

            @pl.when(c == tiles - 1)
            def _():
                tail[:, wide] = total[TILE - 16 :]

        return 0

    lax.fori_loop(0, tiles, outside, 0)
    load(5).start()

    home = remote(
        back.at[0], back.at[1], b_sem.at[0], b_sem.at[1], lax.rem(me + n - 1, n)
    )

    @pl.when(me > 0)
    def _():
        home.start()

    for step in steps[:1]:
        step()

    @pl.when(me < n - 1)
    def _():
        home.wait_recv()

    @pl.when(me == n - 1)
    def _():
        back[1] = jnp.zeros(back.shape[1:], jnp.float32)

    dproj_ref[pl.ds(tiles * TILE - 16, 16), :] = (
        tail[...] + jnp.concatenate([jnp.zeros((8, channels), jnp.float32), back[1]])
    ).astype(dproj_ref.dtype)
    load(6).start()
    for step in steps[1:]:
        step()
    sent()

    @pl.when(me > 0)
    def _():
        home.wait_send()

    for q in (4, 5, 6):
        load(q).wait()


def recurrence_back(
    proj, halo, conv, cum, logits, o, gate, du, starts, cols, rows, taps, gain, grads
):
    n = lax.axis_size("seq")
    sizes = axis_sizes(n)
    length, channels = proj.shape
    keys = cum.shape[1]
    heads = keys // DK
    value = heads * DV
    tiles = length // TILE
    f32 = jnp.float32
    shape = jax.ShapeDtypeStruct
    depth = grads[0].shape[3]
    plan = build_plan(tuple(g.shape[4] // TILE for g in grads), SHARES, BACKWARD_PIECES, SPREAD)
    blocks = sum(g.shape[4] for g in grads) // TILE
    vmem, anywhere = pl.BlockSpec(memory_space=pltpu.VMEM), pl.BlockSpec(memory_space=pl.ANY)
    return pl.pallas_call(
        functools.partial(backward_kernel, n, sizes, plan),
        in_specs=[anywhere, vmem] + [anywhere] * 7 + [vmem] * 4 + [anywhere] * 2,
        out_specs=(anywhere,) * 3 + (vmem,) * 3,
        out_shape=(
            shape((length, channels), jnp.bfloat16),
            shape((length, value), jnp.bfloat16),
            shape((length, keys), f32),
            shape((8, channels), f32),
            shape((8, DV), f32),
            shape((blocks, depth, TILE), jnp.bfloat16),
        ),
        scratch_shapes=[
            pltpu.VMEM((length, channels), jnp.bfloat16),
            pltpu.VMEM((length, channels), f32),
            pltpu.VMEM((length, keys), f32),
            pltpu.VMEM((length, keys), f32),
            pltpu.VMEM((length, value), f32),
            pltpu.VMEM((length, value), f32),
            pltpu.VMEM((length, value), f32),
            pltpu.VMEM(starts.shape, f32),
            pltpu.VMEM((length, channels), jnp.bfloat16),
            pltpu.VMEM((length, value), jnp.bfloat16),
            pltpu.VMEM((length, keys), f32),
            pltpu.SemaphoreType.DMA((5, tiles)),
            pltpu.SemaphoreType.DMA((7,)),
            pltpu.VMEM((length, value), f32),
            pltpu.VMEM((length, channels), f32),
            pltpu.VMEM((heads, DV, DK), f32),
            pltpu.VMEM((tiles, heads, DV, DK), f32),
            pltpu.VMEM((8, channels), f32),
            pltpu.VMEM((2, 8, channels), f32),
            pltpu.VMEM((16, channels), f32),
        ]
        + chain_scratch(sizes, heads * DV // TILE, length)
        + [pltpu.SemaphoreType.DMA((2,))]
        + scatter_scratch(sizes, plan, depth, TILE, jnp.bfloat16),
        compiler_params=pltpu.CompilerParams(
            collective_id=5, has_side_effects=True, vmem_limit_bytes=60 << 20
        ),
    )(proj, halo, conv, cum, logits, o, gate, du, starts, cols, rows, taps, gain, *grads)


def tail_kernel(
    n,
    sizes,
    plan,
    shared,
    taken,
    inv_ref,
    early_ref,
    later_ref,
    dproj_ref,
    dgate_ref,
    normed_ref,
    dlogits_ref,
    lowrank_ref,
    upper_ref,
    down_ref,
    gain_ref,
    gains_two_ref,
    dtaps_ref,
    dhead_ref,
    w_ref,
    tokens_ref,
    dh_ref,
    left_ref,
    out_ref,
    small_out,
    grad_ref,
    left_out,
    grads,
    weights,
    tokens,
    dh,
    total,
    trade,
    fin,
    send,
    small,
    wide,
    narrow,
    b_sem,
    a_send,
    a_recv,
    s_send,
    s_recv,
    l_sem,
    *refs,
):
    me, core = lax.axis_index("seq"), lax.axis_index("head")
    slots, _, rows, bw = out_ref.shape
    length, width = normed_ref.shape
    channels = dproj_ref.shape[1]
    keys, rank, tap_count = dlogits_ref.shape[1], down_ref.shape[0], 4
    downs = early_ref.shape[0] - taken
    count = fin.shape[0] - 1 - early_ref.shape[0] - later_ref.shape[0]
    tiles = s_send.shape[0]
    step_rows = length // tiles
    f32 = jnp.float32
    dot = functools.partial(lax.dot_general, preferred_element_type=f32)
    announce(n, me, True)
    loads = [
        pltpu.make_async_copy(source, target, l_sem.at[1 + q])
        for q, (source, target) in enumerate(((w_ref, weights), (tokens_ref, tokens), (dh_ref, dh)))
    ]
    for load in loads:
        load.start()
    block = wide.shape[1]
    per_slot = left_ref.shape[1] // block
    total_blocks = left_ref.shape[0] * per_slot

    def basis_load(k):
        at = (k // per_slot, pl.ds(k % per_slot * block, block))
        return pltpu.make_async_copy(left_ref.at[at], wide.at[k % 2], b_sem.at[k % 2])

    def basis_store(k):
        at = (k // per_slot, pl.ds(k % per_slot * block, block))
        return pltpu.make_async_copy(narrow.at[k % 2], left_out.at[at], b_sem.at[2 + k % 2])

    pending = list(range(total_blocks))

    def narrow_basis(count):
        for k in pending[:count]:
            basis_load(k).wait()
            if k >= 2:
                basis_store(k - 2).wait()
            narrow[k % 2] = wide[k % 2].astype(narrow.dtype)
            basis_store(k).start()
            if k + 2 < total_blocks:
                basis_load(k + 2).start()
        del pending[:count]

    for k in range(min(2, total_blocks)):
        basis_load(k).start()
    steps, sent = scatter_steps(sizes, plan, [grads], refs[:-5], fin, bw, in_place=True)
    sums = sum_steps(sizes, shared, small, small_out, *refs[-5:])

    def block_grads(lo, hi):
        for source, base in ((dproj_ref, 0), (dgate_ref, channels)):
            first, last = max(lo - base, 0), min(hi - base, source.shape[1])
            if first >= last:
                continue

            part = dot(normed_ref[...], source[:, first:last], dimension_numbers=TN)
            grads[:, :, :, :, base + first : base + last] = part.astype(grads.dtype).reshape(
                sizes + (rows, last - first)
            )

    cut = max(hi for _, _, hi, _, _, group in plan if group == 0) * bw
    block_grads(0, cut)
    pl.semaphore_wait(pltpu.get_barrier_semaphore(), n)
    steps[0]()
    block_grads(cut, grads.shape[4])
    steps[1]()
    fin[fin.shape[0] - 1] = jnp.zeros(fin.shape[1:], fin.dtype)
    if taken:
        fin[count : count + taken] = early_ref[downs:]
    fin[count + taken : fin.shape[0] - 1 - downs] = later_ref[...]
    fin[fin.shape[0] - 1 - downs : fin.shape[0] - 1] = early_ref[0:downs]

    def swap(t):
        at = pl.ds(t * step_rows, step_rows)
        return pltpu.make_async_remote_copy(
            src_ref=total.at[at],
            dst_ref=trade.at[at],
            send_sem=s_send.at[t],
            recv_sem=s_recv.at[t],
            device_id={"head": 1 - core},
            device_id_type=MESH,
        )

    for load in loads:
        load.wait()
    upper = halves(upper_ref[0:rank, :])
    down_low = down_ref[...].astype(jnp.bfloat16)
    small[...] = jnp.zeros_like(small)
    upper_grad = jnp.zeros((rank, keys), f32)
    bias_grad = jnp.zeros((1, keys), f32)
    for t in range(tiles):
        at = slice(t * step_rows, (t + 1) * step_rows)
        dlogits = dlogits_ref[at, :]
        parts = halves(dlogits)
        dlow = product(parts, upper, NT).astype(jnp.bfloat16)
        upper_grad += product(halves(lowrank_ref[at, :]), parts, TN)
        bias_grad += jnp.sum(dlogits, axis=0, keepdims=True)
        small[0:rank, :] += dot(dlow, normed_ref[at, :], dimension_numbers=TN)
        part = (
            dot(dproj_ref[at, :], weights[:, :channels], dimension_numbers=NT)
            + dot(dgate_ref[at, :], weights[:, channels:], dimension_numbers=NT)
            + dot(dlow, down_low, dimension_numbers=NN)
        )
        total[at, :] = part.astype(total.dtype)
        swap(t).start()
        tok = tokens[at, :].astype(f32)
        inverse = lax.rsqrt(jnp.mean(tok * tok, axis=1, keepdims=True) + norm_epsilon)
        small[rank + 1 : rank + 2, :] += jnp.sum(part * (tok * inverse), axis=0, keepdims=True)
    small[rank : rank + 1, 0:DV] = dhead_ref[0:1, :]
    small[shared : shared + 1, :] = gains_two_ref[0:1, :]
    small[shared + 1 : shared + 1 + tap_count, :] = dtaps_ref[0:tap_count, :]
    per = width // keys
    base = shared + 1 + tap_count
    for r in range(rank + 1):
        row = bias_grad if r == rank else upper_grad[r : r + 1]
        small[base + r // per : base + r // per + 1, (r % per) * keys : (r % per + 1) * keys] = row
    sums[0]()
    narrow_basis(2)
    steps[2]()
    sums[1]()

    for t in range(tiles):
        at = slice(t * step_rows, (t + 1) * step_rows)
        swap(t).wait_recv()
        dxn = total[at, :].astype(f32) + trade[at, :].astype(f32)
        tok = tokens[at, :].astype(f32)
        inverse = lax.rsqrt(jnp.mean(tok * tok, axis=1, keepdims=True) + norm_epsilon)
        scaled = gain_ref[0:1, :] * dxn
        mean = jnp.mean(scaled * tok, axis=1, keepdims=True)
        dh[at, :] = dh[at, :] + (
            inverse * scaled - tok * (inverse * inverse * inverse * mean)
        )
    store = pltpu.make_async_copy(dh, grad_ref, l_sem.at[4])
    store.start()
    for s, step in enumerate(steps[3:]):
        narrow_basis(3)
        step()
        if s + 2 < len(sums):
            sums[s + 2]()
    for s in range(send.shape[0]):
        send[s] = fin[inv_ref[0, s]]

    def move(j):
        p = lax.rem(me + j, n)
        return remote(
            send.at[pl.ds(p * slots, slots)], out_ref.at[:, me], a_send.at[j], a_recv.at[j], p
        )

    for j in range(1, n):
        move(j).start()
    mine = pltpu.make_async_copy(
        send.at[pl.ds(me * slots, slots)], out_ref.at[:, me], l_sem.at[0]
    )
    mine.start()
    for step in sums[len(steps) - 1 :]:
        step()
    narrow_basis(len(pending))
    mine.wait()
    for j in range(1, n):
        move(j).wait()
    sent()
    for k in range(max(0, total_blocks - 2), total_blocks):
        basis_store(k).wait()
    for t in range(tiles):
        swap(t).wait_send()
    store.wait()


def tail(
    inverse, early, later, dproj, dgate, normed, dlogits, lowrank, upper, down, gain, gains_two,
    dtaps, dhead, weights, tokens, dh, left, slots, taken
):
    n = lax.axis_size("seq")
    sizes = axis_sizes(n)
    most = max(sizes)
    length, width = normed.shape
    _, rows, bw = early.shape
    columns = dproj.shape[1] + dgate.shape[1]
    blocks = columns // bw
    rank = down.shape[0]
    shared = rank + 8
    plan = build_plan((blocks,), SHARES, 3, SPREAD)
    shape = jax.ShapeDtypeStruct
    vmem, anywhere = pl.BlockSpec(memory_space=pltpu.VMEM), pl.BlockSpec(memory_space=pl.ANY)
    b16, f32 = jnp.bfloat16, jnp.float32
    small = (shared + 16, width)
    tiles = 4
    out, summed, grad, left = pl.pallas_call(
        functools.partial(tail_kernel, n, sizes, plan, shared, taken),
        out_shape=(
            shape((slots, n, rows, bw), b16),
            shape(small, f32),
            shape((length, width), f32),
            shape(left.shape, b16),
        ),
        in_specs=[pl.BlockSpec(memory_space=pltpu.SMEM)] + [vmem] * 13 + [anywhere] * 4,
        out_specs=(anywhere, vmem, anywhere, anywhere),
        scratch_shapes=[
            pltpu.VMEM(sizes + (rows, columns), b16),
            pltpu.VMEM((width, columns), b16),
            pltpu.VMEM((length, width), b16),
            pltpu.VMEM((length, width), f32),
            pltpu.VMEM((length, width), b16),
            pltpu.VMEM((length, width), b16),
            pltpu.VMEM((blocks + early.shape[0] + later.shape[0] + 1, rows, bw), b16),
            pltpu.VMEM((slots * n, rows, bw), b16),
            pltpu.VMEM(small, f32),
            pltpu.VMEM((2, width // 4, width), f32),
            pltpu.VMEM((2, width // 4, width), b16),
            pltpu.SemaphoreType.DMA((4,)),
            pltpu.SemaphoreType.DMA((n,)),
            pltpu.SemaphoreType.DMA((n,)),
            pltpu.SemaphoreType.DMA((tiles,)),
            pltpu.SemaphoreType.DMA((tiles,)),
            pltpu.SemaphoreType.DMA((5,)),
        ]
        + scatter_scratch(sizes, plan, rows, bw, b16, in_place=True)
        + [
            pltpu.VMEM((shared, width), f32),
            pltpu.VMEM((3,) + small, f32),
            pltpu.VMEM((3, most) + small, f32),
            pltpu.SemaphoreType.DMA((1 + 3 * most,)),
            pltpu.SemaphoreType.DMA((1 + 3 * most,)),
        ],
        compiler_params=pltpu.CompilerParams(
            collective_id=2, has_side_effects=True, vmem_limit_bytes=60 << 20
        ),
    )(
        inverse, early, later, dproj, dgate, normed, dlogits, lowrank, upper, down, gain, gains_two,
        dtaps, dhead, weights, tokens, dh, left
    )
    return out.reshape(slots, width, bw), summed, grad, left


def adam_kernel(
    rates,
    rank,
    taps,
    grad_ref,
    left_ref,
    right_ref,
    master_ref,
    first_ref,
    second_ref,
    summed_ref,
    *refs,
):
    params = [refs[3 * q : 3 * q + 3] for q in range(5)]
    grad_in, result_in = refs[15:17]
    grad_out, master_out, first_out, second_out, copy_out = refs[17:22]
    news = [refs[22 + 4 * q : 26 + 4 * q] for q in range(5)]
    grad_pass, result_ref = refs[42:]
    grad_pass[...] = grad_in[...]
    result_ref[...] = result_in[...]

    @pl.when(pl.program_id(0) == 0)
    def _():
        shared = rank + 8
        width = summed_ref.shape[1]
        keys = news[2][0].shape[1]
        per = width // keys
        base = shared + 1 + taps
        gains, down, upper, head, conv = news
        gains[0][0:1, :] = summed_ref[rank + 1 : rank + 2, :]
        gains[0][1:2, :] = summed_ref[shared : shared + 1, :]
        down[0][...] = summed_ref[0:rank, :]
        for r in range(rank + 1):
            upper[0][r : r + 1, :] = summed_ref[
                base + r // per : base + r // per + 1, (r % per) * keys : (r % per + 1) * keys
            ]
        head[0][...] = summed_ref[rank : rank + 1, 0:DV]
        conv[0][...] = summed_ref[shared + 1 : shared + 1 + taps, :]
        for (value, first, second), new, rate in zip(params, news, rates, strict=True):
            new[1][...], new[2][...], new[3][...] = plain_adam(
                value[...], new[0][...], first[...], second[...], rate
            )

    width = left_ref.shape[1]
    step = min(256, width)
    dot = functools.partial(
        lax.dot_general, dimension_numbers=TN, preferred_element_type=jnp.float32
    )
    grad_out[0] = grad_ref[0].astype(jnp.float32)
    left = left_ref[0]
    dot = functools.partial(lax.dot_general, preferred_element_type=jnp.float32)
    right = halves(right_ref[0])
    rotated = dot(left, grad_ref[0], dimension_numbers=TN)
    rotated = product(halves(rotated), right, NN)
    first = moment_decay * first_ref[0] + (1.0 - moment_decay) * rotated
    second = moment_decay * second_ref[0] + (1.0 - moment_decay) * rotated * rotated
    first_out[0] = first
    second_out[0] = second
    direction = first / (jnp.sqrt(second) + adam_epsilon)
    turned = product(halves(direction), right, NT).astype(left.dtype)
    master = master_ref[0] - rate_block * dot(left, turned, dimension_numbers=NN)
    master_out[0] = master
    copy_out[0] = master.astype(copy_out.dtype)


def all_adam(grads, left, right, master, first, second, summed, params, grad, result):
    slots, width, columns = master.shape
    tall = pl.BlockSpec((1, width, columns), lambda i: (i, 0, 0))
    length, model = grad.shape
    wide = pl.BlockSpec((length // slots, model), lambda i: (i, 0))
    shape = jax.ShapeDtypeStruct
    full = shape(master.shape, jnp.float32)

    def whole(array):
        return pl.BlockSpec(array.shape, lambda i: (0, 0))

    flat = [array for triple in params for array in triple]
    rates = (rate_gains, rate_down, rate_upper, rate_head, rate_conv)
    news = [triple[0] for triple in params for _ in range(4)]
    return pl.pallas_call(
        functools.partial(adam_kernel, rates, params[1][0].shape[0], params[4][0].shape[0]),
        grid=(slots,),
        out_shape=tuple(
            [full] * 4
            + [shape(master.shape, jnp.bfloat16)]
            + [shape(new.shape, new.dtype) for new in news]
            + [shape(grad.shape, jnp.float32), shape(grad.shape, jnp.bfloat16)]
        ),
        in_specs=[
            tall,
            pl.BlockSpec((1, width, width), lambda i: (i, 0, 0)),
            pl.BlockSpec((1, columns, columns), lambda i: (i, 0, 0)),
            tall,
            tall,
            tall,
            whole(summed),
        ]
        + [whole(array) for array in flat]
        + [wide] * 2,
        out_specs=[tall] * 5 + [whole(new) for new in news] + [wide] * 2,
        compiler_params=pltpu.CompilerParams(vmem_limit_bytes=56 << 20),
    )(grads, left, right, master, first, second, summed, *flat, grad, result)


def middle_kernel(
    n,
    sizes,
    plan,
    u_ref,
    w_out_ref,
    cols_ref,
    gain_ref,
    tokens_ref,
    w_up_ref,
    w_down_ref,
    cot_ref,
    early_ref,
    sum_ref,
    result_out,
    dh_out,
    du_out,
    g_up_out,
    g_out_out,
    w_up,
    w_down,
    mixed,
    hidden_sum,
    normed,
    inv,
    dy,
    hid,
    dpair,
    send,
    recv,
    g_down,
    g_up,
    g_out,
    du,
    free,
    s_sem,
    r_sem,
    l_sem,
    *scatter_refs,
):
    me, core = lax.axis_index("seq"), lax.axis_index("head")
    length, width = normed.shape
    inner = hid.shape[1]
    rows = g_out.shape[3]
    f32 = jnp.float32
    dot = functools.partial(lax.dot_general, preferred_element_type=f32)
    tiles = s_sem.shape[0] // 3
    block = length // tiles
    ats = [slice(t * block, (t + 1) * block) for t in range(tiles)]
    enter(n, me, True)
    loads = [
        pltpu.make_async_copy(source, target, l_sem.at[q])
        for q, (source, target) in enumerate(
            ((tokens_ref, mixed), (w_up_ref, w_up), (w_down_ref, w_down), (cot_ref, dy))
        )
    ]
    for load in loads:
        load.start()
    flushes = []

    def flush(source, target):
        copy = pltpu.make_async_copy(source, target, l_sem.at[4 + len(flushes)])
        copy.start()
        flushes.append(copy)

    steps, sent = scatter_steps(
        sizes, plan, [g_down, g_up], scatter_refs, early_ref, TILE, in_place=True
    )

    def advance(count=1):
        for step in steps[:count]:
            step()
        del steps[:count]

    def swap(phase, t):
        at = pl.ds(t * block, block)
        return pltpu.make_async_remote_copy(
            src_ref=send.at[at],
            dst_ref=recv.at[at],
            send_sem=s_sem.at[phase * tiles + t],
            recv_sem=r_sem.at[phase * tiles + t],
            device_id={"head": 1 - core},
            device_id_type=MESH,
        )

    def exchange(phase, left, right, close):
        if phase:
            for t in range(tiles):
                swap(phase - 1, t).wait_send()
            pl.semaphore_wait(free, 1)
        for t, at in enumerate(ats):
            send[at, :] = dot(left[at, :], right[...], dimension_numbers=NT).astype(send.dtype)
            swap(phase, t).start()
            if t:
                swap(phase, t - 1).wait_recv()
                close(ats[t - 1])
        swap(phase, tiles - 1).wait_recv()
        close(ats[-1])
        if phase < 2:
            pl.semaphore_signal(
                free, inc=1, device_id={"head": 1 - core}, device_id_type=MESH
            )

    def both(at):
        return send[at, :].astype(f32) + recv[at, :].astype(f32)

    loads[0].wait()

    def close_attn(at):
        total = mixed[at, :].astype(f32) + both(at)
        inverse = lax.rsqrt(jnp.mean(total * total, axis=1, keepdims=True) + norm_epsilon)
        hidden_sum[at, :] = total
        inv[at, :] = inverse
        normed[at, :] = (total * inverse * gain_ref[1:2, :]).astype(normed.dtype)

    exchange(0, u_ref, w_out_ref, close_attn)
    for load in loads[1:]:
        load.wait()

    def feed(t, _):
        at = pl.ds(pl.multiple_of(t * block, block), block)
        x = normed[at, :]
        grad_y = (dy[at, :].astype(f32) * cols_ref[at, 7:8]).astype(dy.dtype)
        dy[at, :] = grad_y
        for lo in range(0, inner, 512):
            hi = min(lo + 512, inner)
            gate = dot(x, w_up[:, lo:hi], dimension_numbers=NN)
            up = dot(x, w_up[:, inner + lo : inner + hi], dimension_numbers=NN)
            grad = dot(grad_y, w_down[:, lo:hi], dimension_numbers=NN)
            sig = sigmoid(gate)
            swish = gate * sig
            hid[at, lo:hi] = (swish * up).astype(hid.dtype)
            dpair[at, lo:hi] = (grad * up * (sig + swish * (1.0 - sig))).astype(dpair.dtype)
            dpair[at, inner + lo : inner + hi] = (grad * swish).astype(dpair.dtype)
        return 0

    lax.fori_loop(0, tiles, feed, 0)

    def block_grads(left, source, target, lo, hi):
        for first in range(lo, hi, 512):
            last = min(first + 512, hi)
            part = dot(left[...], source[:, first:last], dimension_numbers=TN)
            target[:, :, :, :, first:last] = part.astype(target.dtype).reshape(
                sizes + (rows, last - first)
            )

    block_grads(dy, hid, g_down, 0, inner)
    advance()
    block_grads(normed, dpair, g_up, 0, inner)
    advance()
    block_grads(normed, dpair, g_up, inner, 2 * inner)
    taken = g_up.shape[4] - g_up_out.shape[4]
    flush(g_up.at[:, :, :, :, pl.ds(taken, g_up_out.shape[4])], g_up_out)

    def close_mlp(at):
        mixed[at, :] = (hidden_sum[at, :] + both(at)).astype(mixed.dtype)

    exchange(1, hid, w_down, close_mlp)
    flush(mixed, result_out)
    advance()

    sum_ref[...] = jnp.zeros_like(sum_ref)

    def close_back(at):
        grad = both(at)
        total, inverse = hidden_sum[at, :], inv[at, :]
        unit = total * inverse
        scaled = gain_ref[1:2, :] * grad
        mean = jnp.mean(scaled * total, axis=1, keepdims=True)
        dh = dy[at, :].astype(f32) + (inverse * scaled - unit * (inverse * inverse * mean))
        hidden_sum[at, :] = dh
        normed[at, :] = dh.astype(normed.dtype)
        sum_ref[0:1, :] += jnp.sum(grad * unit, axis=0, keepdims=True)
        du[at, :] = dot(normed[at, :], w_out_ref[...], dimension_numbers=NN)

    exchange(2, dpair, w_up, close_back)
    flush(hidden_sum, dh_out)
    flush(du, du_out)
    advance()
    block_grads(normed, u_ref, g_out, 0, u_ref.shape[1])
    flush(g_out, g_out_out)
    advance(len(steps))
    sent()
    for t in range(tiles):
        swap(2, t).wait_send()
    for copy in flushes:
        copy.wait()


def middle(u, w_out, cols, gain, tokens, w_up, w_down, cot, taken):
    n = lax.axis_size("seq")
    sizes = axis_sizes(n)
    length, width = tokens.shape
    value, inner = u.shape[1], w_down.shape[1]
    rows = width // n
    f32, b16 = jnp.float32, jnp.bfloat16
    blocks = inner // TILE
    plan = build_plan((blocks, taken) if taken else (blocks,), SHARES, MIDDLE_PIECES, SPREAD)
    shape = jax.ShapeDtypeStruct
    vmem, anywhere = pl.BlockSpec(memory_space=pltpu.VMEM), pl.BlockSpec(memory_space=pl.ANY)
    tiles = 4
    return pl.pallas_call(
        functools.partial(middle_kernel, n, sizes, plan),
        out_shape=(
            shape((blocks + taken, rows, TILE), b16),
            shape((8, width), f32),
            shape((length, width), b16),
            shape((length, width), f32),
            shape((length, value), f32),
            shape(sizes + (rows, 2 * inner - taken * TILE), b16),
            shape(sizes + (rows, value), b16),
        ),
        in_specs=[vmem] * 4 + [anywhere] * 4,
        out_specs=(vmem, vmem) + (anywhere,) * 5,
        scratch_shapes=[
            pltpu.VMEM((width, 2 * inner), b16),
            pltpu.VMEM((width, inner), b16),
            pltpu.VMEM((length, width), b16),
            pltpu.VMEM((length, width), f32),
            pltpu.VMEM((length, width), b16),
            pltpu.VMEM((length, 1), f32),
            pltpu.VMEM((length, width), b16),
            pltpu.VMEM((length, inner), b16),
            pltpu.VMEM((length, 2 * inner), b16),
            pltpu.VMEM((length, width), b16),
            pltpu.VMEM((length, width), b16),
            pltpu.VMEM(sizes + (rows, inner), b16),
            pltpu.VMEM(sizes + (rows, 2 * inner), b16),
            pltpu.VMEM(sizes + (rows, value), b16),
            pltpu.VMEM((length, value), f32),
            pltpu.SemaphoreType.REGULAR,
            pltpu.SemaphoreType.DMA((3 * tiles,)),
            pltpu.SemaphoreType.DMA((3 * tiles,)),
            pltpu.SemaphoreType.DMA((9,)),
        ]
        + scatter_scratch(sizes, plan, rows, TILE, b16, in_place=True),
        compiler_params=pltpu.CompilerParams(
            collective_id=6, has_side_effects=True, vmem_limit_bytes=62 << 20
        ),
    )(u, w_out, cols, gain, tokens, w_up, w_down, cot)


def plain_adam(param, gradient, first, second, rate):
    first_next = moment_decay * first + (1.0 - moment_decay) * gradient
    second_next = moment_decay * second + (1.0 - moment_decay) * gradient * gradient
    return (
        param - rate * first_next / (jnp.sqrt(second_next) + adam_epsilon),
        first_next,
        second_next,
    )


def body(
    tokens,
    cotangent,
    lengths,
    packing,
    owners,
    slot_copy,
    slot_master,
    slot_first,
    slot_second,
    basis_left,
    basis_right,
    norm_gains,
    gains_first,
    gains_second,
    gate_down,
    down_first,
    down_second,
    gate_up,
    upper_first,
    upper_second,
    head_gain,
    head_first,
    head_second,
    conv_weight,
    conv_first,
    conv_second,
):
    tok_rows = tokens.shape[0]
    model_width = tokens.shape[1]
    block_width = slot_copy.shape[2]
    tap_count = conv_weight.shape[0]
    key_width = gate_up.shape[1]
    channels = conv_weight.shape[1]
    value_width = channels - 2 * key_width
    block_total = owners.shape[1]
    count_in = (channels + value_width) // block_width
    count_out = value_width // block_width
    count_down = (block_total - count_in - count_out) // 3
    count_up = 2 * count_down
    (in_weights, up_weights, out_weights, down_weights), kept = forward(
        owners,
        lengths,
        packing,
        slot_copy,
        tokens,
        norm_gains,
        gate_down.T,
        gate_up,
        conv_weight,
        head_gain[None],
        (count_in, count_up, count_out, count_down),
    )
    normed, lowrank, logits, mixed_proj, halo, gate_pre = kept[:6]
    conv_pre, cumulative, attended, gated_out, starts, cols, rows = kept[6:]
    gain_row = head_gain[None]
    early, gains_two, result, grad_one, grad_gated, grad_up, grad_out = middle(
        gated_out,
        out_weights,
        cols,
        norm_gains,
        tokens,
        up_weights,
        down_weights,
        cotangent,
        MIDDLE_TAKEN,
    )
    grad_mixed, grad_gate_pre, grad_logits, tap_grads, gain_grads, later = recurrence_back(
        mixed_proj,
        halo,
        conv_pre,
        cumulative,
        logits,
        attended,
        gate_pre,
        grad_gated,
        starts,
        cols,
        rows,
        conv_weight,
        gain_row,
        (grad_up, grad_out),
    )
    slots_dev = slot_copy.shape[0]
    slot_total = slots_dev * lax.axis_size("seq")
    named = jnp.arange(slot_total, dtype=jnp.int32)[:, None] == owners
    inverse = jnp.where(
        jnp.any(named, axis=1),
        jnp.sum(named * jnp.arange(block_total, dtype=jnp.int32), axis=1),
        block_total,
    ).astype(jnp.int32)[None]
    owned_grads, summed, grad_input, left_low = tail(
        inverse,
        early,
        later,
        grad_mixed,
        grad_gate_pre,
        normed,
        grad_logits,
        lowrank,
        gate_up,
        gate_down.T,
        norm_gains,
        gains_two,
        tap_grads,
        gain_grads,
        in_weights,
        tokens,
        grad_one,
        basis_left,
        slots_dev,
        MIDDLE_TAKEN,
    )
    params = (
        (norm_gains, gains_first, gains_second),
        (gate_down.T, down_first.T, down_second.T),
        (gate_up, upper_first, upper_second),
        (head_gain[None], head_first[None], head_second[None]),
        (conv_weight, conv_first, conv_second),
    )
    (
        owned_grads,
        master_next,
        first_next,
        second_next,
        copy_next,
        *small_next,
        grad_input,
        result,
    ) = all_adam(
        owned_grads,
        left_low,
        basis_right,
        slot_master,
        slot_first,
        slot_second,
        summed,
        params,
        grad_input,
        result,
    )
    for q in range(4, 8):
        small_next[q] = small_next[q].T
    for q in range(12, 16):
        small_next[q] = small_next[q][0]
    return (
        result,
        grad_input,
        owned_grads,
        master_next,
        first_next,
        second_next,
        copy_next,
        *small_next,
    )


def solution(mesh):
    placed = (
        P("seq", None),
        P("seq", None),
        P(),
        P(),
        P("head", None),
        P(("seq", "head"), None, None),
        P(("seq", "head"), None, None),
        P(("seq", "head"), None, None),
        P(("seq", "head"), None, None),
        P(("seq", "head"), None, None),
        P(("seq", "head"), None, None),
        P(),
        P(),
        P(),
        P(),
        P(),
        P(),
        P(None, "head"),
        P(None, "head"),
        P(None, "head"),
        P(),
        P(),
        P(),
        P(None, "head"),
        P(None, "head"),
        P(None, "head"),
    )
    return jax.shard_map(
        body,
        mesh=mesh,
        in_specs=placed,
        out_specs=(
            P("seq", None),
            P("seq", None),
            P(("seq", "head"), None, None),
            P(("seq", "head"), None, None),
            P(("seq", "head"), None, None),
            P(("seq", "head"), None, None),
            P(("seq", "head"), None, None),
            P(),
            P(),
            P(),
            P(),
            P(),
            P(),
            P(),
            P(),
            P(None, "head"),
            P(None, "head"),
            P(None, "head"),
            P(None, "head"),
            P(),
            P(),
            P(),
            P(),
            P(None, "head"),
            P(None, "head"),
            P(None, "head"),
            P(None, "head"),
        ),
        check_vma=False,
    )
```
